32 devices in a mesh: dp: 8 (over z, y), seq: 4 (over x, core).
Axes of the slice: x: 2, y: 2, z: 4, core: 2. Of those that a mesh axis runs over, the one named last changes fastest.
Arguments:
- states: bfloat16 [8, 2560, 768], P('dp', 'seq'), may hold values from -6 to 6
- lengths: int32 [8], P('dp'), may hold values from 640 to 2560, as said below
- teacher: bfloat16 [8, 2560, 768], P('dp', 'seq'), may hold values from -6 to 6
- out_grad: bfloat16 [8, 2560, 768], P('dp', 'seq'), may hold values from -6 to 6
- q_weight: bfloat16 [768, 192], P('dp'), may hold values from -0.4375 to 0.4375
- k_weight: bfloat16 [768, 192], P('dp'), may hold values from -0.4375 to 0.4375
- v_weight: bfloat16 [768, 192], P('dp'), may hold values from -0.4375 to 0.4375
- q_bias: bfloat16 [768], P('dp'), may hold values from -0.59765625 to 0.59765625
- v_bias: bfloat16 [768], P('dp'), may hold values from -0.119628906 to 0.119628906
- o_weight: bfloat16 [768, 768], P('dp'), may hold values from -6 to 6
- o_bias: bfloat16 [768], P('dp'), may hold values from -0.59765625 to 0.59765625
- attn_gain: bfloat16 [768], P('dp'), may hold values from 0.5 to 1.5
- attn_bias: bfloat16 [768], P('dp'), may hold values from -0.59765625 to 0.59765625
- up_weight: bfloat16 [768, 768], P('dp'), may hold values from -0.4375 to 0.4375
- up_bias: bfloat16 [3072], P('dp'), may hold values from -0.59765625 to 0.59765625
- down_weight: bfloat16 [3072, 192], P('dp'), may hold values from -0.21875 to 0.21875
- down_bias: bfloat16 [768], P('dp'), may hold values from -0.59765625 to 0.59765625
- ffn_gain: bfloat16 [768], P('dp'), may hold values from 0.5 to 1.5
- ffn_bias: bfloat16 [768], P('dp'), may hold values from -0.59765625 to 0.59765625
Outputs:
- layer_out: bfloat16 [8, 2560, 768], P('dp', 'seq')
- loss_value: float32 [], replicated
- states_grad: bfloat16 [8, 2560, 768], P('dp', 'seq')
- grad_qw: float32 [768, 192], P('dp')
- grad_kw: float32 [768, 192], P('dp')
- grad_vw: float32 [768, 192], P('dp')
- grad_qb: float32 [768], P('dp')
- grad_vb: float32 [768], P('dp')
- grad_ow: float32 [768, 768], P('dp')
- grad_ob: float32 [768], P('dp')
- grad_ag: float32 [768], P('dp')
- grad_ab: float32 [768], P('dp')
- grad_uw: float32 [768, 768], P('dp')
- grad_ub: float32 [3072], P('dp')
- grad_dw: float32 [3072, 192], P('dp')
- grad_db: float32 [768], P('dp')
- grad_fg: float32 [768], P('dp')
- grad_fb: float32 [768], P('dp')
The draws below stay inside these ranges and needn't reach their ends.
Inputs may be any that keep to these rules, and one draw needn't show every extreme that they name: `lengths`: every length is an integer from integers from 640 to 2560; some row has exactly 2560 and some other row exactly 640.
All inputs are finite; a program needn't handle non-finite values.
Results may differ from the reference program's by a relative error of at most 0.017.
Values may be sent and summed in bfloat16 or wider, within the bound.
A program may use at most 128 MiB of HBM per device.

```python
import jax
import jax.numpy as jnp
from jax import lax

D = 768
HEADS = 12
HDIM = 64
FF = 3072
GROUPS = 4
SLOTS = 2560
MINLEN = 640
QBLK = 512
ROWS = 8


def draw_lengths(key, part):
    first_key = jax.random.fold_in(key, 11)
    second_key = jax.random.fold_in(key, 12)
    third_key = jax.random.fold_in(key, 13)
    drawn = jax.random.randint(first_key, (ROWS,), MINLEN, SLOTS + 1, dtype=jnp.int32)
    longest = jax.random.randint(second_key, (), 0, ROWS, dtype=jnp.int32)
    offset = jax.random.randint(third_key, (), 1, ROWS, dtype=jnp.int32)
    shortest = (longest + offset) % ROWS
    row_ids = jnp.arange(ROWS, dtype=jnp.int32)
    drawn = jnp.where(row_ids == longest, SLOTS, drawn)
    drawn = jnp.where(row_ids == shortest, MINLEN, drawn)
    return drawn.astype(jnp.int32)


def block_levels(rng, extent, cuts, least, top_value):
    factor_of = 1.0
    for axis_at, blocks in cuts:
        steps = jax.random.uniform(jax.random.fold_in(jax.random.fold_in(rng, 6), axis_at), (blocks,), jnp.float32, least / len(cuts), top_value / len(cuts))
        factor_of = factor_of * jnp.repeat(jnp.exp(steps), extent[axis_at] // blocks).reshape((-1,) + (1,) * (len(extent) - 1 - axis_at))
    return factor_of


def bell_draw(key, shape, scale, most, split=(), kind=jnp.bfloat16):
    level = block_levels(key, shape, split, -0.22, 0.18) if split else 1.0
    entries = jax.random.normal(key, shape, jnp.float32) * scale * level
    return jnp.minimum(jnp.maximum(entries, -most), most).astype(kind)


def setup_inputs(seed: int = 0) -> dict:
    splits = jax.random.split(jax.random.key(seed), 20)
    return {
        "states": bell_draw(splits[0], (ROWS, SLOTS, D), 1.0, 6.0, ((0, 8), (1, 4))),
        "lengths": draw_lengths(jax.random.fold_in(splits[19], 71), 0),
        "teacher": bell_draw(splits[2], (ROWS, SLOTS, D), 1.0, 6.0, ((0, 8), (1, 4))),
        "out_grad": bell_draw(splits[3], (ROWS, SLOTS, D), 1.0, 6.0, ((0, 8), (1, 4))),
        "q_weight": bell_draw(splits[4], (D, D // GROUPS), (D // GROUPS) ** -0.5, 0.4375, ((0, 8),)),
        "k_weight": bell_draw(splits[5], (D, D // GROUPS), (D // GROUPS) ** -0.5, 0.4375, ((0, 8),)),
        "v_weight": bell_draw(splits[6], (D, D // GROUPS), (D // GROUPS) ** -0.5, 0.4375, ((0, 8),)),
        "q_bias": bell_draw(splits[7], (D,), 0.1, 0.59765625, ((0, 8),)),
        "v_bias": bell_draw(splits[8], (D,), 0.02, 0.119628906, ((0, 8),)),
        "o_weight": bell_draw(splits[9], (D, D), 1.0, 6.0, ((0, 8),)),
        "o_bias": bell_draw(splits[10], (D,), 0.1, 0.59765625, ((0, 8),)),
        "attn_gain": jnp.clip(1.0 + 0.1 * jax.random.normal(splits[11], (D,), jnp.float32), 0.5, 1.5).astype(jnp.bfloat16),
        "attn_bias": bell_draw(splits[12], (D,), 0.1, 0.59765625, ((0, 8),)),
        "up_weight": bell_draw(splits[13], (D, FF // GROUPS), (D // GROUPS) ** -0.5, 0.4375, ((0, 8),)),
        "up_bias": bell_draw(splits[14], (FF,), 0.1, 0.59765625, ((0, 8),)),
        "down_weight": bell_draw(splits[15], (FF, D // GROUPS), (FF // GROUPS) ** -0.5, 0.21875, ((0, 8),)),
        "down_bias": bell_draw(splits[16], (D,), 0.1, 0.59765625, ((0, 8),)),
        "ffn_gain": jnp.clip(1.0 + 0.1 * jax.random.normal(splits[17], (D,), jnp.float32), 0.5, 1.5).astype(jnp.bfloat16),
        "ffn_bias": bell_draw(splits[18], (D,), 0.1, 0.59765625, ((0, 8),)),
    }


@jax.custom_vjp
def low(v):
    return lax.optimization_barrier(v.astype(jnp.bfloat16)).astype(jnp.float32)

@jax.custom_vjp
def low_back(v):
    return v

def low_keep(v):
    return (low(v), None)

def low_pass(kept, grad):
    return (grad,)

def back_keep(v):
    return (v, None)

def back_low(kept, grad):
    return (low(grad),)
low.defvjp(low_keep, low_pass)
low_back.defvjp(back_keep, back_low)
EPSILON = 1e-12
NEG_FILL = -1e+30

def layer_norm(values, gain, shift):
    center = values - lax.optimization_barrier(jnp.mean(values, axis=-1, keepdims=True))
    spread = lax.optimization_barrier(jnp.mean(center * center, axis=-1, keepdims=True))
    return center * lax.rsqrt(spread + EPSILON) * gain + shift

def gelu_exact(values):
    return 0.5 * values * (1.0 + lax.erf(values * 0.7071067811865476))

def group_conv(values, weight, groups):
    tok_count = values.shape[0]
    in_width = values.shape[1]
    left_side = values.reshape(tok_count, groups, in_width // groups)
    right_side = weight.reshape(groups, in_width // groups, weight.shape[1])
    result = jnp.einsum('ngi,gio->ngo', left_side, right_side, precision=lax.Precision.HIGHEST)
    return result.reshape(tok_count, groups * weight.shape[1])

def row_forward(params, states, live, teacher):
    q_weight, k_weight, v_weight, q_bias, v_bias, o_weight, o_bias, attn_gain, attn_bias, up_weight, up_bias, down_weight, down_bias, ffn_gain, ffn_bias = params
    factor = HDIM ** (-0.5)
    query = low(low_back(group_conv(states, q_weight, GROUPS) + q_bias))
    keys_all = low(low_back(group_conv(states, k_weight, GROUPS)))
    values = low(low_back(group_conv(states, v_weight, GROUPS) + v_bias))
    key_heads = keys_all.reshape(SLOTS, HEADS, HDIM)
    value_heads = values.reshape(SLOTS, HEADS, HDIM)

    def block_attend(query_block):
        scores = jnp.einsum('qhd,khd->hqk', query_block, key_heads, precision=lax.Precision.HIGHEST) * factor
        scores = low_back(scores)
        scores = jnp.where(live[None, None, :], scores, NEG_FILL)
        shifted = jnp.exp(scores - lax.optimization_barrier(jnp.max(scores, axis=-1, keepdims=True)))
        weights = low(shifted / lax.optimization_barrier(jnp.sum(shifted, axis=-1, keepdims=True)))
        return jnp.einsum('hqk,khd->qhd', weights, value_heads, precision=lax.Precision.HIGHEST)
    attended = lax.map(jax.checkpoint(block_attend), query.reshape(SLOTS // QBLK, QBLK, HEADS, HDIM))
    context = low(low_back(attended.reshape(SLOTS, D)))
    attn_out = low_back(jnp.dot(context, o_weight, precision=lax.Precision.HIGHEST) + o_bias)
    first_out = layer_norm(states + attn_out, attn_gain, attn_bias)
    inner = low_back(group_conv(low(first_out), up_weight, GROUPS) + up_bias)
    activated = low(gelu_exact(inner))
    branch = low_back(group_conv(activated, down_weight, GROUPS) + down_bias)
    layer_full = layer_norm(first_out + branch, ffn_gain, ffn_bias)
    errors = jnp.where(live[:, None], layer_full - teacher, 0.0)
    return (layer_full, jnp.sum(errors * errors))

def reference(states, lengths, teacher, out_grad, q_weight, k_weight, v_weight, q_bias, v_bias, o_weight, o_bias, attn_gain, attn_bias, up_weight, up_bias, down_weight, down_bias, ffn_gain, ffn_bias):
    params = tuple((weight_arg.astype(jnp.float32) for weight_arg in (q_weight, k_weight, v_weight, q_bias, v_bias, o_weight, o_bias, attn_gain, attn_bias, up_weight, up_bias, down_weight, down_bias, ffn_gain, ffn_bias)))
    states_f = states.astype(jnp.float32)
    teacher_f = teacher.astype(jnp.float32)
    slot_ids = jnp.arange(SLOTS, dtype=jnp.int32)
    live_all = slot_ids[None, :] < lengths[:, None]
    token_count = jnp.sum(lengths).astype(jnp.float32)

    def forward(params, states_f):

        def row_step(err_total, row_items):
            row_states, row_teacher, row_live = row_items
            row_out, row_sum = jax.checkpoint(row_forward)(params, row_states, row_live, row_teacher)
            return (err_total + row_sum, row_out)
        err_total, layer_full = lax.scan(row_step, jnp.zeros((), jnp.float32), (states_f, teacher_f, live_all))
        return (layer_full, err_total / (token_count * D))
    (layer_full, loss_value), pull_back = jax.vjp(forward, params, states_f)
    cotangent = out_grad.astype(jnp.float32) * live_all[:, :, None].astype(jnp.float32)
    grads, states_grad = pull_back((cotangent, jnp.ones((), jnp.float32)))
    return (layer_full.astype(jnp.bfloat16), loss_value, states_grad.astype(jnp.bfloat16), grads[0], grads[1], grads[2], grads[3], grads[4], grads[5], grads[6], grads[7], grads[8], grads[9], grads[10], grads[11], grads[12], grads[13], grads[14])
```

```python
import functools
import math

import jax
import jax.numpy as jnp
from jax import lax
from jax.experimental import pallas as pl
from jax.experimental.pallas import tpu as pltpu
from jax.sharding import PartitionSpec as P

HDIM = 64
GROUPS = 4
EPSILON = 1e-12
NEG_FILL = -1e30
LANES = 128
AUG = 16
LOG2E = 1.4426950408889634
MESH = pl.DeviceIdType.MESH
F32 = jnp.float32
BF16 = jnp.bfloat16
VMEM_LIMIT = 60 * 1024 * 1024


def mm(left, right, left_dim, right_dim):
    return lax.dot_general(
        left, right, (((left_dim,), (right_dim,)), ((), ())), preferred_element_type=F32
    )


def iota(shape, dim):
    return lax.broadcasted_iota(jnp.int32, shape, dim)


def remote(src, dst, send_sem, recv_sem, **where):
    return pltpu.make_async_remote_copy(
        src_ref=src,
        dst_ref=dst,
        send_sem=send_sem,
        recv_sem=recv_sem,
        device_id=where,
        device_id_type=MESH,
    )


def three_parts(row):
    high = row.astype(BF16)
    rest = row - high.astype(F32)
    middle = rest.astype(BF16)
    low = (rest - middle.astype(F32)).astype(BF16)
    return high, middle, low


def greet(cfg, me, my_dp, with_dp):
    barrier = pltpu.get_barrier_semaphore()
    count = cfg.seq - 1
    for d in range(1, cfg.seq):
        pl.semaphore_signal(barrier, inc=1, device_id={"seq": me ^ d}, device_id_type=MESH)
    if with_dp:
        count += cfg.dp - 1
        for e in range(1, cfg.dp):
            pl.semaphore_signal(
                barrier, inc=1, device_id={"dp": lax.rem(my_dp + e, cfg.dp)}, device_id_type=MESH
            )
    pl.semaphore_wait(barrier, count)


class Config:
    def __init__(self, dp, seq, piece, width, hidden, shard):
        self.dp, self.seq, self.piece, self.width, self.hidden, self.shard = (
            dp,
            seq,
            piece,
            width,
            hidden,
            shard,
        )
        self.slots = piece * seq
        self.group = width // GROUPS
        self.heads = self.group // HDIM
        self.per_group = dp // GROUPS
        self.split = shard % 32 == 0 and seq == 4
        self.half = shard // 2
        self.quarter = hidden // dp // 4


def attend_kernel(cfg, row, *refs):
    split = cfg.split
    refs = list(refs)
    take = lambda n: [refs.pop(0) for _ in range(n)]
    if split:
        states, small, wq, wk, wv, ow, uw, dw = take(8)
    else:
        states, smalls, wgroup_in = take(3)
    context_r, q_t, k_n, v_n, context_s, x_group, x_own, w_group = take(8)
    if split:
        smalls, gath_ou, gath_d = take(3)
    v_t, scores0, scores1, w_pad = take(4)
    a_send, a_recv, c_send, c_recv = take(4)
    if split:
        w_recv, s_send, s_recv, w_send_sem, w_recv_sem, own_sem = take(6)
        p_send, p_recv, x_send, x_recv, y_send, y_recv, z_send, z_recv = take(8)
    me = lax.axis_index("seq")
    my_dp = lax.axis_index("dp")
    piece, width, group, heads, seq = cfg.piece, cfg.width, cfg.group, cfg.heads, cfg.seq
    slots, shard, n_dp = cfg.slots, cfg.shard, cfg.dp
    order = [d for d in range(seq - 1, -1, -1)]

    for g in range(GROUPS):
        for c in range(0, group, 64):
            x_own[g, c : c + 64, :] = states[:, g * group + c : g * group + c + 64].T

    greet(cfg, me, my_dp, split)

    x_copies = {}
    for d in order[:-1]:
        x_copies[d] = remote(
            x_own.at[me ^ d],
            x_group.at[me, pl.ds(0, group)],
            a_send.at[d],
            a_recv.at[d],
            seq=me ^ d,
        )
        x_copies[d].start()

    if split:
        kinds = (wq, wk, wv)
        my_slot = lax.rem(my_dp, cfg.per_group)
        holder = my_dp // cfg.per_group == me

        def w_copy(kind, e):
            return remote(
                kinds[kind],
                w_recv.at[my_slot, kind],
                w_send_sem.at[e, kind],
                w_recv_sem.at[my_slot, kind],
                dp=lax.rem(my_dp + e, n_dp),
            )

        @pl.when(holder)
        def _():
            for e in range(1, n_dp):
                for kind in range(3):
                    w_copy(kind, e).start()

        s_copies = []
        for e in range(1, n_dp):
            s_copies.append(
                remote(
                    small,
                    smalls.at[my_dp],
                    s_send.at[e],
                    s_recv.at[e],
                    dp=lax.rem(my_dp + e, n_dp),
                )
            )
            s_copies[-1].start()

        xbit, core = me // 2, lax.rem(me, 2)
        half_rows = pl.ds(pl.multiple_of(core * cfg.half, 16), cfg.half)
        quarter_rows = pl.ds(pl.multiple_of(me * cfg.quarter, 16), cfg.quarter)

        def p_pair(e, src):
            target = lax.rem(my_dp + e, n_dp)
            return (
                remote(
                    src.at[half_rows],
                    gath_ou.at[xbit, my_dp, core],
                    p_send.at[e, 0],
                    p_recv.at[e, 0],
                    dp=target,
                ),
                remote(
                    dw.at[quarter_rows],
                    gath_d.at[my_dp, me],
                    p_send.at[e, 1],
                    p_recv.at[e, 1],
                    dp=target,
                ),
            )

        for e in range(1, n_dp):

            @pl.when(xbit == 0)
            def _():
                p_pair(e, ow)[0].start()

            @pl.when(xbit == 1)
            def _():
                p_pair(e, uw)[0].start()

            p_pair(e, ow)[1].start()

        smalls[my_dp] = small[...]
        for x, src in enumerate((ow, uw)):
            for c in range(2):
                gath_ou[x, my_dp, c] = src[c * cfg.half : (c + 1) * cfg.half]
        for q in range(4):
            gath_d[my_dp, q] = dw[q * cfg.quarter : (q + 1) * cfg.quarter]

        @pl.when(holder)
        def _():
            for kind in range(3):
                w_recv[my_slot, kind] = kinds[kind][...]

    x_group[me, 0:group] = x_own[me]

    if split:
        for e in range(1, n_dp):
            s_copies[e - 1].wait_recv()
        for t in range(cfg.per_group):

            @pl.when(me * cfg.per_group + t != my_dp)
            def _():
                for kind in range(3):
                    remote(
                        kinds[kind],
                        w_recv.at[t, kind],
                        w_send_sem.at[0, kind],
                        w_recv_sem.at[t, kind],
                        dp=my_dp,
                    ).wait_recv()

            for kind in range(3):
                w_group[kind, t * shard : (t + 1) * shard] = w_recv[t, kind]
    else:
        for kind in range(3):
            w_group[kind] = wgroup_in[kind]

    cols = heads * LANES
    lane = iota((group, cols), 1)
    spread = jnp.where(
        (((lane >> 7) * HDIM + (lane & 127)) == iota((group, cols), 0)) & ((lane & 127) < HDIM),
        1.0,
        0.0,
    ).astype(BF16)
    for kind in range(3):
        w_pad[kind, 0:group] = mm(w_group[kind], spread, 1, 0).astype(BF16)
    vec_rows = jnp.zeros((AUG, cols), F32)
    lane = iota((LANES, cols), 1)
    source = iota((LANES, cols), 0)
    for t in range(cfg.per_group):
        spread = jnp.where(
            (((lane >> 7) * HDIM + (lane & 127)) == source + t * shard)
            & ((lane & 127) < HDIM)
            & (source < shard),
            1.0,
            0.0,
        ).astype(BF16)
        vec_rows += mm(smalls[me * cfg.per_group + t].astype(BF16), spread, 1, 0)
    row_id = iota((AUG, cols), 0)
    lane = iota((AUG, cols), 1) & 127
    zero = jnp.zeros((AUG, cols), F32)
    first = row_id == 0
    w_pad[0, group : group + AUG] = jnp.where(first, vec_rows[0:1], zero).astype(BF16)
    ones_k = (first & (lane > HDIM) & (lane <= HDIM + 3)) | ((row_id == 1) & (lane == HDIM))
    w_pad[1, group : group + AUG] = jnp.where(ones_k, 1.0, zero).astype(BF16)
    ones_v = (lane >= HDIM) & (lane < HDIM + 3)
    w_pad[2, group : group + AUG] = jnp.where(
        first, jnp.where(ones_v, 1.0, vec_rows[1:2]), zero
    ).astype(BF16)

    length = smalls[my_dp, 12 + row : 13 + row, 0:1]
    aug_row = iota((AUG, piece), 0)
    q_rows = jnp.where(iota((HDIM, piece), 0) == 0, 1.0, 0.0).astype(BF16)
    factor = LOG2E * HDIM**-0.5

    def project(t):
        slot = (iota((AUG, piece), 1) + t * piece).astype(F32)
        mask = jnp.where(slot < length, 0.0, NEG_FILL)
        x_group[t, group : group + AUG] = jnp.where(
            aug_row == 0, 1.0, jnp.where(aug_row == 1, mask, 0.0)
        ).astype(BF16)
        x = x_group[t]
        queries = mm(w_pad[0], x, 0, 0) * factor
        values = mm(w_pad[2], x, 0, 0)
        keys_all = mm(x, w_pad[1], 0, 0)
        values_n = mm(x, w_pad[2], 0, 0)
        at = pl.ds(pl.multiple_of(t * piece, LANES), piece)
        for h in range(heads):
            q_t[h, t, 0:HDIM] = queries[h * LANES : h * LANES + HDIM].astype(BF16)
            q_t[h, t, HDIM:] = q_rows
            v_t[h, :, at] = values[h * LANES : h * LANES + HDIM + AUG].astype(BF16)
            k_n[h, t] = keys_all[:, h * LANES : (h + 1) * LANES].astype(BF16)
            v_n[h, t] = values_n[:, h * LANES : (h + 1) * LANES].astype(BF16)

    def project_step(i, _):
        project(me ^ i)
        return 0

    project(me)
    for d in range(1, seq):
        x_copies[d].wait_recv()
    lax.fori_loop(1, seq, project_step, 0)

    def place(i):
        return me ^ (seq - 1 - i // heads), lax.rem(i, heads)

    def score(i, scores):
        t, h = place(i)
        scores[...] = mm(k_n[h].reshape(slots, LANES), q_t[h, t], 1, 0)

    def finish(i, scores):
        t, h = place(i)
        top = jnp.max(scores[...], axis=0, keepdims=True)
        weights = jnp.exp2(scores[...] - top).astype(BF16)
        result = mm(v_t[h], weights, 1, 0)
        total = result[HDIM : HDIM + 1]
        context_s[t, pl.ds(pl.multiple_of(h * HDIM, HDIM), HDIM)] = (
            result[0:HDIM] / total
        ).astype(BF16)
        lse = top + jnp.log2(total)
        high, middle, low = three_parts(-lse)
        value = jnp.where(aug_row == 0, 1.0, 0.0)
        for r, part in enumerate((high, middle, low)):
            value = jnp.where(aug_row == r + 1, part.astype(F32), value)
        q_t[h, t, HDIM : HDIM + AUG] = value.astype(BF16)

    def c_copy(d):
        return remote(
            context_s.at[me ^ d], context_r.at[me], c_send.at[d], c_recv.at[d], seq=me ^ d
        )

    if split:

        def forward(e):
            src = lax.rem(my_dp + n_dp - e, n_dp)
            ou = gath_ou.at[xbit, src, core]
            dd = gath_d.at[src, me]
            out = []
            for sems, partner in (((x_send, x_recv), me ^ 2), ((y_send, y_recv), me ^ 1)):
                out.append(
                    remote(ou, ou, sems[0].at[e, 0], sems[1].at[e, 0], seq=partner)
                )
                out.append(
                    remote(dd, dd, sems[0].at[e, 1], sems[1].at[e, 1], seq=partner)
                )
            return out

        def onward(e):
            src = lax.rem(my_dp + n_dp - e, n_dp)
            ou = gath_ou.at[1 - xbit, src, core]
            dd = gath_d.at[src, me ^ 2]
            return [
                remote(ou, ou, z_send.at[e, 0], z_recv.at[e, 0], seq=me ^ 1),
                remote(dd, dd, z_send.at[e, 1], z_recv.at[e, 1], seq=me ^ 1),
            ]

        def do_forward(e):
            for copy in p_pair(e, ow):
                copy.wait_recv()
            for copy in forward(e):
                copy.start()

        def do_onward(e):
            for copy in forward(e)[:2]:
                copy.wait_recv()
            for copy in onward(e):
                copy.start()

    blocks = seq * heads
    last = blocks // 2 - 1

    def send_if_done(i):
        d = seq - 1 - i // heads

        @pl.when((lax.rem(i, heads) == heads - 1) & (d > 0))
        def _():
            c_copy(d).start()

    def steps(u):
        if not split:
            return
        for e in range(1, n_dp):

            @pl.when(u == 1 + e // 2)
            def _():
                do_forward(e)

            if 2 + e // 2 < last:

                @pl.when(u == 2 + e // 2)
                def _():
                    do_onward(e)

    def pair(u, _):
        steps(u)
        score(2 * u + 1, scores1)
        finish(2 * u, scores0)
        send_if_done(2 * u)
        score(2 * u + 2, scores0)
        finish(2 * u + 1, scores1)
        send_if_done(2 * u + 1)
        return 0

    score(0, scores0)
    lax.fori_loop(0, last, pair, 0)
    if split:
        for e in range(1, n_dp):
            if 1 + e // 2 >= last:
                do_forward(e)
        for e in range(1, n_dp):
            if 2 + e // 2 >= last:
                do_onward(e)
    score(2 * last + 1, scores1)
    finish(2 * last, scores0)
    finish(2 * last + 1, scores1)
    context_r[me] = context_s[me]

    for d in range(1, seq):
        c_copy(d).wait()
        x_copies[d].wait_send()
    if split:
        for e in range(1, n_dp):
            s_copies[e - 1].wait_send()
            for copy in p_pair(e, ow):
                copy.wait_send()
            for copy in forward(e)[:2]:
                copy.wait_send()
            for copy in forward(e)[2:]:
                copy.wait()
            for copy in onward(e):
                copy.wait()

        @pl.when(holder)
        def _():
            for e in range(1, n_dp):
                for kind in range(3):
                    w_copy(kind, e).wait_send()


def attend(cfg, row, collective_id, *args):
    c = cfg
    g, l, h, s = c.group, c.piece, c.heads, c.seq
    sds = jax.ShapeDtypeStruct
    out_shape = [
        sds((s, g, l), BF16),
        sds((h, s, LANES, l), BF16),
        sds((h, s, l, LANES), BF16),
        sds((h, s, l, LANES), BF16),
        sds((s, g, l), BF16),
        sds((s, g + AUG, l), BF16),
        sds((GROUPS, g, l), BF16),
        sds((3, g, g), BF16),
    ]
    if c.split:
        out_shape += [
            sds((c.dp, 16, LANES), F32),
            sds((2, c.dp, 2, c.half, c.width), BF16),
            sds((c.dp, 4, c.quarter, g), BF16),
        ]
    dma = pltpu.SemaphoreType.DMA
    scratch = [
        pltpu.VMEM((h, HDIM + AUG, c.slots), BF16),
        pltpu.VMEM((c.slots, l), F32),
        pltpu.VMEM((c.slots, l), F32),
        pltpu.VMEM((3, g + AUG, h * LANES), BF16),
        dma((s,)),
        dma((s,)),
        dma((s,)),
        dma((s,)),
    ]
    if c.split:
        scratch += [
            pltpu.VMEM((c.per_group, 3, c.shard, g), BF16),
            dma((c.dp,)),
            dma((c.dp,)),
            dma((c.dp, 3)),
            dma((c.per_group, 3)),
            dma((3,)),
        ] + [dma((c.dp, 2))] * 8
    vmem = pl.BlockSpec(memory_space=pltpu.VMEM)
    return pl.pallas_call(
        functools.partial(attend_kernel, cfg, row),
        out_shape=out_shape,
        in_specs=[vmem] * len(args),
        out_specs=[vmem] * len(out_shape),
        scratch_shapes=scratch,
        compiler_params=pltpu.CompilerParams(
            collective_id=collective_id, has_side_effects=True, vmem_limit_bytes=VMEM_LIMIT
        ),
        name="attend",
    )(*args)


def middle_kernel(
    cfg,
    row,
    context,
    x_own,
    teacher,
    out_grad,
    wo,
    wu,
    wd,
    smalls,
    cols,
    up_rows,
    layer_out,
    c_grad,
    grad_mid,
    g_ou,
    g_d,
    vecs,
    v1,
    first,
    low1,
    act,
    slope,
    v2,
    seed,
    low2,
    inner_low,
    w_up,
    vcols,
    raw,
):
    me = lax.axis_index("seq")
    my_dp = lax.axis_index("dp")
    piece, width, group = cfg.piece, cfg.width, cfg.group
    hid = cfg.hidden // GROUPS
    rows = 32
    chunks = width // rows
    inv = 1.0 / width
    total = jnp.sum(smalls[:, 12:13, 0:1], axis=0)
    for r in range(1, cfg.rows):
        total += jnp.sum(smalls[:, 12 + r : 13 + r, 0:1], axis=0)
    length = smalls[my_dp, 12 + row : 13 + row, 0:1]
    slot = (iota((1, piece), 1) + me * piece).astype(F32)
    live = jnp.where(slot < length, 1.0, 0.0)
    coef = 2.0 / (total * width)

    def at(i, n):
        return pl.ds(pl.multiple_of(i * n, n), n)

    def col(i, n, which):
        return cols[at(i, n), which : which + 1]

    def loop(count, body, *init):
        return lax.fori_loop(0, count, lambda i, c: body(i, *c), tuple(init))

    zero_row = jnp.zeros((1, piece), F32)

    def sub(v):
        return jnp.sum(v, axis=0, keepdims=True)

    for g in range(GROUPS):
        w_up[g, 0:group] = wu[g * group : (g + 1) * group]
        w_up[g, group:] = jnp.where(
            iota((AUG, hid), 0) == 0, up_rows[g : g + 1].astype(F32), 0.0
        ).astype(BF16)
        low1[g, group:] = jnp.where(iota((AUG, piece), 0) == 0, 1.0, 0.0).astype(BF16)
    vcols[...] = jnp.zeros_like(vcols)

    step = 256

    def project(i, acc):
        out = mm(wo[:, at(i, step)], context[...], 0, 0)
        v = out + x_own[at(i, step)].astype(F32) + col(i, step, 0)
        v1[at(i, step)] = v
        return (acc + sub(v),)

    (acc,) = loop(width // step, project, zero_row)
    mean = acc * inv

    def center1(i, acc):
        v = v1[at(i, rows)] - mean
        v1[at(i, rows)] = v
        return (acc + sub(v * v),)

    (acc,) = loop(chunks, center1, zero_row)
    scale1 = lax.rsqrt(acc * inv + EPSILON)
    per = group // rows

    def norm1(i, unused):
        v = v1[at(i, rows)] * scale1
        v1[at(i, rows)] = v
        out = v * col(i, rows, 1) + col(i, rows, 2)
        first[at(i, rows)] = out
        low1[i // per, at(lax.rem(i, per), rows)] = out.astype(BF16)
        return (unused,)

    loop(chunks, norm1, 0)

    parts = hid // step

    def expand(i, unused):
        g, c = i // parts, lax.rem(i, parts)
        raw[...] = mm(w_up[g, :, at(c, step)], low1[g], 0, 0)

        def gelu(k, unused):
            u = raw[at(k, rows)]
            x = jnp.abs(u) * 0.7071067811865476
            d = 1.0 + 0.3275911 * x
            t = pl.reciprocal(d, approx=True)
            t = t * (2.0 - d * t)
            bell = jnp.exp2((u * u) * (-0.5 * LOG2E))
            poly = t * (
                0.127414796
                + t * (-0.142248368 + t * (0.7107068705 + t * (-0.7265760135 + t * 0.5307027145)))
            )
            tail = poly * bell
            phi = jnp.where(u >= 0.0, 1.0 - tail, tail)
            place = pl.ds(pl.multiple_of(i * step + k * rows, rows), rows)
            act[place] = (u * phi).astype(BF16)
            slope[place] = phi + u * bell * 0.3989422804014327
            return (unused,)

        loop(step // rows, gelu, 0)
        return (unused,)

    loop(GROUPS * parts, expand, 0)

    def contract(g, acc):
        out = mm(wd[at(g, hid)], act[at(g, hid)], 0, 0)
        v = out + first[at(g, group)] + col(g, group, 3)
        v2[at(g, group)] = v
        return (acc + sub(v),)

    (acc,) = loop(GROUPS, contract, zero_row)
    mean = acc * inv

    def center2(i, acc):
        v = v2[at(i, rows)] - mean
        v2[at(i, rows)] = v
        return (acc + sub(v * v),)

    (acc,) = loop(chunks, center2, zero_row)
    scale2 = lax.rsqrt(acc * inv + EPSILON)

    loss, sum1, sum2 = zero_row, zero_row, zero_row
    for c in range(width // LANES):
        span = slice(c * LANES, (c + 1) * LANES)
        xhat = v2[span] * scale2
        v2[span] = xhat
        gain = cols[span, 4:5]
        full = xhat * gain + cols[span, 5:6]
        layer_out[:, span] = full.T.astype(BF16)
        error = full - teacher[:, span].astype(F32).T
        loss += sub(live * error * error)
        grad = live * (out_grad[:, span].astype(F32).T + error * coef)
        seed[span] = grad
        vcols[span, 4:5] = jnp.sum(grad * xhat, axis=1, keepdims=True)
        vcols[span, 5:6] = jnp.sum(grad, axis=1, keepdims=True)
        grad = grad * gain
        sum1 += sub(grad)
        sum2 += sub(grad * xhat)
    sum1, sum2 = sum1 * inv, sum2 * inv

    def back2(i, unused):
        place = at(i, rows)
        grad = scale2 * (seed[place] * col(i, rows, 4) - sum1 - v2[place] * sum2)
        seed[place] = grad
        small = grad.astype(BF16)
        low2[place] = small
        vcols[place, 3:4] = jnp.sum(small.astype(F32), axis=1, keepdims=True)
        return (unused,)

    loop(chunks, back2, 0)

    def back_act(i, unused):
        g = i // parts
        raw[...] = mm(wd[at(i, step)], low2[at(g, group)], 1, 0)
        inner_low[at(i, step)] = (raw[...] * slope[at(i, step)]).astype(BF16)
        return (unused,)

    loop(GROUPS * parts, back_act, 0)

    def back_first(g, a, b):
        place = at(g, group)
        grad = seed[place] + mm(w_up[g, 0:group], inner_low[at(g, hid)], 1, 0)
        xhat = v1[place]
        vcols[place, 1:2] = jnp.sum(grad * xhat, axis=1, keepdims=True)
        vcols[place, 2:3] = jnp.sum(grad, axis=1, keepdims=True)
        grad = grad * col(g, group, 1)
        seed[place] = grad
        return (a + sub(grad), b + sub(grad * xhat))

    sum1, sum2 = loop(GROUPS, back_first, zero_row, zero_row)
    sum1, sum2 = sum1 * inv, sum2 * inv

    def down_grad(g, unused):
        g_d[at(g, hid)] = mm(act[at(g, hid)], low2[at(g, group)], 1, 1).astype(BF16)
        return (unused,)

    loop(GROUPS, down_grad, 0)

    def back1(i, unused):
        place = at(i, rows)
        grad = scale1 * (seed[place] - sum1 - v1[place] * sum2)
        grad_mid[place] = grad
        small = grad.astype(BF16)
        low2[place] = small
        vcols[place, 0:1] = jnp.sum(small.astype(F32), axis=1, keepdims=True)
        return (unused,)

    loop(chunks, back1, 0)

    def back_context(i, unused):
        c_grad[at(i, step)] = mm(wo[at(i, step)], low2[...], 1, 0).astype(BF16)
        g_ou[0, at(i, step)] = mm(context[at(i, step)], low2[...], 1, 1).astype(BF16)
        return (unused,)

    loop(width // step, back_context, 0)

    vecs[...] = jnp.zeros_like(vecs)
    vecs[0:8] = vcols[...].T[0:8]
    for g in range(GROUPS):
        out = mm(low1[g], inner_low[g * hid : (g + 1) * hid], 1, 1)
        g_ou[1, g * group : (g + 1) * group] = out[0:group].astype(BF16)
        vecs[8 + g : 9 + g] = out[group : group + 1]
    mean_loss = jnp.sum(loss, axis=1, keepdims=True) / (total * width)
    vecs[12:13] = jnp.broadcast_to(mean_loss, (1, width))


def middle(cfg, row, *args):
    c = cfg
    sds = jax.ShapeDtypeStruct
    w, l, f = c.width, c.piece, c.hidden
    out_shape = [
        sds((l, w), BF16),
        sds((w, l), BF16),
        sds((w, l), F32),
        sds((2, w, w), BF16),
        sds((f, c.group), BF16),
        sds((16, w), F32),
    ]
    scratch = [
        pltpu.VMEM((w, l), F32),
        pltpu.VMEM((w, l), F32),
        pltpu.VMEM((GROUPS, c.group + AUG, l), BF16),
        pltpu.VMEM((f, l), BF16),
        pltpu.VMEM((f, l), F32),
        pltpu.VMEM((w, l), F32),
        pltpu.VMEM((w, l), F32),
        pltpu.VMEM((w, l), BF16),
        pltpu.VMEM((f, l), BF16),
        pltpu.VMEM((GROUPS, c.group + AUG, f // GROUPS), BF16),
        pltpu.VMEM((w, LANES), F32),
        pltpu.VMEM((256, l), F32),
    ]
    vmem = pl.BlockSpec(memory_space=pltpu.VMEM)
    return pl.pallas_call(
        functools.partial(middle_kernel, cfg, row),
        out_shape=out_shape,
        in_specs=[vmem] * len(args),
        out_specs=[vmem] * len(out_shape),
        scratch_shapes=scratch,
        compiler_params=pltpu.CompilerParams(vmem_limit_bytes=VMEM_LIMIT),
        name="middle",
    )(*args)


def backward_kernel(cfg, *refs):
    split = cfg.split
    refs = list(refs)
    take = lambda n: [refs.pop(0) for _ in range(n)]
    c_grad, q_t, k_n, v_n, context_s, x_group, w_group, grad_mid = take(8)
    if split:
        g_ou, g_d, vecs = take(3)
    states_grad, qkv_out = take(2)
    if split:
        o_out, d_out, vec_out = take(3)
    d_in, d_aug, p0, p1, s0, s1, dq, dk, dv, d_t, dx_s, dx_r = take(12)
    a_send, a_recv, x_send, x_recv = take(4)
    if split:
        r1_ou, r1_d, t1_ou, t1_d, r2_ou, r2_d, t2_ou, t2_d, r3_ou, r3_d = take(10)
        vec_in, vec_mid, vec_dp, qkv_s, qkv_r = take(5)
        r1_send, r1_recv, r2_send, r2_recv, r3_send, r3_recv, r4_send, r4_recv = take(8)
        v1_send, v1_recv, v2_send, v2_recv, w1_send, w1_recv, w2_send, w2_recv = take(8)
    me = lax.axis_index("seq")
    my_dp = lax.axis_index("dp")
    piece, width, group, heads, seq = cfg.piece, cfg.width, cfg.group, cfg.heads, cfg.seq
    n_dp, shard = cfg.dp, cfg.shard

    greet(cfg, me, my_dp, split)
    grad_copies = {}
    for d in range(1, seq):
        grad_copies[d] = remote(
            c_grad.at[me ^ d], d_in.at[me], a_send.at[d], a_recv.at[d], seq=me ^ d
        )
        grad_copies[d].start()

    if split:
        xbit, core = me // 2, lax.rem(me, 2)
        first_hop = [
            remote(g_ou.at[:, :, 1 - core], r1_ou, r1_send.at[0], r1_recv.at[0], seq=me ^ 1),
            remote(g_d.at[:, :, 1 - core], r1_d, r1_send.at[1], r1_recv.at[1], seq=me ^ 1),
        ]
        for copy in first_hop:
            copy.start()
        vec_hop = []
        for d in range(1, seq):
            vec_hop.append(
                remote(vecs, vec_in.at[me], v1_send.at[d], v1_recv.at[d], seq=me ^ d)
            )
            vec_hop[-1].start()

        second_hop = [
            remote(t1_ou.at[1 - xbit], r2_ou, r2_send.at[0], r2_recv.at[0], seq=me ^ 2),
            remote(t1_d.at[:, 1 - xbit], r2_d, r2_send.at[1], r2_recv.at[1], seq=me ^ 2),
        ]

        def third_hop(e):
            target = lax.rem(my_dp + e, n_dp)
            return [
                remote(
                    t2_ou.at[target], r3_ou.at[my_dp], r3_send.at[e, 0], r3_recv.at[e, 0], dp=target
                ),
                remote(
                    t2_d.at[target], r3_d.at[my_dp], r3_send.at[e, 1], r3_recv.at[e, 1], dp=target
                ),
            ]

        def fourth_hop(d):
            mine = o_out.at[xbit, core]
            own = d_out.at[me]
            return [
                remote(mine, mine, r4_send.at[d, 0], r4_recv.at[d, 0], seq=me ^ d),
                remote(own, own, r4_send.at[d, 1], r4_recv.at[d, 1], seq=me ^ d),
            ]

        def vec_second(e):
            return remote(
                vec_mid,
                vec_dp.at[my_dp],
                v2_send.at[e],
                v2_recv.at[e],
                dp=lax.rem(my_dp + e, n_dp),
            )

        def phase_one():
            for copy in first_hop:
                copy.wait_recv()
            for copy in vec_hop:
                copy.wait_recv()

            def add(i, _):
                for x in range(2):
                    t1_ou[x, i] = (
                        g_ou[x, i, core].astype(F32) + r1_ou[x, i].astype(F32)
                    ).astype(BF16)
                    t1_d[i, x] = (
                        g_d[i, x, core].astype(F32) + r1_d[i, x].astype(F32)
                    ).astype(BF16)
                return 0

            lax.fori_loop(0, n_dp, add, 0)
            for copy in second_hop:
                copy.start()
            value = vecs[...]
            for d in range(1, seq):
                value += vec_in[me ^ d]
            vec_mid[...] = value
            for e in range(1, n_dp):
                vec_second(e).start()

        def phase_two():
            for copy in second_hop:
                copy.wait_recv()

            def add(i, _):
                t2_ou[i] = (t1_ou[xbit, i].astype(F32) + r2_ou[i].astype(F32)).astype(BF16)
                t2_d[i] = (t1_d[i, xbit].astype(F32) + r2_d[i].astype(F32)).astype(BF16)
                return 0

            lax.fori_loop(0, n_dp, add, 0)
            for e in range(1, n_dp):
                for copy in third_hop(e):
                    copy.start()
            value = vec_mid[...]
            for e in range(1, n_dp):
                vec_second(e).wait_recv()
            for e in range(1, n_dp):
                value += vec_dp[lax.rem(my_dp + e, n_dp)]
            vec_out[...] = value

        def phase_three():
            for e in range(1, n_dp):
                for copy in third_hop(e):
                    copy.wait_recv()
            ou = t2_ou[my_dp].astype(F32)
            dd = t2_d[my_dp].astype(F32)
            for e in range(1, n_dp):
                src = lax.rem(my_dp + e, n_dp)
                ou += r3_ou[src].astype(F32)
                dd += r3_d[src].astype(F32)
            o_out[xbit, core] = ou.astype(BF16)
            d_out[me] = dd.astype(BF16)
            for d in range(1, seq):
                for copy in fourth_hop(d):
                    copy.start()

    def clear(ref):
        def body(i, _):
            ref[i] = jnp.zeros(ref.shape[1:], ref.dtype)
            return 0

        lax.fori_loop(0, ref.shape[0], body, 0)

    clear(dq)
    clear(dk)
    clear(dv)
    aug_row = iota((HDIM, piece), 0)

    def prepare(t):
        for h in range(heads):
            grad = d_in[t, h * HDIM : (h + 1) * HDIM]
            d_aug[h, t, 0:HDIM] = grad
            dot = jnp.sum(
                grad.astype(F32) * context_s[t, h * HDIM : (h + 1) * HDIM].astype(F32),
                axis=0,
                keepdims=True,
            )
            high, middle, low = three_parts(-dot)
            value = jnp.where(aug_row == 0, high.astype(F32), 0.0)
            value = jnp.where(aug_row == 1, middle.astype(F32), value)
            value = jnp.where(aug_row == 2, low.astype(F32), value)
            d_aug[h, t, HDIM:] = value.astype(BF16)

    per_piece = heads * seq
    blocks = seq * per_piece

    def place(i):
        j = lax.rem(i, per_piece)
        return me ^ (i // per_piece), j // seq, lax.rem(j, seq)

    def score(i, p, s):
        a, h, b = place(i)
        weights = jnp.exp2(mm(q_t[h, a], k_n[h, b], 0, 1))
        p[...] = weights.astype(BF16)
        s[...] = (weights * mm(d_aug[h, a], v_n[h, b], 0, 1)).astype(BF16)

    def finish(i, p, s):
        a, h, b = place(i)
        dv[h * seq + b] += mm(d_aug[h, a, 0:HDIM], p[...], 1, 0)
        dk[h * seq + b] += mm(q_t[h, a, 0:HDIM], s[...], 1, 0)
        dq[h * seq + a] += mm(s[...], k_n[h, b], 1, 0)

    d_in[me] = c_grad[me]
    prepare(me)
    steps_piece = per_piece // 2

    def pair(u, _):
        for d in range(1, seq):

            @pl.when(u == d * steps_piece - 1)
            def _():
                grad_copies[d].wait_recv()
                prepare(me ^ d)

        if split:
            pl.when(u == 2)(phase_one)
            pl.when(u == 9)(phase_two)
            pl.when(u == 16)(phase_three)
        score(2 * u + 1, p1, s1)
        finish(2 * u, p0, s0)
        score(2 * u + 2, p0, s0)
        finish(2 * u + 1, p1, s1)
        return 0

    score(0, p0, s0)
    last = blocks // 2 - 1
    lax.fori_loop(0, last, pair, 0)
    score(2 * last + 1, p1, s1)
    finish(2 * last, p0, s0)
    finish(2 * last + 1, p1, s1)

    def collect(t):
        for h in range(heads):
            at = slice(h * HDIM, (h + 1) * HDIM)
            d_t[t, 0, at] = (dq[h * seq + t] * HDIM**-0.5).T[0:HDIM].astype(BF16)
            d_t[t, 1, at] = (dk[h * seq + t] * (1.0 / LOG2E)).astype(BF16)
            d_t[t, 2, at] = dv[h * seq + t].astype(BF16)
        out = mm(w_group[0], d_t[t, 0], 1, 0)
        out += mm(w_group[1], d_t[t, 1], 1, 0)
        out += mm(w_group[2], d_t[t, 2], 1, 0)
        dx_s[t] = out.astype(BF16)

    def slab(t):
        return dx_r.at[pl.ds(pl.multiple_of(t * group, HDIM), group)]

    def dx_copy(d):
        return remote(dx_s.at[me ^ d], slab(me), x_send.at[d], x_recv.at[d], seq=me ^ d)

    def collect_step(i, _):
        collect(me ^ (seq - 1 - i))
        for d in range(1, seq):

            @pl.when(i == seq - 1 - d)
            def _():
                dx_copy(d).start()

        return 0

    lax.fori_loop(0, seq, collect_step, 0)
    for kind in range(3):
        total = mm(x_group[0], d_t[0, kind], 1, 1)
        for t in range(1, seq):
            total += mm(x_group[t], d_t[t, kind], 1, 1)
        if split:
            for t in range(cfg.per_group):
                qkv_s[t, kind, 0:shard] = total[t * shard : (t + 1) * shard].astype(BF16)
                qkv_s[t, kind, shard:] = total[group:].astype(BF16)
        else:
            qkv_out[kind] = total
    dx_r[pl.ds(pl.multiple_of(me * group, HDIM), group)] = dx_s[me]

    if split:
        my_slot = lax.rem(my_dp, cfg.per_group)
        owner_seq = my_dp // cfg.per_group
        owner = owner_seq == me

        def w_first(t):
            return remote(
                qkv_s.at[t],
                qkv_r.at[my_dp],
                w1_send.at[t],
                w1_recv.at[my_dp],
                dp=me * cfg.per_group + t,
            )

        for t in range(cfg.per_group):

            @pl.when(me * cfg.per_group + t != my_dp)
            def _():
                w_first(t).start()

        def w_second(d):
            return remote(qkv_out, qkv_out, w2_send.at[d], w2_recv.at[0], seq=me ^ d)

        @pl.when(owner)
        def _():
            total = qkv_s[my_slot].astype(F32)
            for e in range(1, n_dp):
                src = lax.rem(my_dp + e, n_dp)
                remote(
                    qkv_s.at[0], qkv_r.at[src], w1_send.at[0], w1_recv.at[src], dp=src
                ).wait_recv()
                total += qkv_r[src].astype(F32)
            qkv_out[...] = total.astype(BF16)
            for d in range(1, seq):
                w_second(d).start()

    for d in range(1, seq):
        dx_copy(d).wait_recv()
    for c in range(width // LANES):
        span = slice(c * LANES, (c + 1) * LANES)
        states_grad[:, span] = (dx_r[span].astype(F32) + grad_mid[span]).T.astype(BF16)

    for d in range(1, seq):
        dx_copy(d).wait_send()
        grad_copies[d].wait_send()
    if split:
        for t in range(cfg.per_group):

            @pl.when(me * cfg.per_group + t != my_dp)
            def _():
                w_first(t).wait_send()

        @pl.when(owner)
        def _():
            for d in range(1, seq):
                w_second(d).wait_send()

        @pl.when(jnp.logical_not(owner))
        def _():
            w_second(1).wait_recv()

        for copy in first_hop + second_hop + vec_hop:
            copy.wait_send()
        for e in range(1, n_dp):
            vec_second(e).wait_send()
            for copy in third_hop(e):
                copy.wait_send()
        for d in range(1, seq):
            for copy in fourth_hop(d):
                copy.wait()


def backward(cfg, collective_id, *args):
    c = cfg
    sds = jax.ShapeDtypeStruct
    g, l, h, s, w = c.group, c.piece, c.heads, c.seq, c.width
    if c.split:
        out_shape = [
            sds((l, w), BF16),
            sds((3, c.shard + AUG, g), BF16),
            sds((2, 2, c.half, w), BF16),
            sds((4, c.quarter, g), BF16),
            sds((16, w), F32),
        ]
    else:
        out_shape = [sds((l, w), BF16), sds((3, g + AUG, g), F32)]
    dma = pltpu.SemaphoreType.DMA
    vm = pltpu.VMEM
    scratch = [
        vm((s, g, l), BF16),
        vm((h, s, LANES, l), BF16),
        vm((l, l), BF16),
        vm((l, l), BF16),
        vm((l, l), BF16),
        vm((l, l), BF16),
        vm((h * s, l, LANES), F32),
        vm((h * s, HDIM, l), F32),
        vm((h * s, HDIM, l), F32),
        vm((s, 3, g, l), BF16),
        vm((s, g, l), BF16),
        vm((w, l), BF16),
        dma((s,)),
        dma((s,)),
        dma((s,)),
        dma((s,)),
    ]
    if c.split:
        ou = (c.half, w)
        dd = (c.quarter, g)
        scratch += [
            vm((2, c.dp) + ou, BF16),
            vm((c.dp, 2) + dd, BF16),
            vm((2, c.dp) + ou, BF16),
            vm((c.dp, 2) + dd, BF16),
            vm((c.dp,) + ou, BF16),
            vm((c.dp,) + dd, BF16),
            vm((c.dp,) + ou, BF16),
            vm((c.dp,) + dd, BF16),
            vm((c.dp,) + ou, BF16),
            vm((c.dp,) + dd, BF16),
            vm((s, 16, w), F32),
            vm((16, w), F32),
            vm((c.dp, 16, w), F32),
            vm((c.per_group, 3, c.shard + AUG, g), BF16),
            vm((c.dp, 3, c.shard + AUG, g), BF16),
            dma((2,)),
            dma((2,)),
            dma((2,)),
            dma((2,)),
            dma((c.dp, 2)),
            dma((c.dp, 2)),
            dma((s, 2)),
            dma((s, 2)),
            dma((s,)),
            dma((s,)),
            dma((c.dp,)),
            dma((c.dp,)),
            dma((c.per_group,)),
            dma((c.dp,)),
            dma((s,)),
            dma((1,)),
        ]
    vmem = pl.BlockSpec(memory_space=pltpu.VMEM)
    return pl.pallas_call(
        functools.partial(backward_kernel, cfg),
        out_shape=out_shape,
        in_specs=[vmem] * len(args),
        out_specs=[vmem] * len(out_shape),
        scratch_shapes=scratch,
        compiler_params=pltpu.CompilerParams(
            collective_id=collective_id, has_side_effects=True, vmem_limit_bytes=VMEM_LIMIT
        ),
        name="backward",
    )(*args)


def local(
    states,
    lengths,
    teacher,
    out_grad,
    q_weight,
    k_weight,
    v_weight,
    q_bias,
    v_bias,
    o_weight,
    o_bias,
    attn_gain,
    attn_bias,
    up_weight,
    up_bias,
    down_weight,
    down_bias,
    ffn_gain,
    ffn_bias,
):
    row_count, piece, width = states.shape
    n_dp, n_seq = lax.axis_size("dp"), lax.axis_size("seq")
    me, my_dp = lax.axis_index("seq"), lax.axis_index("dp")
    shard = q_bias.shape[0]
    hidden = up_bias.shape[0] * n_dp
    cfg = Config(n_dp, n_seq, piece, width, hidden, shard)
    cfg.rows = row_count
    group = cfg.group

    def pad(v):
        return jnp.pad(v.astype(F32), ((0, 0), (0, LANES - v.shape[1])))

    vectors = (q_bias, v_bias, o_bias, attn_gain, attn_bias, down_bias, ffn_gain, ffn_bias)
    small = jnp.concatenate(
        [
            pad(jnp.stack(vectors)),
            pad(up_bias.reshape(4, shard)),
            jnp.broadcast_to(lengths.astype(F32)[:, None], (row_count, LANES)),
            jnp.zeros((4 - row_count, LANES), F32),
        ]
    )
    if not cfg.split:
        smalls = lax.all_gather(small, "dp", axis=0)
        qkv = jnp.stack((q_weight, k_weight, v_weight))
        qkv = lax.all_gather(qkv, "dp", axis=1, tiled=True)
        w_group_in = lax.dynamic_slice(qkv, (0, me * group, 0), (3, group, group))
        wo = lax.all_gather(o_weight, "dp", axis=0, tiled=True)
        wu = lax.all_gather(up_weight, "dp", axis=0, tiled=True)
        wd = lax.all_gather(down_weight, "dp", axis=0, tiled=True)

    results = []
    for r in range(row_count):
        if cfg.split:
            (
                context_r,
                q_t,
                k_n,
                v_n,
                context_s,
                x_group,
                x_own,
                w_group,
                smalls,
                gath_ou,
                gath_d,
            ) = attend(
                cfg,
                r,
                2 * r,
                states[r],
                small,
                q_weight,
                k_weight,
                v_weight,
                o_weight,
                up_weight,
                down_weight,
            )
            gath_ou = gath_ou.reshape(2, width, width)
            wo, wu = gath_ou[0], gath_ou[1]
            wd = gath_d.reshape(hidden, group)
        else:
            context_r, q_t, k_n, v_n, context_s, x_group, x_own, w_group = attend(
                cfg, r, 2 * r, states[r], smalls, w_group_in
            )
        cols = smalls[:, 2:8, :shard].transpose(0, 2, 1).reshape(width, 6)
        cols = jnp.pad(cols, ((0, 0), (0, LANES - 6)))
        up_rows = smalls[:, 8:12, :shard].reshape(GROUPS, hidden // GROUPS)
        layer_out, c_grad, grad_mid, g_ou, g_d, vecs = middle(
            cfg,
            r,
            context_r.reshape(width, piece),
            x_own.reshape(width, piece),
            teacher[r],
            out_grad[r],
            wo,
            wu,
            wd,
            smalls,
            cols,
            up_rows,
        )
        c_grad = c_grad.reshape(GROUPS, group, piece)
        common = (c_grad, q_t, k_n, v_n, context_s, x_group, w_group, grad_mid)
        if cfg.split:
            g_ou = g_ou.reshape(2, n_dp, 2, cfg.half, width)
            g_d = g_d.reshape(n_dp, 2, 2, cfg.quarter, group)
            states_grad, qkv, ou, dd, vec = backward(cfg, 2 * r + 1, *common, g_ou, g_d, vecs)
            ou = ou.reshape(2, shard, width).astype(F32)
            grads = (
                qkv[:, :shard].astype(F32),
                qkv[:, shard].astype(F32),
                ou,
                dd.reshape(4 * shard, group).astype(F32),
                vec,
            )
        else:
            states_grad, qkv = backward(cfg, 2 * r + 1, *common)
            grads = (qkv, g_ou.astype(F32), g_d.astype(F32), vecs)
        results.append((layer_out, states_grad, grads))

    layer_out = jnp.stack([item[0] for item in results])
    states_grad = jnp.stack([item[1] for item in results])
    grads = jax.tree.map(lambda *leaves: sum(leaves[1:], leaves[0]), *[i[2] for i in results])
    if cfg.split:
        qkv, qkv_bias, ou, grad_dw, vec = grads
        at = lax.rem(my_dp, cfg.per_group) * shard
        grad_qb = lax.dynamic_slice(qkv_bias[0], (at,), (shard,))
        grad_vb = lax.dynamic_slice(qkv_bias[2], (at,), (shard,))
        grad_ow, grad_uw = ou[0], ou[1]
    else:
        qkv_g, g_ou, g_d, vecs = grads
        whole = jnp.zeros((3, width + GROUPS * AUG, group), F32)
        whole = lax.dynamic_update_slice(whole, qkv_g[:, :group], (0, me * group, 0))
        whole = lax.dynamic_update_slice(whole, qkv_g[:, group:], (0, width + me * AUG, 0))
        whole, g_ou, g_d, vec = lax.psum((whole, g_ou, g_d, vecs), ("dp", "seq"))
        qkv = lax.dynamic_slice(whole, (0, my_dp * shard, 0), (3, shard, group))
        biases = whole[:, width::AUG].reshape(3, width)
        grad_qb = lax.dynamic_slice(biases[0], (my_dp * shard,), (shard,))
        grad_vb = lax.dynamic_slice(biases[2], (my_dp * shard,), (shard,))
        g_ou = lax.dynamic_slice(g_ou, (0, my_dp * shard, 0), (2, shard, width))
        grad_ow, grad_uw = g_ou[0], g_ou[1]
        grad_dw = lax.dynamic_slice(g_d, (my_dp * 4 * shard, 0), (4 * shard, group))

    mine = lax.dynamic_slice(vec[:6], (0, my_dp * shard), (6, shard))
    grad_ub = lax.dynamic_slice(vec[8:12].reshape(-1), (my_dp * 4 * shard,), (4 * shard,))
    return (
        layer_out,
        vec[12, 0],
        states_grad,
        qkv[0],
        qkv[1],
        qkv[2],
        grad_qb,
        grad_vb,
        grad_ow,
        mine[0],
        mine[1],
        mine[2],
        grad_uw,
        grad_ub,
        grad_dw,
        mine[3],
        mine[4],
        mine[5],
    )


def solution(mesh):
    rows3 = P("dp", "seq", None)
    matrix = P("dp", None)
    vector = P("dp")
    return jax.shard_map(
        local,
        mesh=mesh,
        in_specs=(rows3, vector, rows3, rows3)
        + (matrix,) * 3
        + (vector,) * 2
        + (matrix,)
        + (vector,) * 3
        + (matrix, vector, matrix)
        + (vector,) * 3,
        out_specs=(rows3, P(), rows3)
        + (matrix,) * 3
        + (vector,) * 2
        + (matrix,)
        + (vector,) * 3
        + (matrix, vector, matrix)
        + (vector,) * 3,
        check_vma=False,
    )
```

```python
import functools
import math
import types

import jax
import jax.numpy as jnp
from jax import lax
from jax.experimental import pallas as pl
from jax.experimental.pallas import tpu as pltpu
from jax.sharding import PartitionSpec as P

HDIM = 64
GROUPS = 4
EPSILON = 1e-12
NEG_FILL = -1e30
LANES = 128
AUG = 16
LOG2E = 1.4426950408889634
MESH = pl.DeviceIdType.MESH
F32 = jnp.float32
BF16 = jnp.bfloat16
VMEM_LIMIT = 60 * 1024 * 1024


def mm(left, right, left_dim, right_dim):
    return lax.dot_general(
        left, right, (((left_dim,), (right_dim,)), ((), ())), preferred_element_type=F32
    )


def iota(shape, dim):
    return lax.broadcasted_iota(jnp.int32, shape, dim)


def remote(src, dst, send_sem, recv_sem, **where):
    return pltpu.make_async_remote_copy(
        src_ref=src,
        dst_ref=dst,
        send_sem=send_sem,
        recv_sem=recv_sem,
        device_id=where,
        device_id_type=MESH,
    )


def three_parts(row):
    high = row.astype(BF16)
    rest = row - high.astype(F32)
    middle = rest.astype(BF16)
    low = (rest - middle.astype(F32)).astype(BF16)
    return high, middle, low


class Config:
    def __init__(self, dp, seq, piece, width, hidden, shard):
        self.dp, self.seq, self.piece, self.width, self.hidden, self.shard = (
            dp,
            seq,
            piece,
            width,
            hidden,
            shard,
        )
        self.slots = piece * seq
        self.group = width // GROUPS
        self.heads = self.group // HDIM
        self.per_group = dp // GROUPS
        self.split = shard % 32 == 0 and seq == 4 and dp == 8
        self.half = shard // 2
        self.quarter = hidden // dp // 4


def greet(cfg, me, my_dp):
    barrier = pltpu.get_barrier_semaphore()
    count = cfg.seq - 1
    for d in range(1, cfg.seq):
        pl.semaphore_signal(barrier, inc=1, device_id={"seq": me ^ d}, device_id_type=MESH)
    if cfg.split:
        count += cfg.dp - 1
        for e in range(1, cfg.dp):
            pl.semaphore_signal(
                barrier, inc=1, device_id={"dp": lax.rem(my_dp + e, cfg.dp)}, device_id_type=MESH
            )
    return lambda: pl.semaphore_wait(barrier, count)


def layer_kernel(cfg, row, names, *refs):
    r = types.SimpleNamespace(**dict(zip(names, refs, strict=True)))
    split = cfg.split
    me = lax.axis_index("seq")
    my_dp = lax.axis_index("dp")
    piece, width, group, heads, seq = cfg.piece, cfg.width, cfg.group, cfg.heads, cfg.seq
    shard, half, n_dp, per_group = cfg.shard, cfg.half, cfg.dp, cfg.per_group
    hid = cfg.hidden // GROUPS
    n_z = n_dp // 2
    core = lax.rem(me, 2)
    my_z, my_y = my_dp // 2, lax.rem(my_dp, 2)
    far = [d for d in range(seq - 1, 1, -1)]

    states, teacher, out_grad = r.states, r.teacher, r.out_grad
    x_own, x_group, w_group, w_pad, smalls = (
        r.x_own,
        r.x_group,
        r.w_group,
        r.w_pad,
        r.smalls,
    )
    q_t, k_n, k_t, v_n = r.q_t, r.k_n, r.k_t, r.v_n
    context_s, context_r = r.context_s, r.context_r
    cols, vcols = r.cols, r.vcols
    wide, slim = r.wide, r.slim
    wo, w_up, wd = r.wo, r.w_up, r.wd
    c_grad, d_in, d_aug, dx_r = r.c_grad, r.d_in, r.d_aug, r.dx_r
    dx_s = c_grad
    low1, low2 = r.low1, r.low2

    score0, score1 = wide.at[0:piece], wide.at[piece : 2 * piece]
    sums_at = 2 * piece
    v1, first, v2, seed = (wide.at[i * width : (i + 1) * width] for i in range(4))
    dq, dk, dv = (wide.at[i * width : (i + 1) * width] for i in range(3))
    act, slope = slim.at[0 : cfg.hidden], slim.at[cfg.hidden : 2 * cfg.hidden]
    p0, p1, s0, s1 = (slim.at[i * piece : (i + 1) * piece] for i in range(4))
    d_t = slope

    def at(i, n):
        return pl.ds(pl.multiple_of(i * n, n), n)

    def loop(count, body, *init):
        return lax.fori_loop(0, count, lambda i, c: body(i, *c), tuple(init))

    def sub(v):
        return jnp.sum(v, axis=0, keepdims=True)


    def to_seq(sems, src, dst, d):
        return remote(src, dst, sems[0].at[d], sems[1].at[d], seq=me ^ d)

    def x_copy(d):
        return to_seq((r.x_send, r.x_recv), x_own.at[at(me ^ d, group)], x_group.at[me, pl.ds(0, group)], d)

    def c_copy(d):
        return to_seq((r.c_send, r.c_recv), context_s.at[me ^ d], context_r.at[at(me, group)], d)

    def g_copy(d):
        return to_seq((r.g_send, r.g_recv), c_grad.at[at(me ^ d, group)], d_in.at[me], d)

    def dx_copy(d):
        return to_seq((r.dx_send, r.dx_recv), dx_s.at[at(me ^ d, group)], dx_r.at[at(me, group)], d)

    if split:
        small, pack = r.small, r.pack
        w_own, w_in = r.w_own, r.w_in
        my_slot = lax.rem(my_dp, per_group)
        holder = my_dp // per_group == me

        def s_copy(e):
            return remote(
                small,
                smalls.at[my_dp],
                r.s_send.at[e],
                r.s_recv.at[e],
                dp=lax.rem(my_dp + e, n_dp),
            )

        def w_copy(slot, e):
            return remote(
                w_own,
                w_in.at[slot],
                r.w_send.at[e],
                r.w_recv.at[slot],
                dp=lax.rem(my_dp + e, n_dp),
            )

        def hop(kind, i, **where):
            ref = pack.at[i, core]
            return remote(ref, ref, r.hop_send.at[kind, i], r.hop_recv.at[i], **where)

        def up(i):
            return hop(0, i, dp=my_dp + 2)

        def down(i):
            return hop(1, i, dp=my_dp - 2)

        def across(i):
            return hop(2, i, dp=my_dp + 1 - 2 * my_y)

        def beside(i):
            ref = pack.at[i, core]
            return remote(ref, ref, r.sib_send.at[i], r.sib_recv.at[i], seq=me ^ 1)

        def when(condition, fn):
            pl.when(condition)(fn)

        def gather_start():
            when(my_z < n_z - 1, lambda: up(my_dp).start())
            when(my_z > 0, lambda: down(my_dp).start())
            across(my_dp).start()

        def gather_z(k):
            below, above = my_dp - 2 * k, my_dp + 2 * k

            @pl.when(my_z >= k)
            def _():
                hop(0, below, dp=my_dp).wait_recv()
                when(my_z < n_z - 1, lambda: up(below).start())
                across(below).start()
                beside(below).start()

            @pl.when(my_z + k < n_z)
            def _():
                hop(0, above, dp=my_dp).wait_recv()
                when(my_z > 0, lambda: down(above).start())
                across(above).start()
                beside(above).start()

        def gather_y(k):
            other = my_dp + 1 - 2 * my_y

            def take(i):
                hop(2, i, dp=my_dp).wait_recv()
                beside(i).start()

            if k == 0:
                take(other)
            else:
                when(my_z >= k, lambda: take(other - 2 * k))
                when(my_z + k < n_z, lambda: take(other + 2 * k))

        def gather_end():
            for e in range(1, n_dp):
                copy = beside(lax.rem(my_dp + e, n_dp))
                copy.wait()

            when(my_z < n_z - 1, lambda: up(my_dp).wait_send())
            when(my_z > 0, lambda: down(my_dp).wait_send())
            across(my_dp).wait_send()
            for k in range(1, n_z):
                below, above = my_dp - 2 * k, my_dp + 2 * k

                @pl.when(my_z >= k)
                def _():
                    when(my_z < n_z - 1, lambda: up(below).wait_send())
                    across(below).wait_send()

                @pl.when(my_z + k < n_z)
                def _():
                    when(my_z > 0, lambda: down(above).wait_send())
                    across(above).wait_send()


    wait_entry = greet(cfg, me, my_dp)
    for c in range(0, width, LANES):
        x_own[c : c + LANES] = states[:, c : c + LANES].T
    if split:
        for c in range(2):
            pack[my_dp, c, 0] = r.ow[c * half : (c + 1) * half]
            pack[my_dp, c, 1] = r.uw[c * half : (c + 1) * half]
            pack[my_dp, c, 2] = jnp.concatenate(
                [
                    r.dw[(4 * c + k) * half : (4 * c + k + 1) * half].astype(F32)
                    for k in range(4)
                ],
                axis=1,
            ).astype(BF16)
        smalls[my_dp] = small[...]
        w_own[...] = jnp.concatenate(
            [ref[...].astype(F32) for ref in (r.wq, r.wk, r.wv)], axis=1
        ).astype(BF16)
    wait_entry()
    if split:
        for e in range(1, n_dp):
            s_copy(e).start()

        @pl.when(holder)
        def _():
            for e in range(1, n_dp):
                w_copy(my_slot, e).start()

    for d in range(1, seq):
        x_copy(d).start()
    if split:
        gather_start()

        @pl.when(holder)
        def _():
            w_in[my_slot] = w_own[...]

    x_group[me, 0:group] = x_own[at(me, group)]


    n_cols = heads * LANES
    lane = iota((group, n_cols), 1)
    spread = jnp.where(
        (((lane >> 7) * HDIM + (lane & 127)) == iota((group, n_cols), 0)) & ((lane & 127) < HDIM),
        1.0,
        0.0,
    ).astype(BF16)
    if split:
        for e in range(1, n_dp):
            s_copy(e).wait_recv()
        for t in range(per_group):

            @pl.when(me * per_group + t != my_dp)
            def _():
                w_copy(t, 0).wait_recv()

            for kind in range(3):
                w_group[kind, t * shard : (t + 1) * shard] = w_in[
                    t, :, kind * group : (kind + 1) * group
                ]
    else:
        for kind in range(3):
            w_group[kind] = r.w_all[kind]
    for kind in range(3):
        w_pad[kind, 0:group] = mm(w_group[kind], spread, 1, 0).astype(BF16)
    vec_rows = jnp.zeros((AUG, n_cols), F32)
    lane = iota((LANES, n_cols), 1)
    source = iota((LANES, n_cols), 0)
    for t in range(per_group):
        spread = jnp.where(
            (((lane >> 7) * HDIM + (lane & 127)) == source + t * shard)
            & ((lane & 127) < HDIM)
            & (source < shard),
            1.0,
            0.0,
        ).astype(BF16)
        vec_rows += mm(smalls[me * per_group + t].astype(BF16), spread, 1, 0)
    row_id = iota((AUG, n_cols), 0)
    lane = iota((AUG, n_cols), 1) & 127
    zero = jnp.zeros((AUG, n_cols), F32)
    top_row = row_id == 0
    w_pad[0, group:] = jnp.where(top_row, vec_rows[0:1], zero).astype(BF16)
    ones_k = (top_row & (lane > HDIM) & (lane <= HDIM + 3)) | ((row_id == 1) & (lane == HDIM))
    w_pad[1, group:] = jnp.where(ones_k, 1.0, zero).astype(BF16)
    ones_v = (lane >= HDIM) & (lane < HDIM + 3)
    w_pad[2, group:] = jnp.where(top_row, jnp.where(ones_v, 1.0, vec_rows[1:2]), zero).astype(BF16)

    length = smalls[my_dp, 12 + row : 13 + row, 0:1]
    aug_row = iota((AUG, piece), 0)
    factor = LOG2E * HDIM**-0.5
    deep = HDIM + AUG

    def v_t(h, t):
        return pl.ds(pl.multiple_of((h * seq + t) * deep, AUG), deep)

    def project(t):
        slot = (iota((AUG, piece), 1) + t * piece).astype(F32)
        mask = jnp.where(slot < length, 0.0, NEG_FILL)
        x_group[t, group:] = jnp.where(
            aug_row == 0, 1.0, jnp.where(aug_row == 1, mask, 0.0)
        ).astype(BF16)
        x = x_group[t]
        queries = mm(w_pad[0], x, 0, 0) * factor
        keys_t = mm(w_pad[1], x, 0, 0)
        values_t = mm(w_pad[2], x, 0, 0)
        keys_n = mm(x, w_pad[1], 0, 0)
        values_n = mm(x, w_pad[2], 0, 0)
        rest = jnp.where(iota((HDIM, piece), 0) == 0, 1.0, 0.0).astype(BF16)
        for h in range(heads):
            span = slice(h * LANES, h * LANES + HDIM)
            q_t[h, t, 0:HDIM] = queries[span].astype(BF16)
            q_t[h, t, HDIM:] = rest
            k_t[h, t] = keys_t[span].astype(BF16)
            slim[v_t(h, t)] = values_t[h * LANES : h * LANES + deep].astype(BF16)
            k_n[h, t] = keys_n[:, h * LANES : (h + 1) * LANES].astype(BF16)
            v_n[h, t] = values_n[:, h * LANES : (h + 1) * LANES].astype(BF16)


    tops = r.tops

    def sums(h, t):
        return pl.ds(sums_at + pl.multiple_of((h * seq + t) * deep, AUG), deep)

    def clear_sums(i, unused):
        wide[pl.ds(sums_at + pl.multiple_of(i * deep, AUG), deep)] = jnp.zeros((deep, piece), F32)
        tops[i] = jnp.full((1, piece), NEG_FILL, F32)
        return (unused,)

    loop(heads * seq, clear_sums, 0)

    def run(count, place, first_part, last_part, a, b, hooks=()):
        first_part(a, *place(0))

        def two(u, unused):
            for when_u, fn in hooks:
                pl.when(u == when_u)(fn)
            first_part(b, *place(2 * u + 1))
            last_part(a, *place(2 * u))
            first_part(a, *place(2 * u + 2))
            last_part(b, *place(2 * u + 1))
            return (unused,)

        loop(count // 2 - 1, two, 0)
        first_part(b, *place(count - 1))
        last_part(a, *place(count - 2))
        last_part(b, *place(count - 1))

    def score(buffer, t, h, k):
        buffer[...] = mm(k_n[h, k], q_t[h, t], 1, 0)

    def absorb(buffer, t, h, k):
        i = h * seq + t
        old = tops[i]
        top = jnp.maximum(old, jnp.max(buffer[...], axis=0, keepdims=True))
        weights = jnp.exp2(buffer[...] - top).astype(BF16)
        tops[i] = top
        place = sums(h, t)
        wide[place] = wide[place] * jnp.exp2(old - top) + mm(slim[v_t(h, k)], weights, 1, 0)

    def settle(t):
        for h in range(heads):
            total = wide[sums(h, t)]
            mass = total[HDIM : HDIM + 1]
            context_s[t, h * HDIM : (h + 1) * HDIM] = (total[0:HDIM] / mass).astype(BF16)
            parts = three_parts(-(tops[h * seq + t] + jnp.log2(mass)))
            value = jnp.where(aug_row == 0, 1.0, 0.0)
            for n, part in enumerate(parts):
                value = jnp.where(aug_row == n + 1, part.astype(F32), value)
            q_t[h, t, HDIM:deep] = value.astype(BF16)

    def near_near(i):
        j = lax.rem(i, 2 * heads)
        return me ^ (i // (2 * heads)), j // 2, me ^ lax.rem(j, 2)

    def near_far(i):
        j = lax.rem(i, 2 * heads)
        return me ^ (i // (2 * heads)), j // 2, me ^ (2 + lax.rem(j, 2))

    def any_all(d):
        return lambda i: (me ^ d, i // seq, me ^ lax.rem(i, seq))

    pairs = (score, absorb, score0, score1)
    hooks = [(), (), (), ()]
    if split:
        hooks = [
            ((2, lambda: gather_z(1)),),
            (
                (0, lambda: gather_y(0)),
                (1, lambda: gather_z(2)),
                (3, lambda: gather_y(1)),
                (4, lambda: gather_z(3)),
            ),
            ((3, lambda: gather_y(2)),),
            ((3, lambda: gather_y(3)),),
        ]
    project(me)
    x_copy(1).wait_recv()
    project(me ^ 1)
    run(4 * heads, near_near, *pairs, hooks[0])
    for d in far:
        x_copy(d).wait_recv()
    loop(2, lambda i, unused: (project(me ^ (2 + i)), unused)[1:], 0)
    for n, d in enumerate(far):
        run(seq * heads, any_all(d), *pairs, hooks[1 + n])
        settle(me ^ d)
        c_copy(d).start()
    run(4 * heads, near_far, *pairs, hooks[3])
    settle(me ^ 1)
    c_copy(1).start()
    settle(me)
    context_r[at(me, group)] = context_s[me]
    if split:
        gather_end()

        def unpack(i, unused):
            for c in range(2):
                wo[pl.ds(pl.multiple_of(i * shard + c * half, AUG), half)] = pack[i, c, 0]
                w_up[pl.ds(pl.multiple_of(i * shard + c * half, AUG), half)] = pack[i, c, 1]
                block = pack[i, c, 2].astype(F32)
                for k in range(4):
                    wd[pl.ds(pl.multiple_of((i * 8 + c * 4 + k) * half, AUG), half)] = block[
                        :, k * group : (k + 1) * group
                    ].astype(BF16)
            return (unused,)

        loop(n_dp, unpack, 0)


    for i in range(n_dp):
        turned = smalls[i].T
        cols[i * shard : (i + 1) * shard] = turned[0:shard]
    vcols[...] = jnp.zeros_like(vcols)
    inv = 1.0 / width
    total = jnp.sum(smalls[:, 12:13, 0:1], axis=0)
    for n in range(1, cfg.rows):
        total += jnp.sum(smalls[:, 12 + n : 13 + n, 0:1], axis=0)
    slot = (iota((1, piece), 1) + me * piece).astype(F32)
    live = jnp.where(slot < length, 1.0, 0.0)
    coef = 2.0 / (total * width)
    zero_row = jnp.zeros((1, piece), F32)

    def col(i, n, which):
        return cols[at(i, n), which : which + 1]

    for d in range(1, seq):
        c_copy(d).wait_recv()

    step = 256

    def attn_out(i, acc):
        out = mm(wo[:, at(i, step)], context_r[...], 0, 0)
        v = out + x_own[at(i, step)].astype(F32) + col(i, step, 2)
        v1[at(i, step)] = v
        return (acc + sub(v),)

    (acc,) = loop(width // step, attn_out, zero_row)
    mean = acc * inv

    def center(ref):
        def body(g, acc):
            v = ref[at(g, group)] - mean
            ref[at(g, group)] = v
            return (acc + sub(v * v),)

        (acc,) = loop(GROUPS, body, zero_row)
        return lax.rsqrt(acc * inv + EPSILON)

    scale1 = center(v1)

    def norm1(g, unused):
        v = v1[at(g, group)] * scale1
        v1[at(g, group)] = v
        out = v * col(g, group, 3) + col(g, group, 4)
        first[at(g, group)] = out
        low1[g, 0:group] = out.astype(BF16)
        low1[g, group:] = jnp.where(aug_row == 0, 1.0, 0.0).astype(BF16)
        return (unused,)

    loop(GROUPS, norm1, 0)

    def gelu(u):
        x = jnp.abs(u) * 0.7071067811865476
        d = 1.0 + 0.3275911 * x
        t = pl.reciprocal(d, approx=True)
        t = t * (2.0 - d * t)
        bell = jnp.exp2((u * u) * (-0.5 * LOG2E))
        poly = t * (
            0.127414796
            + t * (-0.142248368 + t * (0.7107068705 + t * (-0.7265760135 + t * 0.5307027145)))
        )
        tail = poly * bell
        phi = jnp.where(u >= 0.0, 1.0 - tail, tail)
        return u * phi, phi + u * bell * 0.3989422804014327

    bunch = max(1, LANES // math.gcd(LANES, 4 * shard) if (4 * shard) % LANES else 1)
    span4 = 4 * shard * bunch
    n_steps = n_dp // bunch
    steps_group = n_steps // GROUPS
    tall = span4 // 4

    def expand(i, unused):
        g, c = i // steps_group, lax.rem(i, steps_group)
        raw = mm(w_up[at(g, group), at(c, span4)], low1[g, 0:group], 0, 0)
        bias = jnp.concatenate(
            [cols[at(i * bunch + n, shard), 8 + b : 9 + b] for n in range(bunch) for b in range(4)],
            axis=0,
        )
        for b in range(4):
            part = slice(b * tall, (b + 1) * tall)
            out, grad = gelu(raw[part] + bias[part])
            place = pl.ds(pl.multiple_of((i * 4 + b) * tall, tall), tall)
            act[place] = out.astype(BF16)
            slope[place] = grad.astype(BF16)
        return (unused,)

    loop(n_steps, expand, 0)

    def contract(g, acc):
        out = mm(wd[at(g, hid)], act[at(g, hid)], 0, 0)
        v = out + first[at(g, group)] + col(g, group, 5)
        v2[at(g, group)] = v
        return (acc + sub(v),)

    (acc,) = loop(GROUPS, contract, zero_row)
    mean = acc * inv
    scale2 = center(v2)

    loss, sum1, sum2 = zero_row, zero_row, zero_row
    for c in range(width // LANES):
        span = slice(c * LANES, (c + 1) * LANES)
        xhat = v2[span] * scale2
        v2[span] = xhat
        gain = cols[span, 6:7]
        full = xhat * gain + cols[span, 7:8]
        r.layer_out[:, span] = full.astype(BF16).T
        error = full - teacher[:, span].T.astype(F32)
        loss += sub(live * error * error)
        grad = live * (out_grad[:, span].T.astype(F32) + error * coef)
        vcols[span, 4:5] = jnp.sum(grad * xhat, axis=1, keepdims=True)
        vcols[span, 5:6] = jnp.sum(grad, axis=1, keepdims=True)
        grad = grad * gain
        seed[span] = grad
        sum1 += sub(grad)
        sum2 += sub(grad * xhat)
    sum1, sum2 = sum1 * inv, sum2 * inv

    def back2(g, unused):
        place = at(g, group)
        grad = scale2 * (seed[place] - sum1 - v2[place] * sum2)
        seed[place] = grad
        brief = grad.astype(BF16)
        low2[place] = brief
        vcols[place, 3:4] = jnp.sum(brief.astype(F32), axis=1, keepdims=True)
        return (unused,)

    loop(GROUPS, back2, 0)

    def back_act(i, unused):
        place = at(i, span4)
        raw = mm(wd[place], low2[at(i // steps_group, group)], 1, 0)
        slope[place] = (raw * slope[place].astype(F32)).astype(BF16)
        return (unused,)

    loop(n_steps, back_act, 0)

    def back_first(g, a, b):
        place = at(g, group)
        grad = seed[place] + mm(w_up[place], slope[at(g, hid)], 1, 0)
        xhat = v1[place]
        vcols[place, 1:2] = jnp.sum(grad * xhat, axis=1, keepdims=True)
        vcols[place, 2:3] = jnp.sum(grad, axis=1, keepdims=True)
        grad = grad * col(g, group, 3)
        seed[place] = grad
        return (a + sub(grad), b + sub(grad * xhat))


    vecs = r.vecs
    if split:
        other_y = my_dp + 1 - 2 * my_y
        side, cross, spread_z, spread_v = r.side, r.cross, r.spread_z, r.spread_v
        od_out, vec_out = r.od_out, r.vec_out
        red_send, red_recv = r.red_send, r.red_recv

        def side_copies():
            return (
                remote(
                    pack.at[:, 1 - core, pl.ds(1, 2)],
                    side.at[:, pl.ds(1, 2)],
                    red_send.at[0],
                    red_recv.at[0],
                    seq=me ^ 1,
                ),
                remote(
                    pack.at[:, 1 - core, 0],
                    side.at[:, 0],
                    red_send.at[6],
                    red_recv.at[6],
                    seq=me ^ 1,
                ),
                remote(vecs, r.vec_side, red_send.at[1], red_recv.at[1], seq=me ^ 1),
            )

        def cross_copy(j):
            z = lax.rem(my_z + 1 + j, n_z)
            return remote(
                side.at[2 * z + 1 - my_y],
                cross.at[z],
                r.cross_send.at[z],
                r.cross_recv.at[z],
                dp=other_y,
            )

        def vec_cross():
            return remote(
                r.vec_mine, r.vec_cross, red_send.at[2], red_recv.at[2], dp=other_y
            )

        def z_copy(j):
            z = lax.rem(my_z + 1 + j, n_z)
            return remote(
                side.at[2 * z + my_y],
                spread_z.at[my_z],
                r.z_send.at[j],
                r.z_recv.at[j],
                dp=2 * z + my_y,
            )

        def vz_copy(j):
            z = lax.rem(my_z + 1 + j, n_z)
            return remote(
                r.vec_sum,
                spread_v.at[my_z],
                r.vz_send.at[j],
                r.vz_recv.at[j],
                dp=2 * z + my_y,
            )

        def x_copies():
            return (
                remote(
                    r.x_mine, r.x_theirs, red_send.at[3], red_recv.at[3], seq=me ^ 2
                ),
                remote(r.vec_z, r.vec_x, red_send.at[4], red_recv.at[4], seq=me ^ 2),
            )

        def last_copy():
            return remote(
                od_out.at[core], od_out.at[core], red_send.at[5], red_recv.at[5], seq=me ^ 1
            )

        def reduce_side():
            for copy in side_copies():
                copy.wait_recv()

            def add(i, unused):
                side[i] = (pack[i, core].astype(F32) + side[i].astype(F32)).astype(BF16)
                return (unused,)

            loop(n_dp, add, 0)
            for j in range(n_z):
                cross_copy(j).start()
            r.vec_mine[...] = vecs[...] + r.vec_side[...]
            vec_cross().start()

        def reduce_cross(j):
            cross_copy(j).wait_recv()
            z = lax.rem(my_z + 1 + j, n_z)
            i = 2 * z + my_y
            side[i] = (side[i].astype(F32) + cross[z].astype(F32)).astype(BF16)
            if j < n_z - 1:
                z_copy(j).start()

        def reduce_vec():
            vec_cross().wait_recv()
            value = r.vec_mine[...] + r.vec_cross[...]
            r.vec_sum[...] = value
            spread_v[my_z] = value
            for j in range(n_z - 1):
                vz_copy(j).start()

        def reduce_z():
            for j in range(n_z - 1):
                z_copy(j).wait_recv()
                vz_copy(j).wait_recv()
            spread_z[my_z] = side[my_dp]
            value = spread_z[0].astype(F32)
            vec = spread_v[0]
            for z in range(1, n_z):
                value += spread_z[z].astype(F32)
                vec += spread_v[z]
            r.x_mine[...] = value.astype(BF16)
            r.vec_z[...] = vec
            for copy in x_copies():
                copy.start()

        def reduce_x():
            for copy in x_copies():
                copy.wait_recv()
            od_out[core] = r.x_mine[...].astype(F32) + r.x_theirs[...].astype(F32)
            vec_out[...] = r.vec_z[...] + r.vec_x[...]
            last_copy().start()

    vecs[...] = jnp.zeros_like(vecs)
    for g in range(GROUPS):
        out = mm(low1[g], slope[g * hid : (g + 1) * hid], 1, 1)
        vecs[8 + g : 9 + g] = out[group : group + 1]
        if split:
            for t in range(per_group):
                for c in range(2):
                    base = shard * t + half * c
                    pack[g * per_group + t, c, 1] = out[base : base + half].astype(BF16)
        else:
            r.g_ou[1, g * group : (g + 1) * group] = out[0:group].astype(BF16)
    sum1, sum2 = loop(GROUPS, back_first, zero_row, zero_row)
    sum1, sum2 = sum1 * inv, sum2 * inv

    for g in range(GROUPS):
        out = mm(act[g * hid : (g + 1) * hid], low2[g * group : (g + 1) * group], 1, 1)
        if split:
            for t in range(per_group):
                for c in range(2):
                    base = 4 * shard * t + 2 * shard * c
                    pack[g * per_group + t, c, 2] = jnp.concatenate(
                        [out[base + k * half : base + (k + 1) * half] for k in range(4)], axis=1
                    ).astype(BF16)
        else:
            r.g_d[g * hid : (g + 1) * hid] = out.astype(BF16)

    if split:
        side_copies()[0].start()

    def back1(g, unused):
        place = at(g, group)
        grad = scale1 * (seed[place] - sum1 - v1[place] * sum2)
        seed[place] = grad
        brief = grad.astype(BF16)
        low2[place] = brief
        vcols[place, 0:1] = jnp.sum(brief.astype(F32), axis=1, keepdims=True)
        return (unused,)

    loop(GROUPS, back1, 0)
    grad_mid = seed

    def back_context(i, unused):
        c_grad[at(i, step)] = mm(wo[at(i, step)], low2[...], 1, 0).astype(BF16)
        return (unused,)

    loop(width // step, back_context, 0)
    for d in [1] + far:
        g_copy(d).start()

    vecs[0:8] = vcols[...].T[0:8]
    mean_loss = jnp.sum(loss, axis=1, keepdims=True) / (total * width)
    vecs[12:13] = jnp.broadcast_to(mean_loss, (1, width))
    for j in range(2):
        rows = width // 2
        out = mm(context_r[j * rows : (j + 1) * rows], low2[...], 1, 1)
        if split:
            for t in range(n_dp // 2):
                for c in range(2):
                    base = shard * t + half * c
                    pack[j * (n_dp // 2) + t, c, 0] = out[base : base + half].astype(BF16)
        else:
            r.g_ou[0, j * rows : (j + 1) * rows] = out.astype(BF16)

    if split:
        for copy in side_copies()[1:]:
            copy.start()


    def clear(i, unused):
        for ref in (dq, dk, dv):
            ref[at(i, HDIM)] = jnp.zeros((HDIM, piece), F32)
        return (unused,)

    loop(heads * seq, clear, 0)
    tail_row = iota((HDIM, piece), 0)

    def prepare(t):
        for h in range(heads):
            span = slice(h * HDIM, (h + 1) * HDIM)
            grad = d_in[t, span]
            d_aug[h, t, 0:HDIM] = grad
            parts = three_parts(-sub(grad.astype(F32) * context_s[t, span].astype(F32)))
            value = jnp.zeros((HDIM, piece), F32)
            for n, part in enumerate(parts):
                value = jnp.where(tail_row == n, part.astype(F32), value)
            d_aug[h, t, HDIM:] = value.astype(BF16)

    def rows_of(h, t):
        return at(h * seq + t, HDIM)

    def weigh(buffers, t, h, k):
        p, s = buffers
        weights = jnp.exp2(mm(q_t[h, t], k_n[h, k], 0, 1))
        p[...] = weights.astype(BF16)
        s[...] = (weights * mm(d_aug[h, t], v_n[h, k], 0, 1)).astype(BF16)

    def gather_grads(buffers, t, h, k):
        p, s = buffers
        dv[rows_of(h, k)] += mm(d_aug[h, t, 0:HDIM], p[...], 1, 0)
        dk[rows_of(h, k)] += mm(q_t[h, t, 0:HDIM], s[...], 1, 0)
        dq[rows_of(h, t)] += mm(k_t[h, k], s[...], 1, 1)

    def near_row(d):
        return lambda i: (me ^ d, i // 2, me ^ (2 + lax.rem(i, 2)))

    pairs = (weigh, gather_grads, (p0, s0), (p1, s1))
    d_in[me] = c_grad[at(me, group)]
    prepare(me)
    hooks = [(), (), (), (), ()]
    if split:
        hooks = [
            ((1, reduce_side),),
            ((1, lambda: reduce_cross(0)),),
            (
                (1, lambda: reduce_cross(1)),
                (2, reduce_vec),
                (4, lambda: reduce_cross(2)),
            ),
            ((1, lambda: reduce_cross(3)),),
            ((0, reduce_z), (2, lambda: emit(0)), (4, lambda: emit(1))),
        ]
    run(2 * heads, near_row(0), *pairs, hooks[0])
    g_copy(1).wait_recv()
    prepare(me ^ 1)
    run(2 * heads, near_row(1), *pairs, hooks[1])
    for n, d in enumerate(far):
        g_copy(d).wait_recv()
        prepare(me ^ d)
        run(seq * heads, any_all(d), *pairs, hooks[2 + n])

    def turned(t, kind, h):
        return pl.ds(pl.multiple_of((t * 3 + kind) * group + h * HDIM, HDIM), HDIM)

    def fill(t, h):
        for kind, (ref, scale) in enumerate(((dq, HDIM**-0.5), (dk, 1.0 / LOG2E), (dv, 1.0))):
            d_t[turned(t, kind, h)] = (ref[rows_of(h, t)] * scale).astype(BF16)

    def whole(t, kind):
        return pl.ds(pl.multiple_of((t * 3 + kind) * group, HDIM), group)

    def states_part(t):
        out = mm(w_group[0], d_t[whole(t, 0)], 1, 0)
        out += mm(w_group[1], d_t[whole(t, 1)], 1, 0)
        out += mm(w_group[2], d_t[whole(t, 2)], 1, 0)
        dx_s[at(t, group)] = out.astype(BF16)

    if split:
        qkv_s, qkv_r, qkv_out = r.qkv_s, r.qkv_r, r.qkv_out
        owner = my_dp // per_group == me

        def qkv_copy(h, t):
            return remote(
                qkv_s.at[h, t],
                qkv_r.at[h, my_dp],
                r.q1_send.at[h, t],
                r.q1_recv.at[h, my_dp],
                dp=me * per_group + t,
            )

        def qkv_share(h, d):
            return remote(
                qkv_out.at[h], qkv_out.at[h], r.q2_send.at[h, d], r.q2_recv.at[h], seq=me ^ d
            )

    def emit(h):
        for d in range(2):
            fill(me ^ d, h)
        totals = []
        for kind in range(3):
            value = mm(x_group[0], d_t[turned(0, kind, h)], 1, 1)
            for t in range(1, seq):
                value += mm(x_group[t], d_t[turned(t, kind, h)], 1, 1)
            totals.append(value)
        if split:
            bias_rows = jnp.zeros((shard, HDIM), F32)
            bias_id = iota((shard, HDIM), 0)
            for kind in range(3):
                bias_rows = jnp.where(bias_id == kind, totals[kind][group : group + 1], bias_rows)
            for t in range(per_group):
                qkv_s[h, t] = jnp.concatenate(
                    [value[t * shard : (t + 1) * shard] for value in totals] + [bias_rows], axis=1
                ).astype(BF16)
                when(me * per_group + t != my_dp, lambda: qkv_copy(h, t).start())
        else:
            for kind in range(3):
                r.qkv_raw[h, kind] = totals[kind]

    def near_heads(i):
        j = lax.rem(i, 4)
        return me ^ (j // 2), i // 4, me ^ lax.rem(j, 2)

    for d in range(1, seq):
        g_copy(d).wait_send()
    for d in far:
        for h in range(heads):
            fill(me ^ d, h)
        states_part(me ^ d)
        dx_copy(d).start()
    if not split:
        hooks[4] = ((2, lambda: emit(0)), (4, lambda: emit(1)))
    run(4 * heads, near_heads, *pairs, hooks[4])
    emit(2)
    states_part(me ^ 1)
    dx_copy(1).start()
    states_part(me)
    dx_r[at(me, group)] = dx_s[at(me, group)]
    if split:
        reduce_x()

        @pl.when(owner)
        def _():
            for h in range(heads):
                value = qkv_s[h, my_slot].astype(F32)
                for e in range(1, n_dp):
                    src = lax.rem(my_dp + e, n_dp)
                    remote(
                        qkv_s.at[h, 0],
                        qkv_r.at[h, src],
                        r.q1_send.at[h, 0],
                        r.q1_recv.at[h, src],
                        dp=src,
                    ).wait_recv()
                    value += qkv_r[h, src].astype(F32)
                qkv_out[h] = value.astype(BF16)
                for d in range(1, seq):
                    qkv_share(h, d).start()

    for d in range(1, seq):
        dx_copy(d).wait_recv()
    for c in range(width // LANES):
        span = slice(c * LANES, (c + 1) * LANES)
        r.states_grad[:, span] = (dx_r[span].astype(F32) + grad_mid[span]).astype(BF16).T


    for d in range(1, seq):
        x_copy(d).wait_send()
        c_copy(d).wait_send()
        dx_copy(d).wait_send()
    if split:
        last_copy().wait()
        for h in range(heads):
            for t in range(per_group):
                when(me * per_group + t != my_dp, lambda: qkv_copy(h, t).wait_send())

        @pl.when(owner)
        def _():
            for h in range(heads):
                for d in range(1, seq):
                    qkv_share(h, d).wait_send()

        @pl.when(jnp.logical_not(owner))
        def _():
            for h in range(heads):
                qkv_share(h, 1).wait_recv()

        for e in range(1, n_dp):
            s_copy(e).wait_send()

        @pl.when(holder)
        def _():
            for e in range(1, n_dp):
                w_copy(my_slot, e).wait_send()

        for copy in side_copies() + x_copies():
            copy.wait_send()
        vec_cross().wait_send()
        for j in range(n_z):
            cross_copy(j).wait_send()
        for j in range(n_z - 1):
            z_copy(j).wait_send()
            vz_copy(j).wait_send()


def layer(cfg, row, collective_id, inputs):
    c = cfg
    g, l, h, s, w, f = c.group, c.piece, c.heads, c.seq, c.width, c.hidden
    n_z = c.dp // 2
    sds = jax.ShapeDtypeStruct
    dma = pltpu.SemaphoreType.DMA
    vm = pltpu.VMEM
    outputs = dict(layer_out=sds((l, w), BF16), states_grad=sds((l, w), BF16))
    if c.split:
        outputs |= dict(
            od_out=sds((2, 3, c.half, w), F32),
            qkv_out=sds((h, c.shard, 4 * HDIM), BF16),
            vec_out=sds((16, w), F32),
        )
    else:
        outputs |= dict(
            g_ou=sds((2, w, w), BF16),
            g_d=sds((f, g), BF16),
            qkv_raw=sds((h, 3, g + AUG, HDIM), F32),
            vecs=sds((16, w), F32),
        )
    scratch = dict(
        x_own=vm((w, l), BF16),
        x_group=vm((s, g + AUG, l), BF16),
        w_group=vm((3, g, g), BF16),
        w_pad=vm((3, g + AUG, h * LANES), BF16),
        q_t=vm((h, s, LANES, l), BF16),
        k_n=vm((h, s, l, LANES), BF16),
        k_t=vm((h, s, HDIM, l), BF16),
        v_n=vm((h, s, l, LANES), BF16),
        context_s=vm((s, g, l), BF16),
        context_r=vm((w, l), BF16),
        tops=vm((h * s, 1, l), F32),
        cols=vm((w, 16), F32),
        vcols=vm((w, LANES), F32),
        wide=vm((4 * w, l), F32),
        slim=vm((2 * f, l), BF16),
        c_grad=vm((w, l), BF16),
        d_in=vm((s, g, l), BF16),
        d_aug=vm((h, s, LANES, l), BF16),
        dx_r=vm((w, l), BF16),
        low1=vm((GROUPS, g + AUG, l), BF16),
        low2=vm((w, l), BF16),
        x_send=dma((s,)),
        x_recv=dma((s,)),
        c_send=dma((s,)),
        c_recv=dma((s,)),
        g_send=dma((s,)),
        g_recv=dma((s,)),
        dx_send=dma((s,)),
        dx_recv=dma((s,)),
    )
    if c.split:
        unit = (3, c.half, w)
        vec = (16, w)
        scratch |= dict(
            wo=vm((w, w), BF16),
            w_up=vm((w, w), BF16),
            wd=vm((f, g), BF16),
            smalls=vm((c.dp, 16, LANES), F32),
            pack=vm((c.dp, 2) + unit, BF16),
            w_own=vm((c.shard, 3 * g), BF16),
            w_in=vm((c.per_group, c.shard, 3 * g), BF16),
            vecs=vm(vec, F32),
            side=vm((c.dp,) + unit, BF16),
            cross=vm((n_z,) + unit, BF16),
            spread_z=vm((n_z,) + unit, BF16),
            spread_v=vm((n_z,) + vec, F32),
            x_mine=vm(unit, BF16),
            x_theirs=vm(unit, BF16),
            vec_side=vm(vec, F32),
            vec_mine=vm(vec, F32),
            vec_cross=vm(vec, F32),
            vec_sum=vm(vec, F32),
            vec_z=vm(vec, F32),
            vec_x=vm(vec, F32),
            qkv_s=vm((h, c.per_group, c.shard, 4 * HDIM), BF16),
            qkv_r=vm((h, c.dp, c.shard, 4 * HDIM), BF16),
            s_send=dma((c.dp,)),
            s_recv=dma((c.dp,)),
            w_send=dma((c.dp,)),
            w_recv=dma((c.per_group,)),
            hop_send=dma((3, c.dp)),
            hop_recv=dma((c.dp,)),
            sib_send=dma((c.dp,)),
            sib_recv=dma((c.dp,)),
            red_send=dma((7,)),
            red_recv=dma((7,)),
            cross_send=dma((n_z,)),
            cross_recv=dma((n_z,)),
            z_send=dma((n_z,)),
            z_recv=dma((n_z,)),
            vz_send=dma((n_z,)),
            vz_recv=dma((n_z,)),
            q1_send=dma((h, c.per_group)),
            q1_recv=dma((h, c.dp)),
            q2_send=dma((h, s)),
            q2_recv=dma((h,)),
        )
    names = tuple(inputs) + tuple(outputs) + tuple(scratch)
    vmem = pl.BlockSpec(memory_space=pltpu.VMEM)
    results = pl.pallas_call(
        functools.partial(layer_kernel, cfg, row, names),
        out_shape=list(outputs.values()),
        in_specs=[vmem] * len(inputs),
        out_specs=[vmem] * len(outputs),
        scratch_shapes=list(scratch.values()),
        compiler_params=pltpu.CompilerParams(
            collective_id=collective_id, has_side_effects=True, vmem_limit_bytes=VMEM_LIMIT
        ),
        name="layer",
    )(*inputs.values())
    return dict(zip(outputs, results, strict=True))


def local(
    states,
    lengths,
    teacher,
    out_grad,
    q_weight,
    k_weight,
    v_weight,
    q_bias,
    v_bias,
    o_weight,
    o_bias,
    attn_gain,
    attn_bias,
    up_weight,
    up_bias,
    down_weight,
    down_bias,
    ffn_gain,
    ffn_bias,
):
    row_count, piece, width = states.shape
    n_dp, n_seq = lax.axis_size("dp"), lax.axis_size("seq")
    me, my_dp = lax.axis_index("seq"), lax.axis_index("dp")
    shard = q_bias.shape[0]
    hidden = up_bias.shape[0] * n_dp
    cfg = Config(n_dp, n_seq, piece, width, hidden, shard)
    cfg.rows = row_count
    group = cfg.group

    def pad(v):
        return jnp.pad(v.astype(F32), ((0, 0), (0, LANES - v.shape[1])))

    vectors = (q_bias, v_bias, o_bias, attn_gain, attn_bias, down_bias, ffn_gain, ffn_bias)
    small = jnp.concatenate(
        [
            pad(jnp.stack(vectors)),
            pad(up_bias.reshape(4, shard)),
            jnp.broadcast_to(lengths.astype(F32)[:, None], (row_count, LANES)),
            jnp.zeros((4 - row_count, LANES), F32),
        ]
    )
    if not cfg.split:
        smalls = lax.all_gather(small, "dp", axis=0)
        qkv = jnp.stack((q_weight, k_weight, v_weight))
        qkv = lax.all_gather(qkv, "dp", axis=1, tiled=True)
        w_group_in = lax.dynamic_slice(qkv, (0, me * group, 0), (3, group, group))
        wo = lax.all_gather(o_weight, "dp", axis=0, tiled=True)
        wu = lax.all_gather(up_weight, "dp", axis=0, tiled=True)
        wd = lax.all_gather(down_weight, "dp", axis=0, tiled=True)

    results = []
    for n in range(row_count):
        inputs = dict(states=states[n], teacher=teacher[n], out_grad=out_grad[n])
        if cfg.split:
            inputs |= dict(
                small=small,
                wq=q_weight,
                wk=k_weight,
                wv=v_weight,
                ow=o_weight,
                uw=up_weight,
                dw=down_weight,
            )
        else:
            inputs |= dict(smalls=smalls, w_all=w_group_in, wo=wo, w_up=wu, wd=wd)
        results.append(layer(cfg, n, n, inputs))

    def summed(name):
        return sum((item[name].astype(F32) for item in results[1:]), results[0][name].astype(F32))

    layer_out = jnp.stack([item["layer_out"] for item in results])
    states_grad = jnp.stack([item["states_grad"] for item in results])
    if cfg.split:
        qkv, od, vec = summed("qkv_out"), summed("od_out"), summed("vec_out")
        at = lax.rem(my_dp, cfg.per_group) * shard
        qkv = qkv.transpose(1, 0, 2).reshape(shard, cfg.heads, 4, HDIM)
        qkv = [qkv[:, :, k].reshape(shard, group) for k in range(4)]
        bias = lax.dynamic_slice(qkv[3], (0, at), (4, shard))
        grad_qb, grad_vb = bias[0], bias[2]
        grad_ow = od[:, 0].reshape(shard, width)
        grad_uw = od[:, 1].reshape(shard, width)
        grad_dw = od[:, 2].reshape(2, cfg.half, 4, group).transpose(0, 2, 1, 3)
        grad_dw = grad_dw.reshape(4 * shard, group)
    else:
        qkv_g, g_ou, g_d, vecs = (summed(n) for n in ("qkv_raw", "g_ou", "g_d", "vecs"))
        qkv_g = qkv_g.transpose(1, 2, 0, 3).reshape(3, group + AUG, group)
        whole = jnp.zeros((3, width + GROUPS * AUG, group), F32)
        whole = lax.dynamic_update_slice(whole, qkv_g[:, :group], (0, me * group, 0))
        whole = lax.dynamic_update_slice(whole, qkv_g[:, group:], (0, width + me * AUG, 0))
        whole, g_ou, g_d, vec = lax.psum((whole, g_ou, g_d, vecs), ("dp", "seq"))
        qkv = lax.dynamic_slice(whole, (0, my_dp * shard, 0), (3, shard, group))
        biases = whole[:, width::AUG].reshape(3, width)
        grad_qb = lax.dynamic_slice(biases[0], (my_dp * shard,), (shard,))
        grad_vb = lax.dynamic_slice(biases[2], (my_dp * shard,), (shard,))
        g_ou = lax.dynamic_slice(g_ou, (0, my_dp * shard, 0), (2, shard, width))
        grad_ow, grad_uw = g_ou[0], g_ou[1]
        grad_dw = lax.dynamic_slice(g_d, (my_dp * 4 * shard, 0), (4 * shard, group))

    mine = lax.dynamic_slice(vec[:6], (0, my_dp * shard), (6, shard))
    grad_ub = lax.dynamic_slice(vec[8:12].reshape(-1), (my_dp * 4 * shard,), (4 * shard,))
    return (
        layer_out,
        vec[12, 0],
        states_grad,
        qkv[0],
        qkv[1],
        qkv[2],
        grad_qb,
        grad_vb,
        grad_ow,
        mine[0],
        mine[1],
        mine[2],
        grad_uw,
        grad_ub,
        grad_dw,
        mine[3],
        mine[4],
        mine[5],
    )


def solution(mesh):
    rows3 = P("dp", "seq", None)
    matrix = P("dp", None)
    vector = P("dp")
    return jax.shard_map(
        local,
        mesh=mesh,
        in_specs=(rows3, vector, rows3, rows3)
        + (matrix,) * 3
        + (vector,) * 2
        + (matrix,)
        + (vector,) * 3
        + (matrix, vector, matrix)
        + (vector,) * 3,
        out_specs=(rows3, P(), rows3)
        + (matrix,) * 3
        + (vector,) * 2
        + (matrix,)
        + (vector,) * 3
        + (matrix, vector, matrix)
        + (vector,) * 3,
        check_vma=False,
    )
```

```python
import functools
import math
import types

import jax
import jax.numpy as jnp
from jax import lax
from jax.experimental import pallas as pl
from jax.experimental.pallas import tpu as pltpu
from jax.sharding import PartitionSpec as P

HDIM = 64
GROUPS = 4
EPSILON = 1e-12
NEG_FILL = -1e30
LANES = 128
AUG = 16
LOG2E = 1.4426950408889634
MESH = pl.DeviceIdType.MESH
F32 = jnp.float32
BF16 = jnp.bfloat16
VMEM_LIMIT = 60 * 1024 * 1024


def mm(left, right, left_dim, right_dim):
    return lax.dot_general(
        left, right, (((left_dim,), (right_dim,)), ((), ())), preferred_element_type=F32
    )


def iota(shape, dim):
    return lax.broadcasted_iota(jnp.int32, shape, dim)


def remote(src, dst, send_sem, recv_sem, **where):
    return pltpu.make_async_remote_copy(
        src_ref=src,
        dst_ref=dst,
        send_sem=send_sem,
        recv_sem=recv_sem,
        device_id=where,
        device_id_type=MESH,
    )


def three_parts(row):
    high = row.astype(BF16)
    rest = row - high.astype(F32)
    middle = rest.astype(BF16)
    low = (rest - middle.astype(F32)).astype(BF16)
    return high, middle, low


class Config:
    def __init__(self, dp, seq, piece, width, hidden, shard):
        self.dp, self.seq, self.piece, self.width, self.hidden, self.shard = (
            dp,
            seq,
            piece,
            width,
            hidden,
            shard,
        )
        self.slots = piece * seq
        self.group = width // GROUPS
        self.heads = self.group // HDIM
        self.per_group = dp // GROUPS
        self.split = shard % 32 == 0 and seq == 4 and dp == 8
        self.half = shard // 2
        self.quarter = hidden // dp // 4


def greet(cfg, me, my_dp):
    barrier = pltpu.get_barrier_semaphore()
    count = cfg.seq - 1
    for d in range(1, cfg.seq):
        pl.semaphore_signal(barrier, inc=1, device_id={"seq": me ^ d}, device_id_type=MESH)
    if cfg.split:
        count += cfg.dp - 1
        for e in range(1, cfg.dp):
            pl.semaphore_signal(
                barrier, inc=1, device_id={"dp": lax.rem(my_dp + e, cfg.dp)}, device_id_type=MESH
            )
    return lambda: pl.semaphore_wait(barrier, count)


def layer_kernel(cfg, row, names, *refs):
    r = types.SimpleNamespace(**dict(zip(names, refs, strict=True)))
    split = cfg.split
    me = lax.axis_index("seq")
    my_dp = lax.axis_index("dp")
    piece, width, group, heads, seq = cfg.piece, cfg.width, cfg.group, cfg.heads, cfg.seq
    shard, half, n_dp, per_group = cfg.shard, cfg.half, cfg.dp, cfg.per_group
    hid = cfg.hidden // GROUPS
    n_z = n_dp // 2
    core = lax.rem(me, 2)
    my_z, my_y = my_dp // 2, lax.rem(my_dp, 2)
    far = [d for d in range(seq - 1, 1, -1)]

    states = r.states
    teacher, out_grad = r.states_grad, r.layer_out
    late = [
        pltpu.make_async_copy(r.teacher, teacher, r.late_sem.at[0]),
        pltpu.make_async_copy(r.out_grad, out_grad, r.late_sem.at[1]),
    ]
    x_own, x_group, w_group, w_pad, smalls = (
        r.x_own,
        r.x_group,
        r.w_group,
        r.w_pad,
        r.smalls,
    )
    q_t, k_n, k_t, v_n = r.q_t, r.k_n, r.k_t, r.v_n
    context_s, context_r = r.context_s, r.context_r
    cols, vcols = r.cols, r.vcols
    wide, slim = r.wide, r.slim
    wo, w_up, wd = r.wo, r.w_up, r.wd
    c_grad, d_in, dx_r = r.c_grad, r.d_in, r.dx_r
    dx_s = c_grad
    tall1 = group + AUG
    low = r.low
    low2 = low.at[GROUPS * tall1 :]

    def low1(g, start, size):
        return pl.ds(pl.multiple_of(g * tall1 + start, AUG), size)

    def d_aug(h, t, start, size):
        return pl.ds(pl.multiple_of((h * seq + t) * LANES + start, HDIM), size)

    score0, score1 = wide.at[0:piece], wide.at[piece : 2 * piece]
    gathered = r.gathered
    v1, first, v2, seed = (wide.at[i * width : (i + 1) * width] for i in range(4))
    dq, dk, dv = (wide.at[i * width : (i + 1) * width] for i in range(3))
    act, slope = slim.at[0 : cfg.hidden], slim.at[cfg.hidden : 2 * cfg.hidden]
    p0, p1, s0, s1 = (slim.at[i * piece : (i + 1) * piece] for i in range(4))
    d_t = slope

    def at(i, n):
        return pl.ds(pl.multiple_of(i * n, n), n)

    def loop(count, body, *init):
        return lax.fori_loop(0, count, lambda i, c: body(i, *c), tuple(init))

    def sub(v):
        return jnp.sum(v, axis=0, keepdims=True)


    def to_seq(sems, src, dst, d):
        return remote(src, dst, sems[0].at[d], sems[1].at[d], seq=me ^ d)

    def x_copy(d):
        return to_seq((r.x_send, r.x_recv), x_own.at[at(me ^ d, group)], x_group.at[me, pl.ds(0, group)], d)

    def c_copy(d):
        return to_seq((r.c_send, r.c_recv), context_s.at[me ^ d], context_r.at[at(me, group)], d)

    def g_copy(d):
        return to_seq((r.g_send, r.g_recv), c_grad.at[at(me ^ d, group)], d_in.at[me], d)

    def dx_copy(d):
        return to_seq((r.dx_send, r.dx_recv), dx_s.at[at(me ^ d, group)], dx_r.at[at(me, group)], d)

    if split:
        pack = r.pack
        w_in = r.w_in
        my_slot = lax.rem(my_dp, per_group)
        holder = my_dp // per_group == me

        def s_copy(e):
            return remote(
                smalls.at[my_dp],
                smalls.at[my_dp],
                r.s_send.at[e],
                r.s_recv.at[e],
                dp=lax.rem(my_dp + e, n_dp),
            )

        def w_along(step):
            return remote(
                w_in.at[my_y],
                w_in.at[my_y],
                r.w_send.at[step + 1],
                r.w_recv.at[0],
                dp=my_dp + 2 * step,
            )

        def w_across():
            return remote(
                w_in.at[my_y], w_in.at[my_y], r.w_send.at[1], r.w_recv.at[1], dp=my_dp + 1 - 2 * my_y
            )

        def w_over():
            return remote(
                w_in.at[1 - my_y], w_in.at[1 - my_y], r.w_send.at[1], r.w_recv.at[1], dp=my_dp
            )

        def w_each(fn):
            pl.when((my_z >= me) & (my_z < n_z - 1))(lambda: fn(w_along(1)))
            pl.when((my_z <= me) & (my_z > 0))(lambda: fn(w_along(-1)))
            fn(w_across())

        def hop(kind, i, **where):
            ref = pack.at[i, core]
            return remote(ref, ref, r.hop_send.at[kind, i], r.hop_recv.at[i], **where)

        def up(i):
            return hop(0, i, dp=my_dp + 2)

        def down(i):
            return hop(1, i, dp=my_dp - 2)

        def across(i):
            return hop(2, i, dp=my_dp + 1 - 2 * my_y)

        def beside(i):
            ref = pack.at[i, core]
            return remote(ref, ref, r.sib_send.at[i], r.sib_recv.at[i], seq=me ^ 1)

        def when(condition, fn):
            pl.when(condition)(fn)

        def gather_start():
            when(my_z < n_z - 1, lambda: up(my_dp).start())
            when(my_z > 0, lambda: down(my_dp).start())
            across(my_dp).start()

        def gather_z(k):
            below, above = my_dp - 2 * k, my_dp + 2 * k

            @pl.when(my_z >= k)
            def _():
                hop(0, below, dp=my_dp).wait_recv()
                when(my_z < n_z - 1, lambda: up(below).start())
                across(below).start()
                beside(below).start()

            @pl.when(my_z + k < n_z)
            def _():
                hop(0, above, dp=my_dp).wait_recv()
                when(my_z > 0, lambda: down(above).start())
                across(above).start()
                beside(above).start()

        def gather_y(k):
            other = my_dp + 1 - 2 * my_y

            def take(i):
                hop(2, i, dp=my_dp).wait_recv()
                beside(i).start()

            if k == 0:
                take(other)
            else:
                when(my_z >= k, lambda: take(other - 2 * k))
                when(my_z + k < n_z, lambda: take(other + 2 * k))

        def gather_end():
            for e in range(1, n_dp):
                copy = beside(lax.rem(my_dp + e, n_dp))
                copy.wait()

            when(my_z < n_z - 1, lambda: up(my_dp).wait_send())
            when(my_z > 0, lambda: down(my_dp).wait_send())
            across(my_dp).wait_send()
            for k in range(1, n_z):
                below, above = my_dp - 2 * k, my_dp + 2 * k

                @pl.when(my_z >= k)
                def _():
                    when(my_z < n_z - 1, lambda: up(below).wait_send())
                    across(below).wait_send()

                @pl.when(my_z + k < n_z)
                def _():
                    when(my_z > 0, lambda: down(above).wait_send())
                    across(above).wait_send()


    wait_entry = greet(cfg, me, my_dp)
    for c in range(0, width, LANES):
        x_own[c : c + LANES] = states[:, c : c + LANES].T
    if split:
        for c in range(2):
            pack[my_dp, c, 0] = r.ow[c * half : (c + 1) * half]
            pack[my_dp, c, 1] = r.uw[c * half : (c + 1) * half]
            for k in range(2):
                pack[my_dp, c, 2, :, k * 4 * shard : (k + 1) * 4 * shard] = r.dw[
                    (2 * c + k) * half : (2 * c + k + 1) * half
                ]
        smalls[my_dp] = jnp.zeros((16, LANES), F32)
        for n, ref in enumerate((r.qb, r.vb, r.ob, r.ag, r.ab, r.db, r.fg, r.fb)):
            smalls[my_dp, n : n + 1, 0:shard] = ref[...].astype(F32)
        for n in range(4):
            smalls[my_dp, 8 + n : 9 + n, 0:shard] = r.ub[:, n * shard : (n + 1) * shard].astype(F32)
        for n in range(cfg.rows):
            smalls[my_dp, 12 + n : 13 + n] = jnp.broadcast_to(
                r.lengths[n : n + 1].astype(F32), (1, LANES)
            )

        @pl.when(holder)
        def _():
            w_in[my_y] = jnp.concatenate(
                [ref[...].astype(F32) for ref in (r.wq, r.wk, r.wv)], axis=1
            ).astype(BF16)

    wait_entry()
    if split:
        for e in range(1, n_dp):
            s_copy(e).start()

        @pl.when(holder)
        def _():
            w_each(lambda copy: copy.start())

    for d in range(1, seq):
        x_copy(d).start()
    for copy in late:
        copy.start()
    x_group[me, 0:group] = x_own[at(me, group)]


    n_cols = heads * LANES
    lane = iota((group, n_cols), 1)
    spread = jnp.where(
        (((lane >> 7) * HDIM + (lane & 127)) == iota((group, n_cols), 0)) & ((lane & 127) < HDIM),
        1.0,
        0.0,
    ).astype(BF16)
    if split:
        @pl.when(jnp.logical_not(holder))
        def _():
            remote(
                w_in.at[my_y], w_in.at[my_y], r.w_send.at[1], r.w_recv.at[0], dp=my_dp
            ).wait_recv()
            w_each(lambda copy: copy.start())

        for e in range(1, n_dp):
            s_copy(e).wait_recv()
        w_over().wait_recv()
        for t in range(per_group):
            for kind in range(3):
                w_group[kind, t * shard : (t + 1) * shard] = w_in[
                    t, :, kind * group : (kind + 1) * group
                ]
        gather_start()
    else:
        for kind in range(3):
            w_group[kind] = r.w_all[kind]
    for kind in range(3):
        w_pad[kind, 0:group] = mm(w_group[kind], spread, 1, 0).astype(BF16)
    vec_rows = jnp.zeros((AUG, n_cols), F32)
    lane = iota((LANES, n_cols), 1)
    source = iota((LANES, n_cols), 0)
    for t in range(per_group):
        spread = jnp.where(
            (((lane >> 7) * HDIM + (lane & 127)) == source + t * shard)
            & ((lane & 127) < HDIM)
            & (source < shard),
            1.0,
            0.0,
        ).astype(BF16)
        vec_rows += mm(smalls[me * per_group + t].astype(BF16), spread, 1, 0)
    row_id = iota((AUG, n_cols), 0)
    lane = iota((AUG, n_cols), 1) & 127
    zero = jnp.zeros((AUG, n_cols), F32)
    top_row = row_id == 0
    w_pad[0, group:] = jnp.where(top_row, vec_rows[0:1], zero).astype(BF16)
    ones_k = (top_row & (lane > HDIM) & (lane <= HDIM + 3)) | ((row_id == 1) & (lane == HDIM))
    w_pad[1, group:] = jnp.where(ones_k, 1.0, zero).astype(BF16)
    ones_v = (lane >= HDIM) & (lane < HDIM + 3)
    w_pad[2, group:] = jnp.where(top_row, jnp.where(ones_v, 1.0, vec_rows[1:2]), zero).astype(BF16)

    length = smalls[my_dp, 12 + row : 13 + row, 0:1]
    aug_row = iota((AUG, piece), 0)
    factor = LOG2E * HDIM**-0.5
    deep = HDIM + AUG

    def v_t(h, t):
        return pl.ds(pl.multiple_of((h * seq + t) * deep, AUG), deep)

    def project(t):
        slot = (iota((AUG, piece), 1) + t * piece).astype(F32)
        mask = jnp.where(slot < length, 0.0, NEG_FILL)
        x_group[t, group:] = jnp.where(
            aug_row == 0, 1.0, jnp.where(aug_row == 1, mask, 0.0)
        ).astype(BF16)
        x = x_group[t]
        queries = mm(w_pad[0], x, 0, 0) * factor
        keys_t = mm(w_pad[1], x, 0, 0)
        values_t = mm(w_pad[2], x, 0, 0)
        keys_n = mm(x, w_pad[1], 0, 0)
        values_n = mm(x, w_pad[2], 0, 0)
        rest = jnp.where(iota((HDIM, piece), 0) == 0, 1.0, 0.0).astype(BF16)
        for h in range(heads):
            span = slice(h * LANES, h * LANES + HDIM)
            q_t[h, t, 0:HDIM] = queries[span].astype(BF16)
            q_t[h, t, HDIM:] = rest
            k_t[h, t] = keys_t[span].astype(BF16)
            slim[v_t(h, t)] = values_t[h * LANES : h * LANES + deep].astype(BF16)
            k_n[h, t] = keys_n[:, h * LANES : (h + 1) * LANES].astype(BF16)
            v_n[h, t] = values_n[:, h * LANES : (h + 1) * LANES].astype(BF16)


    tops = r.tops

    def sums(h, t):
        return pl.ds(pl.multiple_of((h * seq + t) * deep, AUG), deep)

    def clear_sums(i, unused):
        gathered[pl.ds(pl.multiple_of(i * deep, AUG), deep)] = jnp.zeros((deep, piece), F32)
        tops[i] = jnp.full((1, piece), NEG_FILL, F32)
        return (unused,)

    loop(heads * seq, clear_sums, 0)

    per_part = seq * heads

    def run(count, place, first_part, last_part, a, b, hooks=()):
        first_part(a, *place(0))

        def two(u, unused):
            if hooks:
                due = u == hooks[0][0]
                for when_u, fn in hooks[1:]:
                    due = due | (u == when_u)

                @pl.when(due)
                def _():
                    for when_u, fn in hooks:
                        pl.when(u == when_u)(fn)

            first_part(b, *place(2 * u + 1))
            last_part(a, *place(2 * u))
            first_part(a, *place(2 * u + 2))
            last_part(b, *place(2 * u + 1))
            return (unused,)

        loop(count // 2 - 1, two, 0)
        first_part(b, *place(count - 1))
        last_part(a, *place(count - 2))
        last_part(b, *place(count - 1))

    def score(buffer, t, h, k):
        buffer[...] = mm(k_n[h, k], q_t[h, t], 1, 0)

    def absorb(buffer, t, h, k):
        i = h * seq + t
        old = tops[i]
        top = jnp.maximum(old, jnp.max(buffer[...], axis=0, keepdims=True))
        weights = jnp.exp2(buffer[...] - top).astype(BF16)
        tops[i] = top
        place = sums(h, t)
        gathered[place] = gathered[place] * jnp.exp2(old - top) + mm(slim[v_t(h, k)], weights, 1, 0)

    def settle(t):
        for h in range(heads):
            total = gathered[sums(h, t)]
            mass = total[HDIM : HDIM + 1]
            context_s[t, h * HDIM : (h + 1) * HDIM] = (total[0:HDIM] / mass).astype(BF16)
            parts = three_parts(-(tops[h * seq + t] + jnp.log2(mass)))
            value = jnp.where(aug_row == 0, 1.0, 0.0)
            for n, part in enumerate(parts):
                value = jnp.where(aug_row == n + 1, part.astype(F32), value)
            q_t[h, t, HDIM:deep] = value.astype(BF16)

    def place_forward(i):
        part, j = i // per_part, lax.rem(i, per_part)
        is_far, tail = lax.rem((part + 1) // 2, 2), part // 3
        d_q = is_far * (4 - part) + (1 - is_far) * (j // (2 * heads))
        h = is_far * (j // seq) + (1 - is_far) * (lax.rem(j, 2 * heads) // 2)
        d_k = is_far * lax.rem(j, seq) + (1 - is_far) * (lax.rem(j, 2) + 2 * tail)
        return me ^ d_q, h, me ^ d_k

    def far_states():
        for d in far:
            x_copy(d).wait_recv()
        loop(2, lambda i, unused: (project(me ^ (2 + i)), unused)[1:], 0)

    def far_context(d):
        settle(me ^ d)
        c_copy(d).start()

    hooks = [
        (per_part // 2 - 1, far_states),
        (per_part, lambda: far_context(far[0])),
        (per_part * 3 // 2, lambda: far_context(far[1])),
    ]
    if split:
        hooks += [
            (6, lambda: gather_z(1)),
            (9, lambda: gather_y(0)),
            (11, lambda: gather_z(2)),
            (13, lambda: gather_y(1)),
            (16, lambda: gather_z(3)),
            (19, lambda: gather_y(2)),
            (22, lambda: gather_y(3)),
        ]
    project(me)
    x_copy(1).wait_recv()
    project(me ^ 1)
    run(4 * per_part, place_forward, score, absorb, score0, score1, hooks)
    settle(me ^ 1)
    c_copy(1).start()
    settle(me)
    context_r[at(me, group)] = context_s[me]
    if split:
        gather_end()

        def unpack(i, unused):
            for c in range(2):
                wo[pl.ds(pl.multiple_of(i * shard + c * half, AUG), half)] = pack[i, c, 0]
                w_up[pl.ds(pl.multiple_of(i * shard + c * half, AUG), half)] = pack[i, c, 1]
                for k in range(2):
                    wd[
                        pl.ds(
                            pl.multiple_of(i // per_group * group + (2 * c + k) * half, AUG), half
                        ),
                        pl.ds(
                            pl.multiple_of(lax.rem(i, per_group) * 4 * shard, LANES), 4 * shard
                        ),
                    ] = pack[i, c, 2, :, k * 4 * shard : (k + 1) * 4 * shard]
            return (unused,)

        loop(n_dp, unpack, 0)


    for i in range(n_dp):
        turned = smalls[i].T
        cols[i * shard : (i + 1) * shard] = turned[0:shard]
    vcols[...] = jnp.zeros_like(vcols)
    inv = 1.0 / width
    total = jnp.sum(smalls[:, 12:13, 0:1], axis=0)
    for n in range(1, cfg.rows):
        total += jnp.sum(smalls[:, 12 + n : 13 + n, 0:1], axis=0)
    slot = (iota((1, piece), 1) + me * piece).astype(F32)
    live = jnp.where(slot < length, 1.0, 0.0)
    coef = 2.0 / (total * width)
    zero_row = jnp.zeros((1, piece), F32)

    def col(i, n, which):
        return cols[at(i, n), which : which + 1]

    for d in range(1, seq):
        c_copy(d).wait_recv()

    step = 256

    def attn_out(i, acc):
        out = mm(wo[:, at(i, step)], context_r[...], 0, 0)
        v = out + x_own[at(i, step)].astype(F32) + col(i, step, 2)
        v1[at(i, step)] = v
        return (acc + sub(v),)

    (acc,) = loop(width // step, attn_out, zero_row)
    mean = acc * inv

    def center(ref):
        def body(g, acc):
            v = ref[at(g, group)] - mean
            ref[at(g, group)] = v
            return (acc + sub(v * v),)

        (acc,) = loop(GROUPS, body, zero_row)
        return lax.rsqrt(acc * inv + EPSILON)

    scale1 = center(v1)

    def norm1(g, unused):
        v = v1[at(g, group)] * scale1
        v1[at(g, group)] = v
        out = v * col(g, group, 3) + col(g, group, 4)
        first[at(g, group)] = out
        low[low1(g, 0, group)] = out.astype(BF16)
        low[low1(g, group, AUG)] = jnp.where(aug_row == 0, 1.0, 0.0).astype(BF16)
        return (unused,)

    loop(GROUPS, norm1, 0)

    def gelu(u):
        d = 1.0 + (0.3275911 * 0.7071067811865476) * jnp.abs(u)
        t = pl.reciprocal(d, approx=True)
        t = t * (2.0 - d * t)
        bell = jnp.exp2((u * u) * (-0.5 * LOG2E))
        poly = t * (
            0.127414796
            + t * (-0.142248368 + t * (0.7107068705 + t * (-0.7265760135 + t * 0.5307027145)))
        )
        tail = poly * bell
        phi = jnp.where(u >= 0.0, 1.0 - tail, tail)
        return u * phi, phi + u * bell * 0.3989422804014327

    bunch = max(1, LANES // math.gcd(LANES, 4 * shard) if (4 * shard) % LANES else 1)
    span4 = 4 * shard * bunch
    n_steps = n_dp // bunch
    steps_group = n_steps // GROUPS
    tall = span4 // 4

    raw0, raw1 = wide.at[2 * width : 2 * width + span4], wide.at[3 * width : 3 * width + span4]

    def expand(raw, i):
        g, c = i // steps_group, lax.rem(i, steps_group)
        raw[...] = mm(w_up[at(g, group), at(c, span4)], low[low1(g, 0, group)], 0, 0)

    def activate(raw, i):
        bias = jnp.concatenate(
            [cols[at(i * bunch + n, shard), 8 + b : 9 + b] for n in range(bunch) for b in range(4)],
            axis=0,
        )
        for b in range(4):
            part = slice(b * tall, (b + 1) * tall)
            out, grad = gelu(raw[part] + bias[part])
            place = pl.ds(pl.multiple_of((i * 4 + b) * tall, tall), tall)
            act[place] = out.astype(BF16)
            slope[place] = grad.astype(BF16)

    run(n_steps, lambda i: (i,), expand, activate, raw0, raw1)

    def contract(g, acc):
        out = mm(wd[at(g, group)], act[at(g, hid)], 1, 0)
        v = out + first[at(g, group)] + col(g, group, 5)
        v2[at(g, group)] = v
        return (acc + sub(v),)

    (acc,) = loop(GROUPS, contract, zero_row)
    mean = acc * inv
    scale2 = center(v2)

    for copy in late:
        copy.wait()
    loss, sum1, sum2 = zero_row, zero_row, zero_row
    for c in range(width // LANES):
        span = slice(c * LANES, (c + 1) * LANES)
        xhat = v2[span] * scale2
        v2[span] = xhat
        gain = cols[span, 6:7]
        full = xhat * gain + cols[span, 7:8]
        error = full - teacher[:, span].T.astype(F32)
        loss += sub(live * error * error)
        grad = live * (out_grad[:, span].T.astype(F32) + error * coef)
        r.layer_out[:, span] = full.astype(BF16).T
        vcols[span, 4:5] = jnp.sum(grad * xhat, axis=1, keepdims=True)
        vcols[span, 5:6] = jnp.sum(grad, axis=1, keepdims=True)
        grad = grad * gain
        seed[span] = grad
        sum1 += sub(grad)
        sum2 += sub(grad * xhat)
    sum1, sum2 = sum1 * inv, sum2 * inv

    def back2(g, unused):
        place = at(g, group)
        grad = scale2 * (seed[place] - sum1 - v2[place] * sum2)
        seed[place] = grad
        brief = grad.astype(BF16)
        low2[place] = brief
        vcols[place, 3:4] = jnp.sum(brief.astype(F32), axis=1, keepdims=True)
        return (unused,)

    loop(GROUPS, back2, 0)

    def back_act(i, unused):
        place = at(i, span4)
        g, c = i // steps_group, lax.rem(i, steps_group)
        raw = mm(wd[at(g, group), at(c, span4)], low2[at(g, group)], 0, 0)
        slope[place] = (raw * slope[place].astype(F32)).astype(BF16)
        return (unused,)

    loop(n_steps, back_act, 0)

    def back_first(g, a, b):
        place = at(g, group)
        grad = seed[place] + mm(w_up[place], slope[at(g, hid)], 1, 0)
        xhat = v1[place]
        vcols[place, 1:2] = jnp.sum(grad * xhat, axis=1, keepdims=True)
        vcols[place, 2:3] = jnp.sum(grad, axis=1, keepdims=True)
        grad = grad * col(g, group, 3)
        seed[place] = grad
        return (a + sub(grad), b + sub(grad * xhat))


    vecs = r.vecs
    if split:
        other_y = my_dp + 1 - 2 * my_y
        side, cross, spread_z, spread_v = r.side, r.cross, r.spread_z, r.spread_v
        od_out, vec_out = r.od_out, r.vec_out
        red_send, red_recv = r.red_send, r.red_recv

        def side_copies():
            return (
                remote(
                    pack.at[:, 1 - core, pl.ds(1, 2)],
                    side.at[:, pl.ds(1, 2)],
                    red_send.at[0],
                    red_recv.at[0],
                    seq=me ^ 1,
                ),
                remote(
                    pack.at[:, 1 - core, 0],
                    side.at[:, 0],
                    red_send.at[6],
                    red_recv.at[6],
                    seq=me ^ 1,
                ),
                remote(vecs, r.vec_side, red_send.at[1], red_recv.at[1], seq=me ^ 1),
            )

        def cross_copy(j):
            z = lax.rem(my_z + 1 + j, n_z)
            return remote(
                side.at[2 * z + 1 - my_y],
                cross.at[z],
                r.cross_send.at[z],
                r.cross_recv.at[z],
                dp=other_y,
            )

        def vec_cross():
            return remote(
                r.vec_mine, r.vec_cross, red_send.at[2], red_recv.at[2], dp=other_y
            )

        def z_copy(j):
            z = lax.rem(my_z + 1 + j, n_z)
            return remote(
                side.at[2 * z + my_y],
                spread_z.at[my_z],
                r.z_send.at[j],
                r.z_recv.at[j],
                dp=2 * z + my_y,
            )

        def vz_copy(j):
            z = lax.rem(my_z + 1 + j, n_z)
            return remote(
                r.vec_sum,
                spread_v.at[my_z],
                r.vz_send.at[j],
                r.vz_recv.at[j],
                dp=2 * z + my_y,
            )

        def x_copies():
            return (
                remote(
                    r.x_mine, r.x_theirs, red_send.at[3], red_recv.at[3], seq=me ^ 2
                ),
                remote(r.vec_z, r.vec_x, red_send.at[4], red_recv.at[4], seq=me ^ 2),
            )

        def last_copy():
            return remote(
                od_out.at[core], od_out.at[core], red_send.at[5], red_recv.at[5], seq=me ^ 1
            )

        def reduce_side():
            for copy in side_copies():
                copy.wait_recv()

            def add(i, unused):
                side[i] = (pack[i, core].astype(F32) + side[i].astype(F32)).astype(BF16)
                return (unused,)

            loop(n_dp, add, 0)
            r.vec_mine[...] = vecs[...] + r.vec_side[...]
            vec_cross().start()
            for j in range(n_z):
                cross_copy(j).start()

        def reduce_cross(j):
            cross_copy(j).wait_recv()
            z = lax.rem(my_z + 1 + j, n_z)
            i = 2 * z + my_y
            side[i] = (side[i].astype(F32) + cross[z].astype(F32)).astype(BF16)
            if j < n_z - 1:
                z_copy(j).start()

        def reduce_vec():
            vec_cross().wait_recv()
            value = r.vec_mine[...] + r.vec_cross[...]
            r.vec_sum[...] = value
            spread_v[my_z] = value
            for j in range(n_z - 1):
                vz_copy(j).start()

        def reduce_z():
            for j in range(n_z - 1):
                z_copy(j).wait_recv()
                vz_copy(j).wait_recv()
            spread_z[my_z] = side[my_dp]
            value = spread_z[0].astype(F32)
            vec = spread_v[0]
            for z in range(1, n_z):
                value += spread_z[z].astype(F32)
                vec += spread_v[z]
            r.x_mine[...] = value.astype(BF16)
            r.vec_z[...] = vec
            for copy in x_copies():
                copy.start()

        def reduce_x():
            for copy in x_copies():
                copy.wait_recv()
            od_out[core] = r.x_mine[...].astype(F32) + r.x_theirs[...].astype(F32)
            vec_out[...] = r.vec_z[...] + r.vec_x[...]
            last_copy().start()

    vecs[...] = jnp.zeros_like(vecs)
    for g in range(GROUPS):
        out = mm(low[low1(g, 0, tall1)], slope[g * hid : (g + 1) * hid], 1, 1)
        vecs[8 + g : 9 + g] = out[group : group + 1]
        if split:
            for t in range(per_group):
                for c in range(2):
                    base = shard * t + half * c
                    pack[g * per_group + t, c, 1] = out[base : base + half].astype(BF16)
        else:
            r.g_all[1, g * group : (g + 1) * group] = out[0:group].astype(BF16)
    sum1, sum2 = loop(GROUPS, back_first, zero_row, zero_row)
    sum1, sum2 = sum1 * inv, sum2 * inv

    for g in range(GROUPS):
        out = mm(low2[g * group : (g + 1) * group], act[g * hid : (g + 1) * hid], 1, 1)
        if split:
            for t in range(per_group):
                for c in range(2):
                    for k in range(2):
                        pack[g * per_group + t, c, 2, :, k * 4 * shard : (k + 1) * 4 * shard] = (
                            out[
                                (2 * c + k) * half : (2 * c + k + 1) * half,
                                t * 4 * shard : (t + 1) * 4 * shard,
                            ].astype(BF16)
                        )
        else:
            r.g_all[2, g * group : (g + 1) * group] = out.astype(BF16)

    if split:
        side_copies()[0].start()

    def back1(g, unused):
        place = at(g, group)
        grad = scale1 * (seed[place] - sum1 - v1[place] * sum2)
        seed[place] = grad
        brief = grad.astype(BF16)
        low2[place] = brief
        vcols[place, 0:1] = jnp.sum(brief.astype(F32), axis=1, keepdims=True)
        return (unused,)

    loop(GROUPS, back1, 0)
    grad_mid = seed

    def back_context(i, unused):
        c_grad[at(i, step)] = mm(wo[at(i, step)], low2[...], 1, 0).astype(BF16)
        return (unused,)

    loop(width // step, back_context, 0)
    for d in [1] + far:
        g_copy(d).start()

    vecs[0:8] = vcols[...].T[0:8]
    mean_loss = jnp.sum(loss, axis=1, keepdims=True) / (total * width)
    vecs[12:13] = jnp.broadcast_to(mean_loss, (1, width))
    for j in range(2):
        rows = width // 2
        out = mm(context_r[j * rows : (j + 1) * rows], low2[...], 1, 1)
        if split:
            for t in range(n_dp // 2):
                for c in range(2):
                    base = shard * t + half * c
                    pack[j * (n_dp // 2) + t, c, 0] = out[base : base + half].astype(BF16)
        else:
            r.g_all[0, j * rows : (j + 1) * rows] = out.astype(BF16)

    if split:
        for copy in side_copies()[1:]:
            copy.start()


    def clear(i, unused):
        for ref in (dq, dk, dv):
            ref[at(i, HDIM)] = jnp.zeros((HDIM, piece), F32)
        return (unused,)

    loop(heads * seq, clear, 0)
    tail_row = iota((HDIM, piece), 0)

    def prepare(t):
        for h in range(heads):
            span = slice(h * HDIM, (h + 1) * HDIM)
            grad = d_in[t, span]
            low[d_aug(h, t, 0, HDIM)] = grad
            parts = three_parts(-sub(grad.astype(F32) * context_s[t, span].astype(F32)))
            value = jnp.zeros((HDIM, piece), F32)
            for n, part in enumerate(parts):
                value = jnp.where(tail_row == n, part.astype(F32), value)
            low[d_aug(h, t, HDIM, HDIM)] = value.astype(BF16)

    def rows_of(h, t):
        return at(h * seq + t, HDIM)

    def weigh(buffers, t, h, k):
        p, s = buffers
        weights = jnp.exp2(mm(q_t[h, t], k_n[h, k], 0, 1))
        p[...] = weights.astype(BF16)
        s[...] = (weights * mm(low[d_aug(h, t, 0, LANES)], v_n[h, k], 0, 1)).astype(BF16)

    def gather_grads(buffers, t, h, k):
        p, s = buffers
        dv[rows_of(h, k)] += mm(low[d_aug(h, t, 0, HDIM)], p[...], 1, 0)
        dk[rows_of(h, k)] += mm(q_t[h, t, 0:HDIM], s[...], 1, 0)
        dq[rows_of(h, t)] += mm(k_t[h, k], s[...], 1, 1)

    def turned(t, kind, h):
        return pl.ds(pl.multiple_of((t * 3 + kind) * group + h * HDIM, HDIM), HDIM)

    def fill(t, h):
        for kind, (ref, scale) in enumerate(((dq, HDIM**-0.5), (dk, 1.0 / LOG2E), (dv, 1.0))):
            d_t[turned(t, kind, h)] = (ref[rows_of(h, t)] * scale).astype(BF16)

    def whole(t, kind):
        return pl.ds(pl.multiple_of((t * 3 + kind) * group, HDIM), group)

    def states_part(t):
        out = mm(w_group[0], d_t[whole(t, 0)], 1, 0)
        out += mm(w_group[1], d_t[whole(t, 1)], 1, 0)
        out += mm(w_group[2], d_t[whole(t, 2)], 1, 0)
        dx_s[at(t, group)] = out.astype(BF16)

    if split:
        qkv_s, qkv_r, qkv_out = r.qkv_s, r.qkv_r, r.qkv_out
        owner = my_dp // per_group == me

        def qkv_copy(h, t):
            return remote(
                qkv_s.at[h, t],
                qkv_r.at[h, my_dp],
                r.q1_send.at[h, t],
                r.q1_recv.at[h, my_dp],
                dp=me * per_group + t,
            )

        def qkv_share(h, d):
            return remote(
                qkv_out.at[h], qkv_out.at[h], r.q2_send.at[h, d], r.q2_recv.at[h], seq=me ^ d
            )

    def emit(h):
        for d in range(2):
            fill(me ^ d, h)
        totals = []
        for kind in range(3):
            value = mm(x_group[0], d_t[turned(0, kind, h)], 1, 1)
            for t in range(1, seq):
                value += mm(x_group[t], d_t[turned(t, kind, h)], 1, 1)
            totals.append(value)
        if split:
            bias_rows = jnp.zeros((shard, HDIM), F32)
            bias_id = iota((shard, HDIM), 0)
            for kind in range(3):
                bias_rows = jnp.where(bias_id == kind, totals[kind][group : group + 1], bias_rows)
            for t in range(per_group):
                qkv_s[h, t] = jnp.concatenate(
                    [value[t * shard : (t + 1) * shard] for value in totals] + [bias_rows], axis=1
                ).astype(BF16)
                when(me * per_group + t != my_dp, lambda: qkv_copy(h, t).start())
        else:
            for kind in range(3):
                r.qkv_raw[h, kind] = totals[kind]

    def place_backward(i):
        part, j = i // per_part, lax.rem(i, per_part)
        is_far, tail = lax.rem((part + 1) // 2, 2), part // 3
        near = 1 - is_far
        d_q = is_far * (4 - part) + near * (
            (1 - tail) * (j // (2 * heads)) + tail * (lax.rem(j, 4) // 2)
        )
        h = is_far * (j // seq) + near * (
            (1 - tail) * (lax.rem(j, 2 * heads) // 2) + tail * (j // 4)
        )
        d_k = is_far * lax.rem(j, seq) + near * (lax.rem(j, 2) + 2 * (1 - tail))
        return me ^ d_q, h, me ^ d_k

    def receive(d):
        g_copy(d).wait_recv()
        prepare(me ^ d)

    def far_states_grads():
        for d in range(1, seq):
            g_copy(d).wait_send()
        for d in far:
            for h in range(heads):
                fill(me ^ d, h)
            states_part(me ^ d)
            dx_copy(d).start()

    hooks = [
        (heads - 1, lambda: receive(1)),
        (per_part // 2 - 1, lambda: receive(far[0])),
        (per_part - 1, lambda: receive(far[1])),
        (per_part * 3 // 2, far_states_grads),
        (per_part * 3 // 2 + 2, lambda: emit(0)),
        (per_part * 3 // 2 + 4, lambda: emit(1)),
    ]
    if split:
        hooks += [
            (1, reduce_side),
            (4, lambda: reduce_cross(0)),
            (7, lambda: reduce_cross(1)),
            (8, reduce_vec),
            (10, lambda: reduce_cross(2)),
            (13, lambda: reduce_cross(3)),
            (19, reduce_z),
        ]
    d_in[me] = c_grad[at(me, group)]
    prepare(me)
    run(4 * per_part, place_backward, weigh, gather_grads, (p0, s0), (p1, s1), hooks)
    emit(2)
    states_part(me ^ 1)
    dx_copy(1).start()
    states_part(me)
    dx_r[at(me, group)] = dx_s[at(me, group)]
    if split:
        reduce_x()

        @pl.when(owner)
        def _():
            for h in range(heads):
                value = qkv_s[h, my_slot].astype(F32)
                for e in range(1, n_dp):
                    src = lax.rem(my_dp + e, n_dp)
                    remote(
                        qkv_s.at[h, 0],
                        qkv_r.at[h, src],
                        r.q1_send.at[h, 0],
                        r.q1_recv.at[h, src],
                        dp=src,
                    ).wait_recv()
                    value += qkv_r[h, src].astype(F32)
                qkv_out[h] = value.astype(BF16)
                for d in range(1, seq):
                    qkv_share(h, d).start()

    for d in range(1, seq):
        dx_copy(d).wait_recv()
    for c in range(width // LANES):
        span = slice(c * LANES, (c + 1) * LANES)
        r.states_grad[:, span] = (dx_r[span].astype(F32) + grad_mid[span]).astype(BF16).T


    for d in range(1, seq):
        x_copy(d).wait_send()
        c_copy(d).wait_send()
        dx_copy(d).wait_send()
    if split:
        last_copy().wait()
        for h in range(heads):
            for t in range(per_group):
                when(me * per_group + t != my_dp, lambda: qkv_copy(h, t).wait_send())

        @pl.when(owner)
        def _():
            for h in range(heads):
                for d in range(1, seq):
                    qkv_share(h, d).wait_send()

        @pl.when(jnp.logical_not(owner))
        def _():
            for h in range(heads):
                qkv_share(h, 1).wait_recv()

        for e in range(1, n_dp):
            s_copy(e).wait_send()

        w_each(lambda copy: copy.wait_send())
        for copy in side_copies() + x_copies():
            copy.wait_send()
        vec_cross().wait_send()
        for j in range(n_z):
            cross_copy(j).wait_send()
        for j in range(n_z - 1):
            z_copy(j).wait_send()
            vz_copy(j).wait_send()


def layer(cfg, row, collective_id, inputs):
    c = cfg
    g, l, h, s, w, f = c.group, c.piece, c.heads, c.seq, c.width, c.hidden
    n_z = c.dp // 2
    sds = jax.ShapeDtypeStruct
    dma = pltpu.SemaphoreType.DMA
    vm = pltpu.VMEM
    outputs = dict(layer_out=sds((l, w), BF16), states_grad=sds((l, w), BF16))
    if c.split:
        outputs |= dict(
            od_out=sds((2, 3, c.half, w), F32),
            qkv_out=sds((h, c.shard, 4 * HDIM), BF16),
            vec_out=sds((16, w), F32),
        )
    else:
        outputs |= dict(
            g_all=sds((3, w, w), BF16),
            qkv_raw=sds((h, 3, g + AUG, HDIM), F32),
            vecs=sds((16, w), F32),
        )
    scratch = dict(
        x_own=vm((w, l), BF16),
        x_group=vm((s, g + AUG, l), BF16),
        w_group=vm((3, g, g), BF16),
        w_pad=vm((3, g + AUG, h * LANES), BF16),
        q_t=vm((h, s, LANES, l), BF16),
        k_n=vm((h, s, l, LANES), BF16),
        k_t=vm((h, s, HDIM, l), BF16),
        v_n=vm((h, s, l, LANES), BF16),
        context_s=vm((s, g, l), BF16),
        context_r=vm((w, l), BF16),
        tops=vm((h * s, 1, l), F32),
        gathered=vm((h * s * (HDIM + AUG), l), F32),
        cols=vm((w, 16), F32),
        vcols=vm((w, LANES), F32),
        wide=vm((4 * w, l), F32),
        slim=vm((2 * f, l), BF16),
        c_grad=vm((w, l), BF16),
        d_in=vm((s, g, l), BF16),
        dx_r=vm((w, l), BF16),
        low=vm((GROUPS * (g + AUG) + w, l), BF16),
        late_sem=dma((2,)),
        x_send=dma((s,)),
        x_recv=dma((s,)),
        c_send=dma((s,)),
        c_recv=dma((s,)),
        g_send=dma((s,)),
        g_recv=dma((s,)),
        dx_send=dma((s,)),
        dx_recv=dma((s,)),
    )
    if c.split:
        unit = (3, c.half, w)
        vec = (16, w)
        scratch |= dict(
            wo=vm((w, w), BF16),
            w_up=vm((w, w), BF16),
            wd=vm((w, f // GROUPS), BF16),
            smalls=vm((c.dp, 16, LANES), F32),
            pack=vm((c.dp, 2) + unit, BF16),
            w_in=vm((c.per_group, c.shard, 3 * g), BF16),
            vecs=vm(vec, F32),
            side=vm((c.dp,) + unit, BF16),
            cross=vm((n_z,) + unit, BF16),
            spread_z=vm((n_z,) + unit, BF16),
            spread_v=vm((n_z,) + vec, F32),
            x_mine=vm(unit, BF16),
            x_theirs=vm(unit, BF16),
            vec_side=vm(vec, F32),
            vec_mine=vm(vec, F32),
            vec_cross=vm(vec, F32),
            vec_sum=vm(vec, F32),
            vec_z=vm(vec, F32),
            vec_x=vm(vec, F32),
            qkv_s=vm((h, c.per_group, c.shard, 4 * HDIM), BF16),
            qkv_r=vm((h, c.dp, c.shard, 4 * HDIM), BF16),
            s_send=dma((c.dp,)),
            s_recv=dma((c.dp,)),
            w_send=dma((3,)),
            w_recv=dma((2,)),
            hop_send=dma((3, c.dp)),
            hop_recv=dma((c.dp,)),
            sib_send=dma((c.dp,)),
            sib_recv=dma((c.dp,)),
            red_send=dma((7,)),
            red_recv=dma((7,)),
            cross_send=dma((n_z,)),
            cross_recv=dma((n_z,)),
            z_send=dma((n_z,)),
            z_recv=dma((n_z,)),
            vz_send=dma((n_z,)),
            vz_recv=dma((n_z,)),
            q1_send=dma((h, c.per_group)),
            q1_recv=dma((h, c.dp)),
            q2_send=dma((h, s)),
            q2_recv=dma((h,)),
        )
    names = tuple(inputs) + tuple(outputs) + tuple(scratch)
    vmem = pl.BlockSpec(memory_space=pltpu.VMEM)
    results = pl.pallas_call(
        functools.partial(layer_kernel, cfg, row, names),
        out_shape=list(outputs.values()),
        in_specs=[
            pl.BlockSpec(memory_space=pl.ANY) if v is inputs["teacher"] or v is inputs["out_grad"] else vmem
            for v in inputs.values()
        ],
        out_specs=[vmem] * len(outputs),
        scratch_shapes=list(scratch.values()),
        compiler_params=pltpu.CompilerParams(
            collective_id=collective_id, has_side_effects=True, vmem_limit_bytes=VMEM_LIMIT
        ),
        name="layer",
    )(*inputs.values())
    return dict(zip(outputs, results, strict=True))


def deliver_kernel(cfg, layer_in, states_in, qkv, od, vec, *outs):
    my_dp = lax.axis_index("dp")
    shard, width, group, half = cfg.shard, cfg.width, cfg.group, cfg.half
    layer_out, states_grad, qw, kw, vw, ow, uw, dw = outs[:8]
    layer_out[...] = layer_in[...]
    states_grad[...] = states_in[...]
    parts = [
        jnp.concatenate(
            [qkv[h, :, k * HDIM : (k + 1) * HDIM].astype(F32) for h in range(cfg.heads)], axis=1
        )
        for k in range(4)
    ]
    for ref, part in zip((qw, kw, vw), parts[:3], strict=True):
        ref[...] = part
    for c in range(2):
        rows = slice(c * half, (c + 1) * half)
        ow[rows] = od[c, 0]
        uw[rows] = od[c, 1]
        for k in range(2):
            dw[(2 * c + k) * half : (2 * c + k + 1) * half] = od[
                c, 2, :, k * 4 * shard : (k + 1) * 4 * shard
            ]
    slot = lax.rem(my_dp, cfg.per_group)
    mine = parts[3][0:8, 0:shard]
    for t in range(1, cfg.per_group):
        mine = jnp.where(slot == t, parts[3][0:8, t * shard : (t + 1) * shard], mine)
    outs[8][...] = mine[0:1]
    outs[9][...] = mine[2:3]
    turned = pltpu.roll(vec[0:8], lax.rem(width - my_dp * shard, width), 1)
    for n in range(6):
        outs[10 + n][...] = turned[n : n + 1, 0:shard]
    outs[16][...] = vec[
        pl.ds(8 + my_dp // cfg.per_group, 1),
        pl.ds(pl.multiple_of(slot * 4 * shard, LANES), 4 * shard),
    ]
    outs[17][...] = vec[12:13, 0:1]


def deliver(cfg, *args):
    sds = jax.ShapeDtypeStruct
    shard, width, group = cfg.shard, cfg.width, cfg.group
    out_shape = [sds(a.shape, a.dtype) for a in args[:2]]
    out_shape += [sds((shard, group), F32)] * 3 + [sds((shard, width), F32)] * 2
    out_shape += [sds((group, 4 * shard), F32)] + [sds((1, shard), F32)] * 8
    out_shape += [sds((1, 4 * shard), F32), sds((1, 1), F32)]
    vmem = pl.BlockSpec(memory_space=pltpu.VMEM)
    return pl.pallas_call(
        functools.partial(deliver_kernel, cfg),
        out_shape=out_shape,
        in_specs=[vmem] * len(args),
        out_specs=[vmem] * len(out_shape),
        name="deliver",
    )(*args)


def local(
    states,
    lengths,
    teacher,
    out_grad,
    q_weight,
    k_weight,
    v_weight,
    q_bias,
    v_bias,
    o_weight,
    o_bias,
    attn_gain,
    attn_bias,
    up_weight,
    up_bias,
    down_weight,
    down_bias,
    ffn_gain,
    ffn_bias,
):
    row_count, piece, width = states.shape
    n_dp, n_seq = lax.axis_size("dp"), lax.axis_size("seq")
    me, my_dp = lax.axis_index("seq"), lax.axis_index("dp")
    shard = q_bias.shape[0]
    hidden = up_bias.shape[0] * n_dp
    cfg = Config(n_dp, n_seq, piece, width, hidden, shard)
    cfg.rows = row_count
    group = cfg.group

    if not cfg.split:

        def pad(v):
            return jnp.pad(v.astype(F32), ((0, 0), (0, LANES - v.shape[1])))

        vectors = (q_bias, v_bias, o_bias, attn_gain, attn_bias, down_bias, ffn_gain, ffn_bias)
        small = jnp.concatenate(
            [
                pad(jnp.stack(vectors)),
                pad(up_bias.reshape(4, shard)),
                jnp.broadcast_to(lengths.astype(F32)[:, None], (row_count, LANES)),
                jnp.zeros((4 - row_count, LANES), F32),
            ]
        )
        smalls = lax.all_gather(small, "dp", axis=0)
        qkv = jnp.stack((q_weight, k_weight, v_weight))
        qkv = lax.all_gather(qkv, "dp", axis=1, tiled=True)
        w_group_in = lax.dynamic_slice(qkv, (0, me * group, 0), (3, group, group))
        wo = lax.all_gather(o_weight, "dp", axis=0, tiled=True)
        wu = lax.all_gather(up_weight, "dp", axis=0, tiled=True)
        wd = lax.all_gather(down_weight, "dp", axis=0, tiled=True)
        wd = wd.reshape(GROUPS, -1, group).transpose(0, 2, 1).reshape(width, -1)

    results = []
    for n in range(row_count):
        inputs = dict(states=states[n], teacher=teacher[n], out_grad=out_grad[n])
        if cfg.split:
            inputs |= dict(
                wq=q_weight,
                wk=k_weight,
                wv=v_weight,
                ow=o_weight,
                uw=up_weight,
                dw=down_weight.T,
                qb=q_bias[None],
                vb=v_bias[None],
                ob=o_bias[None],
                ag=attn_gain[None],
                ab=attn_bias[None],
                db=down_bias[None],
                fg=ffn_gain[None],
                fb=ffn_bias[None],
                ub=up_bias[None],
                lengths=lengths[:, None],
            )
        else:
            inputs |= dict(smalls=smalls, w_all=w_group_in, wo=wo, w_up=wu, wd=wd)
        results.append(layer(cfg, n, n, inputs))

    def summed(name):
        first = results[0][name]
        if row_count == 1:
            return first
        return sum((item[name].astype(F32) for item in results[1:]), first.astype(F32))

    if cfg.split:
        heavy = [jnp.stack([item[n] for item in results]) for n in ("layer_out", "states_grad")]
        out = deliver(cfg, *heavy, summed("qkv_out"), summed("od_out"), summed("vec_out"))
        grad_qw, grad_kw, grad_vw, grad_ow, grad_uw, grad_dw = out[2:8]
        vectors = [v[0] for v in out[8:17]]
        return (
            (out[0], out[17][0, 0], out[1], grad_qw, grad_kw, grad_vw)
            + (vectors[0], vectors[1], grad_ow, *vectors[2:5], grad_uw, vectors[8])
            + (grad_dw.T, *vectors[5:8])
        )

    layer_out = jnp.stack([item["layer_out"] for item in results])
    states_grad = jnp.stack([item["states_grad"] for item in results])
    qkv_g, g_all, vecs = (summed(n).astype(F32) for n in ("qkv_raw", "g_all", "vecs"))
    qkv_g = qkv_g.transpose(1, 2, 0, 3).reshape(3, group + AUG, group)
    whole = jnp.zeros((3, width + GROUPS * AUG, group), F32)
    whole = lax.dynamic_update_slice(whole, qkv_g[:, :group], (0, me * group, 0))
    whole = lax.dynamic_update_slice(whole, qkv_g[:, group:], (0, width + me * AUG, 0))
    whole, g_all, vec = lax.psum((whole, g_all, vecs), ("dp", "seq"))
    qkv = lax.dynamic_slice(whole, (0, my_dp * shard, 0), (3, shard, group))
    biases = whole[:, width::AUG].reshape(3, width)
    grad_qb = lax.dynamic_slice(biases[0], (my_dp * shard,), (shard,))
    grad_vb = lax.dynamic_slice(biases[2], (my_dp * shard,), (shard,))
    g_ou = lax.dynamic_slice(g_all[:2], (0, my_dp * shard, 0), (2, shard, width))
    g_d = g_all[2].reshape(GROUPS, group, -1).transpose(0, 2, 1).reshape(-1, group)
    grad_dw = lax.dynamic_slice(g_d, (my_dp * 4 * shard, 0), (4 * shard, group))
    mine = lax.dynamic_slice(vec[:6], (0, my_dp * shard), (6, shard))
    grad_ub = lax.dynamic_slice(vec[8:12].reshape(-1), (my_dp * 4 * shard,), (4 * shard,))
    return (
        (layer_out, vec[12, 0], states_grad, qkv[0], qkv[1], qkv[2], grad_qb, grad_vb, g_ou[0])
        + (mine[0], mine[1], mine[2], g_ou[1], grad_ub, grad_dw, mine[3], mine[4], mine[5])
    )


def solution(mesh):
    rows3 = P("dp", "seq", None)
    matrix = P("dp", None)
    vector = P("dp")
    return jax.shard_map(
        local,
        mesh=mesh,
        in_specs=(rows3, vector, rows3, rows3)
        + (matrix,) * 3
        + (vector,) * 2
        + (matrix,)
        + (vector,) * 3
        + (matrix, vector, matrix)
        + (vector,) * 3,
        out_specs=(rows3, P(), rows3)
        + (matrix,) * 3
        + (vector,) * 2
        + (matrix,)
        + (vector,) * 3
        + (matrix, vector, matrix)
        + (vector,) * 3,
        check_vma=False,
    )
```

```python
import functools
import math
import types

import jax
import jax.numpy as jnp
from jax import lax
from jax.experimental import pallas as pl
from jax.experimental.pallas import tpu as pltpu
from jax.sharding import PartitionSpec as P

HDIM = 64
GROUPS = 4
EPSILON = 1e-12
NEG_FILL = -1e30
LANES = 128
AUG = 16
LOG2E = 1.4426950408889634
MESH = pl.DeviceIdType.MESH
F32 = jnp.float32
BF16 = jnp.bfloat16
VMEM_LIMIT = 60 * 1024 * 1024


def mm(left, right, left_dim, right_dim):
    return lax.dot_general(
        left, right, (((left_dim,), (right_dim,)), ((), ())), preferred_element_type=F32
    )


def iota(shape, dim):
    return lax.broadcasted_iota(jnp.int32, shape, dim)


def remote(src, dst, send_sem, recv_sem, **where):
    return pltpu.make_async_remote_copy(
        src_ref=src,
        dst_ref=dst,
        send_sem=send_sem,
        recv_sem=recv_sem,
        device_id=where,
        device_id_type=MESH,
    )


def three_parts(row):
    high = row.astype(BF16)
    rest = row - high.astype(F32)
    middle = rest.astype(BF16)
    low = (rest - middle.astype(F32)).astype(BF16)
    return high, middle, low


class Config:
    def __init__(self, dp, seq, piece, width, hidden, shard):
        self.dp, self.seq, self.piece, self.width, self.hidden, self.shard = (
            dp,
            seq,
            piece,
            width,
            hidden,
            shard,
        )
        self.slots = piece * seq
        self.group = width // GROUPS
        self.heads = self.group // HDIM
        self.per_group = dp // GROUPS
        self.split = shard % 32 == 0 and seq == 4 and dp == 8
        self.half = shard // 2
        self.quarter = hidden // dp // 4


def greet(cfg, me, my_dp):
    barrier = pltpu.get_barrier_semaphore()
    count = cfg.seq - 1
    for d in range(1, cfg.seq):
        pl.semaphore_signal(barrier, inc=1, device_id={"seq": me ^ d}, device_id_type=MESH)
    if cfg.split:
        count += cfg.dp - 1
        for e in range(1, cfg.dp):
            pl.semaphore_signal(
                barrier, inc=1, device_id={"dp": lax.rem(my_dp + e, cfg.dp)}, device_id_type=MESH
            )
    return lambda: pl.semaphore_wait(barrier, count)


def layer_kernel(cfg, row, names, *refs):
    r = types.SimpleNamespace(**dict(zip(names, refs, strict=True)))
    split = cfg.split
    me = lax.axis_index("seq")
    my_dp = lax.axis_index("dp")
    piece, width, group, heads, seq = cfg.piece, cfg.width, cfg.group, cfg.heads, cfg.seq
    shard, half, n_dp, per_group = cfg.shard, cfg.half, cfg.dp, cfg.per_group
    hid = cfg.hidden // GROUPS
    n_z = n_dp // 2
    core = lax.rem(me, 2)
    my_z, my_y = my_dp // 2, lax.rem(my_dp, 2)
    far = [d for d in range(seq - 1, 1, -1)]

    states = r.states
    teacher, out_grad = r.states_grad, r.layer_out
    late = [
        pltpu.make_async_copy(r.teacher, teacher, r.late_sem.at[0]),
        pltpu.make_async_copy(r.out_grad, out_grad, r.late_sem.at[1]),
    ]
    x_own, x_group, w_group, w_pad, smalls = (
        r.x_own,
        r.x_group,
        r.w_group,
        r.w_pad,
        r.smalls,
    )
    q_t, k_n, k_t, v_n = r.q_t, r.k_n, r.k_t, r.v_n
    context_s, context_r = r.context_s, r.context_r
    cols, vcols = r.cols, r.vcols
    wide, slim = r.wide, r.slim
    wo, w_up, wd = r.wo, r.w_up, r.wd
    c_grad, d_in, dx_r = r.c_grad, r.d_in, r.dx_r
    dx_s = c_grad
    tall1 = group + AUG
    low = r.low
    low2 = low.at[GROUPS * tall1 :]

    def low1(g, start, size):
        return pl.ds(pl.multiple_of(g * tall1 + start, AUG), size)

    def d_aug(h, t, start, size):
        return pl.ds(pl.multiple_of((h * seq + t) * LANES + start, HDIM), size)

    score0, score1 = wide.at[0:piece], wide.at[piece : 2 * piece]
    gathered = r.gathered
    v1, first, v2, seed = (wide.at[i * width : (i + 1) * width] for i in range(4))
    dq, dk, dv = (wide.at[i * width : (i + 1) * width] for i in range(3))
    act, slope = slim.at[0 : cfg.hidden], slim.at[cfg.hidden : 2 * cfg.hidden]
    p0, p1, s0, s1 = (slim.at[i * piece : (i + 1) * piece] for i in range(4))
    d_t = slope

    def at(i, n):
        return pl.ds(pl.multiple_of(i * n, n), n)

    def loop(count, body, *init):
        return lax.fori_loop(0, count, lambda i, c: body(i, *c), tuple(init))

    def sub(v):
        return jnp.sum(v, axis=0, keepdims=True)


    def to_seq(sems, src, dst, d):
        return remote(src, dst, sems[0].at[d], sems[1].at[d], seq=me ^ d)

    def x_copy(d):
        return to_seq((r.x_send, r.x_recv), x_own.at[at(me ^ d, group)], x_group.at[me, pl.ds(0, group)], d)

    def c_copy(d):
        return to_seq((r.c_send, r.c_recv), context_s.at[me ^ d], context_r.at[at(me, group)], d)

    def g_copy(d):
        return to_seq((r.g_send, r.g_recv), c_grad.at[at(me ^ d, group)], d_in.at[me], d)

    def dx_copy(d):
        return to_seq((r.dx_send, r.dx_recv), dx_s.at[at(me ^ d, group)], dx_r.at[at(me, group)], d)

    if split:
        pack = r.pack
        w_in = r.w_in
        my_slot = lax.rem(my_dp, per_group)

        def s_copy(e):
            return remote(
                smalls.at[my_dp],
                smalls.at[my_dp],
                r.s_send.at[e],
                r.s_recv.at[e],
                dp=lax.rem(my_dp + e, n_dp),
            )

        first_group = me - core

        def w_ref(g):
            return w_in.at[g, my_y, core]

        def w_along(g, j):
            z = lax.rem(my_z + n_z - 1 - j, n_z)
            return remote(
                w_ref(g), w_ref(g), r.w_send.at[g, j], r.w_recv.at[g, 0], dp=2 * z + my_y
            )

        def w_across(g):
            return remote(
                w_ref(g), w_ref(g), r.w_send.at[g, n_z], r.w_recv.at[g, 1], dp=my_dp + 1 - 2 * my_y
            )

        def w_over(g):
            ref = w_in.at[g, 1 - my_y, core]
            return remote(ref, ref, r.w_send.at[g, n_z], r.w_recv.at[g, 1], dp=my_dp)

        def w_beside(g, part, half_of):
            ref = w_in.at[g, my_y if part == 0 else 1 - my_y, half_of]
            return remote(ref, ref, r.wb_send.at[part], r.wb_recv.at[part], seq=me ^ 1)

        def holds(g):
            return my_z == first_group + g

        def hop(kind, i, **where):
            ref = pack.at[i, core]
            return remote(ref, ref, r.hop_send.at[kind, i], r.hop_recv.at[i], **where)

        def up(i):
            return hop(0, i, dp=my_dp + 2)

        def down(i):
            return hop(1, i, dp=my_dp - 2)

        def across(i):
            return hop(2, i, dp=my_dp + 1 - 2 * my_y)

        def beside(i):
            ref = pack.at[i, core]
            return remote(ref, ref, r.sib_send.at[i], r.sib_recv.at[i], seq=me ^ 1)

        def when(condition, fn):
            pl.when(condition)(fn)

        def gather_start():
            when(my_z < n_z - 1, lambda: up(my_dp).start())
            when(my_z > 0, lambda: down(my_dp).start())
            across(my_dp).start()

        def gather_z(k):
            below, above = my_dp - 2 * k, my_dp + 2 * k

            @pl.when(my_z >= k)
            def _():
                hop(0, below, dp=my_dp).wait_recv()
                when(my_z < n_z - 1, lambda: up(below).start())
                across(below).start()
                beside(below).start()

            @pl.when(my_z + k < n_z)
            def _():
                hop(0, above, dp=my_dp).wait_recv()
                when(my_z > 0, lambda: down(above).start())
                across(above).start()
                beside(above).start()

        def gather_y(k):
            other = my_dp + 1 - 2 * my_y

            def take(i):
                hop(2, i, dp=my_dp).wait_recv()
                beside(i).start()

            if k == 0:
                take(other)
            else:
                when(my_z >= k, lambda: take(other - 2 * k))
                when(my_z + k < n_z, lambda: take(other + 2 * k))

        def gather_end():
            for e in range(1, n_dp):
                copy = beside(lax.rem(my_dp + e, n_dp))
                copy.wait()

            when(my_z < n_z - 1, lambda: up(my_dp).wait_send())
            when(my_z > 0, lambda: down(my_dp).wait_send())
            across(my_dp).wait_send()
            for k in range(1, n_z):
                below, above = my_dp - 2 * k, my_dp + 2 * k

                @pl.when(my_z >= k)
                def _():
                    when(my_z < n_z - 1, lambda: up(below).wait_send())
                    across(below).wait_send()

                @pl.when(my_z + k < n_z)
                def _():
                    when(my_z > 0, lambda: down(above).wait_send())
                    across(above).wait_send()


    wait_entry = greet(cfg, me, my_dp)
    for c in range(0, width, LANES):
        x_own[c : c + LANES] = states[:, c : c + LANES].T
    if split:
        for c in range(2):
            pack[my_dp, c, 0] = r.ow[c * half : (c + 1) * half]
            pack[my_dp, c, 1] = r.uw[c * half : (c + 1) * half]
            for k in range(2):
                pack[my_dp, c, 2, :, k * 4 * shard : (k + 1) * 4 * shard] = r.dw[
                    (2 * c + k) * half : (2 * c + k + 1) * half
                ]
        smalls[my_dp] = jnp.zeros((16, LANES), F32)
        for n, ref in enumerate((r.qb, r.vb, r.ob, r.ag, r.ab, r.db, r.fg, r.fb)):
            smalls[my_dp, n : n + 1, 0:shard] = ref[...].reshape(1, shard).astype(F32)
        up_bias = r.ub[...].reshape(1, 4 * shard).astype(F32)
        for n in range(4):
            smalls[my_dp, 8 + n : 9 + n, 0:shard] = up_bias[:, n * shard : (n + 1) * shard]
        for n in range(cfg.rows):
            smalls[my_dp, 12 + n : 13 + n] = jnp.full((1, LANES), r.lengths[n].astype(F32))

        for g in range(2):

            @pl.when(holds(g))
            def _():
                for c in range(2):
                    rows = slice(c * half, (c + 1) * half)
                    w_in[g, my_y, c] = jnp.concatenate(
                        [ref[rows].astype(F32) for ref in (r.wq, r.wk, r.wv)], axis=1
                    ).astype(BF16)

    wait_entry()
    if split:
        for e in range(1, n_dp):
            s_copy(e).start()

        for g in range(2):

            @pl.when(holds(g))
            def _():
                for j in range(n_z - 1):
                    w_along(g, j).start()
                w_across(g).start()

    for d in range(1, seq):
        x_copy(d).start()
    if split:
        gather_start()
    for copy in late:
        copy.start()
    x_group[me, 0:group] = x_own[at(me, group)]


    n_cols = heads * LANES
    lane = iota((group, n_cols), 1)
    spread = jnp.where(
        (((lane >> 7) * HDIM + (lane & 127)) == iota((group, n_cols), 0)) & ((lane & 127) < HDIM),
        1.0,
        0.0,
    ).astype(BF16)
    if split:
        for n, g in enumerate((1 - core, core)):

            @pl.when(jnp.logical_not(holds(g)))
            def _():
                w_along(g, 0).wait_recv()
                w_across(g).start()
                if n == 0:
                    w_beside(g, 0, core).start()

        for n, g in enumerate((1 - core, core)):
            w_over(g).wait_recv()
            if n == 0:
                w_beside(g, 1, core).start()
        for e in range(1, n_dp):
            s_copy(e).wait_recv()
        when(my_z != me, lambda: w_beside(core, 0, 1 - core).wait_recv())
        w_beside(core, 1, 1 - core).wait_recv()
        for t in range(per_group):
            for c in range(2):
                for kind in range(3):
                    w_group[kind, t * shard + c * half : t * shard + (c + 1) * half] = w_in[
                        core, t, c, :, kind * group : (kind + 1) * group
                    ]
    else:
        for kind in range(3):
            w_group[kind] = r.w_all[kind]
    for kind in range(3):
        w_pad[kind, 0:group] = mm(w_group[kind], spread, 1, 0).astype(BF16)
    vec_rows = jnp.zeros((AUG, n_cols), F32)
    lane = iota((LANES, n_cols), 1)
    source = iota((LANES, n_cols), 0)
    for t in range(per_group):
        spread = jnp.where(
            (((lane >> 7) * HDIM + (lane & 127)) == source + t * shard)
            & ((lane & 127) < HDIM)
            & (source < shard),
            1.0,
            0.0,
        ).astype(BF16)
        vec_rows += mm(smalls[me * per_group + t].astype(BF16), spread, 1, 0)
    row_id = iota((AUG, n_cols), 0)
    lane = iota((AUG, n_cols), 1) & 127
    zero = jnp.zeros((AUG, n_cols), F32)
    top_row = row_id == 0
    w_pad[0, group:] = jnp.where(top_row, vec_rows[0:1], zero).astype(BF16)
    ones_k = (top_row & (lane > HDIM) & (lane <= HDIM + 3)) | ((row_id == 1) & (lane == HDIM))
    w_pad[1, group:] = jnp.where(ones_k, 1.0, zero).astype(BF16)
    ones_v = (lane >= HDIM) & (lane < HDIM + 3)
    w_pad[2, group:] = jnp.where(top_row, jnp.where(ones_v, 1.0, vec_rows[1:2]), zero).astype(BF16)

    length = smalls[my_dp, 12 + row : 13 + row, 0:1]
    aug_row = iota((AUG, piece), 0)
    factor = LOG2E * HDIM**-0.5
    deep = HDIM + AUG

    def v_t(h, t):
        return pl.ds(pl.multiple_of((h * seq + t) * deep, AUG), deep)

    def project(t):
        slot = (iota((AUG, piece), 1) + t * piece).astype(F32)
        mask = jnp.where(slot < length, 0.0, NEG_FILL)
        x_group[t, group:] = jnp.where(
            aug_row == 0, 1.0, jnp.where(aug_row == 1, mask, 0.0)
        ).astype(BF16)
        x = x_group[t]
        queries = mm(w_pad[0], x, 0, 0) * factor
        keys_t = mm(w_pad[1], x, 0, 0)
        values_t = mm(w_pad[2], x, 0, 0)
        keys_n = mm(x, w_pad[1], 0, 0)
        values_n = mm(x, w_pad[2], 0, 0)
        rest = jnp.where(iota((HDIM, piece), 0) == 0, 1.0, 0.0).astype(BF16)
        for h in range(heads):
            span = slice(h * LANES, h * LANES + HDIM)
            q_t[h, t, 0:HDIM] = queries[span].astype(BF16)
            q_t[h, t, HDIM:] = rest
            k_t[h, t] = keys_t[span].astype(BF16)
            slim[v_t(h, t)] = values_t[h * LANES : h * LANES + deep].astype(BF16)
            k_n[h, t] = keys_n[:, h * LANES : (h + 1) * LANES].astype(BF16)
            v_n[h, t] = values_n[:, h * LANES : (h + 1) * LANES].astype(BF16)


    tops = r.tops

    def sums(h, t):
        return pl.ds(pl.multiple_of((h * seq + t) * deep, AUG), deep)

    def clear_sums(i, unused):
        gathered[pl.ds(pl.multiple_of(i * deep, AUG), deep)] = jnp.zeros((deep, piece), F32)
        tops[i] = jnp.full((1, piece), NEG_FILL, F32)
        return (unused,)

    loop(heads * seq, clear_sums, 0)

    per_part = seq * heads

    def run(count, place, first_part, last_part, a, b, hooks=()):
        first_part(a, *place(0))

        def two(u, unused):
            if hooks:
                due = u == hooks[0][0]
                for when_u, fn in hooks[1:]:
                    due = due | (u == when_u)

                @pl.when(due)
                def _():
                    for when_u, fn in hooks:
                        pl.when(u == when_u)(fn)

            first_part(b, *place(2 * u + 1))
            last_part(a, *place(2 * u))
            first_part(a, *place(2 * u + 2))
            last_part(b, *place(2 * u + 1))
            return (unused,)

        loop(count // 2 - 1, two, 0)
        first_part(b, *place(count - 1))
        last_part(a, *place(count - 2))
        last_part(b, *place(count - 1))

    def score(buffer, t, h, k):
        buffer[...] = mm(k_n[h, k], q_t[h, t], 1, 0)

    def absorb(buffer, t, h, k):
        i = h * seq + t
        old = tops[i]
        top = jnp.maximum(old, jnp.max(buffer[...], axis=0, keepdims=True))
        weights = jnp.exp2(buffer[...] - top).astype(BF16)
        tops[i] = top
        place = sums(h, t)
        gathered[place] = gathered[place] * jnp.exp2(old - top) + mm(slim[v_t(h, k)], weights, 1, 0)

    def settle(t):
        for h in range(heads):
            total = gathered[sums(h, t)]
            mass = total[HDIM : HDIM + 1]
            context_s[t, h * HDIM : (h + 1) * HDIM] = (total[0:HDIM] / mass).astype(BF16)
            parts = three_parts(-(tops[h * seq + t] + jnp.log2(mass)))
            value = jnp.where(aug_row == 0, 1.0, 0.0)
            for n, part in enumerate(parts):
                value = jnp.where(aug_row == n + 1, part.astype(F32), value)
            q_t[h, t, HDIM:deep] = value.astype(BF16)

    def place_forward(i):
        part, j = i // per_part, lax.rem(i, per_part)
        is_far, tail = lax.rem((part + 1) // 2, 2), part // 3
        d_q = is_far * (4 - part) + (1 - is_far) * (j // (2 * heads))
        h = is_far * (j // seq) + (1 - is_far) * (lax.rem(j, 2 * heads) // 2)
        d_k = is_far * lax.rem(j, seq) + (1 - is_far) * (lax.rem(j, 2) + 2 * tail)
        return me ^ d_q, h, me ^ d_k

    def far_states():
        for d in far:
            x_copy(d).wait_recv()
        loop(2, lambda i, unused: (project(me ^ (2 + i)), unused)[1:], 0)

    def far_context(d):
        settle(me ^ d)
        c_copy(d).start()

    hooks = [
        (per_part // 2 - 1, far_states),
        (per_part, lambda: far_context(far[0])),
        (per_part * 3 // 2, lambda: far_context(far[1])),
    ]
    if split:
        hooks += [
            (2, lambda: gather_z(1)),
            (6, lambda: gather_y(0)),
            (8, lambda: gather_z(2)),
            (11, lambda: gather_y(1)),
            (13, lambda: gather_z(3)),
            (16, lambda: gather_y(2)),
            (20, lambda: gather_y(3)),
        ]
    project(me)
    x_copy(1).wait_recv()
    project(me ^ 1)
    run(4 * per_part, place_forward, score, absorb, score0, score1, hooks)
    settle(me ^ 1)
    c_copy(1).start()
    settle(me)
    context_r[at(me, group)] = context_s[me]
    if split:
        gather_end()

        def unpack(i, unused):
            for c in range(2):
                wo[pl.ds(pl.multiple_of(i * shard + c * half, AUG), half)] = pack[i, c, 0]
                w_up[pl.ds(pl.multiple_of(i * shard + c * half, AUG), half)] = pack[i, c, 1]
                for k in range(2):
                    wd[
                        pl.ds(
                            pl.multiple_of(i // per_group * group + (2 * c + k) * half, AUG), half
                        ),
                        pl.ds(
                            pl.multiple_of(lax.rem(i, per_group) * 4 * shard, LANES), 4 * shard
                        ),
                    ] = pack[i, c, 2, :, k * 4 * shard : (k + 1) * 4 * shard]
            return (unused,)

        loop(n_dp, unpack, 0)


    for i in range(n_dp):
        turned = smalls[i].T
        cols[i * shard : (i + 1) * shard] = turned[0:shard]
    vcols[...] = jnp.zeros_like(vcols)
    inv = 1.0 / width
    total = jnp.sum(smalls[:, 12:13, 0:1], axis=0)
    for n in range(1, cfg.rows):
        total += jnp.sum(smalls[:, 12 + n : 13 + n, 0:1], axis=0)
    slot = (iota((1, piece), 1) + me * piece).astype(F32)
    live = jnp.where(slot < length, 1.0, 0.0)
    coef = 2.0 / (total * width)
    zero_row = jnp.zeros((1, piece), F32)

    def col(i, n, which):
        return cols[at(i, n), which : which + 1]

    for d in range(1, seq):
        c_copy(d).wait_recv()

    step = 256

    def attn_out(i, acc):
        out = mm(wo[:, at(i, step)], context_r[...], 0, 0)
        v = out + x_own[at(i, step)].astype(F32) + col(i, step, 2)
        v1[at(i, step)] = v
        return (acc + sub(v),)

    (acc,) = loop(width // step, attn_out, zero_row)
    mean = acc * inv

    def center(ref):
        def body(g, acc):
            v = ref[at(g, group)] - mean
            ref[at(g, group)] = v
            return (acc + sub(v * v),)

        (acc,) = loop(GROUPS, body, zero_row)
        return lax.rsqrt(acc * inv + EPSILON)

    scale1 = center(v1)

    def norm1(g, unused):
        v = v1[at(g, group)] * scale1
        v1[at(g, group)] = v
        out = v * col(g, group, 3) + col(g, group, 4)
        first[at(g, group)] = out
        low[low1(g, 0, group)] = out.astype(BF16)
        low[low1(g, group, AUG)] = jnp.where(aug_row == 0, 1.0, 0.0).astype(BF16)
        return (unused,)

    loop(GROUPS, norm1, 0)

    def gelu(u):
        d = 1.0 + (0.3275911 * 0.7071067811865476) * jnp.abs(u)
        t = pltpu.reciprocal(d, approx=True)
        bell = jnp.exp2((u * u) * (-0.5 * LOG2E))
        poly = t * (
            0.127414796
            + t * (-0.142248368 + t * (0.7107068705 + t * (-0.7265760135 + t * 0.5307027145)))
        )
        tail = poly * bell
        phi = jnp.where(u >= 0.0, 1.0 - tail, tail)
        return u * phi, phi + u * bell * 0.3989422804014327

    bunch = max(1, LANES // math.gcd(LANES, 4 * shard) if (4 * shard) % LANES else 1)
    span4 = 4 * shard * bunch
    n_steps = n_dp // bunch
    steps_group = n_steps // GROUPS
    tall = span4 // 4

    raw0, raw1 = wide.at[2 * width : 2 * width + span4], wide.at[3 * width : 3 * width + span4]

    def expand(raw, i):
        g, c = i // steps_group, lax.rem(i, steps_group)
        raw[...] = mm(w_up[at(g, group), at(c, span4)], low[low1(g, 0, group)], 0, 0)

    def activate(raw, i):
        bias = jnp.concatenate(
            [cols[at(i * bunch + n, shard), 8 + b : 9 + b] for n in range(bunch) for b in range(4)],
            axis=0,
        )
        for b in range(4):
            part = slice(b * tall, (b + 1) * tall)
            out, grad = gelu(raw[part] + bias[part])
            place = pl.ds(pl.multiple_of((i * 4 + b) * tall, tall), tall)
            act[place] = out.astype(BF16)
            slope[place] = grad.astype(BF16)

    run(n_steps, lambda i: (i,), expand, activate, raw0, raw1)

    def contract(g, acc):
        out = mm(wd[at(g, group)], act[at(g, hid)], 1, 0)
        v = out + first[at(g, group)] + col(g, group, 5)
        v2[at(g, group)] = v
        return (acc + sub(v),)

    (acc,) = loop(GROUPS, contract, zero_row)
    mean = acc * inv
    scale2 = center(v2)

    for copy in late:
        copy.wait()
    loss, sum1, sum2 = zero_row, zero_row, zero_row
    for c in range(width // LANES):
        span = slice(c * LANES, (c + 1) * LANES)
        xhat = v2[span] * scale2
        v2[span] = xhat
        gain = cols[span, 6:7]
        full = xhat * gain + cols[span, 7:8]
        error = full - teacher[:, span].T.astype(F32)
        loss += sub(live * error * error)
        grad = live * (out_grad[:, span].T.astype(F32) + error * coef)
        r.layer_out[:, span] = full.astype(BF16).T
        vcols[span, 4:5] = jnp.sum(grad * xhat, axis=1, keepdims=True)
        vcols[span, 5:6] = jnp.sum(grad, axis=1, keepdims=True)
        grad = grad * gain
        seed[span] = grad
        sum1 += sub(grad)
        sum2 += sub(grad * xhat)
    sum1, sum2 = sum1 * inv, sum2 * inv

    def back2(g, unused):
        place = at(g, group)
        grad = scale2 * (seed[place] - sum1 - v2[place] * sum2)
        seed[place] = grad
        brief = grad.astype(BF16)
        low2[place] = brief
        vcols[place, 3:4] = jnp.sum(brief.astype(F32), axis=1, keepdims=True)
        return (unused,)

    loop(GROUPS, back2, 0)

    def back_act(i, unused):
        place = at(i, span4)
        g, c = i // steps_group, lax.rem(i, steps_group)
        raw = mm(wd[at(g, group), at(c, span4)], low2[at(g, group)], 0, 0)
        slope[place] = (raw * slope[place].astype(F32)).astype(BF16)
        return (unused,)

    loop(n_steps, back_act, 0)

    def back_first(g, a, b):
        place = at(g, group)
        grad = seed[place] + mm(w_up[place], slope[at(g, hid)], 1, 0)
        xhat = v1[place]
        vcols[place, 1:2] = jnp.sum(grad * xhat, axis=1, keepdims=True)
        vcols[place, 2:3] = jnp.sum(grad, axis=1, keepdims=True)
        grad = grad * col(g, group, 3)
        seed[place] = grad
        return (a + sub(grad), b + sub(grad * xhat))


    vecs = r.vecs
    if split:
        other_y = my_dp + 1 - 2 * my_y
        side, cross, spread_z, spread_v = r.side, r.cross, r.spread_z, r.spread_v
        od_out, vec_out = r.od_out, r.vec_out
        red_send, red_recv = r.red_send, r.red_recv

        def side_copies():
            return (
                remote(
                    pack.at[:, 1 - core, pl.ds(1, 2)],
                    side.at[:, pl.ds(1, 2)],
                    red_send.at[0],
                    red_recv.at[0],
                    seq=me ^ 1,
                ),
                remote(
                    pack.at[:, 1 - core, 0],
                    side.at[:, 0],
                    red_send.at[6],
                    red_recv.at[6],
                    seq=me ^ 1,
                ),
                remote(vecs, r.vec_side, red_send.at[1], red_recv.at[1], seq=me ^ 1),
            )

        def cross_copy(j):
            z = lax.rem(my_z + 1 + j, n_z)
            return remote(
                side.at[2 * z + 1 - my_y],
                cross.at[z],
                r.cross_send.at[z],
                r.cross_recv.at[z],
                dp=other_y,
            )

        def vec_cross():
            return remote(
                r.vec_mine, r.vec_cross, red_send.at[2], red_recv.at[2], dp=other_y
            )

        def z_copy(j):
            z = lax.rem(my_z + 1 + j, n_z)
            return remote(
                side.at[2 * z + my_y],
                spread_z.at[my_z],
                r.z_send.at[j],
                r.z_recv.at[j],
                dp=2 * z + my_y,
            )

        def vz_copy(j):
            z = lax.rem(my_z + 1 + j, n_z)
            return remote(
                r.vec_sum,
                spread_v.at[my_z],
                r.vz_send.at[j],
                r.vz_recv.at[j],
                dp=2 * z + my_y,
            )

        def x_copies():
            return (
                remote(
                    r.x_mine, r.x_theirs, red_send.at[3], red_recv.at[3], seq=me ^ 2
                ),
                remote(r.vec_z, r.vec_x, red_send.at[4], red_recv.at[4], seq=me ^ 2),
            )

        def last_copy():
            return remote(
                od_out.at[core], od_out.at[core], red_send.at[5], red_recv.at[5], seq=me ^ 1
            )

        def reduce_side():
            for copy in side_copies():
                copy.wait_recv()

            def add(i, unused):
                side[i] = (pack[i, core].astype(F32) + side[i].astype(F32)).astype(BF16)
                return (unused,)

            loop(n_dp, add, 0)
            r.vec_mine[...] = vecs[...] + r.vec_side[...]
            vec_cross().start()
            for j in range(n_z):
                cross_copy(j).start()

        def reduce_cross(j):
            cross_copy(j).wait_recv()
            z = lax.rem(my_z + 1 + j, n_z)
            i = 2 * z + my_y
            side[i] = (side[i].astype(F32) + cross[z].astype(F32)).astype(BF16)
            if j < n_z - 1:
                z_copy(j).start()

        def reduce_vec():
            vec_cross().wait_recv()
            value = r.vec_mine[...] + r.vec_cross[...]
            r.vec_sum[...] = value
            spread_v[my_z] = value
            for j in range(n_z - 1):
                vz_copy(j).start()

        def reduce_z():
            for j in range(n_z - 1):
                z_copy(j).wait_recv()
                vz_copy(j).wait_recv()
            spread_z[my_z] = side[my_dp]
            value = spread_z[0].astype(F32)
            vec = spread_v[0]
            for z in range(1, n_z):
                value += spread_z[z].astype(F32)
                vec += spread_v[z]
            r.x_mine[...] = value.astype(BF16)
            r.vec_z[...] = vec
            for copy in x_copies():
                copy.start()

        def reduce_x():
            for copy in x_copies():
                copy.wait_recv()
            od_out[core] = r.x_mine[...].astype(F32) + r.x_theirs[...].astype(F32)
            vec_out[...] = r.vec_z[...] + r.vec_x[...]
            last_copy().start()

    vecs[...] = jnp.zeros_like(vecs)
    for g in range(GROUPS):
        out = mm(low[low1(g, 0, tall1)], slope[g * hid : (g + 1) * hid], 1, 1)
        vecs[8 + g : 9 + g] = out[group : group + 1]
        if split:
            for t in range(per_group):
                for c in range(2):
                    base = shard * t + half * c
                    pack[g * per_group + t, c, 1] = out[base : base + half].astype(BF16)
        else:
            r.g_all[1, g * group : (g + 1) * group] = out[0:group].astype(BF16)
    sum1, sum2 = loop(GROUPS, back_first, zero_row, zero_row)
    sum1, sum2 = sum1 * inv, sum2 * inv

    for g in range(GROUPS):
        out = mm(low2[g * group : (g + 1) * group], act[g * hid : (g + 1) * hid], 1, 1)
        if split:
            for t in range(per_group):
                for c in range(2):
                    for k in range(2):
                        pack[g * per_group + t, c, 2, :, k * 4 * shard : (k + 1) * 4 * shard] = (
                            out[
                                (2 * c + k) * half : (2 * c + k + 1) * half,
                                t * 4 * shard : (t + 1) * 4 * shard,
                            ].astype(BF16)
                        )
        else:
            r.g_all[2, g * group : (g + 1) * group] = out.astype(BF16)

    if split:
        side_copies()[0].start()

    def back1(g, unused):
        place = at(g, group)
        grad = scale1 * (seed[place] - sum1 - v1[place] * sum2)
        seed[place] = grad
        brief = grad.astype(BF16)
        low2[place] = brief
        vcols[place, 0:1] = jnp.sum(brief.astype(F32), axis=1, keepdims=True)
        return (unused,)

    loop(GROUPS, back1, 0)
    grad_mid = seed

    def back_context(i, unused):
        c_grad[at(i, step)] = mm(wo[at(i, step)], low2[...], 1, 0).astype(BF16)
        return (unused,)

    loop(width // step, back_context, 0)
    for d in [1] + far:
        g_copy(d).start()

    vecs[0:8] = vcols[...].T[0:8]
    mean_loss = jnp.sum(loss, axis=1, keepdims=True) / (total * width)
    vecs[12:13] = jnp.broadcast_to(mean_loss, (1, width))
    for j in range(2):
        rows = width // 2
        out = mm(context_r[j * rows : (j + 1) * rows], low2[...], 1, 1)
        if split:
            for t in range(n_dp // 2):
                for c in range(2):
                    base = shard * t + half * c
                    pack[j * (n_dp // 2) + t, c, 0] = out[base : base + half].astype(BF16)
        else:
            r.g_all[0, j * rows : (j + 1) * rows] = out.astype(BF16)

    if split:
        for copy in side_copies()[1:]:
            copy.start()


    def clear(i, unused):
        for ref in (dq, dk, dv):
            ref[at(i, HDIM)] = jnp.zeros((HDIM, piece), F32)
        return (unused,)

    loop(heads * seq, clear, 0)
    tail_row = iota((HDIM, piece), 0)

    def prepare(t):
        for h in range(heads):
            span = slice(h * HDIM, (h + 1) * HDIM)
            grad = d_in[t, span]
            low[d_aug(h, t, 0, HDIM)] = grad
            parts = three_parts(-sub(grad.astype(F32) * context_s[t, span].astype(F32)))
            value = jnp.zeros((HDIM, piece), F32)
            for n, part in enumerate(parts):
                value = jnp.where(tail_row == n, part.astype(F32), value)
            low[d_aug(h, t, HDIM, HDIM)] = value.astype(BF16)

    def rows_of(h, t):
        return at(h * seq + t, HDIM)

    def weigh(buffers, t, h, k):
        p, s = buffers
        weights = jnp.exp2(mm(q_t[h, t], k_n[h, k], 0, 1))
        p[...] = weights.astype(BF16)
        s[...] = (weights * mm(low[d_aug(h, t, 0, LANES)], v_n[h, k], 0, 1)).astype(BF16)

    def gather_grads(buffers, t, h, k):
        p, s = buffers
        dv[rows_of(h, k)] += mm(low[d_aug(h, t, 0, HDIM)], p[...], 1, 0)
        dk[rows_of(h, k)] += mm(q_t[h, t, 0:HDIM], s[...], 1, 0)
        dq[rows_of(h, t)] += mm(k_t[h, k], s[...], 1, 1)

    def turned(t, kind, h):
        return pl.ds(pl.multiple_of((t * 3 + kind) * group + h * HDIM, HDIM), HDIM)

    def fill(t, h):
        for kind, (ref, scale) in enumerate(((dq, HDIM**-0.5), (dk, 1.0 / LOG2E), (dv, 1.0))):
            d_t[turned(t, kind, h)] = (ref[rows_of(h, t)] * scale).astype(BF16)

    def whole(t, kind):
        return pl.ds(pl.multiple_of((t * 3 + kind) * group, HDIM), group)

    def states_part(t):
        out = mm(w_group[0], d_t[whole(t, 0)], 1, 0)
        out += mm(w_group[1], d_t[whole(t, 1)], 1, 0)
        out += mm(w_group[2], d_t[whole(t, 2)], 1, 0)
        dx_s[at(t, group)] = out.astype(BF16)

    if split:
        qkv_s, qkv_r, qkv_out = r.qkv_s, r.qkv_r, r.qkv_out
        owner = my_dp // per_group == me

        def qkv_copy(h, t):
            return remote(
                qkv_s.at[h, t],
                qkv_r.at[h, my_dp],
                r.q1_send.at[h, t],
                r.q1_recv.at[h, my_dp],
                dp=me * per_group + t,
            )

        def qkv_share(h, d):
            return remote(
                qkv_out.at[h], qkv_out.at[h], r.q2_send.at[h, d], r.q2_recv.at[h], seq=me ^ d
            )

    def emit(h):
        for d in range(2):
            fill(me ^ d, h)
        totals = []
        for kind in range(3):
            value = mm(x_group[0], d_t[turned(0, kind, h)], 1, 1)
            for t in range(1, seq):
                value += mm(x_group[t], d_t[turned(t, kind, h)], 1, 1)
            totals.append(value)
        if split:
            bias_rows = jnp.zeros((shard, HDIM), F32)
            bias_id = iota((shard, HDIM), 0)
            for kind in range(3):
                bias_rows = jnp.where(bias_id == kind, totals[kind][group : group + 1], bias_rows)
            for t in range(per_group):
                qkv_s[h, t] = jnp.concatenate(
                    [value[t * shard : (t + 1) * shard] for value in totals] + [bias_rows], axis=1
                ).astype(BF16)
                when(me * per_group + t != my_dp, lambda: qkv_copy(h, t).start())
        else:
            for kind in range(3):
                r.qkv_raw[h, kind] = totals[kind]

    def place_backward(i):
        part, j = i // per_part, lax.rem(i, per_part)
        is_far, tail = lax.rem((part + 1) // 2, 2), part // 3
        near = 1 - is_far
        d_q = is_far * (4 - part) + near * (
            (1 - tail) * (j // (2 * heads)) + tail * (lax.rem(j, 4) // 2)
        )
        h = is_far * (j // seq) + near * (
            (1 - tail) * (lax.rem(j, 2 * heads) // 2) + tail * (j // 4)
        )
        d_k = is_far * lax.rem(j, seq) + near * (lax.rem(j, 2) + 2 * (1 - tail))
        return me ^ d_q, h, me ^ d_k

    def receive(d):
        g_copy(d).wait_recv()
        prepare(me ^ d)

    def far_states_grads():
        for d in range(1, seq):
            g_copy(d).wait_send()
        for d in far:
            for h in range(heads):
                fill(me ^ d, h)
            states_part(me ^ d)
            dx_copy(d).start()

    hooks = [
        (heads - 1, lambda: receive(1)),
        (per_part // 2 - 1, lambda: receive(far[0])),
        (per_part - 1, lambda: receive(far[1])),
        (per_part * 3 // 2, far_states_grads),
        (per_part * 3 // 2 + 2, lambda: emit(0)),
        (per_part * 3 // 2 + 4, lambda: emit(1)),
    ]
    if split:
        hooks += [
            (1, reduce_side),
            (5, lambda: reduce_cross(0)),
            (7, lambda: reduce_cross(1)),
            (8, reduce_vec),
            (10, lambda: reduce_cross(2)),
            (13, lambda: reduce_cross(3)),
            (19, reduce_z),
        ]
    d_in[me] = c_grad[at(me, group)]
    prepare(me)
    run(4 * per_part, place_backward, weigh, gather_grads, (p0, s0), (p1, s1), hooks)
    emit(2)
    states_part(me ^ 1)
    dx_copy(1).start()
    states_part(me)
    dx_r[at(me, group)] = dx_s[at(me, group)]
    if split:
        reduce_x()

        @pl.when(owner)
        def _():
            for h in range(heads):
                value = qkv_s[h, my_slot].astype(F32)
                for e in range(1, n_dp):
                    src = lax.rem(my_dp + e, n_dp)
                    remote(
                        qkv_s.at[h, 0],
                        qkv_r.at[h, src],
                        r.q1_send.at[h, 0],
                        r.q1_recv.at[h, src],
                        dp=src,
                    ).wait_recv()
                    value += qkv_r[h, src].astype(F32)
                qkv_out[h] = value.astype(BF16)
                for d in range(1, seq):
                    qkv_share(h, d).start()

    for d in range(1, seq):
        dx_copy(d).wait_recv()
    for c in range(width // LANES):
        span = slice(c * LANES, (c + 1) * LANES)
        r.states_grad[:, span] = (dx_r[span].astype(F32) + grad_mid[span]).astype(BF16).T


    for d in range(1, seq):
        x_copy(d).wait_send()
        c_copy(d).wait_send()
        dx_copy(d).wait_send()
    if split:
        last_copy().wait()
        for h in range(heads):
            for t in range(per_group):
                when(me * per_group + t != my_dp, lambda: qkv_copy(h, t).wait_send())

        @pl.when(owner)
        def _():
            for h in range(heads):
                for d in range(1, seq):
                    qkv_share(h, d).wait_send()

        @pl.when(jnp.logical_not(owner))
        def _():
            for h in range(heads):
                qkv_share(h, 1).wait_recv()

        for e in range(1, n_dp):
            s_copy(e).wait_send()

        for g in range(2):

            @pl.when(holds(g))
            def _():
                for j in range(n_z - 1):
                    w_along(g, j).wait_send()

            w_across(g).wait_send()

            @pl.when(core != g)
            def _():
                when(jnp.logical_not(holds(g)), lambda: w_beside(g, 0, core).wait_send())
                w_beside(g, 1, core).wait_send()

        for copy in side_copies() + x_copies():
            copy.wait_send()
        vec_cross().wait_send()
        for j in range(n_z):
            cross_copy(j).wait_send()
        for j in range(n_z - 1):
            z_copy(j).wait_send()
            vz_copy(j).wait_send()


def layer(cfg, row, collective_id, inputs):
    c = cfg
    g, l, h, s, w, f = c.group, c.piece, c.heads, c.seq, c.width, c.hidden
    n_z = c.dp // 2
    sds = jax.ShapeDtypeStruct
    dma = pltpu.SemaphoreType.DMA
    vm = pltpu.VMEM
    outputs = dict(layer_out=sds((l, w), BF16), states_grad=sds((l, w), BF16))
    if c.split:
        outputs |= dict(
            od_out=sds((2, 3, c.half, w), F32),
            qkv_out=sds((h, c.shard, 4 * HDIM), BF16),
            vec_out=sds((16, w), F32),
        )
    else:
        outputs |= dict(
            g_all=sds((3, w, w), BF16),
            qkv_raw=sds((h, 3, g + AUG, HDIM), F32),
            vecs=sds((16, w), F32),
        )
    scratch = dict(
        x_own=vm((w, l), BF16),
        x_group=vm((s, g + AUG, l), BF16),
        w_group=vm((3, g, g), BF16),
        w_pad=vm((3, g + AUG, h * LANES), BF16),
        q_t=vm((h, s, LANES, l), BF16),
        k_n=vm((h, s, l, LANES), BF16),
        k_t=vm((h, s, HDIM, l), BF16),
        v_n=vm((h, s, l, LANES), BF16),
        context_s=vm((s, g, l), BF16),
        context_r=vm((w, l), BF16),
        tops=vm((h * s, 1, l), F32),
        gathered=vm((h * s * (HDIM + AUG), l), F32),
        cols=vm((w, 16), F32),
        vcols=vm((w, LANES), F32),
        wide=vm((4 * w, l), F32),
        slim=vm((2 * f, l), BF16),
        c_grad=vm((w, l), BF16),
        d_in=vm((s, g, l), BF16),
        dx_r=vm((w, l), BF16),
        low=vm((GROUPS * (g + AUG) + w, l), BF16),
        late_sem=dma((2,)),
        x_send=dma((s,)),
        x_recv=dma((s,)),
        c_send=dma((s,)),
        c_recv=dma((s,)),
        g_send=dma((s,)),
        g_recv=dma((s,)),
        dx_send=dma((s,)),
        dx_recv=dma((s,)),
    )
    if c.split:
        unit = (3, c.half, w)
        vec = (16, w)
        scratch |= dict(
            wo=vm((w, w), BF16),
            w_up=vm((w, w), BF16),
            wd=vm((w, f // GROUPS), BF16),
            smalls=vm((c.dp, 16, LANES), F32),
            pack=vm((c.dp, 2) + unit, BF16),
            w_in=vm((2, c.per_group, 2, c.half, 3 * g), BF16),
            vecs=vm(vec, F32),
            side=vm((c.dp,) + unit, BF16),
            cross=vm((n_z,) + unit, BF16),
            spread_z=vm((n_z,) + unit, BF16),
            spread_v=vm((n_z,) + vec, F32),
            x_mine=vm(unit, BF16),
            x_theirs=vm(unit, BF16),
            vec_side=vm(vec, F32),
            vec_mine=vm(vec, F32),
            vec_cross=vm(vec, F32),
            vec_sum=vm(vec, F32),
            vec_z=vm(vec, F32),
            vec_x=vm(vec, F32),
            qkv_s=vm((h, c.per_group, c.shard, 4 * HDIM), BF16),
            qkv_r=vm((h, c.dp, c.shard, 4 * HDIM), BF16),
            s_send=dma((c.dp,)),
            s_recv=dma((c.dp,)),
            w_send=dma((2, n_z + 1)),
            w_recv=dma((2, 2)),
            wb_send=dma((2,)),
            wb_recv=dma((2,)),
            hop_send=dma((3, c.dp)),
            hop_recv=dma((c.dp,)),
            sib_send=dma((c.dp,)),
            sib_recv=dma((c.dp,)),
            red_send=dma((7,)),
            red_recv=dma((7,)),
            cross_send=dma((n_z,)),
            cross_recv=dma((n_z,)),
            z_send=dma((n_z,)),
            z_recv=dma((n_z,)),
            vz_send=dma((n_z,)),
            vz_recv=dma((n_z,)),
            q1_send=dma((h, c.per_group)),
            q1_recv=dma((h, c.dp)),
            q2_send=dma((h, s)),
            q2_recv=dma((h,)),
        )
    names = tuple(inputs) + tuple(outputs) + tuple(scratch)
    vmem = pl.BlockSpec(memory_space=pltpu.VMEM)
    hbm = pl.BlockSpec(memory_space=pl.ANY)
    special = dict(teacher=hbm, out_grad=hbm, lengths=pl.BlockSpec(memory_space=pltpu.SMEM))
    results = pl.pallas_call(
        functools.partial(layer_kernel, cfg, row, names),
        out_shape=list(outputs.values()),
        in_specs=[special.get(name, vmem) for name in inputs],
        out_specs=[vmem] * len(outputs),
        scratch_shapes=list(scratch.values()),
        compiler_params=pltpu.CompilerParams(
            collective_id=collective_id, has_side_effects=True, vmem_limit_bytes=VMEM_LIMIT
        ),
        name="layer",
    )(*inputs.values())
    return dict(zip(outputs, results, strict=True))


def deliver_kernel(cfg, layer_in, states_in, qkv, od, vec, *refs):
    outs = refs
    my_dp = lax.axis_index("dp")
    shard, width, half = cfg.shard, cfg.width, cfg.half
    outs[0][...] = layer_in[...]
    outs[1][...] = states_in[...]
    qw, kw, vw, ow, uw, dw = outs[2:8]
    parts = [
        jnp.concatenate(
            [qkv[h, :, k * HDIM : (k + 1) * HDIM].astype(F32) for h in range(cfg.heads)], axis=1
        )
        for k in range(4)
    ]
    for ref, part in zip((qw, kw, vw), parts[:3], strict=True):
        ref[...] = part
    for c in range(2):
        rows = slice(c * half, (c + 1) * half)
        ow[rows] = od[c, 0]
        uw[rows] = od[c, 1]
        for k in range(2):
            dw[(2 * c + k) * half : (2 * c + k + 1) * half] = od[
                c, 2, :, k * 4 * shard : (k + 1) * 4 * shard
            ]
    slot = lax.rem(my_dp, cfg.per_group)
    mine = parts[3][0:8, 0:shard]
    for t in range(1, cfg.per_group):
        mine = jnp.where(slot == t, parts[3][0:8, t * shard : (t + 1) * shard], mine)
    outs[8][...] = mine[0]
    outs[9][...] = mine[2]
    turned = pltpu.roll(vec[0:8], lax.rem(width - my_dp * shard, width), 1)
    for n in range(6):
        outs[10 + n][...] = turned[n, 0:shard]
    outs[16][...] = vec[
        pl.ds(8 + my_dp // cfg.per_group, 1),
        pl.ds(pl.multiple_of(slot * 4 * shard, LANES), 4 * shard),
    ][0]
    outs[17][0] = vec[12, 0]


def deliver(cfg, *args):
    sds = jax.ShapeDtypeStruct
    shard, width, group = cfg.shard, cfg.width, cfg.group
    out_shape = [sds(a.shape, a.dtype) for a in args[:2]]
    out_shape += [sds((shard, group), F32)] * 3 + [sds((shard, width), F32)] * 2
    out_shape += [sds((group, 4 * shard), F32)] + [sds((shard,), F32)] * 8
    out_shape += [sds((4 * shard,), F32), sds((1,), F32)]
    vmem = pl.BlockSpec(memory_space=pltpu.VMEM)
    return pl.pallas_call(
        functools.partial(deliver_kernel, cfg),
        out_shape=out_shape,
        in_specs=[vmem] * len(args),
        out_specs=[vmem] * (len(out_shape) - 1) + [pl.BlockSpec(memory_space=pltpu.SMEM)],
        name="deliver",
    )(*args)


def local(
    states,
    lengths,
    teacher,
    out_grad,
    q_weight,
    k_weight,
    v_weight,
    q_bias,
    v_bias,
    o_weight,
    o_bias,
    attn_gain,
    attn_bias,
    up_weight,
    up_bias,
    down_weight,
    down_bias,
    ffn_gain,
    ffn_bias,
):
    row_count, piece, width = states.shape
    n_dp, n_seq = lax.axis_size("dp"), lax.axis_size("seq")
    me, my_dp = lax.axis_index("seq"), lax.axis_index("dp")
    shard = q_bias.shape[0]
    hidden = up_bias.shape[0] * n_dp
    cfg = Config(n_dp, n_seq, piece, width, hidden, shard)
    cfg.rows = row_count
    group = cfg.group

    if not cfg.split:

        def pad(v):
            return jnp.pad(v.astype(F32), ((0, 0), (0, LANES - v.shape[1])))

        vectors = (q_bias, v_bias, o_bias, attn_gain, attn_bias, down_bias, ffn_gain, ffn_bias)
        small = jnp.concatenate(
            [
                pad(jnp.stack(vectors)),
                pad(up_bias.reshape(4, shard)),
                jnp.broadcast_to(lengths.astype(F32)[:, None], (row_count, LANES)),
                jnp.zeros((4 - row_count, LANES), F32),
            ]
        )
        smalls = lax.all_gather(small, "dp", axis=0)
        qkv = jnp.stack((q_weight, k_weight, v_weight))
        qkv = lax.all_gather(qkv, "dp", axis=1, tiled=True)
        w_group_in = lax.dynamic_slice(qkv, (0, me * group, 0), (3, group, group))
        wo = lax.all_gather(o_weight, "dp", axis=0, tiled=True)
        wu = lax.all_gather(up_weight, "dp", axis=0, tiled=True)
        wd = lax.all_gather(down_weight, "dp", axis=0, tiled=True)
        wd = wd.reshape(GROUPS, -1, group).transpose(0, 2, 1).reshape(width, -1)

    results = []
    for n in range(row_count):
        inputs = dict(states=states[n], teacher=teacher[n], out_grad=out_grad[n])
        if cfg.split:
            inputs |= dict(
                wq=q_weight,
                wk=k_weight,
                wv=v_weight,
                ow=o_weight,
                uw=up_weight,
                dw=down_weight.T,
                qb=q_bias,
                vb=v_bias,
                ob=o_bias,
                ag=attn_gain,
                ab=attn_bias,
                db=down_bias,
                fg=ffn_gain,
                fb=ffn_bias,
                ub=up_bias,
                lengths=lengths,
            )
        else:
            inputs |= dict(smalls=smalls, w_all=w_group_in, wo=wo, w_up=wu, wd=wd)
        results.append(layer(cfg, n, n, inputs))

    def summed(name):
        first = results[0][name]
        if row_count == 1:
            return first
        return sum((item[name].astype(F32) for item in results[1:]), first.astype(F32))

    if cfg.split:
        heavy = [jnp.stack([item[n] for item in results]) for n in ("layer_out", "states_grad")]
        out = deliver(cfg, *heavy, summed("qkv_out"), summed("od_out"), summed("vec_out"))
        grad_qw, grad_kw, grad_vw, grad_ow, grad_uw, grad_dw = out[2:8]
        vectors = out[8:17]
        return (
            (out[0], out[17].reshape(()), out[1], grad_qw, grad_kw, grad_vw)
            + (vectors[0], vectors[1], grad_ow, *vectors[2:5], grad_uw, vectors[8])
            + (grad_dw.T, *vectors[5:8])
        )

    layer_out = jnp.stack([item["layer_out"] for item in results])
    states_grad = jnp.stack([item["states_grad"] for item in results])
    qkv_g, g_all, vecs = (summed(n).astype(F32) for n in ("qkv_raw", "g_all", "vecs"))
    qkv_g = qkv_g.transpose(1, 2, 0, 3).reshape(3, group + AUG, group)
    whole = jnp.zeros((3, width + GROUPS * AUG, group), F32)
    whole = lax.dynamic_update_slice(whole, qkv_g[:, :group], (0, me * group, 0))
    whole = lax.dynamic_update_slice(whole, qkv_g[:, group:], (0, width + me * AUG, 0))
    whole, g_all, vec = lax.psum((whole, g_all, vecs), ("dp", "seq"))
    qkv = lax.dynamic_slice(whole, (0, my_dp * shard, 0), (3, shard, group))
    biases = whole[:, width::AUG].reshape(3, width)
    grad_qb = lax.dynamic_slice(biases[0], (my_dp * shard,), (shard,))
    grad_vb = lax.dynamic_slice(biases[2], (my_dp * shard,), (shard,))
    g_ou = lax.dynamic_slice(g_all[:2], (0, my_dp * shard, 0), (2, shard, width))
    g_d = g_all[2].reshape(GROUPS, group, -1).transpose(0, 2, 1).reshape(-1, group)
    grad_dw = lax.dynamic_slice(g_d, (my_dp * 4 * shard, 0), (4 * shard, group))
    mine = lax.dynamic_slice(vec[:6], (0, my_dp * shard), (6, shard))
    grad_ub = lax.dynamic_slice(vec[8:12].reshape(-1), (my_dp * 4 * shard,), (4 * shard,))
    return (
        (layer_out, vec[12, 0], states_grad, qkv[0], qkv[1], qkv[2], grad_qb, grad_vb, g_ou[0])
        + (mine[0], mine[1], mine[2], g_ou[1], grad_ub, grad_dw, mine[3], mine[4], mine[5])
    )


def solution(mesh):
    rows3 = P("dp", "seq", None)
    matrix = P("dp", None)
    vector = P("dp")
    return jax.shard_map(
        local,
        mesh=mesh,
        in_specs=(rows3, vector, rows3, rows3)
        + (matrix,) * 3
        + (vector,) * 2
        + (matrix,)
        + (vector,) * 3
        + (matrix, vector, matrix)
        + (vector,) * 3,
        out_specs=(rows3, P(), rows3)
        + (matrix,) * 3
        + (vector,) * 2
        + (matrix,)
        + (vector,) * 3
        + (matrix, vector, matrix)
        + (vector,) * 3,
        check_vma=False,
    )
```

```python
import functools
import math
import types

import jax
import jax.numpy as jnp
from jax import lax
from jax.experimental import pallas as pl
from jax.experimental.pallas import tpu as pltpu
from jax.sharding import PartitionSpec as P

HDIM = 64
GROUPS = 4
EPSILON = 1e-12
NEG_FILL = -1e30
LANES = 128
AUG = 16
LOG2E = 1.4426950408889634
MESH = pl.DeviceIdType.MESH
F32 = jnp.float32
BF16 = jnp.bfloat16
VMEM_LIMIT = 60 * 1024 * 1024


def mm(left, right, left_dim, right_dim):
    return lax.dot_general(
        left, right, (((left_dim,), (right_dim,)), ((), ())), preferred_element_type=F32
    )


def iota(shape, dim):
    return lax.broadcasted_iota(jnp.int32, shape, dim)


def remote(src, dst, send_sem, recv_sem, **where):
    return pltpu.make_async_remote_copy(
        src_ref=src,
        dst_ref=dst,
        send_sem=send_sem,
        recv_sem=recv_sem,
        device_id=where,
        device_id_type=MESH,
    )


def three_parts(row):
    high = row.astype(BF16)
    rest = row - high.astype(F32)
    middle = rest.astype(BF16)
    low = (rest - middle.astype(F32)).astype(BF16)
    return high, middle, low


class Config:
    def __init__(self, dp, seq, piece, width, hidden, shard):
        self.dp, self.seq, self.piece, self.width, self.hidden, self.shard = (
            dp,
            seq,
            piece,
            width,
            hidden,
            shard,
        )
        self.slots = piece * seq
        self.group = width // GROUPS
        self.heads = self.group // HDIM
        self.per_group = dp // GROUPS
        self.split = shard % 32 == 0 and seq == 4 and dp == 8
        self.half = shard // 2
        self.quarter = hidden // dp // 4


def greet(cfg, me, my_dp):
    barrier = pltpu.get_barrier_semaphore()
    count = cfg.seq - 1
    for d in range(1, cfg.seq):
        pl.semaphore_signal(barrier, inc=1, device_id={"seq": me ^ d}, device_id_type=MESH)
    if cfg.split:
        count += cfg.dp - 1
        for e in range(1, cfg.dp):
            pl.semaphore_signal(
                barrier, inc=1, device_id={"dp": lax.rem(my_dp + e, cfg.dp)}, device_id_type=MESH
            )
    return lambda: pl.semaphore_wait(barrier, count)


def layer_kernel(cfg, row, names, *refs):
    r = types.SimpleNamespace(**dict(zip(names, refs, strict=True)))
    split = cfg.split
    me = lax.axis_index("seq")
    my_dp = lax.axis_index("dp")
    piece, width, group, heads, seq = cfg.piece, cfg.width, cfg.group, cfg.heads, cfg.seq
    shard, half, n_dp, per_group = cfg.shard, cfg.half, cfg.dp, cfg.per_group
    hid = cfg.hidden // GROUPS
    n_z = n_dp // 2
    core = lax.rem(me, 2)
    my_z, my_y = my_dp // 2, lax.rem(my_dp, 2)
    far = [d for d in range(seq - 1, 1, -1)]

    states = r.states
    teacher, out_grad = r.states_grad, r.layer_out
    late = [
        pltpu.make_async_copy(r.teacher, teacher, r.late_sem.at[0]),
        pltpu.make_async_copy(r.out_grad, out_grad, r.late_sem.at[1]),
    ]
    x_own, x_group, w_group, w_pad, smalls = (
        r.x_own,
        r.x_group,
        r.w_group,
        r.w_pad,
        r.smalls,
    )
    q_t, k_n, k_t, v_n = r.q_t, r.k_n, r.k_t, r.v_n
    context_s, context_r = r.context_s, r.context_r
    cols, vcols = r.cols, r.vcols
    wide, slim = r.wide, r.slim
    wo, w_up, wd = r.wo, r.w_up, r.wd
    c_grad, d_in, dx_r = r.c_grad, r.d_in, r.dx_r
    dx_s = c_grad
    tall1 = group + AUG
    low = r.low
    low2 = low.at[GROUPS * tall1 :]

    def low1(g, start, size):
        return pl.ds(pl.multiple_of(g * tall1 + start, AUG), size)

    def d_aug(h, t, start, size):
        return pl.ds(pl.multiple_of((h * seq + t) * LANES + start, HDIM), size)

    score0, score1 = wide.at[0:piece], wide.at[piece : 2 * piece]
    gathered = r.gathered
    v1, first, v2, seed = (wide.at[i * width : (i + 1) * width] for i in range(4))
    dq, dk, dv = (wide.at[i * width : (i + 1) * width] for i in range(3))
    act, slope = slim.at[0 : cfg.hidden], slim.at[cfg.hidden : 2 * cfg.hidden]
    p0, p1, s0, s1 = (slim.at[i * piece : (i + 1) * piece] for i in range(4))
    d_t = slope

    def at(i, n):
        return pl.ds(pl.multiple_of(i * n, n), n)

    def loop(count, body, *init):
        return lax.fori_loop(0, count, lambda i, c: body(i, *c), tuple(init))

    def sub(v):
        return jnp.sum(v, axis=0, keepdims=True)


    def to_seq(sems, src, dst, d):
        return remote(src, dst, sems[0].at[d], sems[1].at[d], seq=me ^ d)

    def x_copy(d):
        return to_seq((r.x_send, r.x_recv), x_own.at[at(me ^ d, group)], x_group.at[me, pl.ds(0, group)], d)

    def c_copy(d):
        return to_seq((r.c_send, r.c_recv), context_s.at[me ^ d], context_r.at[at(me, group)], d)

    def g_copy(d):
        return to_seq((r.g_send, r.g_recv), c_grad.at[at(me ^ d, group)], d_in.at[me], d)

    def dx_copy(d):
        return to_seq((r.dx_send, r.dx_recv), dx_s.at[at(me ^ d, group)], dx_r.at[at(me, group)], d)

    if split:
        pack = r.pack
        w_in = r.w_in
        my_slot = lax.rem(my_dp, per_group)

        def s_copy(e):
            return remote(
                smalls.at[my_dp],
                smalls.at[my_dp],
                r.s_send.at[e],
                r.s_recv.at[e],
                dp=lax.rem(my_dp + e, n_dp),
            )

        first_group = me - core

        def w_ref(g):
            return w_in.at[g, my_y, core]

        def w_along(g, j):
            z = lax.rem(my_z + n_z - 1 - j, n_z)
            return remote(
                w_ref(g), w_ref(g), r.w_send.at[g, j], r.w_recv.at[g, 0], dp=2 * z + my_y
            )

        def w_across(g):
            return remote(
                w_ref(g), w_ref(g), r.w_send.at[g, n_z], r.w_recv.at[g, 1], dp=my_dp + 1 - 2 * my_y
            )

        def w_over(g):
            ref = w_in.at[g, 1 - my_y, core]
            return remote(ref, ref, r.w_send.at[g, n_z], r.w_recv.at[g, 1], dp=my_dp)

        def w_beside(g, part, half_of):
            ref = w_in.at[g, my_y if part == 0 else 1 - my_y, half_of]
            return remote(ref, ref, r.wb_send.at[part], r.wb_recv.at[part], seq=me ^ 1)

        def holds(g):
            return my_z == first_group + g

        def hop(kind, i, **where):
            ref = pack.at[i, core]
            return remote(ref, ref, r.hop_send.at[kind, i], r.hop_recv.at[i], **where)

        def up(i):
            return hop(0, i, dp=my_dp + 2)

        def down(i):
            return hop(1, i, dp=my_dp - 2)

        def across(i):
            return hop(2, i, dp=my_dp + 1 - 2 * my_y)

        def beside(i):
            ref = pack.at[i, core]
            return remote(ref, ref, r.sib_send.at[i], r.sib_recv.at[i], seq=me ^ 1)

        def when(condition, fn):
            pl.when(condition)(fn)

        def gather_start():
            when(my_z < n_z - 1, lambda: up(my_dp).start())
            when(my_z > 0, lambda: down(my_dp).start())

        def gather_z(k):
            below, above = my_dp - 2 * k, my_dp + 2 * k

            @pl.when(my_z >= k)
            def _():
                hop(0, below, dp=my_dp).wait_recv()
                when(my_z < n_z - 1, lambda: up(below).start())
                across(below).start()
                beside(below).start()

            @pl.when(my_z + k < n_z)
            def _():
                hop(0, above, dp=my_dp).wait_recv()
                when(my_z > 0, lambda: down(above).start())
                across(above).start()
                beside(above).start()

        def gather_y(k):
            other = my_dp + 1 - 2 * my_y

            def take(i):
                hop(2, i, dp=my_dp).wait_recv()
                beside(i).start()

            if k == 0:
                take(other)
            else:
                when(my_z >= k, lambda: take(other - 2 * k))
                when(my_z + k < n_z, lambda: take(other + 2 * k))

        def gather_end():
            for e in range(1, n_dp):
                copy = beside(lax.rem(my_dp + e, n_dp))
                copy.wait()

            when(my_z < n_z - 1, lambda: up(my_dp).wait_send())
            when(my_z > 0, lambda: down(my_dp).wait_send())
            across(my_dp).wait_send()
            for k in range(1, n_z):
                below, above = my_dp - 2 * k, my_dp + 2 * k

                @pl.when(my_z >= k)
                def _():
                    when(my_z < n_z - 1, lambda: up(below).wait_send())
                    across(below).wait_send()

                @pl.when(my_z + k < n_z)
                def _():
                    when(my_z > 0, lambda: down(above).wait_send())
                    across(above).wait_send()


    wait_entry = greet(cfg, me, my_dp)
    for c in range(0, width, LANES):
        x_own[c : c + LANES] = states[:, c : c + LANES].T
    if split:
        for c in range(2):
            pack[my_dp, c, 0] = r.ow[c * half : (c + 1) * half]
            pack[my_dp, c, 1] = r.uw[c * half : (c + 1) * half]
            for k in range(2):
                pack[my_dp, c, 2, :, k * 4 * shard : (k + 1) * 4 * shard] = r.dw[
                    (2 * c + k) * half : (2 * c + k + 1) * half
                ]
        smalls[my_dp] = jnp.zeros((16, LANES), F32)
        for n, ref in enumerate((r.qb, r.vb, r.ob, r.ag, r.ab, r.db, r.fg, r.fb)):
            smalls[my_dp, n : n + 1, 0:shard] = ref[...].reshape(1, shard).astype(F32)
        up_bias = r.ub[...].reshape(1, 4 * shard).astype(F32)
        for n in range(4):
            smalls[my_dp, 8 + n : 9 + n, 0:shard] = up_bias[:, n * shard : (n + 1) * shard]
        for n in range(cfg.rows):
            smalls[my_dp, 12 + n : 13 + n] = jnp.full((1, LANES), r.lengths[n].astype(F32))

        for g in range(2):

            @pl.when(holds(g))
            def _():
                for c in range(2):
                    rows = slice(c * half, (c + 1) * half)
                    w_in[g, my_y, c] = jnp.concatenate(
                        [ref[rows].astype(F32) for ref in (r.wq, r.wk, r.wv)], axis=1
                    ).astype(BF16)

    wait_entry()
    if split:
        for e in range(1, n_dp):
            s_copy(e).start()

        for g in range(2):

            @pl.when(holds(g))
            def _():
                for j in range(n_z - 1):
                    w_along(g, j).start()
                w_across(g).start()

    for d in range(1, seq):
        x_copy(d).start()
    for copy in late:
        copy.start()
    x_group[me, 0:group] = x_own[at(me, group)]


    deep = HDIM + AUG
    tops = r.tops

    def sums(h, t):
        return pl.ds(pl.multiple_of((h * seq + t) * deep, AUG), deep)

    def clear_sums(i, unused):
        gathered[pl.ds(pl.multiple_of(i * deep, AUG), deep)] = jnp.zeros((deep, piece), F32)
        tops[i] = jnp.full((1, piece), NEG_FILL, F32)
        return (unused,)

    loop(heads * seq, clear_sums, 0)
    n_cols = heads * LANES
    if split:
        for n, g in enumerate((1 - core, core)):

            @pl.when(jnp.logical_not(holds(g)))
            def _():
                w_along(g, 0).wait_recv()
                w_across(g).start()
                if n == 0:
                    w_beside(g, 0, core).start()

        gather_start()
        for e in range(1, n_dp):
            s_copy(e).wait_recv()
    for i in range(n_dp):
        turned_small = smalls[i].T
        cols[i * shard : (i + 1) * shard] = turned_small[0:shard]
    vec_rows = jnp.zeros((AUG, n_cols), F32)
    lane = iota((LANES, n_cols), 1)
    source = iota((LANES, n_cols), 0)
    for t in range(per_group):
        spread = jnp.where(
            (((lane >> 7) * HDIM + (lane & 127)) == source + t * shard)
            & ((lane & 127) < HDIM)
            & (source < shard),
            1.0,
            0.0,
        ).astype(BF16)
        vec_rows += mm(smalls[me * per_group + t].astype(BF16), spread, 1, 0)
    row_id = iota((AUG, n_cols), 0)
    lane = iota((AUG, n_cols), 1) & 127
    zero = jnp.zeros((AUG, n_cols), F32)
    top_row = row_id == 0
    w_pad[0, group:] = jnp.where(top_row, vec_rows[0:1], zero).astype(BF16)
    ones_k = (top_row & (lane > HDIM) & (lane <= HDIM + 3)) | ((row_id == 1) & (lane == HDIM))
    w_pad[1, group:] = jnp.where(ones_k, 1.0, zero).astype(BF16)
    ones_v = (lane >= HDIM) & (lane < HDIM + 3)
    w_pad[2, group:] = jnp.where(top_row, jnp.where(ones_v, 1.0, vec_rows[1:2]), zero).astype(BF16)

    if split:
        for n, g in enumerate((1 - core, core)):
            w_over(g).wait_recv()
            if n == 0:
                w_beside(g, 1, core).start()
        across(my_dp).start()
        when(my_z != me, lambda: w_beside(core, 0, 1 - core).wait_recv())
        w_beside(core, 1, 1 - core).wait_recv()
        for t in range(per_group):
            for c in range(2):
                for kind in range(3):
                    w_group[kind, t * shard + c * half : t * shard + (c + 1) * half] = w_in[
                        core, t, c, :, kind * group : (kind + 1) * group
                    ]
    else:
        for kind in range(3):
            w_group[kind] = r.w_all[kind]
    lane = iota((group, n_cols), 1)
    spread = jnp.where(
        (((lane >> 7) * HDIM + (lane & 127)) == iota((group, n_cols), 0)) & ((lane & 127) < HDIM),
        1.0,
        0.0,
    ).astype(BF16)
    for kind in range(3):
        w_pad[kind, 0:group] = mm(w_group[kind], spread, 1, 0).astype(BF16)

    length = smalls[my_dp, 12 + row : 13 + row, 0:1]
    aug_row = iota((AUG, piece), 0)
    factor = LOG2E * HDIM**-0.5
    def v_t(h, t):
        return pl.ds(pl.multiple_of((h * seq + t) * deep, AUG), deep)

    def project(t):
        slot = (iota((AUG, piece), 1) + t * piece).astype(F32)
        mask = jnp.where(slot < length, 0.0, NEG_FILL)
        x_group[t, group:] = jnp.where(
            aug_row == 0, 1.0, jnp.where(aug_row == 1, mask, 0.0)
        ).astype(BF16)
        x = x_group[t]
        queries = mm(w_pad[0], x, 0, 0) * factor
        keys_t = mm(w_pad[1], x, 0, 0)
        values_t = mm(w_pad[2], x, 0, 0)
        keys_n = mm(x, w_pad[1], 0, 0)
        values_n = mm(x, w_pad[2], 0, 0)
        rest = jnp.where(iota((HDIM, piece), 0) == 0, 1.0, 0.0).astype(BF16)
        for h in range(heads):
            span = slice(h * LANES, h * LANES + HDIM)
            q_t[h, t, 0:HDIM] = queries[span].astype(BF16)
            q_t[h, t, HDIM:] = rest
            k_t[h, t] = keys_t[span].astype(BF16)
            slim[v_t(h, t)] = values_t[h * LANES : h * LANES + deep].astype(BF16)
            k_n[h, t] = keys_n[:, h * LANES : (h + 1) * LANES].astype(BF16)
            v_n[h, t] = values_n[:, h * LANES : (h + 1) * LANES].astype(BF16)


    per_part = seq * heads

    def run(count, place, first_part, last_part, a, b, hooks=(), rest=None, unroll=2):
        buffers = (a, b)
        first_part(a, *place(0))

        def several(u, unused):
            if hooks:
                due = u == hooks[0][0]
                for when_u, fn in hooks[1:]:
                    due = due | (u == when_u)

                @pl.when(due)
                def _():
                    for when_u, fn in hooks:
                        pl.when(u == when_u)(fn)

            for j in range(unroll):
                first_part(buffers[(j + 1) % 2], *place(unroll * u + j + 1))
                last_part(buffers[j % 2], *place(unroll * u + j))
            return (unused,)

        turns = (count - 1) // unroll
        loop(turns, several, 0)
        if rest is not None:
            rest()
        for i in range(turns * unroll, count - 1):
            first_part(buffers[(i + 1) % 2], *place(i + 1))
            last_part(buffers[i % 2], *place(i))
        last_part(buffers[(count - 1) % 2], *place(count - 1))

    unroll = 4

    def before(step):
        return (step - 1) // unroll

    def after(step):
        return step // unroll + 1

    def score(buffer, t, h, k):
        buffer[...] = mm(k_n[h, k], q_t[h, t], 1, 0)

    def absorb(buffer, t, h, k):
        i = h * seq + t
        old = tops[i]
        top = jnp.maximum(old, jnp.max(buffer[...], axis=0, keepdims=True))
        weights = jnp.exp2(buffer[...] - top).astype(BF16)
        tops[i] = top
        place = sums(h, t)
        gathered[place] = gathered[place] * jnp.exp2(old - top) + mm(slim[v_t(h, k)], weights, 1, 0)

    def settle(t):
        for h in range(heads):
            total = gathered[sums(h, t)]
            mass = total[HDIM : HDIM + 1]
            context_s[t, h * HDIM : (h + 1) * HDIM] = (total[0:HDIM] / mass).astype(BF16)
            parts = three_parts(-(tops[h * seq + t] + jnp.log2(mass)))
            value = jnp.where(aug_row == 0, 1.0, 0.0)
            for n, part in enumerate(parts):
                value = jnp.where(aug_row == n + 1, part.astype(F32), value)
            q_t[h, t, HDIM:deep] = value.astype(BF16)

    def place_forward(i):
        part, j = i // per_part, lax.rem(i, per_part)
        is_far, tail = lax.rem((part + 1) // 2, 2), part // 3
        d_q = is_far * (4 - part) + (1 - is_far) * (j // (2 * heads))
        h = is_far * (j // seq) + (1 - is_far) * (lax.rem(j, 2 * heads) // 2)
        d_k = is_far * lax.rem(j, seq) + (1 - is_far) * (lax.rem(j, 2) + 2 * tail)
        return me ^ d_q, h, me ^ d_k

    def far_states():
        for d in far:
            x_copy(d).wait_recv()
        loop(2, lambda i, unused: (project(me ^ (2 + i)), unused)[1:], 0)

    def far_context(d):
        settle(me ^ d)
        c_copy(d).start()

    hooks = [
        (before(per_part), far_states),
        (after(2 * per_part - 1), lambda: far_context(far[0])),
        (after(3 * per_part - 1), lambda: far_context(far[1])),
    ]
    if split:
        hooks += [
            (1, lambda: gather_z(1)),
            (3, lambda: gather_y(0)),
            (4, lambda: gather_z(2)),
            (6, lambda: gather_y(1)),
            (7, lambda: gather_z(3)),
            (8, lambda: gather_y(2)),
            (10, lambda: gather_y(3)),
        ]
    project(me)
    x_copy(1).wait_recv()
    project(me ^ 1)
    run(4 * per_part, place_forward, score, absorb, score0, score1, hooks, unroll=unroll)
    settle(me ^ 1)
    c_copy(1).start()
    settle(me)
    context_r[at(me, group)] = context_s[me]
    if split:
        gather_end()

        def unpack(i, unused):
            for c in range(2):
                wo[pl.ds(pl.multiple_of(i * shard + c * half, AUG), half)] = pack[i, c, 0]
                w_up[pl.ds(pl.multiple_of(i * shard + c * half, AUG), half)] = pack[i, c, 1]
                for k in range(2):
                    wd[
                        pl.ds(
                            pl.multiple_of(i // per_group * group + (2 * c + k) * half, AUG), half
                        ),
                        pl.ds(
                            pl.multiple_of(lax.rem(i, per_group) * 4 * shard, LANES), 4 * shard
                        ),
                    ] = pack[i, c, 2, :, k * 4 * shard : (k + 1) * 4 * shard]
            return (unused,)

        loop(n_dp, unpack, 0)


    vcols[...] = jnp.zeros_like(vcols)
    inv = 1.0 / width
    total = jnp.sum(smalls[:, 12:13, 0:1], axis=0)
    for n in range(1, cfg.rows):
        total += jnp.sum(smalls[:, 12 + n : 13 + n, 0:1], axis=0)
    slot = (iota((1, piece), 1) + me * piece).astype(F32)
    live = jnp.where(slot < length, 1.0, 0.0)
    coef = 2.0 / (total * width)
    zero_row = jnp.zeros((1, piece), F32)

    def col(i, n, which):
        return cols[at(i, n), which : which + 1]

    for d in range(1, seq):
        c_copy(d).wait_recv()

    step = 256

    def attn_out(i, acc):
        out = mm(wo[:, at(i, step)], context_r[...], 0, 0)
        v = out + x_own[at(i, step)].astype(F32) + col(i, step, 2)
        v1[at(i, step)] = v
        return (acc + sub(v),)

    (acc,) = loop(width // step, attn_out, zero_row)
    mean = acc * inv

    def center(ref):
        def body(g, acc):
            v = ref[at(g, group)] - mean
            ref[at(g, group)] = v
            return (acc + sub(v * v),)

        (acc,) = loop(GROUPS, body, zero_row)
        return lax.rsqrt(acc * inv + EPSILON)

    scale1 = center(v1)

    def norm1(g, unused):
        v = v1[at(g, group)] * scale1
        v1[at(g, group)] = v
        out = v * col(g, group, 3) + col(g, group, 4)
        first[at(g, group)] = out
        low[low1(g, 0, group)] = out.astype(BF16)
        low[low1(g, group, AUG)] = jnp.where(aug_row == 0, 1.0, 0.0).astype(BF16)
        return (unused,)

    loop(GROUPS, norm1, 0)

    def gelu(u):
        d = 1.0 + (0.3275911 * 0.7071067811865476) * jnp.abs(u)
        t = pltpu.reciprocal(d, approx=True)
        bell = jnp.exp2((u * u) * (-0.5 * LOG2E))
        poly = t * (
            0.127414796
            + t * (-0.142248368 + t * (0.7107068705 + t * (-0.7265760135 + t * 0.5307027145)))
        )
        tail = poly * bell
        phi = jnp.where(u >= 0.0, 1.0 - tail, tail)
        return u * phi, phi + u * bell * 0.3989422804014327

    bunch = max(1, LANES // math.gcd(LANES, 4 * shard) if (4 * shard) % LANES else 1)
    span4 = 4 * shard * bunch
    n_steps = n_dp // bunch
    steps_group = n_steps // GROUPS
    tall = span4 // 4

    raw0, raw1 = wide.at[2 * width : 2 * width + span4], wide.at[3 * width : 3 * width + span4]

    def expand(raw, i):
        g, c = i // steps_group, lax.rem(i, steps_group)
        raw[...] = mm(w_up[at(g, group), at(c, span4)], low[low1(g, 0, group)], 0, 0)

    def activate(raw, i):
        bias = jnp.concatenate(
            [cols[at(i * bunch + n, shard), 8 + b : 9 + b] for n in range(bunch) for b in range(4)],
            axis=0,
        )
        for b in range(4):
            part = slice(b * tall, (b + 1) * tall)
            out, grad = gelu(raw[part] + bias[part])
            place = pl.ds(pl.multiple_of((i * 4 + b) * tall, tall), tall)
            act[place] = out.astype(BF16)
            slope[place] = grad.astype(BF16)

    run(n_steps, lambda i: (i,), expand, activate, raw0, raw1)

    def contract(g, acc):
        out = mm(wd[at(g, group)], act[at(g, hid)], 1, 0)
        v = out + first[at(g, group)] + col(g, group, 5)
        v2[at(g, group)] = v
        return (acc + sub(v),)

    (acc,) = loop(GROUPS, contract, zero_row)
    mean = acc * inv
    scale2 = center(v2)

    for copy in late:
        copy.wait()
    loss, sum1, sum2 = zero_row, zero_row, zero_row
    for c in range(width // LANES):
        span = slice(c * LANES, (c + 1) * LANES)
        xhat = v2[span] * scale2
        v2[span] = xhat
        gain = cols[span, 6:7]
        full = xhat * gain + cols[span, 7:8]
        error = full - teacher[:, span].T.astype(F32)
        loss += sub(live * error * error)
        grad = live * (out_grad[:, span].T.astype(F32) + error * coef)
        r.layer_out[:, span] = full.astype(BF16).T
        vcols[span, 4:5] = jnp.sum(grad * xhat, axis=1, keepdims=True)
        vcols[span, 5:6] = jnp.sum(grad, axis=1, keepdims=True)
        grad = grad * gain
        seed[span] = grad
        sum1 += sub(grad)
        sum2 += sub(grad * xhat)
    sum1, sum2 = sum1 * inv, sum2 * inv

    def back2(g, unused):
        place = at(g, group)
        grad = scale2 * (seed[place] - sum1 - v2[place] * sum2)
        seed[place] = grad
        brief = grad.astype(BF16)
        low2[place] = brief
        vcols[place, 3:4] = jnp.sum(brief.astype(F32), axis=1, keepdims=True)
        return (unused,)

    loop(GROUPS, back2, 0)

    def back_act(i, unused):
        place = at(i, span4)
        g, c = i // steps_group, lax.rem(i, steps_group)
        raw = mm(wd[at(g, group), at(c, span4)], low2[at(g, group)], 0, 0)
        slope[place] = (raw * slope[place].astype(F32)).astype(BF16)
        return (unused,)

    loop(n_steps, back_act, 0)

    def back_first(g, a, b):
        place = at(g, group)
        grad = seed[place] + mm(w_up[place], slope[at(g, hid)], 1, 0)
        xhat = v1[place]
        vcols[place, 1:2] = jnp.sum(grad * xhat, axis=1, keepdims=True)
        vcols[place, 2:3] = jnp.sum(grad, axis=1, keepdims=True)
        grad = grad * col(g, group, 3)
        seed[place] = grad
        return (a + sub(grad), b + sub(grad * xhat))


    vecs = r.vecs
    if split:
        other_y = my_dp + 1 - 2 * my_y
        side, cross, spread_z, spread_v = r.side, r.cross, r.spread_z, r.spread_v
        od_out, vec_out = r.od_out, r.vec_out
        red_send, red_recv = r.red_send, r.red_recv

        def side_copies():
            return (
                remote(
                    pack.at[:, 1 - core, pl.ds(1, 2)],
                    side.at[:, pl.ds(1, 2)],
                    red_send.at[0],
                    red_recv.at[0],
                    seq=me ^ 1,
                ),
                remote(
                    pack.at[:, 1 - core, 0],
                    side.at[:, 0],
                    red_send.at[6],
                    red_recv.at[6],
                    seq=me ^ 1,
                ),
                remote(vecs, r.vec_side, red_send.at[1], red_recv.at[1], seq=me ^ 1),
            )

        def cross_copy(j):
            z = lax.rem(my_z + 1 + j, n_z)
            return remote(
                side.at[2 * z + 1 - my_y],
                cross.at[z],
                r.cross_send.at[z],
                r.cross_recv.at[z],
                dp=other_y,
            )

        def vec_cross():
            return remote(
                r.vec_mine, r.vec_cross, red_send.at[2], red_recv.at[2], dp=other_y
            )

        def z_copy(j):
            z = lax.rem(my_z + 1 + j, n_z)
            return remote(
                side.at[2 * z + my_y],
                spread_z.at[my_z],
                r.z_send.at[j],
                r.z_recv.at[j],
                dp=2 * z + my_y,
            )

        def vz_copy(j):
            z = lax.rem(my_z + 1 + j, n_z)
            return remote(
                r.vec_sum,
                spread_v.at[my_z],
                r.vz_send.at[j],
                r.vz_recv.at[j],
                dp=2 * z + my_y,
            )

        def x_copies():
            return (
                remote(
                    r.x_mine, r.x_theirs, red_send.at[3], red_recv.at[3], seq=me ^ 2
                ),
                remote(r.vec_z, r.vec_x, red_send.at[4], red_recv.at[4], seq=me ^ 2),
            )

        def last_copy():
            return remote(
                od_out.at[core], od_out.at[core], red_send.at[5], red_recv.at[5], seq=me ^ 1
            )

        def reduce_side():
            for copy in side_copies():
                copy.wait_recv()

            def add(i, unused):
                side[i] = (pack[i, core].astype(F32) + side[i].astype(F32)).astype(BF16)
                return (unused,)

            loop(n_dp, add, 0)
            r.vec_mine[...] = vecs[...] + r.vec_side[...]
            vec_cross().start()
            for j in range(n_z):
                cross_copy(j).start()

        def reduce_cross(j):
            cross_copy(j).wait_recv()
            z = lax.rem(my_z + 1 + j, n_z)
            i = 2 * z + my_y
            side[i] = (side[i].astype(F32) + cross[z].astype(F32)).astype(BF16)
            if j < n_z - 1:
                z_copy(j).start()

        def reduce_vec():
            vec_cross().wait_recv()
            value = r.vec_mine[...] + r.vec_cross[...]
            r.vec_sum[...] = value
            spread_v[my_z] = value
            for j in range(n_z - 1):
                vz_copy(j).start()

        def reduce_z():
            for j in range(n_z - 1):
                z_copy(j).wait_recv()
                vz_copy(j).wait_recv()
            spread_z[my_z] = side[my_dp]
            value = spread_z[0].astype(F32)
            vec = spread_v[0]
            for z in range(1, n_z):
                value += spread_z[z].astype(F32)
                vec += spread_v[z]
            r.x_mine[...] = value.astype(BF16)
            r.vec_z[...] = vec
            for copy in x_copies():
                copy.start()

        def reduce_x():
            for copy in x_copies():
                copy.wait_recv()
            od_out[core] = r.x_mine[...].astype(F32) + r.x_theirs[...].astype(F32)
            vec_out[...] = r.vec_z[...] + r.vec_x[...]
            last_copy().start()

    vecs[...] = jnp.zeros_like(vecs)
    for g in range(GROUPS):
        out = mm(low[low1(g, 0, tall1)], slope[g * hid : (g + 1) * hid], 1, 1)
        vecs[8 + g : 9 + g] = out[group : group + 1]
        if split:
            for t in range(per_group):
                for c in range(2):
                    base = shard * t + half * c
                    pack[g * per_group + t, c, 1] = out[base : base + half].astype(BF16)
        else:
            r.g_all[1, g * group : (g + 1) * group] = out[0:group].astype(BF16)
    sum1, sum2 = loop(GROUPS, back_first, zero_row, zero_row)
    sum1, sum2 = sum1 * inv, sum2 * inv

    for g in range(GROUPS):
        out = mm(low2[g * group : (g + 1) * group], act[g * hid : (g + 1) * hid], 1, 1)
        if split:
            for t in range(per_group):
                for c in range(2):
                    for k in range(2):
                        pack[g * per_group + t, c, 2, :, k * 4 * shard : (k + 1) * 4 * shard] = (
                            out[
                                (2 * c + k) * half : (2 * c + k + 1) * half,
                                t * 4 * shard : (t + 1) * 4 * shard,
                            ].astype(BF16)
                        )
        else:
            r.g_all[2, g * group : (g + 1) * group] = out.astype(BF16)

    if split:
        side_copies()[0].start()

    def back1(g, unused):
        place = at(g, group)
        grad = scale1 * (seed[place] - sum1 - v1[place] * sum2)
        seed[place] = grad
        brief = grad.astype(BF16)
        low2[place] = brief
        vcols[place, 0:1] = jnp.sum(brief.astype(F32), axis=1, keepdims=True)
        return (unused,)

    loop(GROUPS, back1, 0)
    grad_mid = seed

    def back_context(i, unused):
        c_grad[at(i, step)] = mm(wo[at(i, step)], low2[...], 1, 0).astype(BF16)
        return (unused,)

    loop(width // step, back_context, 0)
    for d in [1] + far:
        g_copy(d).start()

    vecs[0:8] = vcols[...].T[0:8]
    mean_loss = jnp.sum(loss, axis=1, keepdims=True) / (total * width)
    vecs[12:13] = jnp.broadcast_to(mean_loss, (1, width))
    for j in range(2):
        rows = width // 2
        out = mm(context_r[j * rows : (j + 1) * rows], low2[...], 1, 1)
        if split:
            for t in range(n_dp // 2):
                for c in range(2):
                    base = shard * t + half * c
                    pack[j * (n_dp // 2) + t, c, 0] = out[base : base + half].astype(BF16)
        else:
            r.g_all[0, j * rows : (j + 1) * rows] = out.astype(BF16)

    if split:
        for copy in side_copies()[1:]:
            copy.start()


    def clear(i, unused):
        for ref in (dq, dk, dv):
            ref[at(i, HDIM)] = jnp.zeros((HDIM, piece), F32)
        return (unused,)

    loop(heads * seq, clear, 0)
    tail_row = iota((HDIM, piece), 0)

    def prepare(t):
        for h in range(heads):
            span = slice(h * HDIM, (h + 1) * HDIM)
            grad = d_in[t, span]
            low[d_aug(h, t, 0, HDIM)] = grad
            parts = three_parts(-sub(grad.astype(F32) * context_s[t, span].astype(F32)))
            value = jnp.zeros((HDIM, piece), F32)
            for n, part in enumerate(parts):
                value = jnp.where(tail_row == n, part.astype(F32), value)
            low[d_aug(h, t, HDIM, HDIM)] = value.astype(BF16)

    def rows_of(h, t):
        return at(h * seq + t, HDIM)

    def weigh(buffers, t, h, k):
        p, s = buffers
        weights = jnp.exp2(mm(q_t[h, t], k_n[h, k], 0, 1))
        p[...] = weights.astype(BF16)
        s[...] = (weights * mm(low[d_aug(h, t, 0, LANES)], v_n[h, k], 0, 1)).astype(BF16)

    def gather_grads(buffers, t, h, k):
        p, s = buffers
        dv[rows_of(h, k)] += mm(low[d_aug(h, t, 0, HDIM)], p[...], 1, 0)
        dk[rows_of(h, k)] += mm(q_t[h, t, 0:HDIM], s[...], 1, 0)
        dq[rows_of(h, t)] += mm(k_t[h, k], s[...], 1, 1)

    def turned(t, kind, h):
        return pl.ds(pl.multiple_of((t * 3 + kind) * group + h * HDIM, HDIM), HDIM)

    def fill(t, h):
        for kind, (ref, scale) in enumerate(((dq, HDIM**-0.5), (dk, 1.0 / LOG2E), (dv, 1.0))):
            d_t[turned(t, kind, h)] = (ref[rows_of(h, t)] * scale).astype(BF16)

    def whole(t, kind):
        return pl.ds(pl.multiple_of((t * 3 + kind) * group, HDIM), group)

    def states_part(t):
        out = mm(w_group[0], d_t[whole(t, 0)], 1, 0)
        out += mm(w_group[1], d_t[whole(t, 1)], 1, 0)
        out += mm(w_group[2], d_t[whole(t, 2)], 1, 0)
        dx_s[at(t, group)] = out.astype(BF16)

    if split:
        qkv_s, qkv_r, qkv_out = r.qkv_s, r.qkv_r, r.qkv_out
        owner = my_dp // per_group == me

        def qkv_copy(h, t):
            return remote(
                qkv_s.at[h, t],
                qkv_r.at[h, my_dp],
                r.q1_send.at[h, t],
                r.q1_recv.at[h, my_dp],
                dp=me * per_group + t,
            )

        def qkv_share(h, d):
            return remote(
                qkv_out.at[h], qkv_out.at[h], r.q2_send.at[h, d], r.q2_recv.at[h], seq=me ^ d
            )

    def emit(h):
        for d in range(2):
            fill(me ^ d, h)
        totals = []
        for kind in range(3):
            value = mm(x_group[0], d_t[turned(0, kind, h)], 1, 1)
            for t in range(1, seq):
                value += mm(x_group[t], d_t[turned(t, kind, h)], 1, 1)
            totals.append(value)
        if split:
            bias_rows = jnp.zeros((shard, HDIM), F32)
            bias_id = iota((shard, HDIM), 0)
            for kind in range(3):
                bias_rows = jnp.where(bias_id == kind, totals[kind][group : group + 1], bias_rows)
            for t in range(per_group):
                qkv_s[h, t] = jnp.concatenate(
                    [value[t * shard : (t + 1) * shard] for value in totals] + [bias_rows], axis=1
                ).astype(BF16)
                when(me * per_group + t != my_dp, lambda: qkv_copy(h, t).start())
        else:
            for kind in range(3):
                r.qkv_raw[h, kind] = totals[kind]

    early = 2 * (2 * heads + 2)
    shift = 2 * per_part - early

    def place_backward(i):
        part, m = (i + shift) // (2 * per_part), lax.rem(i + shift, 2 * per_part)
        is_far, tail = lax.rem(part, 2), part // 2
        start = (1 - is_far) * (1 - tail)
        j = lax.rem(i, early // 2)
        own = j // (2 * heads)
        n = lax.rem(m, per_part)
        d_q = (
            start * (i // (early // 2))
            + is_far * (seq - 1 - m // per_part)
            + tail * (lax.rem(m, 4) // 2)
        )
        h = start * (1 - own) * (j // 2) + is_far * (n // seq) + tail * (1 + m // 4)
        d_k = (
            start * ((1 - own) * (2 + lax.rem(j, 2)) + own * (j - 2 * heads))
            + is_far * lax.rem(m, seq)
            + tail * lax.rem(m, 2)
        )
        return me ^ d_q, h, me ^ d_k

    def receive(d):
        g_copy(d).wait_recv()
        prepare(me ^ d)

    def far_states_grads():
        for d in range(1, seq):
            g_copy(d).wait_send()
        for d in far:
            for h in range(heads):
                fill(me ^ d, h)
            states_part(me ^ d)
            dx_copy(d).start()

    far_done = after(early + 2 * per_part - 1)
    hooks = [
        (before(early // 2), lambda: receive(1)),
        (before(early), lambda: receive(far[0])),
        (before(early + per_part), lambda: receive(far[1])),
        (far_done, far_states_grads),
        (far_done, lambda: emit(0)),
    ]
    if split:
        hooks += [
            (1, reduce_side),
            (3, lambda: reduce_cross(0)),
            (3, reduce_vec),
            (4, lambda: reduce_cross(1)),
            (5, lambda: reduce_cross(2)),
            (7, lambda: reduce_cross(3)),
            (10, reduce_z),
        ]
    d_in[me] = c_grad[at(me, group)]
    prepare(me)
    run(
        4 * per_part,
        place_backward,
        weigh,
        gather_grads,
        (p0, s0),
        (p1, s1),
        hooks,
        lambda: emit(1),
        unroll,
    )
    emit(2)
    states_part(me ^ 1)
    dx_copy(1).start()
    states_part(me)
    dx_r[at(me, group)] = dx_s[at(me, group)]
    if split:
        reduce_x()

        @pl.when(owner)
        def _():
            for h in range(heads):
                value = qkv_s[h, my_slot].astype(F32)
                for e in range(1, n_dp):
                    src = lax.rem(my_dp + e, n_dp)
                    remote(
                        qkv_s.at[h, 0],
                        qkv_r.at[h, src],
                        r.q1_send.at[h, 0],
                        r.q1_recv.at[h, src],
                        dp=src,
                    ).wait_recv()
                    value += qkv_r[h, src].astype(F32)
                qkv_out[h] = value.astype(BF16)
                for d in range(1, seq):
                    qkv_share(h, d).start()

    for d in range(1, seq):
        dx_copy(d).wait_recv()
    for c in range(width // LANES):
        span = slice(c * LANES, (c + 1) * LANES)
        r.states_grad[:, span] = (dx_r[span].astype(F32) + grad_mid[span]).astype(BF16).T


    for d in range(1, seq):
        x_copy(d).wait_send()
        c_copy(d).wait_send()
        dx_copy(d).wait_send()
    if split:
        last_copy().wait()
        for h in range(heads):
            for t in range(per_group):
                when(me * per_group + t != my_dp, lambda: qkv_copy(h, t).wait_send())

        @pl.when(owner)
        def _():
            for h in range(heads):
                for d in range(1, seq):
                    qkv_share(h, d).wait_send()

        @pl.when(jnp.logical_not(owner))
        def _():
            for h in range(heads):
                qkv_share(h, 1).wait_recv()

        for e in range(1, n_dp):
            s_copy(e).wait_send()

        for g in range(2):

            @pl.when(holds(g))
            def _():
                for j in range(n_z - 1):
                    w_along(g, j).wait_send()

            w_across(g).wait_send()

            @pl.when(core != g)
            def _():
                when(jnp.logical_not(holds(g)), lambda: w_beside(g, 0, core).wait_send())
                w_beside(g, 1, core).wait_send()

        for copy in side_copies() + x_copies():
            copy.wait_send()
        vec_cross().wait_send()
        for j in range(n_z):
            cross_copy(j).wait_send()
        for j in range(n_z - 1):
            z_copy(j).wait_send()
            vz_copy(j).wait_send()


def layer(cfg, row, collective_id, inputs):
    c = cfg
    g, l, h, s, w, f = c.group, c.piece, c.heads, c.seq, c.width, c.hidden
    n_z = c.dp // 2
    sds = jax.ShapeDtypeStruct
    dma = pltpu.SemaphoreType.DMA
    vm = pltpu.VMEM
    outputs = dict(layer_out=sds((l, w), BF16), states_grad=sds((l, w), BF16))
    if c.split:
        outputs |= dict(
            od_out=sds((2, 3, c.half, w), F32),
            qkv_out=sds((h, c.shard, 4 * HDIM), BF16),
            vec_out=sds((16, w), F32),
        )
    else:
        outputs |= dict(
            g_all=sds((3, w, w), BF16),
            qkv_raw=sds((h, 3, g + AUG, HDIM), F32),
            vecs=sds((16, w), F32),
        )
    scratch = dict(
        x_own=vm((w, l), BF16),
        x_group=vm((s, g + AUG, l), BF16),
        w_group=vm((3, g, g), BF16),
        w_pad=vm((3, g + AUG, h * LANES), BF16),
        q_t=vm((h, s, LANES, l), BF16),
        k_n=vm((h, s, l, LANES), BF16),
        k_t=vm((h, s, HDIM, l), BF16),
        v_n=vm((h, s, l, LANES), BF16),
        context_s=vm((s, g, l), BF16),
        context_r=vm((w, l), BF16),
        tops=vm((h * s, 1, l), F32),
        gathered=vm((h * s * (HDIM + AUG), l), F32),
        cols=vm((w, 16), F32),
        vcols=vm((w, LANES), F32),
        wide=vm((4 * w, l), F32),
        slim=vm((2 * f, l), BF16),
        c_grad=vm((w, l), BF16),
        d_in=vm((s, g, l), BF16),
        dx_r=vm((w, l), BF16),
        low=vm((GROUPS * (g + AUG) + w, l), BF16),
        late_sem=dma((2,)),
        x_send=dma((s,)),
        x_recv=dma((s,)),
        c_send=dma((s,)),
        c_recv=dma((s,)),
        g_send=dma((s,)),
        g_recv=dma((s,)),
        dx_send=dma((s,)),
        dx_recv=dma((s,)),
    )
    if c.split:
        unit = (3, c.half, w)
        vec = (16, w)
        scratch |= dict(
            wo=vm((w, w), BF16),
            w_up=vm((w, w), BF16),
            wd=vm((w, f // GROUPS), BF16),
            smalls=vm((c.dp, 16, LANES), F32),
            pack=vm((c.dp, 2) + unit, BF16),
            w_in=vm((2, c.per_group, 2, c.half, 3 * g), BF16),
            vecs=vm(vec, F32),
            side=vm((c.dp,) + unit, BF16),
            cross=vm((n_z,) + unit, BF16),
            spread_z=vm((n_z,) + unit, BF16),
            spread_v=vm((n_z,) + vec, F32),
            x_mine=vm(unit, BF16),
            x_theirs=vm(unit, BF16),
            vec_side=vm(vec, F32),
            vec_mine=vm(vec, F32),
            vec_cross=vm(vec, F32),
            vec_sum=vm(vec, F32),
            vec_z=vm(vec, F32),
            vec_x=vm(vec, F32),
            qkv_s=vm((h, c.per_group, c.shard, 4 * HDIM), BF16),
            qkv_r=vm((h, c.dp, c.shard, 4 * HDIM), BF16),
            s_send=dma((c.dp,)),
            s_recv=dma((c.dp,)),
            w_send=dma((2, n_z + 1)),
            w_recv=dma((2, 2)),
            wb_send=dma((2,)),
            wb_recv=dma((2,)),
            hop_send=dma((3, c.dp)),
            hop_recv=dma((c.dp,)),
            sib_send=dma((c.dp,)),
            sib_recv=dma((c.dp,)),
            red_send=dma((7,)),
            red_recv=dma((7,)),
            cross_send=dma((n_z,)),
            cross_recv=dma((n_z,)),
            z_send=dma((n_z,)),
            z_recv=dma((n_z,)),
            vz_send=dma((n_z,)),
            vz_recv=dma((n_z,)),
            q1_send=dma((h, c.per_group)),
            q1_recv=dma((h, c.dp)),
            q2_send=dma((h, s)),
            q2_recv=dma((h,)),
        )
    names = tuple(inputs) + tuple(outputs) + tuple(scratch)
    vmem = pl.BlockSpec(memory_space=pltpu.VMEM)
    hbm = pl.BlockSpec(memory_space=pl.ANY)
    special = dict(teacher=hbm, out_grad=hbm, lengths=pl.BlockSpec(memory_space=pltpu.SMEM))
    results = pl.pallas_call(
        functools.partial(layer_kernel, cfg, row, names),
        out_shape=list(outputs.values()),
        in_specs=[special.get(name, vmem) for name in inputs],
        out_specs=[vmem] * len(outputs),
        scratch_shapes=list(scratch.values()),
        compiler_params=pltpu.CompilerParams(
            collective_id=collective_id, has_side_effects=True, vmem_limit_bytes=VMEM_LIMIT
        ),
        name="layer",
    )(*inputs.values())
    return dict(zip(outputs, results, strict=True))


def deliver_kernel(cfg, layer_in, states_in, qkv, od, vec, *refs):
    outs = refs
    my_dp = lax.axis_index("dp")
    shard, width, half = cfg.shard, cfg.width, cfg.half
    outs[0][...] = layer_in[...]
    outs[1][...] = states_in[...]
    qw, kw, vw, ow, uw, dw = outs[2:8]
    parts = [
        jnp.concatenate(
            [qkv[h, :, k * HDIM : (k + 1) * HDIM].astype(F32) for h in range(cfg.heads)], axis=1
        )
        for k in range(4)
    ]
    for ref, part in zip((qw, kw, vw), parts[:3], strict=True):
        ref[...] = part
    for c in range(2):
        rows = slice(c * half, (c + 1) * half)
        ow[rows] = od[c, 0]
        uw[rows] = od[c, 1]
        for k in range(2):
            dw[(2 * c + k) * half : (2 * c + k + 1) * half] = od[
                c, 2, :, k * 4 * shard : (k + 1) * 4 * shard
            ]
    slot = lax.rem(my_dp, cfg.per_group)
    mine = parts[3][0:8, 0:shard]
    for t in range(1, cfg.per_group):
        mine = jnp.where(slot == t, parts[3][0:8, t * shard : (t + 1) * shard], mine)
    outs[8][...] = mine[0]
    outs[9][...] = mine[2]
    turned = pltpu.roll(vec[0:8], lax.rem(width - my_dp * shard, width), 1)
    for n in range(6):
        outs[10 + n][...] = turned[n, 0:shard]
    outs[16][...] = vec[
        pl.ds(8 + my_dp // cfg.per_group, 1),
        pl.ds(pl.multiple_of(slot * 4 * shard, LANES), 4 * shard),
    ][0]
    outs[17][0] = vec[12, 0]


def deliver(cfg, *args):
    sds = jax.ShapeDtypeStruct
    shard, width, group = cfg.shard, cfg.width, cfg.group
    out_shape = [sds(a.shape, a.dtype) for a in args[:2]]
    out_shape += [sds((shard, group), F32)] * 3 + [sds((shard, width), F32)] * 2
    out_shape += [sds((group, 4 * shard), F32)] + [sds((shard,), F32)] * 8
    out_shape += [sds((4 * shard,), F32), sds((1,), F32)]
    vmem = pl.BlockSpec(memory_space=pltpu.VMEM)
    return pl.pallas_call(
        functools.partial(deliver_kernel, cfg),
        out_shape=out_shape,
        in_specs=[vmem] * len(args),
        out_specs=[vmem] * (len(out_shape) - 1) + [pl.BlockSpec(memory_space=pltpu.SMEM)],
        name="deliver",
    )(*args)


def local(
    states,
    lengths,
    teacher,
    out_grad,
    q_weight,
    k_weight,
    v_weight,
    q_bias,
    v_bias,
    o_weight,
    o_bias,
    attn_gain,
    attn_bias,
    up_weight,
    up_bias,
    down_weight,
    down_bias,
    ffn_gain,
    ffn_bias,
):
    row_count, piece, width = states.shape
    n_dp, n_seq = lax.axis_size("dp"), lax.axis_size("seq")
    me, my_dp = lax.axis_index("seq"), lax.axis_index("dp")
    shard = q_bias.shape[0]
    hidden = up_bias.shape[0] * n_dp
    cfg = Config(n_dp, n_seq, piece, width, hidden, shard)
    cfg.rows = row_count
    group = cfg.group

    if not cfg.split:

        def pad(v):
            return jnp.pad(v.astype(F32), ((0, 0), (0, LANES - v.shape[1])))

        vectors = (q_bias, v_bias, o_bias, attn_gain, attn_bias, down_bias, ffn_gain, ffn_bias)
        small = jnp.concatenate(
            [
                pad(jnp.stack(vectors)),
                pad(up_bias.reshape(4, shard)),
                jnp.broadcast_to(lengths.astype(F32)[:, None], (row_count, LANES)),
                jnp.zeros((4 - row_count, LANES), F32),
            ]
        )
        smalls = lax.all_gather(small, "dp", axis=0)
        qkv = jnp.stack((q_weight, k_weight, v_weight))
        qkv = lax.all_gather(qkv, "dp", axis=1, tiled=True)
        w_group_in = lax.dynamic_slice(qkv, (0, me * group, 0), (3, group, group))
        wo = lax.all_gather(o_weight, "dp", axis=0, tiled=True)
        wu = lax.all_gather(up_weight, "dp", axis=0, tiled=True)
        wd = lax.all_gather(down_weight, "dp", axis=0, tiled=True)
        wd = wd.reshape(GROUPS, -1, group).transpose(0, 2, 1).reshape(width, -1)

    results = []
    for n in range(row_count):
        inputs = dict(states=states[n], teacher=teacher[n], out_grad=out_grad[n])
        if cfg.split:
            inputs |= dict(
                wq=q_weight,
                wk=k_weight,
                wv=v_weight,
                ow=o_weight,
                uw=up_weight,
                dw=down_weight.T,
                qb=q_bias,
                vb=v_bias,
                ob=o_bias,
                ag=attn_gain,
                ab=attn_bias,
                db=down_bias,
                fg=ffn_gain,
                fb=ffn_bias,
                ub=up_bias,
                lengths=lengths,
            )
        else:
            inputs |= dict(smalls=smalls, w_all=w_group_in, wo=wo, w_up=wu, wd=wd)
        results.append(layer(cfg, n, n, inputs))

    def summed(name):
        first = results[0][name]
        if row_count == 1:
            return first
        return sum((item[name].astype(F32) for item in results[1:]), first.astype(F32))

    if cfg.split:
        heavy = [jnp.stack([item[n] for item in results]) for n in ("layer_out", "states_grad")]
        out = deliver(cfg, *heavy, summed("qkv_out"), summed("od_out"), summed("vec_out"))
        grad_qw, grad_kw, grad_vw, grad_ow, grad_uw, grad_dw = out[2:8]
        vectors = out[8:17]
        return (
            (out[0], out[17].reshape(()), out[1], grad_qw, grad_kw, grad_vw)
            + (vectors[0], vectors[1], grad_ow, *vectors[2:5], grad_uw, vectors[8])
            + (grad_dw.T, *vectors[5:8])
        )

    layer_out = jnp.stack([item["layer_out"] for item in results])
    states_grad = jnp.stack([item["states_grad"] for item in results])
    qkv_g, g_all, vecs = (summed(n).astype(F32) for n in ("qkv_raw", "g_all", "vecs"))
    qkv_g = qkv_g.transpose(1, 2, 0, 3).reshape(3, group + AUG, group)
    whole = jnp.zeros((3, width + GROUPS * AUG, group), F32)
    whole = lax.dynamic_update_slice(whole, qkv_g[:, :group], (0, me * group, 0))
    whole = lax.dynamic_update_slice(whole, qkv_g[:, group:], (0, width + me * AUG, 0))
    whole, g_all, vec = lax.psum((whole, g_all, vecs), ("dp", "seq"))
    qkv = lax.dynamic_slice(whole, (0, my_dp * shard, 0), (3, shard, group))
    biases = whole[:, width::AUG].reshape(3, width)
    grad_qb = lax.dynamic_slice(biases[0], (my_dp * shard,), (shard,))
    grad_vb = lax.dynamic_slice(biases[2], (my_dp * shard,), (shard,))
    g_ou = lax.dynamic_slice(g_all[:2], (0, my_dp * shard, 0), (2, shard, width))
    g_d = g_all[2].reshape(GROUPS, group, -1).transpose(0, 2, 1).reshape(-1, group)
    grad_dw = lax.dynamic_slice(g_d, (my_dp * 4 * shard, 0), (4 * shard, group))
    mine = lax.dynamic_slice(vec[:6], (0, my_dp * shard), (6, shard))
    grad_ub = lax.dynamic_slice(vec[8:12].reshape(-1), (my_dp * 4 * shard,), (4 * shard,))
    return (
        (layer_out, vec[12, 0], states_grad, qkv[0], qkv[1], qkv[2], grad_qb, grad_vb, g_ou[0])
        + (mine[0], mine[1], mine[2], g_ou[1], grad_ub, grad_dw, mine[3], mine[4], mine[5])
    )


def solution(mesh):
    rows3 = P("dp", "seq", None)
    matrix = P("dp", None)
    vector = P("dp")
    return jax.shard_map(
        local,
        mesh=mesh,
        in_specs=(rows3, vector, rows3, rows3)
        + (matrix,) * 3
        + (vector,) * 2
        + (matrix,)
        + (vector,) * 3
        + (matrix, vector, matrix)
        + (vector,) * 3,
        out_specs=(rows3, P(), rows3)
        + (matrix,) * 3
        + (vector,) * 2
        + (matrix,)
        + (vector,) * 3
        + (matrix, vector, matrix)
        + (vector,) * 3,
        check_vma=False,
    )
```

```python
import functools
import math
import types

import jax
import jax.numpy as jnp
from jax import lax
from jax.experimental import pallas as pl
from jax.experimental.pallas import tpu as pltpu
from jax.sharding import PartitionSpec as P

HDIM = 64
GROUPS = 4
EPSILON = 1e-12
NEG_FILL = -1e30
LANES = 128
AUG = 16
LOG2E = 1.4426950408889634
MESH = pl.DeviceIdType.MESH
F32 = jnp.float32
BF16 = jnp.bfloat16
VMEM_LIMIT = 60 * 1024 * 1024


def mm(left, right, left_dim, right_dim):
    return lax.dot_general(
        left, right, (((left_dim,), (right_dim,)), ((), ())), preferred_element_type=F32
    )


def iota(shape, dim):
    return lax.broadcasted_iota(jnp.int32, shape, dim)


def remote(src, dst, send_sem, recv_sem, **where):
    return pltpu.make_async_remote_copy(
        src_ref=src,
        dst_ref=dst,
        send_sem=send_sem,
        recv_sem=recv_sem,
        device_id=where,
        device_id_type=MESH,
    )


def three_parts(row):
    high = row.astype(BF16)
    rest = row - high.astype(F32)
    middle = rest.astype(BF16)
    low = (rest - middle.astype(F32)).astype(BF16)
    return high, middle, low


class Config:
    def __init__(self, dp, seq, piece, width, hidden, shard):
        self.dp, self.seq, self.piece, self.width, self.hidden, self.shard = (
            dp,
            seq,
            piece,
            width,
            hidden,
            shard,
        )
        self.slots = piece * seq
        self.group = width // GROUPS
        self.heads = self.group // HDIM
        self.per_group = dp // GROUPS
        self.split = shard % 32 == 0 and seq == 4 and dp == 8
        self.half = shard // 2
        self.quarter = hidden // dp // 4


def greet(cfg, me, my_dp):
    barrier = pltpu.get_barrier_semaphore()
    count = cfg.seq - 1
    for d in range(1, cfg.seq):
        pl.semaphore_signal(barrier, inc=1, device_id={"seq": me ^ d}, device_id_type=MESH)
    if cfg.split:
        count += cfg.dp - 1
        for e in range(1, cfg.dp):
            pl.semaphore_signal(
                barrier, inc=1, device_id={"dp": lax.rem(my_dp + e, cfg.dp)}, device_id_type=MESH
            )
    return lambda: pl.semaphore_wait(barrier, count)


def layer_kernel(cfg, row, names, *refs):
    r = types.SimpleNamespace(**dict(zip(names, refs, strict=True)))
    split = cfg.split
    me = lax.axis_index("seq")
    my_dp = lax.axis_index("dp")
    piece, width, group, heads, seq = cfg.piece, cfg.width, cfg.group, cfg.heads, cfg.seq
    shard, half, n_dp, per_group = cfg.shard, cfg.half, cfg.dp, cfg.per_group
    hid = cfg.hidden // GROUPS
    n_z = n_dp // 2
    core = lax.rem(me, 2)
    my_z, my_y = my_dp // 2, lax.rem(my_dp, 2)
    far = [d for d in range(seq - 1, 1, -1)]

    states = r.states
    teacher, out_grad = r.states_grad, r.layer_out
    late = [
        pltpu.make_async_copy(r.teacher, teacher, r.late_sem.at[0]),
        pltpu.make_async_copy(r.out_grad, out_grad, r.late_sem.at[1]),
    ]
    x_own, x_group, w_group, w_pad, smalls = (
        r.x_own,
        r.x_group,
        r.w_group,
        r.w_pad,
        r.smalls,
    )
    q_t, k_n, k_t, v_n = r.q_t, r.k_n, r.k_t, r.v_n
    context_s, context_r = r.context_s, r.context_r
    cols, vcols = r.cols, r.vcols
    wide, slim = r.wide, r.slim
    wo, w_up, wd = r.wo, r.w_up, r.wd
    c_grad, d_in, dx_r = r.c_grad, r.d_in, r.dx_r
    dx_s = c_grad
    tall1 = group + AUG
    low = r.low
    low2 = low.at[GROUPS * tall1 :]

    def low1(g, start, size):
        return pl.ds(pl.multiple_of(g * tall1 + start, AUG), size)

    def d_aug(h, t, start, size):
        return pl.ds(pl.multiple_of((h * seq + t) * LANES + start, HDIM), size)

    score0, score1 = wide.at[0:piece], wide.at[piece : 2 * piece]
    gathered = r.gathered
    v1, first, v2, seed = (wide.at[i * width : (i + 1) * width] for i in range(4))
    dq, dk, dv = (wide.at[i * width : (i + 1) * width] for i in range(3))
    act, slope = slim.at[0 : cfg.hidden], slim.at[cfg.hidden : 2 * cfg.hidden]
    p0, p1, s0, s1 = (slim.at[i * piece : (i + 1) * piece] for i in range(4))
    d_t = slope

    def at(i, n):
        return pl.ds(pl.multiple_of(i * n, n), n)

    def loop(count, body, *init):
        return lax.fori_loop(0, count, lambda i, c: body(i, *c), tuple(init))

    def sub(v):
        return jnp.sum(v, axis=0, keepdims=True)


    def to_seq(sems, src, dst, d):
        return remote(src, dst, sems[0].at[d], sems[1].at[d], seq=me ^ d)

    def x_copy(d):
        return to_seq((r.x_send, r.x_recv), x_own.at[at(me ^ d, group)], x_group.at[me, pl.ds(0, group)], d)

    def c_copy(d):
        return to_seq((r.c_send, r.c_recv), context_s.at[me ^ d], context_r.at[at(me, group)], d)

    def g_copy(d):
        return to_seq((r.g_send, r.g_recv), c_grad.at[at(me ^ d, group)], d_in.at[me], d)

    def dx_copy(d):
        return to_seq((r.dx_send, r.dx_recv), dx_s.at[at(me ^ d, group)], dx_r.at[at(me, group)], d)

    if split:
        pack = r.pack
        w_in = r.w_in
        my_slot = lax.rem(my_dp, per_group)

        def s_copy(e):
            return remote(
                smalls.at[my_dp],
                smalls.at[my_dp],
                r.s_send.at[e],
                r.s_recv.at[e],
                dp=lax.rem(my_dp + e, n_dp),
            )

        first_group = me - core

        def w_ref(g):
            return w_in.at[g, my_y, core]

        def w_along(g, j):
            z = lax.rem(my_z + n_z - 1 - j, n_z)
            return remote(
                w_ref(g), w_ref(g), r.w_send.at[g, j], r.w_recv.at[g, 0], dp=2 * z + my_y
            )

        def w_across(g):
            return remote(
                w_ref(g), w_ref(g), r.w_send.at[g, n_z], r.w_recv.at[g, 1], dp=my_dp + 1 - 2 * my_y
            )

        def w_over(g):
            ref = w_in.at[g, 1 - my_y, core]
            return remote(ref, ref, r.w_send.at[g, n_z], r.w_recv.at[g, 1], dp=my_dp)

        def w_beside(g, part, half_of):
            ref = w_in.at[g, my_y if part == 0 else 1 - my_y, half_of]
            return remote(ref, ref, r.wb_send.at[part], r.wb_recv.at[part], seq=me ^ 1)

        def holds(g):
            return my_z == first_group + g

        def hop(kind, i, **where):
            ref = pack.at[i, core]
            return remote(ref, ref, r.hop_send.at[kind, i], r.hop_recv.at[i], **where)

        def up(i):
            return hop(0, i, dp=my_dp + 2)

        def down(i):
            return hop(1, i, dp=my_dp - 2)

        def across(i):
            return hop(2, i, dp=my_dp + 1 - 2 * my_y)

        def beside(i):
            ref = pack.at[i, core]
            return remote(ref, ref, r.sib_send.at[i], r.sib_recv.at[i], seq=me ^ 1)

        def when(condition, fn):
            pl.when(condition)(fn)

        def gather_start():
            when(my_z < n_z - 1, lambda: up(my_dp).start())
            when(my_z > 0, lambda: down(my_dp).start())

        def gather_z(k):
            below, above = my_dp - 2 * k, my_dp + 2 * k

            @pl.when(my_z >= k)
            def _():
                hop(0, below, dp=my_dp).wait_recv()
                when(my_z < n_z - 1, lambda: up(below).start())
                across(below).start()
                beside(below).start()

            @pl.when(my_z + k < n_z)
            def _():
                hop(0, above, dp=my_dp).wait_recv()
                when(my_z > 0, lambda: down(above).start())
                across(above).start()
                beside(above).start()

        def gather_y(k):
            other = my_dp + 1 - 2 * my_y

            def take(i):
                hop(2, i, dp=my_dp).wait_recv()
                beside(i).start()

            if k == 0:
                take(other)
            else:
                when(my_z >= k, lambda: take(other - 2 * k))
                when(my_z + k < n_z, lambda: take(other + 2 * k))

        def gather_end():
            for e in range(1, n_dp):
                copy = beside(lax.rem(my_dp + e, n_dp))
                copy.wait()

            when(my_z < n_z - 1, lambda: up(my_dp).wait_send())
            when(my_z > 0, lambda: down(my_dp).wait_send())
            across(my_dp).wait_send()
            for k in range(1, n_z):
                below, above = my_dp - 2 * k, my_dp + 2 * k

                @pl.when(my_z >= k)
                def _():
                    when(my_z < n_z - 1, lambda: up(below).wait_send())
                    across(below).wait_send()

                @pl.when(my_z + k < n_z)
                def _():
                    when(my_z > 0, lambda: down(above).wait_send())
                    across(above).wait_send()


    wait_entry = greet(cfg, me, my_dp)
    for c in range(0, width, LANES):
        x_own[c : c + LANES] = states[:, c : c + LANES].T
    if split:
        for c in range(2):
            pack[my_dp, c, 0] = r.ow[c * half : (c + 1) * half]
            pack[my_dp, c, 1] = r.uw[c * half : (c + 1) * half]
            for k in range(2):
                pack[my_dp, c, 2, :, k * 4 * shard : (k + 1) * 4 * shard] = r.dw[
                    (2 * c + k) * half : (2 * c + k + 1) * half
                ]
        smalls[my_dp] = jnp.zeros((16, LANES), F32)
        for n, ref in enumerate((r.qb, r.vb, r.ob, r.ag, r.ab, r.db, r.fg, r.fb)):
            smalls[my_dp, n : n + 1, 0:shard] = ref[...].reshape(1, shard).astype(F32)
        up_bias = r.ub[...].reshape(1, 4 * shard).astype(F32)
        for n in range(4):
            smalls[my_dp, 8 + n : 9 + n, 0:shard] = up_bias[:, n * shard : (n + 1) * shard]
        for n in range(cfg.rows):
            smalls[my_dp, 12 + n : 13 + n] = jnp.full((1, LANES), r.lengths[n].astype(F32))

        for g in range(2):

            @pl.when(holds(g))
            def _():
                for c in range(2):
                    rows = slice(c * half, (c + 1) * half)
                    w_in[g, my_y, c] = jnp.concatenate(
                        [ref[rows].astype(F32) for ref in (r.wq, r.wk, r.wv)], axis=1
                    ).astype(BF16)

    wait_entry()
    if split:
        for e in range(1, n_dp):
            s_copy(e).start()

        for g in range(2):

            @pl.when(holds(g))
            def _():
                for j in range(n_z - 1):
                    w_along(g, j).start()
                w_across(g).start()

    for d in range(1, seq):
        x_copy(d).start()
    for copy in late:
        copy.start()
    x_group[me, 0:group] = x_own[at(me, group)]


    deep = HDIM + AUG
    tops = r.tops

    def sums(h, t):
        return pl.ds(pl.multiple_of((h * seq + t) * deep, AUG), deep)

    def clear_sums(i, unused):
        gathered[pl.ds(pl.multiple_of(i * deep, AUG), deep)] = jnp.zeros((deep, piece), F32)
        tops[i] = jnp.full((1, piece), NEG_FILL, F32)
        return (unused,)

    loop(heads * seq, clear_sums, 0)
    n_cols = heads * LANES
    if split:
        for n, g in enumerate((1 - core, core)):

            @pl.when(jnp.logical_not(holds(g)))
            def _():
                w_along(g, 0).wait_recv()
                w_across(g).start()
                if n == 0:
                    w_beside(g, 0, core).start()

        gather_start()
        for e in range(1, n_dp):
            s_copy(e).wait_recv()
    for i in range(n_dp):
        turned_small = smalls[i].T
        cols[i * shard : (i + 1) * shard] = turned_small[0:shard]
    vec_rows = jnp.zeros((AUG, n_cols), F32)
    lane = iota((LANES, n_cols), 1)
    source = iota((LANES, n_cols), 0)
    for t in range(per_group):
        spread = jnp.where(
            (((lane >> 7) * HDIM + (lane & 127)) == source + t * shard)
            & ((lane & 127) < HDIM)
            & (source < shard),
            1.0,
            0.0,
        ).astype(BF16)
        vec_rows += mm(smalls[me * per_group + t].astype(BF16), spread, 1, 0)
    row_id = iota((AUG, n_cols), 0)
    lane = iota((AUG, n_cols), 1) & 127
    zero = jnp.zeros((AUG, n_cols), F32)
    top_row = row_id == 0
    w_pad[0, group:] = jnp.where(top_row, vec_rows[0:1], zero).astype(BF16)
    ones_k = (top_row & (lane > HDIM) & (lane <= HDIM + 3)) | ((row_id == 1) & (lane == HDIM))
    w_pad[1, group:] = jnp.where(ones_k, 1.0, zero).astype(BF16)
    ones_v = (lane >= HDIM) & (lane < HDIM + 3)
    w_pad[2, group:] = jnp.where(top_row, jnp.where(ones_v, 1.0, vec_rows[1:2]), zero).astype(BF16)

    if split:
        for n, g in enumerate((1 - core, core)):
            w_over(g).wait_recv()
            if n == 0:
                w_beside(g, 1, core).start()
        across(my_dp).start()
        when(my_z != me, lambda: w_beside(core, 0, 1 - core).wait_recv())
        w_beside(core, 1, 1 - core).wait_recv()
        for t in range(per_group):
            for c in range(2):
                for kind in range(3):
                    w_group[kind, t * shard + c * half : t * shard + (c + 1) * half] = w_in[
                        core, t, c, :, kind * group : (kind + 1) * group
                    ]
    else:
        for kind in range(3):
            w_group[kind] = r.w_all[kind]
    lane = iota((group, n_cols), 1)
    spread = jnp.where(
        (((lane >> 7) * HDIM + (lane & 127)) == iota((group, n_cols), 0)) & ((lane & 127) < HDIM),
        1.0,
        0.0,
    ).astype(BF16)
    for kind in range(3):
        w_pad[kind, 0:group] = mm(w_group[kind], spread, 1, 0).astype(BF16)

    length = smalls[my_dp, 12 + row : 13 + row, 0:1]
    aug_row = iota((AUG, piece), 0)
    factor = LOG2E * HDIM**-0.5
    def v_t(h, t):
        return pl.ds(pl.multiple_of((h * seq + t) * deep, AUG), deep)

    def project(t):
        slot = (iota((AUG, piece), 1) + t * piece).astype(F32)
        mask = jnp.where(slot < length, 0.0, NEG_FILL)
        x_group[t, group:] = jnp.where(
            aug_row == 0, 1.0, jnp.where(aug_row == 1, mask, 0.0)
        ).astype(BF16)
        x = x_group[t]
        queries = mm(w_pad[0], x, 0, 0) * factor
        keys_t = mm(w_pad[1], x, 0, 0)
        values_t = mm(w_pad[2], x, 0, 0)
        keys_n = mm(x, w_pad[1], 0, 0)
        values_n = mm(x, w_pad[2], 0, 0)
        rest = jnp.where(iota((HDIM, piece), 0) == 0, 1.0, 0.0).astype(BF16)
        for h in range(heads):
            span = slice(h * LANES, h * LANES + HDIM)
            q_t[h, t, 0:HDIM] = queries[span].astype(BF16)
            q_t[h, t, HDIM:] = rest
            k_t[h, t] = keys_t[span].astype(BF16)
            slim[v_t(h, t)] = values_t[h * LANES : h * LANES + deep].astype(BF16)
            k_n[h, t] = keys_n[:, h * LANES : (h + 1) * LANES].astype(BF16)
            v_n[h, t] = values_n[:, h * LANES : (h + 1) * LANES].astype(BF16)


    per_part = seq * heads

    def run(count, place, first_part, last_part, a, b, hooks=(), rest=None, unroll=2):
        buffers = (a, b)
        first_part(a, *place(0))

        def several(u, unused):
            if hooks:
                due = u == hooks[0][0]
                for when_u, fn in hooks[1:]:
                    due = due | (u == when_u)

                @pl.when(due)
                def _():
                    for when_u, fn in hooks:
                        pl.when(u == when_u)(fn)

            for j in range(unroll):
                first_part(buffers[(j + 1) % 2], *place(unroll * u + j + 1))
                last_part(buffers[j % 2], *place(unroll * u + j))
            return (unused,)

        turns = (count - 1) // unroll
        loop(turns, several, 0)
        if rest is not None:
            rest()
        for i in range(turns * unroll, count - 1):
            first_part(buffers[(i + 1) % 2], *place(i + 1))
            last_part(buffers[i % 2], *place(i))
        last_part(buffers[(count - 1) % 2], *place(count - 1))

    unroll = 4

    def before(step):
        return (step - 1) // unroll

    def after(step):
        return step // unroll + 1

    def score(buffer, t, h, k):
        buffer[...] = mm(k_n[h, k], q_t[h, t], 1, 0)

    def absorb(buffer, t, h, k):
        i = h * seq + t
        old = tops[i]
        top = jnp.maximum(old, jnp.max(buffer[...], axis=0, keepdims=True))
        weights = jnp.exp2(buffer[...] - top).astype(BF16)
        tops[i] = top
        place = sums(h, t)
        gathered[place] = gathered[place] * jnp.exp2(old - top) + mm(slim[v_t(h, k)], weights, 1, 0)

    def settle(t):
        for h in range(heads):
            total = gathered[sums(h, t)]
            mass = total[HDIM : HDIM + 1]
            context_s[t, h * HDIM : (h + 1) * HDIM] = (total[0:HDIM] / mass).astype(BF16)
            parts = three_parts(-(tops[h * seq + t] + jnp.log2(mass)))
            value = jnp.where(aug_row == 0, 1.0, 0.0)
            for n, part in enumerate(parts):
                value = jnp.where(aug_row == n + 1, part.astype(F32), value)
            q_t[h, t, HDIM:deep] = value.astype(BF16)

    def place_forward(i):
        part, j = i // per_part, lax.rem(i, per_part)
        is_far, tail = lax.rem((part + 1) // 2, 2), part // 3
        d_q = is_far * (4 - part) + (1 - is_far) * (j // (2 * heads))
        h = is_far * (j // seq) + (1 - is_far) * (lax.rem(j, 2 * heads) // 2)
        d_k = is_far * lax.rem(j, seq) + (1 - is_far) * (lax.rem(j, 2) + 2 * tail)
        return me ^ d_q, h, me ^ d_k

    def far_states():
        for d in far:
            x_copy(d).wait_recv()
        loop(2, lambda i, unused: (project(me ^ (2 + i)), unused)[1:], 0)

    def far_context(d):
        settle(me ^ d)
        c_copy(d).start()

    hooks = [
        (before(per_part), far_states),
        (after(2 * per_part - 1), lambda: far_context(far[0])),
        (after(3 * per_part - 1), lambda: far_context(far[1])),
    ]
    if split:
        hooks += [
            (1, lambda: gather_z(1)),
            (3, lambda: gather_y(0)),
            (4, lambda: gather_z(2)),
            (6, lambda: gather_y(1)),
            (8, lambda: gather_z(3)),
            (9, lambda: gather_y(2)),
        ]
    project(me)
    x_copy(1).wait_recv()
    project(me ^ 1)
    run(4 * per_part, place_forward, score, absorb, score0, score1, hooks, unroll=unroll)
    settle(me ^ 1)
    c_copy(1).start()
    settle(me)
    context_r[at(me, group)] = context_s[me]
    if split:
        gather_y(3)
        gather_end()

        def unpack(i, unused):
            for c in range(2):
                wo[pl.ds(pl.multiple_of(i * shard + c * half, AUG), half)] = pack[i, c, 0]
                w_up[pl.ds(pl.multiple_of(i * shard + c * half, AUG), half)] = pack[i, c, 1]
                for k in range(2):
                    wd[
                        pl.ds(
                            pl.multiple_of(i // per_group * group + (2 * c + k) * half, AUG), half
                        ),
                        pl.ds(
                            pl.multiple_of(lax.rem(i, per_group) * 4 * shard, LANES), 4 * shard
                        ),
                    ] = pack[i, c, 2, :, k * 4 * shard : (k + 1) * 4 * shard]
            return (unused,)

        loop(n_dp, unpack, 0)


    vcols[...] = jnp.zeros_like(vcols)
    inv = 1.0 / width
    total = jnp.sum(smalls[:, 12:13, 0:1], axis=0)
    for n in range(1, cfg.rows):
        total += jnp.sum(smalls[:, 12 + n : 13 + n, 0:1], axis=0)
    slot = (iota((1, piece), 1) + me * piece).astype(F32)
    live = jnp.where(slot < length, 1.0, 0.0)
    coef = 2.0 / (total * width)
    zero_row = jnp.zeros((1, piece), F32)

    def col(i, n, which):
        return cols[at(i, n), which : which + 1]

    for d in range(1, seq):
        c_copy(d).wait_recv()

    step = 256

    def attn_out(i, acc):
        out = mm(wo[:, at(i, step)], context_r[...], 0, 0)
        v = out + x_own[at(i, step)].astype(F32) + col(i, step, 2)
        v1[at(i, step)] = v
        return (acc + sub(v),)

    (acc,) = loop(width // step, attn_out, zero_row)
    mean = acc * inv

    def center(ref):
        def body(g, acc):
            v = ref[at(g, group)] - mean
            ref[at(g, group)] = v
            return (acc + sub(v * v),)

        (acc,) = loop(GROUPS, body, zero_row)
        return lax.rsqrt(acc * inv + EPSILON)

    scale1 = center(v1)

    def norm1(g, unused):
        v = v1[at(g, group)] * scale1
        v1[at(g, group)] = v
        out = v * col(g, group, 3) + col(g, group, 4)
        first[at(g, group)] = out
        low[low1(g, 0, group)] = out.astype(BF16)
        low[low1(g, group, AUG)] = jnp.where(aug_row == 0, 1.0, 0.0).astype(BF16)
        return (unused,)

    loop(GROUPS, norm1, 0)

    def gelu(u):
        d = 1.0 + (0.3275911 * 0.7071067811865476) * jnp.abs(u)
        t = pltpu.reciprocal(d, approx=True)
        bell = jnp.exp2((u * u) * (-0.5 * LOG2E))
        poly = t * (
            0.127414796
            + t * (-0.142248368 + t * (0.7107068705 + t * (-0.7265760135 + t * 0.5307027145)))
        )
        tail = poly * bell
        phi = jnp.where(u >= 0.0, 1.0 - tail, tail)
        return u * phi, phi + u * bell * 0.3989422804014327

    bunch = max(1, LANES // math.gcd(LANES, 4 * shard) if (4 * shard) % LANES else 1)
    span4 = 4 * shard * bunch
    n_steps = n_dp // bunch
    steps_group = n_steps // GROUPS
    tall = span4 // 4

    raw0, raw1 = wide.at[2 * width : 2 * width + span4], wide.at[3 * width : 3 * width + span4]

    def expand(raw, i):
        g, c = i // steps_group, lax.rem(i, steps_group)
        raw[...] = mm(w_up[at(g, group), at(c, span4)], low[low1(g, 0, group)], 0, 0)

    def activate(raw, i):
        bias = jnp.concatenate(
            [cols[at(i * bunch + n, shard), 8 + b : 9 + b] for n in range(bunch) for b in range(4)],
            axis=0,
        )
        for b in range(4):
            part = slice(b * tall, (b + 1) * tall)
            out, grad = gelu(raw[part] + bias[part])
            place = pl.ds(pl.multiple_of((i * 4 + b) * tall, tall), tall)
            act[place] = out.astype(BF16)
            slope[place] = grad.astype(BF16)

    run(n_steps, lambda i: (i,), expand, activate, raw0, raw1)

    def clear_rows(count):
        for n in range(count):
            tops[n] = zero_row

    part0, part1 = seed.at[0:group], seed.at[group : 2 * group]

    def contract(raw, g):
        raw[...] = mm(wd[at(g, group)], act[at(g, hid)], 1, 0)

    def add_branch(raw, g):
        v = raw[...] + first[at(g, group)] + col(g, group, 5)
        v2[at(g, group)] = v
        tops[0] += sub(v)

    clear_rows(1)
    run(GROUPS, lambda g: (g,), contract, add_branch, part0, part1)
    acc = tops[0]
    mean = acc * inv
    scale2 = center(v2)

    for copy in late:
        copy.wait()
    loss, sum1, sum2 = zero_row, zero_row, zero_row
    for c in range(width // LANES):
        span = slice(c * LANES, (c + 1) * LANES)
        xhat = v2[span] * scale2
        v2[span] = xhat
        gain = cols[span, 6:7]
        full = xhat * gain + cols[span, 7:8]
        error = full - teacher[:, span].T.astype(F32)
        loss += sub(live * error * error)
        grad = live * (out_grad[:, span].T.astype(F32) + error * coef)
        r.layer_out[:, span] = full.astype(BF16).T
        vcols[span, 4:5] = jnp.sum(grad * xhat, axis=1, keepdims=True)
        vcols[span, 5:6] = jnp.sum(grad, axis=1, keepdims=True)
        grad = grad * gain
        seed[span] = grad
        sum1 += sub(grad)
        sum2 += sub(grad * xhat)
    sum1, sum2 = sum1 * inv, sum2 * inv

    def back2(g, unused):
        place = at(g, group)
        grad = scale2 * (seed[place] - sum1 - v2[place] * sum2)
        seed[place] = grad
        brief = grad.astype(BF16)
        low2[place] = brief
        vcols[place, 3:4] = jnp.sum(brief.astype(F32), axis=1, keepdims=True)
        return (unused,)

    loop(GROUPS, back2, 0)

    raw0, raw1 = v2.at[0:span4], v2.at[span4 : 2 * span4]

    def back_act(raw, i):
        g, c = i // steps_group, lax.rem(i, steps_group)
        raw[...] = mm(wd[at(g, group), at(c, span4)], low2[at(g, group)], 0, 0)

    def times_slope(raw, i):
        place = at(i, span4)
        slope[place] = (raw[...] * slope[place].astype(F32)).astype(BF16)

    run(n_steps, lambda i: (i,), back_act, times_slope, raw0, raw1)
    part0, part1 = v2.at[0:group], v2.at[group : 2 * group]

    def back_first(raw, g):
        raw[...] = mm(w_up[at(g, group)], slope[at(g, hid)], 1, 0)

    def add_first(raw, g):
        place = at(g, group)
        grad = seed[place] + raw[...]
        xhat = v1[place]
        vcols[place, 1:2] = jnp.sum(grad * xhat, axis=1, keepdims=True)
        vcols[place, 2:3] = jnp.sum(grad, axis=1, keepdims=True)
        grad = grad * col(g, group, 3)
        seed[place] = grad
        tops[0] += sub(grad)
        tops[1] += sub(grad * xhat)


    vecs = r.vecs
    if split:
        other_y = my_dp + 1 - 2 * my_y
        side, cross, spread_z, spread_v = r.side, r.cross, r.spread_z, r.spread_v
        od_out, vec_out = r.od_out, r.vec_out
        red_send, red_recv = r.red_send, r.red_recv

        def side_copies():
            return (
                remote(
                    pack.at[:, 1 - core, pl.ds(1, 2)],
                    side.at[:, pl.ds(1, 2)],
                    red_send.at[0],
                    red_recv.at[0],
                    seq=me ^ 1,
                ),
                remote(
                    pack.at[:, 1 - core, 0],
                    side.at[:, 0],
                    red_send.at[6],
                    red_recv.at[6],
                    seq=me ^ 1,
                ),
                remote(vecs, r.vec_side, red_send.at[1], red_recv.at[1], seq=me ^ 1),
            )

        def cross_copy(j):
            z = lax.rem(my_z + 1 + j, n_z)
            return remote(
                side.at[2 * z + 1 - my_y],
                cross.at[z],
                r.cross_send.at[z],
                r.cross_recv.at[z],
                dp=other_y,
            )

        def vec_cross():
            return remote(
                r.vec_mine, r.vec_cross, red_send.at[2], red_recv.at[2], dp=other_y
            )

        def z_copy(j):
            z = lax.rem(my_z + 1 + j, n_z)
            return remote(
                side.at[2 * z + my_y],
                spread_z.at[my_z],
                r.z_send.at[j],
                r.z_recv.at[j],
                dp=2 * z + my_y,
            )

        def vz_copy(j):
            z = lax.rem(my_z + 1 + j, n_z)
            return remote(
                r.vec_sum,
                spread_v.at[my_z],
                r.vz_send.at[j],
                r.vz_recv.at[j],
                dp=2 * z + my_y,
            )

        def x_copies():
            return (
                remote(
                    r.x_mine, r.x_theirs, red_send.at[3], red_recv.at[3], seq=me ^ 2
                ),
                remote(r.vec_z, r.vec_x, red_send.at[4], red_recv.at[4], seq=me ^ 2),
            )

        def last_copy():
            return remote(
                od_out.at[core], od_out.at[core], red_send.at[5], red_recv.at[5], seq=me ^ 1
            )

        def reduce_side():
            for copy in side_copies():
                copy.wait_recv()

            def add(i, unused):
                side[i] = (pack[i, core].astype(F32) + side[i].astype(F32)).astype(BF16)
                return (unused,)

            loop(n_dp, add, 0)
            r.vec_mine[...] = vecs[...] + r.vec_side[...]
            vec_cross().start()
            for j in range(n_z):
                cross_copy(j).start()

        def reduce_cross(j):
            cross_copy(j).wait_recv()
            z = lax.rem(my_z + 1 + j, n_z)
            i = 2 * z + my_y
            side[i] = (side[i].astype(F32) + cross[z].astype(F32)).astype(BF16)
            if j < n_z - 1:
                z_copy(j).start()

        def reduce_vec():
            vec_cross().wait_recv()
            value = r.vec_mine[...] + r.vec_cross[...]
            r.vec_sum[...] = value
            spread_v[my_z] = value
            for j in range(n_z - 1):
                vz_copy(j).start()

        def reduce_z():
            for j in range(n_z - 1):
                z_copy(j).wait_recv()
                vz_copy(j).wait_recv()
            spread_z[my_z] = side[my_dp]
            value = spread_z[0].astype(F32)
            vec = spread_v[0]
            for z in range(1, n_z):
                value += spread_z[z].astype(F32)
                vec += spread_v[z]
            r.x_mine[...] = value.astype(BF16)
            r.vec_z[...] = vec
            for copy in x_copies():
                copy.start()

        def reduce_x():
            for copy in x_copies():
                copy.wait_recv()
            od_out[core] = r.x_mine[...].astype(F32) + r.x_theirs[...].astype(F32)
            vec_out[...] = r.vec_z[...] + r.vec_x[...]
            last_copy().start()

    vecs[...] = jnp.zeros_like(vecs)
    for g in range(GROUPS):
        out = mm(low[low1(g, 0, tall1)], slope[g * hid : (g + 1) * hid], 1, 1)
        vecs[8 + g : 9 + g] = out[group : group + 1]
        if split:
            for t in range(per_group):
                for c in range(2):
                    base = shard * t + half * c
                    pack[g * per_group + t, c, 1] = out[base : base + half].astype(BF16)
        else:
            r.g_all[1, g * group : (g + 1) * group] = out[0:group].astype(BF16)
    clear_rows(2)
    run(GROUPS, lambda g: (g,), back_first, add_first, part0, part1)
    sum1, sum2 = tops[0] * inv, tops[1] * inv

    for g in range(GROUPS):
        out = mm(low2[g * group : (g + 1) * group], act[g * hid : (g + 1) * hid], 1, 1)
        if split:
            for t in range(per_group):
                for c in range(2):
                    for k in range(2):
                        pack[g * per_group + t, c, 2, :, k * 4 * shard : (k + 1) * 4 * shard] = (
                            out[
                                (2 * c + k) * half : (2 * c + k + 1) * half,
                                t * 4 * shard : (t + 1) * 4 * shard,
                            ].astype(BF16)
                        )
        else:
            r.g_all[2, g * group : (g + 1) * group] = out.astype(BF16)

    if split:
        side_copies()[0].start()

    def back1(g, unused):
        place = at(g, group)
        grad = scale1 * (seed[place] - sum1 - v1[place] * sum2)
        seed[place] = grad
        brief = grad.astype(BF16)
        low2[place] = brief
        vcols[place, 0:1] = jnp.sum(brief.astype(F32), axis=1, keepdims=True)
        return (unused,)

    loop(GROUPS, back1, 0)
    grad_mid = seed

    def back_context(i, unused):
        c_grad[at(i, step)] = mm(wo[at(i, step)], low2[...], 1, 0).astype(BF16)
        return (unused,)

    loop(width // step, back_context, 0)
    for d in [1] + far:
        g_copy(d).start()

    vecs[0:8] = vcols[...].T[0:8]
    mean_loss = jnp.sum(loss, axis=1, keepdims=True) / (total * width)
    vecs[12:13] = jnp.broadcast_to(mean_loss, (1, width))
    for j in range(2):
        rows = width // 2
        out = mm(context_r[j * rows : (j + 1) * rows], low2[...], 1, 1)
        if split:
            for t in range(n_dp // 2):
                for c in range(2):
                    base = shard * t + half * c
                    pack[j * (n_dp // 2) + t, c, 0] = out[base : base + half].astype(BF16)
        else:
            r.g_all[0, j * rows : (j + 1) * rows] = out.astype(BF16)

    if split:
        for copy in side_copies()[1:]:
            copy.start()


    def clear(i, unused):
        for ref in (dq, dk, dv):
            ref[at(i, HDIM)] = jnp.zeros((HDIM, piece), F32)
        return (unused,)

    loop(heads * seq, clear, 0)
    tail_row = iota((HDIM, piece), 0)

    def prepare(t):
        for h in range(heads):
            span = slice(h * HDIM, (h + 1) * HDIM)
            grad = d_in[t, span]
            low[d_aug(h, t, 0, HDIM)] = grad
            parts = three_parts(-sub(grad.astype(F32) * context_s[t, span].astype(F32)))
            value = jnp.zeros((HDIM, piece), F32)
            for n, part in enumerate(parts):
                value = jnp.where(tail_row == n, part.astype(F32), value)
            low[d_aug(h, t, HDIM, HDIM)] = value.astype(BF16)

    def rows_of(h, t):
        return at(h * seq + t, HDIM)

    def weigh(buffers, t, h, k):
        p, s = buffers
        weights = jnp.exp2(mm(q_t[h, t], k_n[h, k], 0, 1))
        p[...] = weights.astype(BF16)
        s[...] = (weights * mm(low[d_aug(h, t, 0, LANES)], v_n[h, k], 0, 1)).astype(BF16)

    def gather_grads(buffers, t, h, k):
        p, s = buffers
        dv[rows_of(h, k)] += mm(low[d_aug(h, t, 0, HDIM)], p[...], 1, 0)
        dk[rows_of(h, k)] += mm(q_t[h, t, 0:HDIM], s[...], 1, 0)
        dq[rows_of(h, t)] += mm(k_t[h, k], s[...], 1, 1)

    def turned(t, kind, h):
        return pl.ds(pl.multiple_of((t * 3 + kind) * group + h * HDIM, HDIM), HDIM)

    def fill(t, h):
        for kind, (ref, scale) in enumerate(((dq, HDIM**-0.5), (dk, 1.0 / LOG2E), (dv, 1.0))):
            d_t[turned(t, kind, h)] = (ref[rows_of(h, t)] * scale).astype(BF16)

    def whole(t, kind):
        return pl.ds(pl.multiple_of((t * 3 + kind) * group, HDIM), group)

    def states_part(t):
        out = mm(w_group[0], d_t[whole(t, 0)], 1, 0)
        out += mm(w_group[1], d_t[whole(t, 1)], 1, 0)
        out += mm(w_group[2], d_t[whole(t, 2)], 1, 0)
        dx_s[at(t, group)] = out.astype(BF16)

    if split:
        qkv_s, qkv_r, qkv_out = r.qkv_s, r.qkv_r, r.qkv_out
        owner = my_dp // per_group == me

        def qkv_copy(h, t):
            return remote(
                qkv_s.at[h, t],
                qkv_r.at[h, my_dp],
                r.q1_send.at[h, t],
                r.q1_recv.at[h, my_dp],
                dp=me * per_group + t,
            )

        def qkv_share(h, d):
            return remote(
                qkv_out.at[h], qkv_out.at[h], r.q2_send.at[h, d], r.q2_recv.at[h], seq=me ^ d
            )

    def emit(h):
        for d in range(2):
            fill(me ^ d, h)
        totals = []
        for kind in range(3):
            value = mm(x_group[0], d_t[turned(0, kind, h)], 1, 1)
            for t in range(1, seq):
                value += mm(x_group[t], d_t[turned(t, kind, h)], 1, 1)
            totals.append(value)
        if split:
            bias_rows = jnp.zeros((shard, HDIM), F32)
            bias_id = iota((shard, HDIM), 0)
            for kind in range(3):
                bias_rows = jnp.where(bias_id == kind, totals[kind][group : group + 1], bias_rows)
            for t in range(per_group):
                qkv_s[h, t] = jnp.concatenate(
                    [value[t * shard : (t + 1) * shard] for value in totals] + [bias_rows], axis=1
                ).astype(BF16)
                when(me * per_group + t != my_dp, lambda: qkv_copy(h, t).start())
        else:
            for kind in range(3):
                r.qkv_raw[h, kind] = totals[kind]

    early = 2 * (2 * heads + 2)
    shift = 2 * per_part - early

    def place_backward(i):
        part, m = (i + shift) // (2 * per_part), lax.rem(i + shift, 2 * per_part)
        is_far, tail = lax.rem(part, 2), part // 2
        start = (1 - is_far) * (1 - tail)
        j = lax.rem(i, early // 2)
        own = j // (2 * heads)
        n = lax.rem(m, per_part)
        d_q = (
            start * (i // (early // 2))
            + is_far * (seq - 1 - m // per_part)
            + tail * (lax.rem(m, 4) // 2)
        )
        h = start * (1 - own) * (j // 2) + is_far * (n // seq) + tail * (1 + m // 4)
        d_k = (
            start * ((1 - own) * (2 + lax.rem(j, 2)) + own * (j - 2 * heads))
            + is_far * lax.rem(m, seq)
            + tail * lax.rem(m, 2)
        )
        return me ^ d_q, h, me ^ d_k

    def receive(d):
        g_copy(d).wait_recv()
        prepare(me ^ d)

    def far_states_grads():
        for d in range(1, seq):
            g_copy(d).wait_send()
        for d in far:
            for h in range(heads):
                fill(me ^ d, h)
            states_part(me ^ d)
            dx_copy(d).start()

    far_done = after(early + 2 * per_part - 1)
    hooks = [
        (before(early // 2), lambda: receive(1)),
        (before(early), lambda: receive(far[0])),
        (before(early + per_part), lambda: receive(far[1])),
        (far_done, far_states_grads),
        (far_done, lambda: emit(0)),
    ]
    if split:
        hooks += [
            (1, reduce_side),
            (3, lambda: reduce_cross(0)),
            (3, reduce_vec),
            (4, lambda: reduce_cross(1)),
            (5, lambda: reduce_cross(2)),
            (7, lambda: reduce_cross(3)),
            (10, reduce_z),
        ]
    d_in[me] = c_grad[at(me, group)]
    prepare(me)
    run(
        4 * per_part,
        place_backward,
        weigh,
        gather_grads,
        (p0, s0),
        (p1, s1),
        hooks,
        lambda: emit(1),
        unroll,
    )
    emit(2)
    states_part(me ^ 1)
    dx_copy(1).start()
    states_part(me)
    dx_r[at(me, group)] = dx_s[at(me, group)]
    if split:
        reduce_x()

        @pl.when(owner)
        def _():
            for h in range(heads):
                value = qkv_s[h, my_slot].astype(F32)
                for e in range(1, n_dp):
                    src = lax.rem(my_dp + e, n_dp)
                    remote(
                        qkv_s.at[h, 0],
                        qkv_r.at[h, src],
                        r.q1_send.at[h, 0],
                        r.q1_recv.at[h, src],
                        dp=src,
                    ).wait_recv()
                    value += qkv_r[h, src].astype(F32)
                qkv_out[h] = value.astype(BF16)
                for d in range(1, seq):
                    qkv_share(h, d).start()

    for d in range(1, seq):
        dx_copy(d).wait_recv()
    for c in range(width // LANES):
        span = slice(c * LANES, (c + 1) * LANES)
        r.states_grad[:, span] = (dx_r[span].astype(F32) + grad_mid[span]).astype(BF16).T


    for d in range(1, seq):
        x_copy(d).wait_send()
        c_copy(d).wait_send()
        dx_copy(d).wait_send()
    if split:
        last_copy().wait()
        for h in range(heads):
            for t in range(per_group):
                when(me * per_group + t != my_dp, lambda: qkv_copy(h, t).wait_send())

        @pl.when(owner)
        def _():
            for h in range(heads):
                for d in range(1, seq):
                    qkv_share(h, d).wait_send()

        @pl.when(jnp.logical_not(owner))
        def _():
            for h in range(heads):
                qkv_share(h, 1).wait_recv()

        for e in range(1, n_dp):
            s_copy(e).wait_send()

        for g in range(2):

            @pl.when(holds(g))
            def _():
                for j in range(n_z - 1):
                    w_along(g, j).wait_send()

            w_across(g).wait_send()

            @pl.when(core != g)
            def _():
                when(jnp.logical_not(holds(g)), lambda: w_beside(g, 0, core).wait_send())
                w_beside(g, 1, core).wait_send()

        for copy in side_copies() + x_copies():
            copy.wait_send()
        vec_cross().wait_send()
        for j in range(n_z):
            cross_copy(j).wait_send()
        for j in range(n_z - 1):
            z_copy(j).wait_send()
            vz_copy(j).wait_send()


def layer(cfg, row, collective_id, inputs):
    c = cfg
    g, l, h, s, w, f = c.group, c.piece, c.heads, c.seq, c.width, c.hidden
    n_z = c.dp // 2
    sds = jax.ShapeDtypeStruct
    dma = pltpu.SemaphoreType.DMA
    vm = pltpu.VMEM
    outputs = dict(layer_out=sds((l, w), BF16), states_grad=sds((l, w), BF16))
    if c.split:
        outputs |= dict(
            od_out=sds((2, 3, c.half, w), F32),
            qkv_out=sds((h, c.shard, 4 * HDIM), BF16),
            vec_out=sds((16, w), F32),
        )
    else:
        outputs |= dict(
            g_all=sds((3, w, w), BF16),
            qkv_raw=sds((h, 3, g + AUG, HDIM), F32),
            vecs=sds((16, w), F32),
        )
    scratch = dict(
        x_own=vm((w, l), BF16),
        x_group=vm((s, g + AUG, l), BF16),
        w_group=vm((3, g, g), BF16),
        w_pad=vm((3, g + AUG, h * LANES), BF16),
        q_t=vm((h, s, LANES, l), BF16),
        k_n=vm((h, s, l, LANES), BF16),
        k_t=vm((h, s, HDIM, l), BF16),
        v_n=vm((h, s, l, LANES), BF16),
        context_s=vm((s, g, l), BF16),
        context_r=vm((w, l), BF16),
        tops=vm((h * s, 1, l), F32),
        gathered=vm((h * s * (HDIM + AUG), l), F32),
        cols=vm((w, 16), F32),
        vcols=vm((w, LANES), F32),
        wide=vm((4 * w, l), F32),
        slim=vm((2 * f, l), BF16),
        c_grad=vm((w, l), BF16),
        d_in=vm((s, g, l), BF16),
        dx_r=vm((w, l), BF16),
        low=vm((GROUPS * (g + AUG) + w, l), BF16),
        late_sem=dma((2,)),
        x_send=dma((s,)),
        x_recv=dma((s,)),
        c_send=dma((s,)),
        c_recv=dma((s,)),
        g_send=dma((s,)),
        g_recv=dma((s,)),
        dx_send=dma((s,)),
        dx_recv=dma((s,)),
    )
    if c.split:
        unit = (3, c.half, w)
        vec = (16, w)
        scratch |= dict(
            wo=vm((w, w), BF16),
            w_up=vm((w, w), BF16),
            wd=vm((w, f // GROUPS), BF16),
            smalls=vm((c.dp, 16, LANES), F32),
            pack=vm((c.dp, 2) + unit, BF16),
            w_in=vm((2, c.per_group, 2, c.half, 3 * g), BF16),
            vecs=vm(vec, F32),
            side=vm((c.dp,) + unit, BF16),
            cross=vm((n_z,) + unit, BF16),
            spread_z=vm((n_z,) + unit, BF16),
            spread_v=vm((n_z,) + vec, F32),
            x_mine=vm(unit, BF16),
            x_theirs=vm(unit, BF16),
            vec_side=vm(vec, F32),
            vec_mine=vm(vec, F32),
            vec_cross=vm(vec, F32),
            vec_sum=vm(vec, F32),
            vec_z=vm(vec, F32),
            vec_x=vm(vec, F32),
            qkv_s=vm((h, c.per_group, c.shard, 4 * HDIM), BF16),
            qkv_r=vm((h, c.dp, c.shard, 4 * HDIM), BF16),
            s_send=dma((c.dp,)),
            s_recv=dma((c.dp,)),
            w_send=dma((2, n_z + 1)),
            w_recv=dma((2, 2)),
            wb_send=dma((2,)),
            wb_recv=dma((2,)),
            hop_send=dma((3, c.dp)),
            hop_recv=dma((c.dp,)),
            sib_send=dma((c.dp,)),
            sib_recv=dma((c.dp,)),
            red_send=dma((7,)),
            red_recv=dma((7,)),
            cross_send=dma((n_z,)),
            cross_recv=dma((n_z,)),
            z_send=dma((n_z,)),
            z_recv=dma((n_z,)),
            vz_send=dma((n_z,)),
            vz_recv=dma((n_z,)),
            q1_send=dma((h, c.per_group)),
            q1_recv=dma((h, c.dp)),
            q2_send=dma((h, s)),
            q2_recv=dma((h,)),
        )
    names = tuple(inputs) + tuple(outputs) + tuple(scratch)
    vmem = pl.BlockSpec(memory_space=pltpu.VMEM)
    hbm = pl.BlockSpec(memory_space=pl.ANY)
    special = dict(teacher=hbm, out_grad=hbm, lengths=pl.BlockSpec(memory_space=pltpu.SMEM))
    results = pl.pallas_call(
        functools.partial(layer_kernel, cfg, row, names),
        out_shape=list(outputs.values()),
        in_specs=[special.get(name, vmem) for name in inputs],
        out_specs=[vmem] * len(outputs),
        scratch_shapes=list(scratch.values()),
        compiler_params=pltpu.CompilerParams(
            collective_id=collective_id, has_side_effects=True, vmem_limit_bytes=VMEM_LIMIT
        ),
        name="layer",
    )(*inputs.values())
    return dict(zip(outputs, results, strict=True))


def deliver_kernel(cfg, layer_in, states_in, qkv, od, vec, *refs):
    outs = refs
    my_dp = lax.axis_index("dp")
    shard, width, half = cfg.shard, cfg.width, cfg.half
    outs[0][...] = layer_in[...]
    outs[1][...] = states_in[...]
    qw, kw, vw, ow, uw, dw = outs[2:8]
    parts = [
        jnp.concatenate(
            [qkv[h, :, k * HDIM : (k + 1) * HDIM].astype(F32) for h in range(cfg.heads)], axis=1
        )
        for k in range(4)
    ]
    for ref, part in zip((qw, kw, vw), parts[:3], strict=True):
        ref[...] = part
    for c in range(2):
        rows = slice(c * half, (c + 1) * half)
        ow[rows] = od[c, 0]
        uw[rows] = od[c, 1]
        for k in range(2):
            dw[(2 * c + k) * half : (2 * c + k + 1) * half] = od[
                c, 2, :, k * 4 * shard : (k + 1) * 4 * shard
            ]
    slot = lax.rem(my_dp, cfg.per_group)
    mine = parts[3][0:8, 0:shard]
    for t in range(1, cfg.per_group):
        mine = jnp.where(slot == t, parts[3][0:8, t * shard : (t + 1) * shard], mine)
    outs[8][...] = mine[0]
    outs[9][...] = mine[2]
    turned = pltpu.roll(vec[0:8], lax.rem(width - my_dp * shard, width), 1)
    for n in range(6):
        outs[10 + n][...] = turned[n, 0:shard]
    outs[16][...] = vec[
        pl.ds(8 + my_dp // cfg.per_group, 1),
        pl.ds(pl.multiple_of(slot * 4 * shard, LANES), 4 * shard),
    ][0]
    outs[17][0] = vec[12, 0]


def deliver(cfg, *args):
    sds = jax.ShapeDtypeStruct
    shard, width, group = cfg.shard, cfg.width, cfg.group
    out_shape = [sds(a.shape, a.dtype) for a in args[:2]]
    out_shape += [sds((shard, group), F32)] * 3 + [sds((shard, width), F32)] * 2
    out_shape += [sds((group, 4 * shard), F32)] + [sds((shard,), F32)] * 8
    out_shape += [sds((4 * shard,), F32), sds((1,), F32)]
    vmem = pl.BlockSpec(memory_space=pltpu.VMEM)
    return pl.pallas_call(
        functools.partial(deliver_kernel, cfg),
        out_shape=out_shape,
        in_specs=[vmem] * len(args),
        out_specs=[vmem] * (len(out_shape) - 1) + [pl.BlockSpec(memory_space=pltpu.SMEM)],
        name="deliver",
    )(*args)


def local(
    states,
    lengths,
    teacher,
    out_grad,
    q_weight,
    k_weight,
    v_weight,
    q_bias,
    v_bias,
    o_weight,
    o_bias,
    attn_gain,
    attn_bias,
    up_weight,
    up_bias,
    down_weight,
    down_bias,
    ffn_gain,
    ffn_bias,
):
    row_count, piece, width = states.shape
    n_dp, n_seq = lax.axis_size("dp"), lax.axis_size("seq")
    me, my_dp = lax.axis_index("seq"), lax.axis_index("dp")
    shard = q_bias.shape[0]
    hidden = up_bias.shape[0] * n_dp
    cfg = Config(n_dp, n_seq, piece, width, hidden, shard)
    cfg.rows = row_count
    group = cfg.group

    if not cfg.split:

        def pad(v):
            return jnp.pad(v.astype(F32), ((0, 0), (0, LANES - v.shape[1])))

        vectors = (q_bias, v_bias, o_bias, attn_gain, attn_bias, down_bias, ffn_gain, ffn_bias)
        small = jnp.concatenate(
            [
                pad(jnp.stack(vectors)),
                pad(up_bias.reshape(4, shard)),
                jnp.broadcast_to(lengths.astype(F32)[:, None], (row_count, LANES)),
                jnp.zeros((4 - row_count, LANES), F32),
            ]
        )
        smalls = lax.all_gather(small, "dp", axis=0)
        qkv = jnp.stack((q_weight, k_weight, v_weight))
        qkv = lax.all_gather(qkv, "dp", axis=1, tiled=True)
        w_group_in = lax.dynamic_slice(qkv, (0, me * group, 0), (3, group, group))
        wo = lax.all_gather(o_weight, "dp", axis=0, tiled=True)
        wu = lax.all_gather(up_weight, "dp", axis=0, tiled=True)
        wd = lax.all_gather(down_weight, "dp", axis=0, tiled=True)
        wd = wd.reshape(GROUPS, -1, group).transpose(0, 2, 1).reshape(width, -1)

    results = []
    for n in range(row_count):
        inputs = dict(states=states[n], teacher=teacher[n], out_grad=out_grad[n])
        if cfg.split:
            inputs |= dict(
                wq=q_weight,
                wk=k_weight,
                wv=v_weight,
                ow=o_weight,
                uw=up_weight,
                dw=down_weight.T,
                qb=q_bias,
                vb=v_bias,
                ob=o_bias,
                ag=attn_gain,
                ab=attn_bias,
                db=down_bias,
                fg=ffn_gain,
                fb=ffn_bias,
                ub=up_bias,
                lengths=lengths,
            )
        else:
            inputs |= dict(smalls=smalls, w_all=w_group_in, wo=wo, w_up=wu, wd=wd)
        results.append(layer(cfg, n, n, inputs))

    def summed(name):
        first = results[0][name]
        if row_count == 1:
            return first
        return sum((item[name].astype(F32) for item in results[1:]), first.astype(F32))

    if cfg.split:
        heavy = [jnp.stack([item[n] for item in results]) for n in ("layer_out", "states_grad")]
        out = deliver(cfg, *heavy, summed("qkv_out"), summed("od_out"), summed("vec_out"))
        grad_qw, grad_kw, grad_vw, grad_ow, grad_uw, grad_dw = out[2:8]
        vectors = out[8:17]
        return (
            (out[0], out[17].reshape(()), out[1], grad_qw, grad_kw, grad_vw)
            + (vectors[0], vectors[1], grad_ow, *vectors[2:5], grad_uw, vectors[8])
            + (grad_dw.T, *vectors[5:8])
        )

    layer_out = jnp.stack([item["layer_out"] for item in results])
    states_grad = jnp.stack([item["states_grad"] for item in results])
    qkv_g, g_all, vecs = (summed(n).astype(F32) for n in ("qkv_raw", "g_all", "vecs"))
    qkv_g = qkv_g.transpose(1, 2, 0, 3).reshape(3, group + AUG, group)
    whole = jnp.zeros((3, width + GROUPS * AUG, group), F32)
    whole = lax.dynamic_update_slice(whole, qkv_g[:, :group], (0, me * group, 0))
    whole = lax.dynamic_update_slice(whole, qkv_g[:, group:], (0, width + me * AUG, 0))
    whole, g_all, vec = lax.psum((whole, g_all, vecs), ("dp", "seq"))
    qkv = lax.dynamic_slice(whole, (0, my_dp * shard, 0), (3, shard, group))
    biases = whole[:, width::AUG].reshape(3, width)
    grad_qb = lax.dynamic_slice(biases[0], (my_dp * shard,), (shard,))
    grad_vb = lax.dynamic_slice(biases[2], (my_dp * shard,), (shard,))
    g_ou = lax.dynamic_slice(g_all[:2], (0, my_dp * shard, 0), (2, shard, width))
    g_d = g_all[2].reshape(GROUPS, group, -1).transpose(0, 2, 1).reshape(-1, group)
    grad_dw = lax.dynamic_slice(g_d, (my_dp * 4 * shard, 0), (4 * shard, group))
    mine = lax.dynamic_slice(vec[:6], (0, my_dp * shard), (6, shard))
    grad_ub = lax.dynamic_slice(vec[8:12].reshape(-1), (my_dp * 4 * shard,), (4 * shard,))
    return (
        (layer_out, vec[12, 0], states_grad, qkv[0], qkv[1], qkv[2], grad_qb, grad_vb, g_ou[0])
        + (mine[0], mine[1], mine[2], g_ou[1], grad_ub, grad_dw, mine[3], mine[4], mine[5])
    )


def solution(mesh):
    rows3 = P("dp", "seq", None)
    matrix = P("dp", None)
    vector = P("dp")
    return jax.shard_map(
        local,
        mesh=mesh,
        in_specs=(rows3, vector, rows3, rows3)
        + (matrix,) * 3
        + (vector,) * 2
        + (matrix,)
        + (vector,) * 3
        + (matrix, vector, matrix)
        + (vector,) * 3,
        out_specs=(rows3, P(), rows3)
        + (matrix,) * 3
        + (vector,) * 2
        + (matrix,)
        + (vector,) * 3
        + (matrix, vector, matrix)
        + (vector,) * 3,
        check_vma=False,
    )
```

```python
import functools
import math
import types

import jax
import jax.numpy as jnp
from jax import lax
from jax.experimental import pallas as pl
from jax.experimental.pallas import tpu as pltpu
from jax.sharding import PartitionSpec as P

HDIM = 64
GROUPS = 4
EPSILON = 1e-12
NEG_FILL = -1e30
LANES = 128
AUG = 16
LOG2E = 1.4426950408889634
MESH = pl.DeviceIdType.MESH
F32 = jnp.float32
BF16 = jnp.bfloat16
VMEM_LIMIT = 61 * 1024 * 1024


def mm(left, right, left_dim, right_dim):
    return lax.dot_general(
        left, right, (((left_dim,), (right_dim,)), ((), ())), preferred_element_type=F32
    )


def iota(shape, dim):
    return lax.broadcasted_iota(jnp.int32, shape, dim)


def remote(src, dst, send_sem, recv_sem, **where):
    return pltpu.make_async_remote_copy(
        src_ref=src,
        dst_ref=dst,
        send_sem=send_sem,
        recv_sem=recv_sem,
        device_id=where,
        device_id_type=MESH,
    )


def three_parts(row):
    high = row.astype(BF16)
    rest = row - high.astype(F32)
    middle = rest.astype(BF16)
    low = (rest - middle.astype(F32)).astype(BF16)
    return high, middle, low


class Config:
    def __init__(self, dp, seq, piece, width, hidden, shard):
        self.dp, self.seq, self.piece, self.width, self.hidden, self.shard = (
            dp,
            seq,
            piece,
            width,
            hidden,
            shard,
        )
        self.slots = piece * seq
        self.group = width // GROUPS
        self.heads = self.group // HDIM
        self.per_group = dp // GROUPS
        self.split = shard % 32 == 0 and seq == 4 and dp == 8
        self.half = shard // 2
        self.quarter = hidden // dp // 4


def greet(cfg, me, my_dp):
    barrier = pltpu.get_barrier_semaphore()
    count = cfg.seq - 1
    for d in range(1, cfg.seq):
        pl.semaphore_signal(barrier, inc=1, device_id={"seq": me ^ d}, device_id_type=MESH)
    if cfg.split:
        count += cfg.dp - 1
        for e in range(1, cfg.dp):
            pl.semaphore_signal(
                barrier, inc=1, device_id={"dp": lax.rem(my_dp + e, cfg.dp)}, device_id_type=MESH
            )
    return lambda: pl.semaphore_wait(barrier, count)


def layer_kernel(cfg, row, names, *refs):
    r = types.SimpleNamespace(**dict(zip(names, refs, strict=True)))
    split = cfg.split
    me = lax.axis_index("seq")
    my_dp = lax.axis_index("dp")
    piece, width, group, heads, seq = cfg.piece, cfg.width, cfg.group, cfg.heads, cfg.seq
    shard, half, n_dp, per_group = cfg.shard, cfg.half, cfg.dp, cfg.per_group
    hid = cfg.hidden // GROUPS
    n_z = n_dp // 2
    core = lax.rem(me, 2)
    my_z, my_y = my_dp // 2, lax.rem(my_dp, 2)
    far = [d for d in range(seq - 1, 1, -1)]

    states = r.states
    teacher, out_grad = r.states_grad, r.layer_out
    late = [
        pltpu.make_async_copy(r.teacher, teacher, r.late_sem.at[0]),
        pltpu.make_async_copy(r.out_grad, out_grad, r.late_sem.at[1]),
    ]
    x_own, x_group, w_group, w_pad, smalls = (
        r.x_own,
        r.x_group,
        r.w_group,
        r.w_pad,
        r.smalls,
    )
    q_t, k_n, k_t, v_n = r.q_t, r.k_n, r.k_t, r.v_n
    context_s, context_r = r.context_s, r.context_r
    cols, vcols = r.cols, r.vcols
    wide, slim = r.wide, r.slim
    wo, w_up, wd = r.wo, r.w_up, r.wd
    c_grad, d_in, dx_r = r.c_grad, r.d_in, r.dx_r
    dx_s = c_grad
    tall1 = group + AUG
    low = r.low
    low2 = low.at[GROUPS * tall1 :]

    def low1(g, start, size):
        return pl.ds(pl.multiple_of(g * tall1 + start, AUG), size)

    def d_aug(h, t, start, size):
        return pl.ds(pl.multiple_of((h * seq + t) * LANES + start, HDIM), size)

    score0, score1 = wide.at[0:piece], wide.at[piece : 2 * piece]
    gathered = r.gathered
    v1, first, v2, seed = (wide.at[i * width : (i + 1) * width] for i in range(4))
    dq, dk, dv = (wide.at[i * width : (i + 1) * width] for i in range(3))
    act, slope = slim.at[0 : cfg.hidden], slim.at[cfg.hidden : 2 * cfg.hidden]
    p0, p1, s0, s1 = (slim.at[i * piece : (i + 1) * piece] for i in range(4))
    d_t = slope

    def at(i, n):
        return pl.ds(pl.multiple_of(i * n, n), n)

    def loop(count, body, *init):
        return lax.fori_loop(0, count, lambda i, c: body(i, *c), tuple(init))

    def sub(v):
        return jnp.sum(v, axis=0, keepdims=True)


    def to_seq(sems, src, dst, d):
        return remote(src, dst, sems[0].at[d], sems[1].at[d], seq=me ^ d)

    def x_copy(d):
        return to_seq((r.x_send, r.x_recv), x_own.at[at(me ^ d, group)], x_group.at[me, pl.ds(0, group)], d)

    def c_copy(d):
        return to_seq((r.c_send, r.c_recv), context_s.at[me ^ d], context_r.at[at(me, group)], d)

    def g_copy(d):
        return to_seq((r.g_send, r.g_recv), c_grad.at[at(me ^ d, group)], d_in.at[me], d)

    def dx_copy(d):
        return to_seq((r.dx_send, r.dx_recv), dx_s.at[at(me ^ d, group)], dx_r.at[at(me, group)], d)

    if split:
        pack = r.pack
        w_in = r.w_in
        my_slot = lax.rem(my_dp, per_group)

        def s_copy(e):
            return remote(
                smalls.at[my_dp],
                smalls.at[my_dp],
                r.s_send.at[e],
                r.s_recv.at[e],
                dp=lax.rem(my_dp + e, n_dp),
            )

        first_group = me - core

        def w_ref(g):
            return w_in.at[g, my_y, core]

        def w_along(g, j):
            z = lax.rem(my_z + n_z - 1 - j, n_z)
            return remote(
                w_ref(g), w_ref(g), r.w_send.at[g, j], r.w_recv.at[g, 0], dp=2 * z + my_y
            )

        def w_across(g):
            return remote(
                w_ref(g), w_ref(g), r.w_send.at[g, n_z], r.w_recv.at[g, 1], dp=my_dp + 1 - 2 * my_y
            )

        def w_over(g):
            ref = w_in.at[g, 1 - my_y, core]
            return remote(ref, ref, r.w_send.at[g, n_z], r.w_recv.at[g, 1], dp=my_dp)

        def w_beside(g, part, half_of):
            ref = w_in.at[g, my_y if part == 0 else 1 - my_y, half_of]
            return remote(ref, ref, r.wb_send.at[part], r.wb_recv.at[part], seq=me ^ 1)

        def holds(g):
            return my_z == first_group + g

        def hop(kind, i, **where):
            ref = pack.at[i, core]
            return remote(ref, ref, r.hop_send.at[kind, i], r.hop_recv.at[i], **where)

        def up(i):
            return hop(0, i, dp=my_dp + 2)

        def down(i):
            return hop(1, i, dp=my_dp - 2)

        def across(i):
            return hop(2, i, dp=my_dp + 1 - 2 * my_y)

        def beside(i):
            ref = pack.at[i, core]
            return remote(ref, ref, r.sib_send.at[i], r.sib_recv.at[i], seq=me ^ 1)

        def when(condition, fn):
            pl.when(condition)(fn)

        def gather_start():
            when(my_z < n_z - 1, lambda: up(my_dp).start())
            when(my_z > 0, lambda: down(my_dp).start())

        def gather_z(k):
            below, above = my_dp - 2 * k, my_dp + 2 * k

            @pl.when(my_z >= k)
            def _():
                hop(0, below, dp=my_dp).wait_recv()
                when(my_z < n_z - 1, lambda: up(below).start())
                across(below).start()
                beside(below).start()

            @pl.when(my_z + k < n_z)
            def _():
                hop(0, above, dp=my_dp).wait_recv()
                when(my_z > 0, lambda: down(above).start())
                across(above).start()
                beside(above).start()

        def gather_y(k):
            other = my_dp + 1 - 2 * my_y

            def take(i):
                hop(2, i, dp=my_dp).wait_recv()
                beside(i).start()

            if k == 0:
                take(other)
            else:
                when(my_z >= k, lambda: take(other - 2 * k))
                when(my_z + k < n_z, lambda: take(other + 2 * k))

        def gather_end():
            for e in range(1, n_dp):
                copy = beside(lax.rem(my_dp + e, n_dp))
                copy.wait()

            when(my_z < n_z - 1, lambda: up(my_dp).wait_send())
            when(my_z > 0, lambda: down(my_dp).wait_send())
            across(my_dp).wait_send()
            for k in range(1, n_z):
                below, above = my_dp - 2 * k, my_dp + 2 * k

                @pl.when(my_z >= k)
                def _():
                    when(my_z < n_z - 1, lambda: up(below).wait_send())
                    across(below).wait_send()

                @pl.when(my_z + k < n_z)
                def _():
                    when(my_z > 0, lambda: down(above).wait_send())
                    across(above).wait_send()


    wait_entry = greet(cfg, me, my_dp)
    for c in range(0, width, LANES):
        x_own[c : c + LANES] = states[:, c : c + LANES].T
    if split:
        for c in range(2):
            pack[my_dp, c, 0] = r.ow[c * half : (c + 1) * half]
            pack[my_dp, c, 1] = r.uw[c * half : (c + 1) * half]
            for k in range(2):
                pack[my_dp, c, 2, :, k * 4 * shard : (k + 1) * 4 * shard] = r.dw[
                    (2 * c + k) * half : (2 * c + k + 1) * half
                ]
        smalls[my_dp] = jnp.zeros((16, LANES), F32)
        for n, ref in enumerate((r.qb, r.vb, r.ob, r.ag, r.ab, r.db, r.fg, r.fb)):
            smalls[my_dp, n : n + 1, 0:shard] = ref[...].reshape(1, shard).astype(F32)
        up_bias = r.ub[...].reshape(1, 4 * shard).astype(F32)
        for n in range(4):
            smalls[my_dp, 8 + n : 9 + n, 0:shard] = up_bias[:, n * shard : (n + 1) * shard]
        for n in range(cfg.rows):
            smalls[my_dp, 12 + n : 13 + n] = jnp.full((1, LANES), r.lengths[n].astype(F32))

        for g in range(2):

            @pl.when(holds(g))
            def _():
                for c in range(2):
                    rows = slice(c * half, (c + 1) * half)
                    w_in[g, my_y, c] = jnp.concatenate(
                        [ref[rows].astype(F32) for ref in (r.wq, r.wk, r.wv)], axis=1
                    ).astype(BF16)

    wait_entry()
    if split:
        for e in range(1, n_dp):
            s_copy(e).start()

        for g in range(2):

            @pl.when(holds(g))
            def _():
                for j in range(n_z - 1):
                    w_along(g, j).start()
                w_across(g).start()

    for d in range(1, seq):
        x_copy(d).start()
    for copy in late:
        copy.start()
    x_group[me, 0:group] = x_own[at(me, group)]


    deep = HDIM + AUG
    tops = r.tops

    def sums(h, t):
        return pl.ds(pl.multiple_of((h * seq + t) * deep, AUG), deep)

    def clear_sums(i, unused):
        gathered[pl.ds(pl.multiple_of(i * deep, AUG), deep)] = jnp.zeros((deep, piece), F32)
        tops[i] = jnp.full((1, piece), NEG_FILL, F32)
        return (unused,)

    loop(heads * seq, clear_sums, 0)
    n_cols = heads * LANES
    if split:
        for n, g in enumerate((1 - core, core)):

            @pl.when(jnp.logical_not(holds(g)))
            def _():
                w_along(g, 0).wait_recv()
                w_across(g).start()
                if n == 0:
                    w_beside(g, 0, core).start()

        gather_start()
        for e in range(1, n_dp):
            s_copy(e).wait_recv()
    for i in range(n_dp):
        turned_small = smalls[i].T
        cols[i * shard : (i + 1) * shard] = turned_small[0:shard]
    vec_rows = jnp.zeros((AUG, n_cols), F32)
    lane = iota((LANES, n_cols), 1)
    source = iota((LANES, n_cols), 0)
    for t in range(per_group):
        spread = jnp.where(
            (((lane >> 7) * HDIM + (lane & 127)) == source + t * shard)
            & ((lane & 127) < HDIM)
            & (source < shard),
            1.0,
            0.0,
        ).astype(BF16)
        vec_rows += mm(smalls[me * per_group + t].astype(BF16), spread, 1, 0)
    row_id = iota((AUG, n_cols), 0)
    lane = iota((AUG, n_cols), 1) & 127
    zero = jnp.zeros((AUG, n_cols), F32)
    top_row = row_id == 0
    w_pad[0, group:] = jnp.where(top_row, vec_rows[0:1], zero).astype(BF16)
    ones_k = (top_row & (lane > HDIM) & (lane <= HDIM + 3)) | ((row_id == 1) & (lane == HDIM))
    w_pad[1, group:] = jnp.where(ones_k, 1.0, zero).astype(BF16)
    ones_v = (lane >= HDIM) & (lane < HDIM + 3)
    w_pad[2, group:] = jnp.where(top_row, jnp.where(ones_v, 1.0, vec_rows[1:2]), zero).astype(BF16)

    if split:
        for n, g in enumerate((1 - core, core)):
            w_over(g).wait_recv()
            if n == 0:
                w_beside(g, 1, core).start()
        across(my_dp).start()
        when(my_z != me, lambda: w_beside(core, 0, 1 - core).wait_recv())
        w_beside(core, 1, 1 - core).wait_recv()
        for t in range(per_group):
            for c in range(2):
                for kind in range(3):
                    w_group[kind, t * shard + c * half : t * shard + (c + 1) * half] = w_in[
                        core, t, c, :, kind * group : (kind + 1) * group
                    ]
    else:
        for kind in range(3):
            w_group[kind] = r.w_all[kind]
    lane = iota((group, n_cols), 1)
    spread = jnp.where(
        (((lane >> 7) * HDIM + (lane & 127)) == iota((group, n_cols), 0)) & ((lane & 127) < HDIM),
        1.0,
        0.0,
    ).astype(BF16)
    for kind in range(3):
        w_pad[kind, 0:group] = mm(w_group[kind], spread, 1, 0).astype(BF16)

    length = smalls[my_dp, 12 + row : 13 + row, 0:1]
    aug_row = iota((AUG, piece), 0)
    factor = LOG2E * HDIM**-0.5
    def v_t(h, t):
        return pl.ds(pl.multiple_of((h * seq + t) * deep, AUG), deep)

    def project(t):
        slot = (iota((AUG, piece), 1) + t * piece).astype(F32)
        mask = jnp.where(slot < length, 0.0, NEG_FILL)
        x_group[t, group:] = jnp.where(
            aug_row == 0, 1.0, jnp.where(aug_row == 1, mask, 0.0)
        ).astype(BF16)
        x = x_group[t]
        queries = mm(w_pad[0], x, 0, 0) * factor
        keys_t = mm(w_pad[1], x, 0, 0)
        values_t = mm(w_pad[2], x, 0, 0)
        keys_n = mm(x, w_pad[1], 0, 0)
        values_n = mm(x, w_pad[2], 0, 0)
        rest = jnp.where(iota((HDIM, piece), 0) == 0, 1.0, 0.0).astype(BF16)
        for h in range(heads):
            span = slice(h * LANES, h * LANES + HDIM)
            q_t[h, t, 0:HDIM] = queries[span].astype(BF16)
            q_t[h, t, HDIM:] = rest
            k_t[h, t] = keys_t[span].astype(BF16)
            slim[v_t(h, t)] = values_t[h * LANES : h * LANES + deep].astype(BF16)
            k_n[h, t] = keys_n[:, h * LANES : (h + 1) * LANES].astype(BF16)
            v_n[h, t] = values_n[:, h * LANES : (h + 1) * LANES].astype(BF16)


    per_part = seq * heads

    def run(count, place, first_part, last_part, a, b, hooks=(), rest=None, unroll=2):
        buffers = (a, b)
        first_part(a, *place(0))

        def several(u, unused):
            if hooks:
                due = u == hooks[0][0]
                for when_u, fn in hooks[1:]:
                    due = due | (u == when_u)

                @pl.when(due)
                def _():
                    for when_u, fn in hooks:
                        pl.when(u == when_u)(fn)

            for j in range(unroll):
                first_part(buffers[(j + 1) % 2], *place(unroll * u + j + 1))
                last_part(buffers[j % 2], *place(unroll * u + j))
            return (unused,)

        turns = (count - 1) // unroll
        loop(turns, several, 0)
        if rest is not None:
            rest()
        for i in range(turns * unroll, count - 1):
            first_part(buffers[(i + 1) % 2], *place(i + 1))
            last_part(buffers[i % 2], *place(i))
        last_part(buffers[(count - 1) % 2], *place(count - 1))

    unroll = 4

    def before(step):
        return (step - 1) // unroll

    def after(step):
        return step // unroll + 1

    def score(buffer, t, h, k):
        buffer[...] = mm(k_n[h, k], q_t[h, t], 1, 0)

    def absorb(buffer, t, h, k):
        i = h * seq + t
        old = tops[i]
        top = jnp.maximum(old, jnp.max(buffer[...], axis=0, keepdims=True))
        weights = jnp.exp2(buffer[...] - top).astype(BF16)
        tops[i] = top
        place = sums(h, t)
        gathered[place] = gathered[place] * jnp.exp2(old - top) + mm(slim[v_t(h, k)], weights, 1, 0)

    def settle(t):
        for h in range(heads):
            total = gathered[sums(h, t)]
            mass = total[HDIM : HDIM + 1]
            context_s[t, h * HDIM : (h + 1) * HDIM] = (total[0:HDIM] / mass).astype(BF16)
            parts = three_parts(-(tops[h * seq + t] + jnp.log2(mass)))
            value = jnp.where(aug_row == 0, 1.0, 0.0)
            for n, part in enumerate(parts):
                value = jnp.where(aug_row == n + 1, part.astype(F32), value)
            q_t[h, t, HDIM:deep] = value.astype(BF16)

    def place_forward(i):
        part, j = i // per_part, lax.rem(i, per_part)
        is_far, tail = lax.rem((part + 1) // 2, 2), part // 3
        d_q = is_far * (4 - part) + (1 - is_far) * (j // (2 * heads))
        h = is_far * (j // seq) + (1 - is_far) * (lax.rem(j, 2 * heads) // 2)
        d_k = is_far * lax.rem(j, seq) + (1 - is_far) * (lax.rem(j, 2) + 2 * tail)
        return me ^ d_q, h, me ^ d_k

    def far_states():
        for d in far:
            x_copy(d).wait_recv()
        loop(2, lambda i, unused: (project(me ^ (2 + i)), unused)[1:], 0)

    def far_context(d):
        settle(me ^ d)
        c_copy(d).start()

    hooks = [
        (before(per_part), far_states),
        (after(2 * per_part - 1), lambda: far_context(far[0])),
        (after(3 * per_part - 1), lambda: far_context(far[1])),
    ]
    if split:
        hooks += [
            (1, lambda: gather_z(1)),
            (3, lambda: gather_y(0)),
            (4, lambda: gather_z(2)),
            (6, lambda: gather_y(1)),
            (8, lambda: gather_z(3)),
            (9, lambda: gather_y(2)),
        ]
    project(me)
    x_copy(1).wait_recv()
    project(me ^ 1)
    run(4 * per_part, place_forward, score, absorb, score0, score1, hooks, unroll=unroll)
    settle(me ^ 1)
    c_copy(1).start()
    settle(me)
    context_r[at(me, group)] = context_s[me]
    if split:
        gather_y(3)
        gather_end()

        def unpack(i, unused):
            for c in range(2):
                wo[pl.ds(pl.multiple_of(i * shard + c * half, AUG), half)] = pack[i, c, 0]
                w_up[pl.ds(pl.multiple_of(i * shard + c * half, AUG), half)] = pack[i, c, 1]
                for k in range(2):
                    wd[
                        pl.ds(
                            pl.multiple_of(i // per_group * group + (2 * c + k) * half, AUG), half
                        ),
                        pl.ds(
                            pl.multiple_of(lax.rem(i, per_group) * 4 * shard, LANES), 4 * shard
                        ),
                    ] = pack[i, c, 2, :, k * 4 * shard : (k + 1) * 4 * shard]
            return (unused,)

        loop(n_dp, unpack, 0)


    vcols[...] = jnp.zeros_like(vcols)
    inv = 1.0 / width
    total = jnp.sum(smalls[:, 12:13, 0:1], axis=0)
    for n in range(1, cfg.rows):
        total += jnp.sum(smalls[:, 12 + n : 13 + n, 0:1], axis=0)
    slot = (iota((1, piece), 1) + me * piece).astype(F32)
    live = jnp.where(slot < length, 1.0, 0.0)
    coef = 2.0 / (total * width)
    zero_row = jnp.zeros((1, piece), F32)

    def col(i, n, which):
        return cols[at(i, n), which : which + 1]

    for d in range(1, seq):
        c_copy(d).wait_recv()

    step = 256

    raw0, raw1 = seed.at[0:step], seed.at[step : 2 * step]

    def attn_out(raw, i):
        raw[...] = mm(wo[:, at(i, step)], context_r[...], 0, 0)

    def add_states(raw, i):
        v = raw[...] + x_own[at(i, step)].astype(F32) + col(i, step, 2)
        v1[at(i, step)] = v
        tops[0] += sub(v)

    tops[0] = zero_row
    run(width // step, lambda i: (i,), attn_out, add_states, raw0, raw1)
    acc = tops[0]
    mean = acc * inv

    def center(ref):
        def body(g, acc):
            v = ref[at(g, group)] - mean
            ref[at(g, group)] = v
            return (acc + sub(v * v),)

        (acc,) = loop(GROUPS, body, zero_row)
        return lax.rsqrt(acc * inv + EPSILON)

    scale1 = center(v1)

    def norm1(g, unused):
        v = v1[at(g, group)] * scale1
        v1[at(g, group)] = v
        out = v * col(g, group, 3) + col(g, group, 4)
        first[at(g, group)] = out
        low[low1(g, 0, group)] = out.astype(BF16)
        low[low1(g, group, AUG)] = jnp.where(aug_row == 0, 1.0, 0.0).astype(BF16)
        return (unused,)

    loop(GROUPS, norm1, 0)

    def gelu(u):
        d = 1.0 + (0.3275911 * 0.7071067811865476) * jnp.abs(u)
        t = pltpu.reciprocal(d, approx=True)
        bell = jnp.exp2((u * u) * (-0.5 * LOG2E))
        poly = t * (
            0.127414796
            + t * (-0.142248368 + t * (0.7107068705 + t * (-0.7265760135 + t * 0.5307027145)))
        )
        tail = poly * bell
        phi = jnp.where(u >= 0.0, 1.0 - tail, tail)
        return u * phi, phi + u * bell * 0.3989422804014327

    bunch = max(1, LANES // math.gcd(LANES, 4 * shard) if (4 * shard) % LANES else 1)
    span4 = 4 * shard * bunch
    n_steps = n_dp // bunch
    steps_group = n_steps // GROUPS
    tall = span4 // 4

    raw0, raw1 = wide.at[2 * width : 2 * width + span4], wide.at[3 * width : 3 * width + span4]

    def expand(raw, i):
        g, c = i // steps_group, lax.rem(i, steps_group)
        raw[...] = mm(w_up[at(g, group), at(c, span4)], low[low1(g, 0, group)], 0, 0)

    def activate(raw, i):
        bias = jnp.concatenate(
            [cols[at(i * bunch + n, shard), 8 + b : 9 + b] for n in range(bunch) for b in range(4)],
            axis=0,
        )
        for b in range(4):
            part = slice(b * tall, (b + 1) * tall)
            out, grad = gelu(raw[part] + bias[part])
            place = pl.ds(pl.multiple_of((i * 4 + b) * tall, tall), tall)
            act[place] = out.astype(BF16)
            slope[place] = grad.astype(BF16)

    run(n_steps, lambda i: (i,), expand, activate, raw0, raw1)

    def clear_rows(count):
        for n in range(count):
            tops[n] = zero_row

    part0, part1 = seed.at[0:group], seed.at[group : 2 * group]

    def contract(raw, g):
        raw[...] = mm(wd[at(g, group)], act[at(g, hid)], 1, 0)

    def add_branch(raw, g):
        v = raw[...] + first[at(g, group)] + col(g, group, 5)
        v2[at(g, group)] = v
        tops[0] += sub(v)

    clear_rows(1)
    run(GROUPS, lambda g: (g,), contract, add_branch, part0, part1)
    acc = tops[0]
    mean = acc * inv
    scale2 = center(v2)

    for copy in late:
        copy.wait()
    loss, sum1, sum2 = zero_row, zero_row, zero_row
    for c in range(width // LANES):
        span = slice(c * LANES, (c + 1) * LANES)
        xhat = v2[span] * scale2
        v2[span] = xhat
        gain = cols[span, 6:7]
        full = xhat * gain + cols[span, 7:8]
        error = full - teacher[:, span].T.astype(F32)
        loss += sub(live * error * error)
        grad = live * (out_grad[:, span].T.astype(F32) + error * coef)
        r.layer_out[:, span] = full.astype(BF16).T
        vcols[span, 4:5] = jnp.sum(grad * xhat, axis=1, keepdims=True)
        vcols[span, 5:6] = jnp.sum(grad, axis=1, keepdims=True)
        grad = grad * gain
        seed[span] = grad
        sum1 += sub(grad)
        sum2 += sub(grad * xhat)
    sum1, sum2 = sum1 * inv, sum2 * inv

    def back2(g, unused):
        place = at(g, group)
        grad = scale2 * (seed[place] - sum1 - v2[place] * sum2)
        seed[place] = grad
        brief = grad.astype(BF16)
        low2[place] = brief
        vcols[place, 3:4] = jnp.sum(brief.astype(F32), axis=1, keepdims=True)
        return (unused,)

    loop(GROUPS, back2, 0)

    raw0, raw1 = v2.at[0:span4], v2.at[span4 : 2 * span4]

    def back_act(raw, i):
        g, c = i // steps_group, lax.rem(i, steps_group)
        raw[...] = mm(wd[at(g, group), at(c, span4)], low2[at(g, group)], 0, 0)

    def times_slope(raw, i):
        place = at(i, span4)
        slope[place] = (raw[...] * slope[place].astype(F32)).astype(BF16)

    run(n_steps, lambda i: (i,), back_act, times_slope, raw0, raw1)
    part0, part1 = v2.at[0:group], v2.at[group : 2 * group]

    def back_first(raw, g):
        raw[...] = mm(w_up[at(g, group)], slope[at(g, hid)], 1, 0)

    def add_first(raw, g):
        place = at(g, group)
        grad = seed[place] + raw[...]
        xhat = v1[place]
        vcols[place, 1:2] = jnp.sum(grad * xhat, axis=1, keepdims=True)
        vcols[place, 2:3] = jnp.sum(grad, axis=1, keepdims=True)
        grad = grad * col(g, group, 3)
        seed[place] = grad
        tops[0] += sub(grad)
        tops[1] += sub(grad * xhat)


    vecs = r.vecs
    if split:
        other_y = my_dp + 1 - 2 * my_y
        side, cross, spread_z, spread_v = r.side, r.cross, r.spread_z, r.spread_v
        od_out, vec_out = r.od_out, r.vec_out
        red_send, red_recv = r.red_send, r.red_recv

        def side_copies():
            return (
                remote(
                    pack.at[:, 1 - core, pl.ds(1, 2)],
                    side.at[:, pl.ds(1, 2)],
                    red_send.at[0],
                    red_recv.at[0],
                    seq=me ^ 1,
                ),
                remote(
                    pack.at[:, 1 - core, 0],
                    side.at[:, 0],
                    red_send.at[6],
                    red_recv.at[6],
                    seq=me ^ 1,
                ),
                remote(vecs, r.vec_side, red_send.at[1], red_recv.at[1], seq=me ^ 1),
            )

        def cross_copy(j):
            z = lax.rem(my_z + 1 + j, n_z)
            return remote(
                side.at[2 * z + 1 - my_y],
                cross.at[z],
                r.cross_send.at[z],
                r.cross_recv.at[z],
                dp=other_y,
            )

        def vec_cross():
            return remote(
                r.vec_mine, r.vec_cross, red_send.at[2], red_recv.at[2], dp=other_y
            )

        def z_copy(j):
            z = lax.rem(my_z + 1 + j, n_z)
            return remote(
                side.at[2 * z + my_y],
                spread_z.at[my_z],
                r.z_send.at[j],
                r.z_recv.at[j],
                dp=2 * z + my_y,
            )

        def vz_copy(j):
            z = lax.rem(my_z + 1 + j, n_z)
            return remote(
                r.vec_sum,
                spread_v.at[my_z],
                r.vz_send.at[j],
                r.vz_recv.at[j],
                dp=2 * z + my_y,
            )

        def x_copies():
            return (
                remote(
                    r.x_mine, r.x_theirs, red_send.at[3], red_recv.at[3], seq=me ^ 2
                ),
                remote(r.vec_z, r.vec_x, red_send.at[4], red_recv.at[4], seq=me ^ 2),
            )

        def last_copy():
            return remote(
                od_out.at[core], od_out.at[core], red_send.at[5], red_recv.at[5], seq=me ^ 1
            )

        def reduce_side():
            for copy in side_copies():
                copy.wait_recv()

            def add(i, unused):
                side[i] = pack[i, core] + side[i]
                return (unused,)

            loop(n_dp, add, 0)
            r.vec_mine[...] = vecs[...] + r.vec_side[...]
            vec_cross().start()
            for j in range(n_z):
                cross_copy(j).start()

        def reduce_cross(j):
            cross_copy(j).wait_recv()
            z = lax.rem(my_z + 1 + j, n_z)
            i = 2 * z + my_y
            side[i] = side[i] + cross[z]
            if j < n_z - 1:
                z_copy(j).start()

        def reduce_vec():
            vec_cross().wait_recv()
            value = r.vec_mine[...] + r.vec_cross[...]
            r.vec_sum[...] = value
            spread_v[my_z] = value
            for j in range(n_z - 1):
                vz_copy(j).start()

        def reduce_z():
            for j in range(n_z - 1):
                z_copy(j).wait_recv()
                vz_copy(j).wait_recv()
            spread_z[my_z] = side[my_dp]
            value = spread_z[0].astype(F32)
            vec = spread_v[0]
            for z in range(1, n_z):
                value += spread_z[z].astype(F32)
                vec += spread_v[z]
            r.x_mine[...] = value.astype(BF16)
            r.vec_z[...] = vec
            for copy in x_copies():
                copy.start()

        def reduce_x():
            for copy in x_copies():
                copy.wait_recv()
            od_out[core] = r.x_mine[...].astype(F32) + r.x_theirs[...].astype(F32)
            vec_out[...] = r.vec_z[...] + r.vec_x[...]
            last_copy().start()

    vecs[...] = jnp.zeros_like(vecs)
    for g in range(GROUPS):
        out = mm(low[low1(g, 0, tall1)], slope[g * hid : (g + 1) * hid], 1, 1)
        vecs[8 + g : 9 + g] = out[group : group + 1]
        if split:
            for t in range(per_group):
                for c in range(2):
                    base = shard * t + half * c
                    pack[g * per_group + t, c, 1] = out[base : base + half].astype(BF16)
        else:
            r.g_all[1, g * group : (g + 1) * group] = out[0:group].astype(BF16)
    clear_rows(2)
    run(GROUPS, lambda g: (g,), back_first, add_first, part0, part1)
    sum1, sum2 = tops[0] * inv, tops[1] * inv

    for g in range(GROUPS):
        out = mm(low2[g * group : (g + 1) * group], act[g * hid : (g + 1) * hid], 1, 1)
        if split:
            for t in range(per_group):
                for c in range(2):
                    for k in range(2):
                        pack[g * per_group + t, c, 2, :, k * 4 * shard : (k + 1) * 4 * shard] = (
                            out[
                                (2 * c + k) * half : (2 * c + k + 1) * half,
                                t * 4 * shard : (t + 1) * 4 * shard,
                            ].astype(BF16)
                        )
        else:
            r.g_all[2, g * group : (g + 1) * group] = out.astype(BF16)

    if split:
        side_copies()[0].start()

    def back1(g, unused):
        place = at(g, group)
        grad = scale1 * (seed[place] - sum1 - v1[place] * sum2)
        seed[place] = grad
        brief = grad.astype(BF16)
        low2[place] = brief
        vcols[place, 0:1] = jnp.sum(brief.astype(F32), axis=1, keepdims=True)
        return (unused,)

    loop(GROUPS, back1, 0)
    grad_mid = seed

    def back_context(i, unused):
        c_grad[at(i, step)] = mm(wo[at(i, step)], low2[...], 1, 0).astype(BF16)
        return (unused,)

    loop(width // step, back_context, 0)
    for d in [1] + far:
        g_copy(d).start()

    vecs[0:8] = vcols[...].T[0:8]
    mean_loss = jnp.sum(loss, axis=1, keepdims=True) / (total * width)
    vecs[12:13] = jnp.broadcast_to(mean_loss, (1, width))
    for j in range(2):
        rows = width // 2
        out = mm(context_r[j * rows : (j + 1) * rows], low2[...], 1, 1)
        if split:
            for t in range(n_dp // 2):
                for c in range(2):
                    base = shard * t + half * c
                    pack[j * (n_dp // 2) + t, c, 0] = out[base : base + half].astype(BF16)
        else:
            r.g_all[0, j * rows : (j + 1) * rows] = out.astype(BF16)

    if split:
        for copy in side_copies()[1:]:
            copy.start()


    def clear(i, unused):
        for ref in (dq, dk, dv):
            ref[at(i, HDIM)] = jnp.zeros((HDIM, piece), F32)
        return (unused,)

    loop(heads * seq, clear, 0)
    tail_row = iota((HDIM, piece), 0)

    def prepare(t):
        for h in range(heads):
            span = slice(h * HDIM, (h + 1) * HDIM)
            grad = d_in[t, span]
            low[d_aug(h, t, 0, HDIM)] = grad
            parts = three_parts(-sub(grad.astype(F32) * context_s[t, span].astype(F32)))
            value = jnp.zeros((HDIM, piece), F32)
            for n, part in enumerate(parts):
                value = jnp.where(tail_row == n, part.astype(F32), value)
            low[d_aug(h, t, HDIM, HDIM)] = value.astype(BF16)

    def rows_of(h, t):
        return at(h * seq + t, HDIM)

    def weigh(buffers, t, h, k):
        p, s = buffers
        weights = jnp.exp2(mm(q_t[h, t], k_n[h, k], 0, 1))
        p[...] = weights.astype(BF16)
        s[...] = (weights * mm(low[d_aug(h, t, 0, LANES)], v_n[h, k], 0, 1)).astype(BF16)

    def gather_grads(buffers, t, h, k):
        p, s = buffers
        dv[rows_of(h, k)] += mm(low[d_aug(h, t, 0, HDIM)], p[...], 1, 0)
        dk[rows_of(h, k)] += mm(q_t[h, t, 0:HDIM], s[...], 1, 0)
        dq[rows_of(h, t)] += mm(k_t[h, k], s[...], 1, 1)

    def fill(t, h):
        for kind, (ref, scale) in enumerate(((dq, HDIM**-0.5), (dk, 1.0 / LOG2E), (dv, 1.0))):
            place = pl.ds(pl.multiple_of(((t * heads + h) * 3 + kind) * HDIM, HDIM), HDIM)
            d_t[place] = (ref[rows_of(h, t)] * scale).astype(BF16)

    w_rows = r.w_rows

    def states_part(t):
        dx_s[at(t, group)] = mm(w_rows[...], d_t[at(t, 3 * group)], 1, 0).astype(BF16)

    if split:
        qkv_s, qkv_r, qkv_out = r.qkv_s, r.qkv_r, r.qkv_out
        owner = my_dp // per_group == me

        def qkv_copy(h, t):
            return remote(
                qkv_s.at[h, t],
                qkv_r.at[h, my_dp],
                r.q1_send.at[h, t],
                r.q1_recv.at[h, my_dp],
                dp=me * per_group + t,
            )

        def qkv_share(h, d):
            return remote(
                qkv_out.at[h], qkv_out.at[h], r.q2_send.at[h, d], r.q2_recv.at[h], seq=me ^ d
            )

    def emit(h):
        for d in range(2):
            fill(me ^ d, h)
        total = mm(x_group[0], d_t[at(h, 3 * HDIM)], 1, 1)
        for t in range(1, seq):
            total += mm(x_group[t], d_t[at(t * heads + h, 3 * HDIM)], 1, 1)
        if split:
            bias_rows = jnp.zeros((shard, HDIM), F32)
            bias_id = iota((shard, HDIM), 0)
            for kind in range(3):
                bias_rows = jnp.where(
                    bias_id == kind,
                    total[group : group + 1, kind * HDIM : (kind + 1) * HDIM],
                    bias_rows,
                )
            for t in range(per_group):
                qkv_s[h, t] = jnp.concatenate(
                    [total[t * shard : (t + 1) * shard], bias_rows], axis=1
                ).astype(BF16)
                when(me * per_group + t != my_dp, lambda: qkv_copy(h, t).start())
        else:
            for kind in range(3):
                r.qkv_raw[h, kind] = total[:, kind * HDIM : (kind + 1) * HDIM]

    early = 2 * (2 * heads + 2)
    shift = 2 * per_part - early

    def place_backward(i):
        part, m = (i + shift) // (2 * per_part), lax.rem(i + shift, 2 * per_part)
        is_far, tail = lax.rem(part, 2), part // 2
        start = (1 - is_far) * (1 - tail)
        j = lax.rem(i, early // 2)
        own = j // (2 * heads)
        n = lax.rem(m, per_part)
        d_q = (
            start * (i // (early // 2))
            + is_far * (seq - 1 - m // per_part)
            + tail * (lax.rem(m, 4) // 2)
        )
        h = start * (1 - own) * (j // 2) + is_far * (n // seq) + tail * (1 + m // 4)
        d_k = (
            start * ((1 - own) * (2 + lax.rem(j, 2)) + own * (j - 2 * heads))
            + is_far * lax.rem(m, seq)
            + tail * lax.rem(m, 2)
        )
        return me ^ d_q, h, me ^ d_k

    def receive(d):
        g_copy(d).wait_recv()
        prepare(me ^ d)

    def far_states_grads():
        for d in range(1, seq):
            g_copy(d).wait_send()
        for d in far:
            for h in range(heads):
                fill(me ^ d, h)
            states_part(me ^ d)
            dx_copy(d).start()

    far_done = after(early + 2 * per_part - 1)
    hooks = [
        (before(early // 2), lambda: receive(1)),
        (before(early), lambda: receive(far[0])),
        (before(early + per_part), lambda: receive(far[1])),
        (far_done, far_states_grads),
        (far_done, lambda: emit(0)),
    ]
    if split:
        hooks += [
            (1, reduce_side),
            (3, lambda: reduce_cross(0)),
            (3, reduce_vec),
            (4, lambda: reduce_cross(1)),
            (5, lambda: reduce_cross(2)),
            (7, lambda: reduce_cross(3)),
            (10, reduce_z),
        ]
    d_in[me] = c_grad[at(me, group)]
    prepare(me)
    w_rows[...] = jnp.concatenate(
        [
            w_group[kind, :, h * HDIM : (h + 1) * HDIM].astype(F32)
            for h in range(heads)
            for kind in range(3)
        ],
        axis=1,
    ).astype(BF16)
    run(
        4 * per_part,
        place_backward,
        weigh,
        gather_grads,
        (p0, s0),
        (p1, s1),
        hooks,
        lambda: emit(1),
        unroll,
    )
    emit(2)
    states_part(me ^ 1)
    dx_copy(1).start()
    states_part(me)
    dx_r[at(me, group)] = dx_s[at(me, group)]
    if split:
        reduce_x()

        @pl.when(owner)
        def _():
            for h in range(heads):
                value = qkv_s[h, my_slot].astype(F32)
                for e in range(1, n_dp):
                    src = lax.rem(my_dp + e, n_dp)
                    remote(
                        qkv_s.at[h, 0],
                        qkv_r.at[h, src],
                        r.q1_send.at[h, 0],
                        r.q1_recv.at[h, src],
                        dp=src,
                    ).wait_recv()
                    value += qkv_r[h, src].astype(F32)
                qkv_out[h] = value.astype(BF16)
                for d in range(1, seq):
                    qkv_share(h, d).start()

    for d in range(1, seq):
        dx_copy(d).wait_recv()
    for c in range(width // LANES):
        span = slice(c * LANES, (c + 1) * LANES)
        r.states_grad[:, span] = (dx_r[span].astype(F32) + grad_mid[span]).astype(BF16).T


    for d in range(1, seq):
        x_copy(d).wait_send()
        c_copy(d).wait_send()
        dx_copy(d).wait_send()
    if split:
        last_copy().wait()
        for h in range(heads):
            for t in range(per_group):
                when(me * per_group + t != my_dp, lambda: qkv_copy(h, t).wait_send())

        @pl.when(owner)
        def _():
            for h in range(heads):
                for d in range(1, seq):
                    qkv_share(h, d).wait_send()

        @pl.when(jnp.logical_not(owner))
        def _():
            for h in range(heads):
                qkv_share(h, 1).wait_recv()

        for e in range(1, n_dp):
            s_copy(e).wait_send()

        for g in range(2):

            @pl.when(holds(g))
            def _():
                for j in range(n_z - 1):
                    w_along(g, j).wait_send()

            w_across(g).wait_send()

            @pl.when(core != g)
            def _():
                when(jnp.logical_not(holds(g)), lambda: w_beside(g, 0, core).wait_send())
                w_beside(g, 1, core).wait_send()

        for copy in side_copies() + x_copies():
            copy.wait_send()
        vec_cross().wait_send()
        for j in range(n_z):
            cross_copy(j).wait_send()
        for j in range(n_z - 1):
            z_copy(j).wait_send()
            vz_copy(j).wait_send()


def layer(cfg, row, collective_id, inputs):
    c = cfg
    g, l, h, s, w, f = c.group, c.piece, c.heads, c.seq, c.width, c.hidden
    n_z = c.dp // 2
    sds = jax.ShapeDtypeStruct
    dma = pltpu.SemaphoreType.DMA
    vm = pltpu.VMEM
    outputs = dict(layer_out=sds((l, w), BF16), states_grad=sds((l, w), BF16))
    if c.split:
        outputs |= dict(
            od_out=sds((2, 3, c.half, w), F32),
            qkv_out=sds((h, c.shard, 4 * HDIM), BF16),
            vec_out=sds((16, w), F32),
        )
    else:
        outputs |= dict(
            g_all=sds((3, w, w), BF16),
            qkv_raw=sds((h, 3, g + AUG, HDIM), F32),
            vecs=sds((16, w), F32),
        )
    scratch = dict(
        x_own=vm((w, l), BF16),
        x_group=vm((s, g + AUG, l), BF16),
        w_group=vm((3, g, g), BF16),
        w_rows=vm((g, 3 * g), BF16),
        w_pad=vm((3, g + AUG, h * LANES), BF16),
        q_t=vm((h, s, LANES, l), BF16),
        k_n=vm((h, s, l, LANES), BF16),
        k_t=vm((h, s, HDIM, l), BF16),
        v_n=vm((h, s, l, LANES), BF16),
        context_s=vm((s, g, l), BF16),
        context_r=vm((w, l), BF16),
        tops=vm((h * s, 1, l), F32),
        gathered=vm((h * s * (HDIM + AUG), l), F32),
        cols=vm((w, 16), F32),
        vcols=vm((w, LANES), F32),
        wide=vm((4 * w, l), F32),
        slim=vm((2 * f, l), BF16),
        c_grad=vm((w, l), BF16),
        d_in=vm((s, g, l), BF16),
        dx_r=vm((w, l), BF16),
        low=vm((GROUPS * (g + AUG) + w, l), BF16),
        late_sem=dma((2,)),
        x_send=dma((s,)),
        x_recv=dma((s,)),
        c_send=dma((s,)),
        c_recv=dma((s,)),
        g_send=dma((s,)),
        g_recv=dma((s,)),
        dx_send=dma((s,)),
        dx_recv=dma((s,)),
    )
    if c.split:
        unit = (3, c.half, w)
        vec = (16, w)
        scratch |= dict(
            wo=vm((w, w), BF16),
            w_up=vm((w, w), BF16),
            wd=vm((w, f // GROUPS), BF16),
            smalls=vm((c.dp, 16, LANES), F32),
            pack=vm((c.dp, 2) + unit, BF16),
            w_in=vm((2, c.per_group, 2, c.half, 3 * g), BF16),
            vecs=vm(vec, F32),
            side=vm((c.dp,) + unit, BF16),
            cross=vm((n_z,) + unit, BF16),
            spread_z=vm((n_z,) + unit, BF16),
            spread_v=vm((n_z,) + vec, F32),
            x_mine=vm(unit, BF16),
            x_theirs=vm(unit, BF16),
            vec_side=vm(vec, F32),
            vec_mine=vm(vec, F32),
            vec_cross=vm(vec, F32),
            vec_sum=vm(vec, F32),
            vec_z=vm(vec, F32),
            vec_x=vm(vec, F32),
            qkv_s=vm((h, c.per_group, c.shard, 4 * HDIM), BF16),
            qkv_r=vm((h, c.dp, c.shard, 4 * HDIM), BF16),
            s_send=dma((c.dp,)),
            s_recv=dma((c.dp,)),
            w_send=dma((2, n_z + 1)),
            w_recv=dma((2, 2)),
            wb_send=dma((2,)),
            wb_recv=dma((2,)),
            hop_send=dma((3, c.dp)),
            hop_recv=dma((c.dp,)),
            sib_send=dma((c.dp,)),
            sib_recv=dma((c.dp,)),
            red_send=dma((7,)),
            red_recv=dma((7,)),
            cross_send=dma((n_z,)),
            cross_recv=dma((n_z,)),
            z_send=dma((n_z,)),
            z_recv=dma((n_z,)),
            vz_send=dma((n_z,)),
            vz_recv=dma((n_z,)),
            q1_send=dma((h, c.per_group)),
            q1_recv=dma((h, c.dp)),
            q2_send=dma((h, s)),
            q2_recv=dma((h,)),
        )
    names = tuple(inputs) + tuple(outputs) + tuple(scratch)
    vmem = pl.BlockSpec(memory_space=pltpu.VMEM)
    hbm = pl.BlockSpec(memory_space=pl.ANY)
    special = dict(teacher=hbm, out_grad=hbm, lengths=pl.BlockSpec(memory_space=pltpu.SMEM))
    results = pl.pallas_call(
        functools.partial(layer_kernel, cfg, row, names),
        out_shape=list(outputs.values()),
        in_specs=[special.get(name, vmem) for name in inputs],
        out_specs=[vmem] * len(outputs),
        scratch_shapes=list(scratch.values()),
        compiler_params=pltpu.CompilerParams(
            collective_id=collective_id, has_side_effects=True, vmem_limit_bytes=VMEM_LIMIT
        ),
        name="layer",
    )(*inputs.values())
    return dict(zip(outputs, results, strict=True))


def deliver_kernel(cfg, layer_in, states_in, qkv, od, vec, *refs):
    outs = refs
    my_dp = lax.axis_index("dp")
    shard, width, half = cfg.shard, cfg.width, cfg.half
    outs[0][...] = layer_in[...]
    outs[1][...] = states_in[...]
    qw, kw, vw, ow, uw, dw = outs[2:8]
    parts = [
        jnp.concatenate(
            [qkv[h, :, k * HDIM : (k + 1) * HDIM].astype(F32) for h in range(cfg.heads)], axis=1
        )
        for k in range(4)
    ]
    for ref, part in zip((qw, kw, vw), parts[:3], strict=True):
        ref[...] = part
    for c in range(2):
        rows = slice(c * half, (c + 1) * half)
        ow[rows] = od[c, 0]
        uw[rows] = od[c, 1]
        for k in range(2):
            dw[(2 * c + k) * half : (2 * c + k + 1) * half] = od[
                c, 2, :, k * 4 * shard : (k + 1) * 4 * shard
            ]
    slot = lax.rem(my_dp, cfg.per_group)
    mine = parts[3][0:8, 0:shard]
    for t in range(1, cfg.per_group):
        mine = jnp.where(slot == t, parts[3][0:8, t * shard : (t + 1) * shard], mine)
    outs[8][...] = mine[0]
    outs[9][...] = mine[2]
    turned = pltpu.roll(vec[0:8], lax.rem(width - my_dp * shard, width), 1)
    for n in range(6):
        outs[10 + n][...] = turned[n, 0:shard]
    outs[16][...] = vec[
        pl.ds(8 + my_dp // cfg.per_group, 1),
        pl.ds(pl.multiple_of(slot * 4 * shard, LANES), 4 * shard),
    ][0]
    outs[17][0] = vec[12, 0]


def deliver(cfg, *args):
    sds = jax.ShapeDtypeStruct
    shard, width, group = cfg.shard, cfg.width, cfg.group
    out_shape = [sds(a.shape, a.dtype) for a in args[:2]]
    out_shape += [sds((shard, group), F32)] * 3 + [sds((shard, width), F32)] * 2
    out_shape += [sds((group, 4 * shard), F32)] + [sds((shard,), F32)] * 8
    out_shape += [sds((4 * shard,), F32), sds((1,), F32)]
    vmem = pl.BlockSpec(memory_space=pltpu.VMEM)
    return pl.pallas_call(
        functools.partial(deliver_kernel, cfg),
        out_shape=out_shape,
        in_specs=[vmem] * len(args),
        out_specs=[vmem] * (len(out_shape) - 1) + [pl.BlockSpec(memory_space=pltpu.SMEM)],
        name="deliver",
    )(*args)


def local(
    states,
    lengths,
    teacher,
    out_grad,
    q_weight,
    k_weight,
    v_weight,
    q_bias,
    v_bias,
    o_weight,
    o_bias,
    attn_gain,
    attn_bias,
    up_weight,
    up_bias,
    down_weight,
    down_bias,
    ffn_gain,
    ffn_bias,
):
    row_count, piece, width = states.shape
    n_dp, n_seq = lax.axis_size("dp"), lax.axis_size("seq")
    me, my_dp = lax.axis_index("seq"), lax.axis_index("dp")
    shard = q_bias.shape[0]
    hidden = up_bias.shape[0] * n_dp
    cfg = Config(n_dp, n_seq, piece, width, hidden, shard)
    cfg.rows = row_count
    group = cfg.group

    if not cfg.split:

        def pad(v):
            return jnp.pad(v.astype(F32), ((0, 0), (0, LANES - v.shape[1])))

        vectors = (q_bias, v_bias, o_bias, attn_gain, attn_bias, down_bias, ffn_gain, ffn_bias)
        small = jnp.concatenate(
            [
                pad(jnp.stack(vectors)),
                pad(up_bias.reshape(4, shard)),
                jnp.broadcast_to(lengths.astype(F32)[:, None], (row_count, LANES)),
                jnp.zeros((4 - row_count, LANES), F32),
            ]
        )
        smalls = lax.all_gather(small, "dp", axis=0)
        qkv = jnp.stack((q_weight, k_weight, v_weight))
        qkv = lax.all_gather(qkv, "dp", axis=1, tiled=True)
        w_group_in = lax.dynamic_slice(qkv, (0, me * group, 0), (3, group, group))
        wo = lax.all_gather(o_weight, "dp", axis=0, tiled=True)
        wu = lax.all_gather(up_weight, "dp", axis=0, tiled=True)
        wd = lax.all_gather(down_weight, "dp", axis=0, tiled=True)
        wd = wd.reshape(GROUPS, -1, group).transpose(0, 2, 1).reshape(width, -1)

    results = []
    for n in range(row_count):
        inputs = dict(states=states[n], teacher=teacher[n], out_grad=out_grad[n])
        if cfg.split:
            inputs |= dict(
                wq=q_weight,
                wk=k_weight,
                wv=v_weight,
                ow=o_weight,
                uw=up_weight,
                dw=down_weight.T,
                qb=q_bias,
                vb=v_bias,
                ob=o_bias,
                ag=attn_gain,
                ab=attn_bias,
                db=down_bias,
                fg=ffn_gain,
                fb=ffn_bias,
                ub=up_bias,
                lengths=lengths,
            )
        else:
            inputs |= dict(smalls=smalls, w_all=w_group_in, wo=wo, w_up=wu, wd=wd)
        results.append(layer(cfg, n, n, inputs))

    def summed(name):
        first = results[0][name]
        if row_count == 1:
            return first
        return sum((item[name].astype(F32) for item in results[1:]), first.astype(F32))

    if cfg.split:
        heavy = [jnp.stack([item[n] for item in results]) for n in ("layer_out", "states_grad")]
        out = deliver(cfg, *heavy, summed("qkv_out"), summed("od_out"), summed("vec_out"))
        grad_qw, grad_kw, grad_vw, grad_ow, grad_uw, grad_dw = out[2:8]
        vectors = out[8:17]
        return (
            (out[0], out[17].reshape(()), out[1], grad_qw, grad_kw, grad_vw)
            + (vectors[0], vectors[1], grad_ow, *vectors[2:5], grad_uw, vectors[8])
            + (grad_dw.T, *vectors[5:8])
        )

    layer_out = jnp.stack([item["layer_out"] for item in results])
    states_grad = jnp.stack([item["states_grad"] for item in results])
    qkv_g, g_all, vecs = (summed(n).astype(F32) for n in ("qkv_raw", "g_all", "vecs"))
    qkv_g = qkv_g.transpose(1, 2, 0, 3).reshape(3, group + AUG, group)
    whole = jnp.zeros((3, width + GROUPS * AUG, group), F32)
    whole = lax.dynamic_update_slice(whole, qkv_g[:, :group], (0, me * group, 0))
    whole = lax.dynamic_update_slice(whole, qkv_g[:, group:], (0, width + me * AUG, 0))
    whole, g_all, vec = lax.psum((whole, g_all, vecs), ("dp", "seq"))
    qkv = lax.dynamic_slice(whole, (0, my_dp * shard, 0), (3, shard, group))
    biases = whole[:, width::AUG].reshape(3, width)
    grad_qb = lax.dynamic_slice(biases[0], (my_dp * shard,), (shard,))
    grad_vb = lax.dynamic_slice(biases[2], (my_dp * shard,), (shard,))
    g_ou = lax.dynamic_slice(g_all[:2], (0, my_dp * shard, 0), (2, shard, width))
    g_d = g_all[2].reshape(GROUPS, group, -1).transpose(0, 2, 1).reshape(-1, group)
    grad_dw = lax.dynamic_slice(g_d, (my_dp * 4 * shard, 0), (4 * shard, group))
    mine = lax.dynamic_slice(vec[:6], (0, my_dp * shard), (6, shard))
    grad_ub = lax.dynamic_slice(vec[8:12].reshape(-1), (my_dp * 4 * shard,), (4 * shard,))
    return (
        (layer_out, vec[12, 0], states_grad, qkv[0], qkv[1], qkv[2], grad_qb, grad_vb, g_ou[0])
        + (mine[0], mine[1], mine[2], g_ou[1], grad_ub, grad_dw, mine[3], mine[4], mine[5])
    )


def solution(mesh):
    rows3 = P("dp", "seq", None)
    matrix = P("dp", None)
    vector = P("dp")
    return jax.shard_map(
        local,
        mesh=mesh,
        in_specs=(rows3, vector, rows3, rows3)
        + (matrix,) * 3
        + (vector,) * 2
        + (matrix,)
        + (vector,) * 3
        + (matrix, vector, matrix)
        + (vector,) * 3,
        out_specs=(rows3, P(), rows3)
        + (matrix,) * 3
        + (vector,) * 2
        + (matrix,)
        + (vector,) * 3
        + (matrix, vector, matrix)
        + (vector,) * 3,
        check_vma=False,
    )
```

```python
import functools
import math
import types

import jax
import jax.numpy as jnp
from jax import lax
from jax.experimental import pallas as pl
from jax.experimental.pallas import tpu as pltpu
from jax.sharding import PartitionSpec as P

HDIM = 64
GROUPS = 4
EPSILON = 1e-12
NEG_FILL = -1e30
LANES = 128
AUG = 16
LOG2E = 1.4426950408889634
MESH = pl.DeviceIdType.MESH
F32 = jnp.float32
BF16 = jnp.bfloat16
VMEM_LIMIT = 61 * 1024 * 1024


def mm(left, right, left_dim, right_dim):
    return lax.dot_general(
        left, right, (((left_dim,), (right_dim,)), ((), ())), preferred_element_type=F32
    )


def iota(shape, dim):
    return lax.broadcasted_iota(jnp.int32, shape, dim)


def remote(src, dst, send_sem, recv_sem, **where):
    return pltpu.make_async_remote_copy(
        src_ref=src,
        dst_ref=dst,
        send_sem=send_sem,
        recv_sem=recv_sem,
        device_id=where,
        device_id_type=MESH,
    )


def three_parts(row):
    high = row.astype(BF16)
    rest = row - high.astype(F32)
    middle = rest.astype(BF16)
    low = (rest - middle.astype(F32)).astype(BF16)
    return high, middle, low


class Config:
    def __init__(self, dp, seq, piece, width, hidden, shard):
        self.dp, self.seq, self.piece, self.width, self.hidden, self.shard = (
            dp,
            seq,
            piece,
            width,
            hidden,
            shard,
        )
        self.slots = piece * seq
        self.group = width // GROUPS
        self.heads = self.group // HDIM
        self.per_group = dp // GROUPS
        self.split = shard % 32 == 0 and seq == 4 and dp == 8
        self.half = shard // 2
        self.quarter = hidden // dp // 4


def greet(cfg, me, my_dp):
    barrier = pltpu.get_barrier_semaphore()
    count = cfg.seq - 1
    for d in range(1, cfg.seq):
        pl.semaphore_signal(barrier, inc=1, device_id={"seq": me ^ d}, device_id_type=MESH)
    if cfg.split:
        count += cfg.dp - 1
        for e in range(1, cfg.dp):
            pl.semaphore_signal(
                barrier, inc=1, device_id={"dp": lax.rem(my_dp + e, cfg.dp)}, device_id_type=MESH
            )
    return lambda: pl.semaphore_wait(barrier, count)


def layer_kernel(cfg, row, names, *refs):
    r = types.SimpleNamespace(**dict(zip(names, refs, strict=True)))
    split = cfg.split
    me = lax.axis_index("seq")
    my_dp = lax.axis_index("dp")
    piece, width, group, heads, seq = cfg.piece, cfg.width, cfg.group, cfg.heads, cfg.seq
    shard, half, n_dp, per_group = cfg.shard, cfg.half, cfg.dp, cfg.per_group
    hid = cfg.hidden // GROUPS
    n_z = n_dp // 2
    core = lax.rem(me, 2)
    my_z, my_y = my_dp // 2, lax.rem(my_dp, 2)
    far = [d for d in range(seq - 1, 1, -1)]

    states = r.states
    teacher, out_grad = r.states_grad, r.layer_out
    late = [
        pltpu.make_async_copy(r.teacher, teacher, r.late_sem.at[0]),
        pltpu.make_async_copy(r.out_grad, out_grad, r.late_sem.at[1]),
    ]
    x_own, x_group, w_group, w_pad, smalls = (
        r.x_own,
        r.x_group,
        r.w_group,
        r.w_pad,
        r.smalls,
    )
    q_t, k_n, k_t, v_n = r.q_t, r.k_n, r.k_t, r.v_n
    context_s, context_r = r.context_s, r.context_r
    cols, vcols = r.cols, r.vcols
    wide, slim = r.wide, r.slim
    wo, w_up, wd = r.wo, r.w_up, r.wd
    c_grad, d_in, dx_r = r.c_grad, r.d_in, r.dx_r
    dx_s = c_grad
    tall1 = group + AUG
    low = r.low
    low2 = low.at[GROUPS * tall1 :]

    def low1(g, start, size):
        return pl.ds(pl.multiple_of(g * tall1 + start, AUG), size)

    def d_aug(h, t, start, size):
        return pl.ds(pl.multiple_of((h * seq + t) * LANES + start, HDIM), size)

    score0, score1 = wide.at[0:piece], wide.at[piece : 2 * piece]
    gathered = r.gathered
    v1, first, v2, seed = (wide.at[i * width : (i + 1) * width] for i in range(4))
    dq, dk, dv = (wide.at[i * width : (i + 1) * width] for i in range(3))
    act, slope = slim.at[0 : cfg.hidden], slim.at[cfg.hidden : 2 * cfg.hidden]
    p0, p1, s0, s1 = (slim.at[i * piece : (i + 1) * piece] for i in range(4))
    d_t = slope

    def at(i, n):
        return pl.ds(pl.multiple_of(i * n, n), n)

    def loop(count, body, *init):
        return lax.fori_loop(0, count, lambda i, c: body(i, *c), tuple(init))

    def sub(v):
        return jnp.sum(v, axis=0, keepdims=True)


    def to_seq(sems, src, dst, d):
        return remote(src, dst, sems[0].at[d], sems[1].at[d], seq=me ^ d)

    def x_copy(d):
        return to_seq((r.x_send, r.x_recv), x_own.at[at(me ^ d, group)], x_group.at[me, pl.ds(0, group)], d)

    def c_copy(d):
        return to_seq((r.c_send, r.c_recv), context_s.at[me ^ d], context_r.at[at(me, group)], d)

    def g_copy(d):
        return to_seq((r.g_send, r.g_recv), c_grad.at[at(me ^ d, group)], d_in.at[me], d)

    def dx_copy(d):
        return to_seq((r.dx_send, r.dx_recv), dx_s.at[at(me ^ d, group)], dx_r.at[at(me, group)], d)

    if split:
        pack = r.pack
        w_in = r.w_in
        my_slot = lax.rem(my_dp, per_group)

        def s_copy(e):
            return remote(
                smalls.at[my_dp],
                smalls.at[my_dp],
                r.s_send.at[e],
                r.s_recv.at[e],
                dp=lax.rem(my_dp + e, n_dp),
            )

        first_group = me - core

        def w_ref(g):
            return w_in.at[g, my_y, core]

        def w_along(g, j):
            z = lax.rem(my_z + n_z - 1 - j, n_z)
            return remote(
                w_ref(g), w_ref(g), r.w_send.at[g, j], r.w_recv.at[g, 0], dp=2 * z + my_y
            )

        def w_across(g):
            return remote(
                w_ref(g), w_ref(g), r.w_send.at[g, n_z], r.w_recv.at[g, 1], dp=my_dp + 1 - 2 * my_y
            )

        def w_over(g):
            ref = w_in.at[g, 1 - my_y, core]
            return remote(ref, ref, r.w_send.at[g, n_z], r.w_recv.at[g, 1], dp=my_dp)

        def w_beside(g, part, half_of):
            ref = w_in.at[g, my_y if part == 0 else 1 - my_y, half_of]
            return remote(ref, ref, r.wb_send.at[part], r.wb_recv.at[part], seq=me ^ 1)

        def holds(g):
            return my_z == first_group + g

        def hop(kind, i, **where):
            ref = pack.at[i, core]
            return remote(ref, ref, r.hop_send.at[kind, i], r.hop_recv.at[i], **where)

        def up(i):
            return hop(0, i, dp=my_dp + 2)

        def down(i):
            return hop(1, i, dp=my_dp - 2)

        def across(i):
            return hop(2, i, dp=my_dp + 1 - 2 * my_y)

        def beside(i):
            ref = pack.at[i, core]
            return remote(ref, ref, r.sib_send.at[i], r.sib_recv.at[i], seq=me ^ 1)

        def when(condition, fn):
            pl.when(condition)(fn)

        def gather_start():
            when(my_z < n_z - 1, lambda: up(my_dp).start())
            when(my_z > 0, lambda: down(my_dp).start())

        def gather_z(k):
            below, above = my_dp - 2 * k, my_dp + 2 * k

            @pl.when(my_z >= k)
            def _():
                hop(0, below, dp=my_dp).wait_recv()
                when(my_z < n_z - 1, lambda: up(below).start())
                across(below).start()
                beside(below).start()

            @pl.when(my_z + k < n_z)
            def _():
                hop(0, above, dp=my_dp).wait_recv()
                when(my_z > 0, lambda: down(above).start())
                across(above).start()
                beside(above).start()

        def gather_y(k):
            other = my_dp + 1 - 2 * my_y

            def take(i):
                hop(2, i, dp=my_dp).wait_recv()
                beside(i).start()

            if k == 0:
                take(other)
            else:
                when(my_z >= k, lambda: take(other - 2 * k))
                when(my_z + k < n_z, lambda: take(other + 2 * k))

        def gather_end():
            for e in range(1, n_dp):
                copy = beside(lax.rem(my_dp + e, n_dp))
                copy.wait()

            when(my_z < n_z - 1, lambda: up(my_dp).wait_send())
            when(my_z > 0, lambda: down(my_dp).wait_send())
            across(my_dp).wait_send()
            for k in range(1, n_z):
                below, above = my_dp - 2 * k, my_dp + 2 * k

                @pl.when(my_z >= k)
                def _():
                    when(my_z < n_z - 1, lambda: up(below).wait_send())
                    across(below).wait_send()

                @pl.when(my_z + k < n_z)
                def _():
                    when(my_z > 0, lambda: down(above).wait_send())
                    across(above).wait_send()


    wait_entry = greet(cfg, me, my_dp)
    for c in range(0, width, LANES):
        x_own[c : c + LANES] = states[:, c : c + LANES].T
    if split:
        for c in range(2):
            pack[my_dp, c, 0] = r.ow[c * half : (c + 1) * half]
            pack[my_dp, c, 1] = r.uw[c * half : (c + 1) * half]
            for k in range(2):
                pack[my_dp, c, 2, :, k * 4 * shard : (k + 1) * 4 * shard] = r.dw[
                    (2 * c + k) * half : (2 * c + k + 1) * half
                ]
        smalls[my_dp] = jnp.zeros((16, LANES), F32)
        for n, ref in enumerate((r.qb, r.vb, r.ob, r.ag, r.ab, r.db, r.fg, r.fb)):
            smalls[my_dp, n : n + 1, 0:shard] = ref[...].reshape(1, shard).astype(F32)
        up_bias = r.ub[...].reshape(1, 4 * shard).astype(F32)
        for n in range(4):
            smalls[my_dp, 8 + n : 9 + n, 0:shard] = up_bias[:, n * shard : (n + 1) * shard]
        for n in range(cfg.rows):
            smalls[my_dp, 12 + n : 13 + n] = jnp.full((1, LANES), r.lengths[n].astype(F32))

        for g in range(2):

            @pl.when(holds(g))
            def _():
                for c in range(2):
                    rows = slice(c * half, (c + 1) * half)
                    w_in[g, my_y, c] = jnp.concatenate(
                        [ref[rows].astype(F32) for ref in (r.wq, r.wk, r.wv)], axis=1
                    ).astype(BF16)

    wait_entry()
    if split:
        for e in range(1, n_dp):
            s_copy(e).start()

        for g in range(2):

            @pl.when(holds(g))
            def _():
                for j in range(n_z - 1):
                    w_along(g, j).start()
                w_across(g).start()

    for d in range(1, seq):
        x_copy(d).start()
    for copy in late:
        copy.start()
    x_group[me, 0:group] = x_own[at(me, group)]


    deep = HDIM + AUG
    tops = r.tops

    def sums(h, t):
        return pl.ds(pl.multiple_of((h * seq + t) * deep, AUG), deep)

    def clear_sums(i, unused):
        gathered[pl.ds(pl.multiple_of(i * deep, AUG), deep)] = jnp.zeros((deep, piece), F32)
        tops[i] = jnp.full((1, piece), NEG_FILL, F32)
        return (unused,)

    loop(heads * seq, clear_sums, 0)
    n_cols = heads * LANES
    if split:
        for n, g in enumerate((1 - core, core)):

            @pl.when(jnp.logical_not(holds(g)))
            def _():
                w_along(g, 0).wait_recv()
                w_across(g).start()
                if n == 0:
                    w_beside(g, 0, core).start()

        gather_start()
        for e in range(1, n_dp):
            s_copy(e).wait_recv()
    for i in range(n_dp):
        turned_small = smalls[i].T
        cols[i * shard : (i + 1) * shard] = turned_small[0:shard]
    vec_rows = jnp.zeros((AUG, n_cols), F32)
    lane = iota((LANES, n_cols), 1)
    source = iota((LANES, n_cols), 0)
    for t in range(per_group):
        spread = jnp.where(
            (((lane >> 7) * HDIM + (lane & 127)) == source + t * shard)
            & ((lane & 127) < HDIM)
            & (source < shard),
            1.0,
            0.0,
        ).astype(BF16)
        vec_rows += mm(smalls[me * per_group + t].astype(BF16), spread, 1, 0)
    row_id = iota((AUG, n_cols), 0)
    lane = iota((AUG, n_cols), 1) & 127
    zero = jnp.zeros((AUG, n_cols), F32)
    top_row = row_id == 0
    w_pad[0, group:] = jnp.where(top_row, vec_rows[0:1], zero).astype(BF16)
    ones_k = (top_row & (lane > HDIM) & (lane <= HDIM + 3)) | ((row_id == 1) & (lane == HDIM))
    w_pad[1, group:] = jnp.where(ones_k, 1.0, zero).astype(BF16)
    ones_v = (lane >= HDIM) & (lane < HDIM + 3)
    w_pad[2, group:] = jnp.where(top_row, jnp.where(ones_v, 1.0, vec_rows[1:2]), zero).astype(BF16)

    if split:
        for n, g in enumerate((1 - core, core)):
            w_over(g).wait_recv()
            if n == 0:
                w_beside(g, 1, core).start()
        across(my_dp).start()
        when(my_z != me, lambda: w_beside(core, 0, 1 - core).wait_recv())
        w_beside(core, 1, 1 - core).wait_recv()
        for t in range(per_group):
            for c in range(2):
                for kind in range(3):
                    w_group[kind, t * shard + c * half : t * shard + (c + 1) * half] = w_in[
                        core, t, c, :, kind * group : (kind + 1) * group
                    ]
    else:
        for kind in range(3):
            w_group[kind] = r.w_all[kind]
    lane = iota((group, n_cols), 1)
    spread = jnp.where(
        (((lane >> 7) * HDIM + (lane & 127)) == iota((group, n_cols), 0)) & ((lane & 127) < HDIM),
        1.0,
        0.0,
    ).astype(BF16)
    for kind in range(3):
        w_pad[kind, 0:group] = mm(w_group[kind], spread, 1, 0).astype(BF16)

    length = smalls[my_dp, 12 + row : 13 + row, 0:1]
    aug_row = iota((AUG, piece), 0)
    factor = LOG2E * HDIM**-0.5
    def v_t(h, t):
        return pl.ds(pl.multiple_of((h * seq + t) * deep, AUG), deep)

    def project(t):
        slot = (iota((AUG, piece), 1) + t * piece).astype(F32)
        mask = jnp.where(slot < length, 0.0, NEG_FILL)
        x_group[t, group:] = jnp.where(
            aug_row == 0, 1.0, jnp.where(aug_row == 1, mask, 0.0)
        ).astype(BF16)
        x = x_group[t]
        queries = mm(w_pad[0], x, 0, 0) * factor
        keys_t = mm(w_pad[1], x, 0, 0)
        values_t = mm(w_pad[2], x, 0, 0)
        keys_n = mm(x, w_pad[1], 0, 0)
        values_n = mm(x, w_pad[2], 0, 0)
        rest = jnp.where(iota((HDIM, piece), 0) == 0, 1.0, 0.0).astype(BF16)
        for h in range(heads):
            span = slice(h * LANES, h * LANES + HDIM)
            q_t[h, t, 0:HDIM] = queries[span].astype(BF16)
            q_t[h, t, HDIM:] = rest
            k_t[h, t] = keys_t[span].astype(BF16)
            slim[v_t(h, t)] = values_t[h * LANES : h * LANES + deep].astype(BF16)
            k_n[h, t] = keys_n[:, h * LANES : (h + 1) * LANES].astype(BF16)
            v_n[h, t] = values_n[:, h * LANES : (h + 1) * LANES].astype(BF16)


    per_part = seq * heads

    def run(count, place, first_part, last_part, a, b, hooks=(), rest=None, unroll=2):
        buffers = (a, b)
        first_part(a, *place(0))

        def several(u, unused):
            if hooks:
                due = u == hooks[0][0]
                for when_u, fn in hooks[1:]:
                    due = due | (u == when_u)

                @pl.when(due)
                def _():
                    for when_u, fn in hooks:
                        pl.when(u == when_u)(fn)

            for j in range(unroll):
                first_part(buffers[(j + 1) % 2], *place(unroll * u + j + 1))
                last_part(buffers[j % 2], *place(unroll * u + j))
            return (unused,)

        turns = (count - 1) // unroll
        loop(turns, several, 0)
        if rest is not None:
            rest()
        for i in range(turns * unroll, count - 1):
            first_part(buffers[(i + 1) % 2], *place(i + 1))
            last_part(buffers[i % 2], *place(i))
        last_part(buffers[(count - 1) % 2], *place(count - 1))

    unroll = 4

    def before(step):
        return (step - 1) // unroll

    def after(step):
        return step // unroll + 1

    def score(buffer, t, h, k):
        buffer[...] = mm(k_n[h, k], q_t[h, t], 1, 0)

    def absorb(buffer, t, h, k):
        i = h * seq + t
        old = tops[i]
        top = jnp.maximum(old, jnp.max(buffer[...], axis=0, keepdims=True))
        weights = jnp.exp2(buffer[...] - top).astype(BF16)
        tops[i] = top
        place = sums(h, t)
        gathered[place] = gathered[place] * jnp.exp2(old - top) + mm(slim[v_t(h, k)], weights, 1, 0)

    def settle(t):
        for h in range(heads):
            total = gathered[sums(h, t)]
            mass = total[HDIM : HDIM + 1]
            context_s[t, h * HDIM : (h + 1) * HDIM] = (total[0:HDIM] / mass).astype(BF16)
            parts = three_parts(-(tops[h * seq + t] + jnp.log2(mass)))
            value = jnp.where(aug_row == 0, 1.0, 0.0)
            for n, part in enumerate(parts):
                value = jnp.where(aug_row == n + 1, part.astype(F32), value)
            q_t[h, t, HDIM:deep] = value.astype(BF16)

    def place_forward(i):
        part, j = i // per_part, lax.rem(i, per_part)
        is_far, tail = lax.rem((part + 1) // 2, 2), part // 3
        d_q = is_far * (4 - part) + (1 - is_far) * (j // (2 * heads))
        h = is_far * (j // seq) + (1 - is_far) * (lax.rem(j, 2 * heads) // 2)
        d_k = is_far * lax.rem(j, seq) + (1 - is_far) * (lax.rem(j, 2) + 2 * tail)
        return me ^ d_q, h, me ^ d_k

    def far_states():
        for d in far:
            x_copy(d).wait_recv()
        loop(2, lambda i, unused: (project(me ^ (2 + i)), unused)[1:], 0)

    def far_context(d):
        settle(me ^ d)
        c_copy(d).start()

    hooks = [
        (before(per_part), far_states),
        (after(2 * per_part - 1), lambda: far_context(far[0])),
        (after(3 * per_part - 1), lambda: far_context(far[1])),
    ]
    if split:
        hooks += [
            (1, lambda: gather_z(1)),
            (3, lambda: gather_y(0)),
            (4, lambda: gather_z(2)),
            (6, lambda: gather_y(1)),
            (8, lambda: gather_z(3)),
            (9, lambda: gather_y(2)),
        ]
    project(me)
    x_copy(1).wait_recv()
    project(me ^ 1)
    run(4 * per_part, place_forward, score, absorb, score0, score1, hooks, unroll=unroll)
    settle(me ^ 1)
    c_copy(1).start()
    settle(me)
    context_r[at(me, group)] = context_s[me]
    if split:
        gather_y(3)
        gather_end()

        def unpack(i, unused):
            for c in range(2):
                wo[pl.ds(pl.multiple_of(i * shard + c * half, AUG), half)] = pack[i, c, 0]
                w_up[pl.ds(pl.multiple_of(i * shard + c * half, AUG), half)] = pack[i, c, 1]
                for k in range(2):
                    wd[
                        pl.ds(
                            pl.multiple_of(i // per_group * group + (2 * c + k) * half, AUG), half
                        ),
                        pl.ds(
                            pl.multiple_of(lax.rem(i, per_group) * 4 * shard, LANES), 4 * shard
                        ),
                    ] = pack[i, c, 2, :, k * 4 * shard : (k + 1) * 4 * shard]
            return (unused,)

        loop(n_dp, unpack, 0)


    vcols[...] = jnp.zeros_like(vcols)
    inv = 1.0 / width
    total = jnp.sum(smalls[:, 12:13, 0:1], axis=0)
    for n in range(1, cfg.rows):
        total += jnp.sum(smalls[:, 12 + n : 13 + n, 0:1], axis=0)
    slot = (iota((1, piece), 1) + me * piece).astype(F32)
    live = jnp.where(slot < length, 1.0, 0.0)
    coef = 2.0 / (total * width)
    zero_row = jnp.zeros((1, piece), F32)

    def col(i, n, which):
        return cols[at(i, n), which : which + 1]

    for d in range(1, seq):
        c_copy(d).wait_recv()

    step = 256

    raw0, raw1 = seed.at[0:step], seed.at[step : 2 * step]

    def attn_out(raw, i):
        raw[...] = mm(wo[:, at(i, step)], context_r[...], 0, 0)

    def add_states(raw, i):
        v = raw[...] + x_own[at(i, step)].astype(F32) + col(i, step, 2)
        v1[at(i, step)] = v
        tops[0] += sub(v)

    tops[0] = zero_row
    run(width // step, lambda i: (i,), attn_out, add_states, raw0, raw1)
    acc = tops[0]
    mean = acc * inv

    def center(ref):
        def body(g, acc):
            v = ref[at(g, group)] - mean
            ref[at(g, group)] = v
            return (acc + sub(v * v),)

        (acc,) = loop(GROUPS, body, zero_row)
        return lax.rsqrt(acc * inv + EPSILON)

    scale1 = center(v1)

    def norm1(g, unused):
        v = v1[at(g, group)] * scale1
        v1[at(g, group)] = v
        out = v * col(g, group, 3) + col(g, group, 4)
        first[at(g, group)] = out
        low[low1(g, 0, group)] = out.astype(BF16)
        low[low1(g, group, AUG)] = jnp.where(aug_row == 0, 1.0, 0.0).astype(BF16)
        return (unused,)

    loop(GROUPS, norm1, 0)

    def gelu(u):
        d = 1.0 + (0.3275911 * 0.7071067811865476) * jnp.abs(u)
        t = pltpu.reciprocal(d, approx=True)
        bell = jnp.exp2((u * u) * (-0.5 * LOG2E))
        poly = t * (
            0.127414796
            + t * (-0.142248368 + t * (0.7107068705 + t * (-0.7265760135 + t * 0.5307027145)))
        )
        tail = poly * bell
        phi = jnp.where(u >= 0.0, 1.0 - tail, tail)
        return u * phi, phi + u * bell * 0.3989422804014327

    bunch = max(1, LANES // math.gcd(LANES, 4 * shard) if (4 * shard) % LANES else 1)
    span4 = 4 * shard * bunch
    n_steps = n_dp // bunch
    steps_group = n_steps // GROUPS
    tall = span4 // 4

    raw0, raw1 = wide.at[2 * width : 2 * width + span4], wide.at[3 * width : 3 * width + span4]

    def expand(raw, i):
        g, c = i // steps_group, lax.rem(i, steps_group)
        raw[...] = mm(w_up[at(g, group), at(c, span4)], low[low1(g, 0, group)], 0, 0)

    def activate(raw, i):
        bias = jnp.concatenate(
            [cols[at(i * bunch + n, shard), 8 + b : 9 + b] for n in range(bunch) for b in range(4)],
            axis=0,
        )
        for b in range(4):
            part = slice(b * tall, (b + 1) * tall)
            out, grad = gelu(raw[part] + bias[part])
            place = pl.ds(pl.multiple_of((i * 4 + b) * tall, tall), tall)
            act[place] = out.astype(BF16)
            slope[place] = grad.astype(BF16)

    run(n_steps, lambda i: (i,), expand, activate, raw0, raw1)

    def clear_rows(count):
        for n in range(count):
            tops[n] = zero_row

    part0, part1 = seed.at[0:group], seed.at[group : 2 * group]

    def contract(raw, g):
        raw[...] = mm(wd[at(g, group)], act[at(g, hid)], 1, 0)

    def add_branch(raw, g):
        v = raw[...] + first[at(g, group)] + col(g, group, 5)
        v2[at(g, group)] = v
        tops[0] += sub(v)

    clear_rows(1)
    run(GROUPS, lambda g: (g,), contract, add_branch, part0, part1)
    acc = tops[0]
    mean = acc * inv
    scale2 = center(v2)

    for copy in late:
        copy.wait()
    loss, sum1, sum2 = zero_row, zero_row, zero_row
    for c in range(width // LANES):
        span = slice(c * LANES, (c + 1) * LANES)
        xhat = v2[span] * scale2
        v2[span] = xhat
        gain = cols[span, 6:7]
        full = xhat * gain + cols[span, 7:8]
        error = full - teacher[:, span].T.astype(F32)
        loss += sub(live * error * error)
        grad = live * (out_grad[:, span].T.astype(F32) + error * coef)
        r.layer_out[:, span] = full.astype(BF16).T
        vcols[span, 4:5] = jnp.sum(grad * xhat, axis=1, keepdims=True)
        vcols[span, 5:6] = jnp.sum(grad, axis=1, keepdims=True)
        grad = grad * gain
        seed[span] = grad
        sum1 += sub(grad)
        sum2 += sub(grad * xhat)
    sum1, sum2 = sum1 * inv, sum2 * inv

    def back2(g, unused):
        place = at(g, group)
        grad = scale2 * (seed[place] - sum1 - v2[place] * sum2)
        seed[place] = grad
        brief = grad.astype(BF16)
        low2[place] = brief
        vcols[place, 3:4] = jnp.sum(brief.astype(F32), axis=1, keepdims=True)
        return (unused,)

    loop(GROUPS, back2, 0)

    raw0, raw1 = v2.at[0:span4], v2.at[span4 : 2 * span4]

    def back_act(raw, i):
        g, c = i // steps_group, lax.rem(i, steps_group)
        raw[...] = mm(wd[at(g, group), at(c, span4)], low2[at(g, group)], 0, 0)

    def times_slope(raw, i):
        place = at(i, span4)
        slope[place] = (raw[...] * slope[place].astype(F32)).astype(BF16)

    run(n_steps, lambda i: (i,), back_act, times_slope, raw0, raw1)
    part0, part1 = v2.at[0:group], v2.at[group : 2 * group]

    def back_first(raw, g):
        raw[...] = mm(w_up[at(g, group)], slope[at(g, hid)], 1, 0)

    def add_first(raw, g):
        place = at(g, group)
        grad = seed[place] + raw[...]
        xhat = v1[place]
        vcols[place, 1:2] = jnp.sum(grad * xhat, axis=1, keepdims=True)
        vcols[place, 2:3] = jnp.sum(grad, axis=1, keepdims=True)
        grad = grad * col(g, group, 3)
        seed[place] = grad
        tops[0] += sub(grad)
        tops[1] += sub(grad * xhat)


    vecs = r.vecs
    if split:
        other_y = my_dp + 1 - 2 * my_y
        side, cross, spread_z, spread_v = r.side, r.cross, r.spread_z, r.spread_v
        od_out, vec_out = r.od_out, r.vec_out
        red_send, red_recv = r.red_send, r.red_recv

        def side_copies():
            return (
                remote(
                    pack.at[:, 1 - core, pl.ds(1, 2)],
                    side.at[:, pl.ds(1, 2)],
                    red_send.at[0],
                    red_recv.at[0],
                    seq=me ^ 1,
                ),
                remote(
                    pack.at[:, 1 - core, 0],
                    side.at[:, 0],
                    red_send.at[6],
                    red_recv.at[6],
                    seq=me ^ 1,
                ),
                remote(vecs, r.vec_side, red_send.at[1], red_recv.at[1], seq=me ^ 1),
            )

        def cross_copy(j):
            z = lax.rem(my_z + 1 + j, n_z)
            return remote(
                side.at[2 * z + 1 - my_y],
                cross.at[z],
                r.cross_send.at[z],
                r.cross_recv.at[z],
                dp=other_y,
            )

        def vec_cross():
            return remote(
                r.vec_mine, r.vec_cross, red_send.at[2], red_recv.at[2], dp=other_y
            )

        def z_copy(j):
            z = lax.rem(my_z + 1 + j, n_z)
            return remote(
                side.at[2 * z + my_y],
                spread_z.at[my_z],
                r.z_send.at[j],
                r.z_recv.at[j],
                dp=2 * z + my_y,
            )

        def vz_copy(j):
            z = lax.rem(my_z + 1 + j, n_z)
            return remote(
                r.vec_sum,
                spread_v.at[my_z],
                r.vz_send.at[j],
                r.vz_recv.at[j],
                dp=2 * z + my_y,
            )

        def x_copies():
            return (
                remote(
                    r.x_mine, r.x_theirs, red_send.at[3], red_recv.at[3], seq=me ^ 2
                ),
                remote(r.vec_z, r.vec_x, red_send.at[4], red_recv.at[4], seq=me ^ 2),
            )

        def last_copy():
            return remote(
                od_out.at[core], od_out.at[core], red_send.at[5], red_recv.at[5], seq=me ^ 1
            )

        def reduce_side():
            for copy in side_copies():
                copy.wait_recv()

            def add(i, unused):
                side[i] = pack[i, core] + side[i]
                return (unused,)

            loop(n_dp, add, 0)
            r.vec_mine[...] = vecs[...] + r.vec_side[...]
            vec_cross().start()
            for j in range(n_z):
                cross_copy(j).start()

        def reduce_cross(j):
            cross_copy(j).wait_recv()
            z = lax.rem(my_z + 1 + j, n_z)
            i = 2 * z + my_y
            side[i] = side[i] + cross[z]
            if j < n_z - 1:
                z_copy(j).start()

        def reduce_vec():
            vec_cross().wait_recv()
            value = r.vec_mine[...] + r.vec_cross[...]
            r.vec_sum[...] = value
            spread_v[my_z] = value
            for j in range(n_z - 1):
                vz_copy(j).start()

        def reduce_z():
            for j in range(n_z - 1):
                z_copy(j).wait_recv()
                vz_copy(j).wait_recv()
            spread_z[my_z] = side[my_dp]
            value = spread_z[0].astype(F32)
            vec = spread_v[0]
            for z in range(1, n_z):
                value += spread_z[z].astype(F32)
                vec += spread_v[z]
            r.x_mine[...] = value.astype(BF16)
            r.vec_z[...] = vec
            for copy in x_copies():
                copy.start()

        def reduce_x():
            for copy in x_copies():
                copy.wait_recv()
            od_out[core] = r.x_mine[...].astype(F32) + r.x_theirs[...].astype(F32)
            vec_out[...] = r.vec_z[...] + r.vec_x[...]
            last_copy().start()

    vecs[...] = jnp.zeros_like(vecs)
    for g in range(GROUPS):
        out = mm(low[low1(g, 0, tall1)], slope[g * hid : (g + 1) * hid], 1, 1)
        vecs[8 + g : 9 + g] = out[group : group + 1]
        if split:
            for t in range(per_group):
                for c in range(2):
                    base = shard * t + half * c
                    pack[g * per_group + t, c, 1] = out[base : base + half].astype(BF16)
        else:
            r.g_all[1, g * group : (g + 1) * group] = out[0:group].astype(BF16)
    clear_rows(2)
    run(GROUPS, lambda g: (g,), back_first, add_first, part0, part1)
    sum1, sum2 = tops[0] * inv, tops[1] * inv

    for g in range(GROUPS):
        out = mm(low2[g * group : (g + 1) * group], act[g * hid : (g + 1) * hid], 1, 1)
        if split:
            for t in range(per_group):
                for c in range(2):
                    for k in range(2):
                        pack[g * per_group + t, c, 2, :, k * 4 * shard : (k + 1) * 4 * shard] = (
                            out[
                                (2 * c + k) * half : (2 * c + k + 1) * half,
                                t * 4 * shard : (t + 1) * 4 * shard,
                            ].astype(BF16)
                        )
        else:
            r.g_all[2, g * group : (g + 1) * group] = out.astype(BF16)

    if split:
        side_copies()[0].start()

    def back1(g, unused):
        place = at(g, group)
        grad = scale1 * (seed[place] - sum1 - v1[place] * sum2)
        seed[place] = grad
        brief = grad.astype(BF16)
        low2[place] = brief
        vcols[place, 0:1] = jnp.sum(brief.astype(F32), axis=1, keepdims=True)
        return (unused,)

    loop(GROUPS, back1, 0)
    grad_mid = seed

    def back_context(i, unused):
        c_grad[at(i, step)] = mm(wo[at(i, step)], low2[...], 1, 0).astype(BF16)
        return (unused,)

    loop(width // step, back_context, 0)
    for d in [1] + far:
        g_copy(d).start()

    vecs[0:8] = vcols[...].T[0:8]
    mean_loss = jnp.sum(loss, axis=1, keepdims=True) / (total * width)
    vecs[12:13] = jnp.broadcast_to(mean_loss, (1, width))
    for j in range(2):
        rows = width // 2
        out = mm(context_r[j * rows : (j + 1) * rows], low2[...], 1, 1)
        if split:
            for t in range(n_dp // 2):
                for c in range(2):
                    base = shard * t + half * c
                    pack[j * (n_dp // 2) + t, c, 0] = out[base : base + half].astype(BF16)
        else:
            r.g_all[0, j * rows : (j + 1) * rows] = out.astype(BF16)

    if split:
        for copy in side_copies()[1:]:
            copy.start()


    def clear(i, unused):
        for ref in (dq, dk, dv):
            ref[at(i, HDIM)] = jnp.zeros((HDIM, piece), F32)
        return (unused,)

    loop(heads * seq, clear, 0)
    tail_row = iota((HDIM, piece), 0)

    def prepare(t):
        for h in range(heads):
            span = slice(h * HDIM, (h + 1) * HDIM)
            grad = d_in[t, span]
            low[d_aug(h, t, 0, HDIM)] = grad
            parts = three_parts(-sub(grad.astype(F32) * context_s[t, span].astype(F32)))
            value = jnp.zeros((HDIM, piece), F32)
            for n, part in enumerate(parts):
                value = jnp.where(tail_row == n, part.astype(F32), value)
            low[d_aug(h, t, HDIM, HDIM)] = value.astype(BF16)

    def rows_of(h, t):
        return at(h * seq + t, HDIM)

    def weigh(buffers, t, h, k):
        p, s = buffers
        weights = jnp.exp2(mm(q_t[h, t], k_n[h, k], 0, 1))
        p[...] = weights.astype(BF16)
        s[...] = (weights * mm(low[d_aug(h, t, 0, LANES)], v_n[h, k], 0, 1)).astype(BF16)

    def gather_grads(buffers, t, h, k):
        p, s = buffers
        dv[rows_of(h, k)] += mm(low[d_aug(h, t, 0, HDIM)], p[...], 1, 0)
        dk[rows_of(h, k)] += mm(q_t[h, t, 0:HDIM], s[...], 1, 0)
        dq[rows_of(h, t)] += mm(k_t[h, k], s[...], 1, 1)

    def fill(t, h):
        for kind, (ref, scale) in enumerate(((dq, HDIM**-0.5), (dk, 1.0 / LOG2E), (dv, 1.0))):
            place = pl.ds(pl.multiple_of(((t * heads + h) * 3 + kind) * HDIM, HDIM), HDIM)
            d_t[place] = (ref[rows_of(h, t)] * scale).astype(BF16)

    w_rows = r.w_rows

    def states_part(t):
        dx_s[at(t, group)] = mm(w_rows[...], d_t[at(t, 3 * group)], 1, 0).astype(BF16)

    if split:
        qkv_s, qkv_r, qkv_out = r.qkv_s, r.qkv_r, r.qkv_out
        owner = my_dp // per_group == me

        def qkv_copy(h, t):
            return remote(
                qkv_s.at[h, t],
                qkv_r.at[h, my_dp],
                r.q1_send.at[h, t],
                r.q1_recv.at[h, my_dp],
                dp=me * per_group + t,
            )

        def qkv_share(h, d):
            return remote(
                qkv_out.at[h], qkv_out.at[h], r.q2_send.at[h, d], r.q2_recv.at[h], seq=me ^ d
            )

    def emit(h):
        for d in range(2):
            fill(me ^ d, h)
        total = mm(x_group[0], d_t[at(h, 3 * HDIM)], 1, 1)
        for t in range(1, seq):
            total += mm(x_group[t], d_t[at(t * heads + h, 3 * HDIM)], 1, 1)
        if split:
            bias_rows = jnp.zeros((shard, HDIM), F32)
            bias_id = iota((shard, HDIM), 0)
            for kind in range(3):
                bias_rows = jnp.where(
                    bias_id == kind,
                    total[group : group + 1, kind * HDIM : (kind + 1) * HDIM],
                    bias_rows,
                )
            for t in range(per_group):
                qkv_s[h, t] = jnp.concatenate(
                    [total[t * shard : (t + 1) * shard], bias_rows], axis=1
                ).astype(BF16)
                when(me * per_group + t != my_dp, lambda: qkv_copy(h, t).start())
        else:
            for kind in range(3):
                r.qkv_raw[h, kind] = total[:, kind * HDIM : (kind + 1) * HDIM]

    early = 2 * (2 * heads + 2)
    shift = 2 * per_part - early

    def place_backward(i):
        part, m = (i + shift) // (2 * per_part), lax.rem(i + shift, 2 * per_part)
        is_far, tail = lax.rem(part, 2), part // 2
        start = (1 - is_far) * (1 - tail)
        j = lax.rem(i, early // 2)
        own = j // (2 * heads)
        n = lax.rem(m, per_part)
        d_q = (
            start * (i // (early // 2))
            + is_far * (seq - 1 - m // per_part)
            + tail * (lax.rem(m, 4) // 2)
        )
        h = start * (1 - own) * (j // 2) + is_far * (n // seq) + tail * (1 + m // 4)
        d_k = (
            start * ((1 - own) * (2 + lax.rem(j, 2)) + own * (j - 2 * heads))
            + is_far * lax.rem(m, seq)
            + tail * lax.rem(m, 2)
        )
        return me ^ d_q, h, me ^ d_k

    def receive(d):
        g_copy(d).wait_recv()
        prepare(me ^ d)

    def far_states_grads():
        for d in range(1, seq):
            g_copy(d).wait_send()
        for d in far:
            for h in range(heads):
                fill(me ^ d, h)
            states_part(me ^ d)
            dx_copy(d).start()

    far_done = after(early + 2 * per_part - 1)
    hooks = [
        (before(early // 2), lambda: receive(1)),
        (before(early), lambda: receive(far[0])),
        (before(early + per_part), lambda: receive(far[1])),
        (far_done, far_states_grads),
        (far_done, lambda: emit(0)),
    ]
    if split:
        hooks += [
            (1, reduce_side),
            (3, lambda: reduce_cross(0)),
            (3, reduce_vec),
            (4, lambda: reduce_cross(1)),
            (5, lambda: reduce_cross(2)),
            (7, lambda: reduce_cross(3)),
            (10, reduce_z),
        ]
    d_in[me] = c_grad[at(me, group)]
    prepare(me)
    w_rows[...] = jnp.concatenate(
        [
            w_group[kind, :, h * HDIM : (h + 1) * HDIM].astype(F32)
            for h in range(heads)
            for kind in range(3)
        ],
        axis=1,
    ).astype(BF16)
    run(
        4 * per_part,
        place_backward,
        weigh,
        gather_grads,
        (p0, s0),
        (p1, s1),
        hooks,
        lambda: emit(1),
        unroll,
    )
    emit(2)
    states_part(me ^ 1)
    dx_copy(1).start()
    states_part(me)
    dx_r[at(me, group)] = dx_s[at(me, group)]
    if split:
        reduce_x()

        @pl.when(owner)
        def _():
            for h in range(heads):
                value = qkv_s[h, my_slot].astype(F32)
                for e in range(1, n_dp):
                    src = lax.rem(my_dp + e, n_dp)
                    remote(
                        qkv_s.at[h, 0],
                        qkv_r.at[h, src],
                        r.q1_send.at[h, 0],
                        r.q1_recv.at[h, src],
                        dp=src,
                    ).wait_recv()
                    value += qkv_r[h, src].astype(F32)
                qkv_out[h] = value.astype(BF16)
                for d in range(1, seq):
                    qkv_share(h, d).start()

    for d in range(1, seq):
        dx_copy(d).wait_recv()
    for c in range(width // LANES):
        span = slice(c * LANES, (c + 1) * LANES)
        r.states_grad[:, span] = (dx_r[span].astype(F32) + grad_mid[span]).astype(BF16).T


    for d in range(1, seq):
        x_copy(d).wait_send()
        c_copy(d).wait_send()
        dx_copy(d).wait_send()
    if split:
        last_copy().wait()
        for h in range(heads):
            for t in range(per_group):
                when(me * per_group + t != my_dp, lambda: qkv_copy(h, t).wait_send())

        @pl.when(owner)
        def _():
            for h in range(heads):
                for d in range(1, seq):
                    qkv_share(h, d).wait_send()

        @pl.when(jnp.logical_not(owner))
        def _():
            for h in range(heads):
                qkv_share(h, 1).wait_recv()

        for e in range(1, n_dp):
            s_copy(e).wait_send()

        for g in range(2):

            @pl.when(holds(g))
            def _():
                for j in range(n_z - 1):
                    w_along(g, j).wait_send()

            w_across(g).wait_send()

            @pl.when(core != g)
            def _():
                when(jnp.logical_not(holds(g)), lambda: w_beside(g, 0, core).wait_send())
                w_beside(g, 1, core).wait_send()

        for copy in side_copies() + x_copies():
            copy.wait_send()
        vec_cross().wait_send()
        for j in range(n_z):
            cross_copy(j).wait_send()
        for j in range(n_z - 1):
            z_copy(j).wait_send()
            vz_copy(j).wait_send()


def layer(cfg, row, collective_id, inputs):
    c = cfg
    g, l, h, s, w, f = c.group, c.piece, c.heads, c.seq, c.width, c.hidden
    n_z = c.dp // 2
    sds = jax.ShapeDtypeStruct
    dma = pltpu.SemaphoreType.DMA
    vm = pltpu.VMEM
    outputs = dict(layer_out=sds((l, w), BF16), states_grad=sds((l, w), BF16))
    if c.split:
        outputs |= dict(
            od_out=sds((2, 3, c.half, w), F32),
            qkv_out=sds((h, c.shard, 4 * HDIM), BF16),
            vec_out=sds((16, w), F32),
        )
    else:
        outputs |= dict(
            g_all=sds((3, w, w), BF16),
            qkv_raw=sds((h, 3, g + AUG, HDIM), F32),
            vecs=sds((16, w), F32),
        )
    scratch = dict(
        x_own=vm((w, l), BF16),
        x_group=vm((s, g + AUG, l), BF16),
        w_group=vm((3, g, g), BF16),
        w_rows=vm((g, 3 * g), BF16),
        w_pad=vm((3, g + AUG, h * LANES), BF16),
        q_t=vm((h, s, LANES, l), BF16),
        k_n=vm((h, s, l, LANES), BF16),
        k_t=vm((h, s, HDIM, l), BF16),
        v_n=vm((h, s, l, LANES), BF16),
        context_s=vm((s, g, l), BF16),
        context_r=vm((w, l), BF16),
        tops=vm((h * s, 1, l), F32),
        gathered=vm((h * s * (HDIM + AUG), l), F32),
        cols=vm((w, 16), F32),
        vcols=vm((w, LANES), F32),
        wide=vm((4 * w, l), F32),
        slim=vm((2 * f, l), BF16),
        c_grad=vm((w, l), BF16),
        d_in=vm((s, g, l), BF16),
        dx_r=vm((w, l), BF16),
        low=vm((GROUPS * (g + AUG) + w, l), BF16),
        late_sem=dma((2,)),
        x_send=dma((s,)),
        x_recv=dma((s,)),
        c_send=dma((s,)),
        c_recv=dma((s,)),
        g_send=dma((s,)),
        g_recv=dma((s,)),
        dx_send=dma((s,)),
        dx_recv=dma((s,)),
    )
    if c.split:
        unit = (3, c.half, w)
        vec = (16, w)
        scratch |= dict(
            wo=vm((w, w), BF16),
            w_up=vm((w, w), BF16),
            wd=vm((w, f // GROUPS), BF16),
            smalls=vm((c.dp, 16, LANES), F32),
            pack=vm((c.dp, 2) + unit, BF16),
            w_in=vm((2, c.per_group, 2, c.half, 3 * g), BF16),
            vecs=vm(vec, F32),
            side=vm((c.dp,) + unit, BF16),
            cross=vm((n_z,) + unit, BF16),
            spread_z=vm((n_z,) + unit, BF16),
            spread_v=vm((n_z,) + vec, F32),
            x_mine=vm(unit, BF16),
            x_theirs=vm(unit, BF16),
            vec_side=vm(vec, F32),
            vec_mine=vm(vec, F32),
            vec_cross=vm(vec, F32),
            vec_sum=vm(vec, F32),
            vec_z=vm(vec, F32),
            vec_x=vm(vec, F32),
            qkv_s=vm((h, c.per_group, c.shard, 4 * HDIM), BF16),
            qkv_r=vm((h, c.dp, c.shard, 4 * HDIM), BF16),
            s_send=dma((c.dp,)),
            s_recv=dma((c.dp,)),
            w_send=dma((2, n_z + 1)),
            w_recv=dma((2, 2)),
            wb_send=dma((2,)),
            wb_recv=dma((2,)),
            hop_send=dma((3, c.dp)),
            hop_recv=dma((c.dp,)),
            sib_send=dma((c.dp,)),
            sib_recv=dma((c.dp,)),
            red_send=dma((7,)),
            red_recv=dma((7,)),
            cross_send=dma((n_z,)),
            cross_recv=dma((n_z,)),
            z_send=dma((n_z,)),
            z_recv=dma((n_z,)),
            vz_send=dma((n_z,)),
            vz_recv=dma((n_z,)),
            q1_send=dma((h, c.per_group)),
            q1_recv=dma((h, c.dp)),
            q2_send=dma((h, s)),
            q2_recv=dma((h,)),
        )
    names = tuple(inputs) + tuple(outputs) + tuple(scratch)
    vmem = pl.BlockSpec(memory_space=pltpu.VMEM)
    hbm = pl.BlockSpec(memory_space=pl.ANY)
    special = dict(teacher=hbm, out_grad=hbm, lengths=pl.BlockSpec(memory_space=pltpu.SMEM))
    results = pl.pallas_call(
        functools.partial(layer_kernel, cfg, row, names),
        out_shape=list(outputs.values()),
        in_specs=[special.get(name, vmem) for name in inputs],
        out_specs=[vmem] * len(outputs),
        scratch_shapes=list(scratch.values()),
        compiler_params=pltpu.CompilerParams(
            collective_id=collective_id, has_side_effects=True, vmem_limit_bytes=VMEM_LIMIT
        ),
        name="layer",
    )(*inputs.values())
    return dict(zip(outputs, results, strict=True))


def deliver_kernel(cfg, layer_in, states_in, qkv, od, vec, *outs):
    outs[0][...] = layer_in[...]
    outs[1][...] = states_in[...]
    pl.when((pl.program_id(0) == 0) & (pl.program_id(1) == 0))(
        lambda: deliver_rest(cfg, qkv, od, vec, outs)
    )


def deliver_rest(cfg, qkv, od, vec, outs):
    my_dp = lax.axis_index("dp")
    shard, width, half = cfg.shard, cfg.width, cfg.half
    qw, kw, vw, ow, uw, dw = outs[2:8]
    parts = [
        jnp.concatenate(
            [qkv[h, :, k * HDIM : (k + 1) * HDIM].astype(F32) for h in range(cfg.heads)], axis=1
        )
        for k in range(4)
    ]
    for ref, part in zip((qw, kw, vw), parts[:3], strict=True):
        ref[...] = part
    for c in range(2):
        rows = slice(c * half, (c + 1) * half)
        ow[rows] = od[c, 0]
        uw[rows] = od[c, 1]
        for k in range(2):
            dw[(2 * c + k) * half : (2 * c + k + 1) * half] = od[
                c, 2, :, k * 4 * shard : (k + 1) * 4 * shard
            ]
    slot = lax.rem(my_dp, cfg.per_group)
    mine = parts[3][0:8, 0:shard]
    for t in range(1, cfg.per_group):
        mine = jnp.where(slot == t, parts[3][0:8, t * shard : (t + 1) * shard], mine)
    outs[8][...] = mine[0]
    outs[9][...] = mine[2]
    turned = pltpu.roll(vec[0:8], lax.rem(width - my_dp * shard, width), 1)
    for n in range(6):
        outs[10 + n][...] = turned[n, 0:shard]
    outs[16][...] = vec[
        pl.ds(8 + my_dp // cfg.per_group, 1),
        pl.ds(pl.multiple_of(slot * 4 * shard, LANES), 4 * shard),
    ][0]
    outs[17][0] = vec[12, 0]


def deliver(cfg, *args):
    sds = jax.ShapeDtypeStruct
    shard, width, group = cfg.shard, cfg.width, cfg.group
    out_shape = [sds(a.shape, a.dtype) for a in args[:2]]
    out_shape += [sds((shard, group), F32)] * 3 + [sds((shard, width), F32)] * 2
    out_shape += [sds((group, 4 * shard), F32)] + [sds((shard,), F32)] * 8
    out_shape += [sds((4 * shard,), F32), sds((1,), F32)]
    rows, slots, _ = args[0].shape
    step = slots // 2 if slots % 32 == 0 else slots
    tiles = pl.BlockSpec((1, step, width), lambda i, j: (i, j, 0))

    def whole(a):
        return pl.BlockSpec(a.shape, lambda i, j: (0,) * len(a.shape))

    return pl.pallas_call(
        functools.partial(deliver_kernel, cfg),
        out_shape=out_shape,
        grid=(rows, slots // step),
        in_specs=[tiles] * 2 + [whole(a) for a in args[2:]],
        out_specs=[tiles] * 2
        + [whole(a) for a in out_shape[2:-1]]
        + [pl.BlockSpec((1,), lambda i, j: (0,), memory_space=pltpu.SMEM)],
        name="deliver",
    )(*args)


def local(
    states,
    lengths,
    teacher,
    out_grad,
    q_weight,
    k_weight,
    v_weight,
    q_bias,
    v_bias,
    o_weight,
    o_bias,
    attn_gain,
    attn_bias,
    up_weight,
    up_bias,
    down_weight,
    down_bias,
    ffn_gain,
    ffn_bias,
):
    row_count, piece, width = states.shape
    n_dp, n_seq = lax.axis_size("dp"), lax.axis_size("seq")
    me, my_dp = lax.axis_index("seq"), lax.axis_index("dp")
    shard = q_bias.shape[0]
    hidden = up_bias.shape[0] * n_dp
    cfg = Config(n_dp, n_seq, piece, width, hidden, shard)
    cfg.rows = row_count
    group = cfg.group

    if not cfg.split:

        def pad(v):
            return jnp.pad(v.astype(F32), ((0, 0), (0, LANES - v.shape[1])))

        vectors = (q_bias, v_bias, o_bias, attn_gain, attn_bias, down_bias, ffn_gain, ffn_bias)
        small = jnp.concatenate(
            [
                pad(jnp.stack(vectors)),
                pad(up_bias.reshape(4, shard)),
                jnp.broadcast_to(lengths.astype(F32)[:, None], (row_count, LANES)),
                jnp.zeros((4 - row_count, LANES), F32),
            ]
        )
        smalls = lax.all_gather(small, "dp", axis=0)
        qkv = jnp.stack((q_weight, k_weight, v_weight))
        qkv = lax.all_gather(qkv, "dp", axis=1, tiled=True)
        w_group_in = lax.dynamic_slice(qkv, (0, me * group, 0), (3, group, group))
        wo = lax.all_gather(o_weight, "dp", axis=0, tiled=True)
        wu = lax.all_gather(up_weight, "dp", axis=0, tiled=True)
        wd = lax.all_gather(down_weight, "dp", axis=0, tiled=True)
        wd = wd.reshape(GROUPS, -1, group).transpose(0, 2, 1).reshape(width, -1)

    results = []
    for n in range(row_count):
        inputs = dict(states=states[n], teacher=teacher[n], out_grad=out_grad[n])
        if cfg.split:
            inputs |= dict(
                wq=q_weight,
                wk=k_weight,
                wv=v_weight,
                ow=o_weight,
                uw=up_weight,
                dw=down_weight.T,
                qb=q_bias,
                vb=v_bias,
                ob=o_bias,
                ag=attn_gain,
                ab=attn_bias,
                db=down_bias,
                fg=ffn_gain,
                fb=ffn_bias,
                ub=up_bias,
                lengths=lengths,
            )
        else:
            inputs |= dict(smalls=smalls, w_all=w_group_in, wo=wo, w_up=wu, wd=wd)
        results.append(layer(cfg, n, n, inputs))

    def summed(name):
        first = results[0][name]
        if row_count == 1:
            return first
        return sum((item[name].astype(F32) for item in results[1:]), first.astype(F32))

    if cfg.split:
        heavy = [jnp.stack([item[n] for item in results]) for n in ("layer_out", "states_grad")]
        out = deliver(cfg, *heavy, summed("qkv_out"), summed("od_out"), summed("vec_out"))
        grad_qw, grad_kw, grad_vw, grad_ow, grad_uw, grad_dw = out[2:8]
        vectors = out[8:17]
        return (
            (out[0], out[17].reshape(()), out[1], grad_qw, grad_kw, grad_vw)
            + (vectors[0], vectors[1], grad_ow, *vectors[2:5], grad_uw, vectors[8])
            + (grad_dw.T, *vectors[5:8])
        )

    layer_out = jnp.stack([item["layer_out"] for item in results])
    states_grad = jnp.stack([item["states_grad"] for item in results])
    qkv_g, g_all, vecs = (summed(n).astype(F32) for n in ("qkv_raw", "g_all", "vecs"))
    qkv_g = qkv_g.transpose(1, 2, 0, 3).reshape(3, group + AUG, group)
    whole = jnp.zeros((3, width + GROUPS * AUG, group), F32)
    whole = lax.dynamic_update_slice(whole, qkv_g[:, :group], (0, me * group, 0))
    whole = lax.dynamic_update_slice(whole, qkv_g[:, group:], (0, width + me * AUG, 0))
    whole, g_all, vec = lax.psum((whole, g_all, vecs), ("dp", "seq"))
    qkv = lax.dynamic_slice(whole, (0, my_dp * shard, 0), (3, shard, group))
    biases = whole[:, width::AUG].reshape(3, width)
    grad_qb = lax.dynamic_slice(biases[0], (my_dp * shard,), (shard,))
    grad_vb = lax.dynamic_slice(biases[2], (my_dp * shard,), (shard,))
    g_ou = lax.dynamic_slice(g_all[:2], (0, my_dp * shard, 0), (2, shard, width))
    g_d = g_all[2].reshape(GROUPS, group, -1).transpose(0, 2, 1).reshape(-1, group)
    grad_dw = lax.dynamic_slice(g_d, (my_dp * 4 * shard, 0), (4 * shard, group))
    mine = lax.dynamic_slice(vec[:6], (0, my_dp * shard), (6, shard))
    grad_ub = lax.dynamic_slice(vec[8:12].reshape(-1), (my_dp * 4 * shard,), (4 * shard,))
    return (
        (layer_out, vec[12, 0], states_grad, qkv[0], qkv[1], qkv[2], grad_qb, grad_vb, g_ou[0])
        + (mine[0], mine[1], mine[2], g_ou[1], grad_ub, grad_dw, mine[3], mine[4], mine[5])
    )


def solution(mesh):
    rows3 = P("dp", "seq", None)
    matrix = P("dp", None)
    vector = P("dp")
    return jax.shard_map(
        local,
        mesh=mesh,
        in_specs=(rows3, vector, rows3, rows3)
        + (matrix,) * 3
        + (vector,) * 2
        + (matrix,)
        + (vector,) * 3
        + (matrix, vector, matrix)
        + (vector,) * 3,
        out_specs=(rows3, P(), rows3)
        + (matrix,) * 3
        + (vector,) * 2
        + (matrix,)
        + (vector,) * 3
        + (matrix, vector, matrix)
        + (vector,) * 3,
        check_vma=False,
    )
```
